32 devices in a mesh: grp: 8 (over z, core), fsdp: 4 (over y, x).
Axes of the slice: x: 2, y: 2, z: 4, core: 2. Of those that a mesh axis runs over, the one named last changes fastest.
Arguments:
- tokens: bfloat16 [8192, 2048], P(('grp', 'fsdp')), may hold values from -6 to 6
- cotangent: bfloat16 [8192, 2048], P(('grp', 'fsdp')), may hold values from -6 to 6
- segment: int32 [8192], P(('grp', 'fsdp')), may hold values from 0 to 55, as said below
- ancestry: int32 [8192, 3], P(('grp', 'fsdp')), may hold values from 0 to 55, as said below
- position: int32 [8192], P(('grp', 'fsdp')), may hold values from 0 to 767, as said below
- routes: int32 [8192, 4], P(('grp', 'fsdp')), may hold values from 0 to 7, all different within a row; in each aligned block of 256 rows (0 to 255, 256 to 511, ...) at most 160 rows name the same one
- attn_gain: bfloat16 [2048], P('fsdp'), may hold values from 0.5 to 1.5
- w_query: bfloat16 [2048, 2048], P('fsdp'), may hold values from -0.125 to 0.125
- w_key: bfloat16 [2048, 2048], P('fsdp'), may hold values from -0.125 to 0.125
- w_value: bfloat16 [2048, 2048], P('fsdp'), may hold values from -0.125 to 0.125
- b_query: bfloat16 [2048], P('fsdp'), may hold values from -1.75 to 1.75
- b_key: bfloat16 [2048], P('fsdp'), may hold values from -1.75 to 1.75
- b_value: bfloat16 [2048], P('fsdp'), may hold values from -1.75 to 1.75
- w_output: bfloat16 [2048, 2048], P('fsdp'), may hold values from -1 to 1
- moe_gain: bfloat16 [2048], P('fsdp'), may hold values from 0.5 to 1.5
- w_router: bfloat16 [2048, 8], P('fsdp'), may hold values from -0.0625 to 0.0625
- shared_switch: bfloat16 [2048], P('fsdp'), may hold values from -0.125 to 0.125
- shared_gate: bfloat16 [2048, 5632], P(None, 'fsdp'), may hold values from -0.125 to 0.125
- shared_up: bfloat16 [2048, 5632], P(None, 'fsdp'), may hold values from -0.125 to 0.125
- shared_down: bfloat16 [5632, 2048], P('fsdp'), may hold values from -0.21875 to 0.21875
- expert_gate: bfloat16 [8, 2048, 1408], P('fsdp'), may hold values from -0.125 to 0.125
- routed_up_weight: bfloat16 [8, 2048, 1408], P('fsdp'), may hold values from -0.125 to 0.125
- expert_down: bfloat16 [8, 1408, 2048], P('fsdp'), may hold values from -0.625 to 0.625
Outputs:
- output: bfloat16 [8192, 2048], P(('grp', 'fsdp'))
- grad_tokens: float32 [8192, 2048], P(('grp', 'fsdp'))
- grad_attn_gain: float32 [2048], P(('fsdp', 'grp'))
- grad_w_query: float32 [2048, 2048], P('fsdp', 'grp')
- grad_w_key: float32 [2048, 2048], P('fsdp', 'grp')
- grad_w_value: float32 [2048, 2048], P('fsdp', 'grp')
- grad_b_query: float32 [2048], P(('fsdp', 'grp'))
- grad_b_key: float32 [2048], P(('fsdp', 'grp'))
- grad_b_value: float32 [2048], P(('fsdp', 'grp'))
- grad_w_output: float32 [2048, 2048], P('fsdp', 'grp')
- grad_moe_gain: float32 [2048], P(('fsdp', 'grp'))
- grad_w_router: float32 [2048, 8], P(('fsdp', 'grp'))
- grad_shared_switch: float32 [2048], P(('fsdp', 'grp'))
- grad_shared_gate: float32 [2048, 5632], P('grp', 'fsdp')
- grad_shared_up: float32 [2048, 5632], P('grp', 'fsdp')
- grad_shared_down: float32 [5632, 2048], P('fsdp', 'grp')
- grad_expert_gate: float32 [8, 2048, 1408], P('fsdp', 'grp')
- grad_expert_up: float32 [8, 2048, 1408], P('fsdp', 'grp')
- grad_expert_down: float32 [8, 1408, 2048], P('fsdp', None, 'grp')
The draws below stay inside these ranges and needn't reach their ends.
Inputs may be any that keep to these rules, and one draw needn't show every extreme that they name: Tokens 1024 * k to 1024 * (k + 1) - 1 form tree k, of seven segments in this order: a trunk of 512 tokens, a first branch, its two leaves, a second branch, its two leaves; segment = 7 k + the segment's place in that order. ancestry(t) lists the trunk, the branch and the leaf on t's path; where t is in the trunk or a branch, its own segment stands in the deeper places. position counts the tokens before t on its path: trunk, then the branch, then the leaf; in every tree the path through the first leaf has exactly 768 tokens, and no path has more. `routes`: in the rows of one device no expert is named by more than 160 rows.
All inputs are finite; a program needn't handle non-finite values.
Results may differ from the reference program's by a relative error of at most 0.03.
Values may be sent and summed in bfloat16 or wider, within the bound.
A program may use at most 448 MiB of HBM per device.

```python
import math
import jax
import jax.numpy as jnp
import numpy as np
from jax import lax

D = 2048
HEADS = 16
HEAD_DIM = 128
FE = 1408
FFS = 5632
EXPERTS = 8
TOP = 4
TREE = 1024
TREES = 8
TOKENS = 8192
TOK_DEV = 256
CAP = 160


def tree_layout(key):
    base = jax.random.fold_in(key, 4242)
    streams = jax.random.split(base, 2)
    remain = TREE // 2
    eighth = remain // 8
    sixteenth = remain // 16
    shift_branch = jax.random.randint(streams[0], (TREES,), 1, eighth)
    leaf_gap = eighth - shift_branch
    shift_second = jax.random.randint(streams[1], (TREES,), -sixteenth + 1, sixteenth)
    trunk = jnp.full((TREES,), remain, jnp.int32)
    lengths = jnp.stack([trunk, remain // 4 + shift_branch, eighth + leaf_gap, eighth - leaf_gap, remain // 4 - shift_branch, eighth + shift_second, eighth - shift_second], axis=1).astype(jnp.int32)
    ends = jnp.cumsum(lengths, axis=1)
    starts = ends - lengths
    index = jnp.arange(TREE, dtype=jnp.int32)
    place = jnp.sum((index[None, :, None] >= ends[:, None, :]).astype(jnp.int32), axis=2)
    onehot = place[:, :, None] == jnp.arange(7, dtype=jnp.int32)[None, None, :]
    offset = index[None, :] - jnp.sum(jnp.where(onehot, starts[:, None, :], 0), axis=2)
    zeros_col = jnp.zeros((TREES,), jnp.int32)
    after_a = trunk + lengths[:, 1]
    after_b = trunk + lengths[:, 4]
    depth_base = jnp.stack([zeros_col, trunk, after_a, after_a, trunk, after_b, after_b], axis=1)
    position = offset + jnp.sum(jnp.where(onehot, depth_base[:, None, :], 0), axis=2)
    tree_base = 7 * jnp.arange(TREES, dtype=jnp.int32)[:, None]
    segment = tree_base + place
    middle_table = jnp.array([0, 1, 1, 1, 4, 4, 4], jnp.int32)
    middle = jnp.sum(jnp.where(onehot, middle_table[None, None, :], 0), axis=2)
    ancestry = jnp.stack([tree_base + 0 * place, tree_base + middle, segment], axis=-1)
    return (segment.astype(jnp.int32), ancestry.astype(jnp.int32), position.astype(jnp.int32))


def draw_segment(key, part):
    return tree_layout(key)[0].reshape(-1)


def draw_ancestry(key, part):
    return tree_layout(key)[1].reshape(-1, 3)


def draw_position(key, part):
    return tree_layout(key)[2].reshape(-1)


def levels(own_key, dims, cuts, low, top_value):
    factor_of, own = 1.0, jax.random.fold_in(own_key, 6)
    for dim, parts in cuts:
        steps = jnp.exp(jax.random.uniform(jax.random.fold_in(own, dim), (parts,), jnp.float32, low / len(cuts), top_value / len(cuts)))
        factor_of = factor_of * jnp.repeat(steps, dims[dim] // parts).reshape([-1 if axis == dim else 1 for axis in range(len(dims))])
    return factor_of


def deal_out(key, own, number, rows, count, top, most, skew):
    ranking = jax.random.permutation(key, count)
    crowded, usual = portions_of(count, rows * top, most, skew, True), portions_of(count, rows * top, most, skew, False)
    places = jnp.arange(count)

    def named(sizes, turn):
        used = int((sizes > 0).sum())
        fixed = max(1, used // 4)
        passed = fixed + (places - fixed + turn * (used - fixed)) % max(1, count - fixed)
        return jnp.zeros((count,), jnp.int32).at[ranking[jnp.where(places < fixed, places, passed)]].set(jnp.asarray(sizes, jnp.int32))

    sizes = jnp.where(number % 4 == 0, named(crowded, number // 4), named(usual, number - number // 4 - 1))
    mixed = jax.random.permutation(jax.random.fold_in(own, 3), count)
    source_of, taker = mixed[0:count // 2 * 2:2], mixed[1:count // 2 * 2:2]
    room = jnp.minimum(sizes[source_of] - 1, most - sizes[taker]) // 2
    room = jnp.where((source_of == ranking[0]) | (taker == ranking[0]) | (sizes[taker] == 0), 0, jnp.maximum(room, 0))
    passed = jax.random.randint(jax.random.fold_in(own, 4), (count // 2,), 0, 1 << 20) % (room + 1)
    sizes = sizes.at[source_of].add(-passed).at[taker].add(passed)
    items = jnp.searchsorted(jnp.cumsum(sizes), jnp.arange(rows * top), side="right").astype(jnp.int32)
    table = items.reshape(top, rows).T
    table = table[jax.random.permutation(jax.random.fold_in(own, 1), rows)]
    turn = jax.random.randint(jax.random.fold_in(own, 2), (rows, 1), 0, top)
    return jnp.take_along_axis(table, (jnp.arange(top)[None, :] + turn) % top, axis=1)


def portions_of(number_of, total, bound, slope, full):
    loads = [(1 << 20) // math.isqrt(grade ** slope) + 1 for grade in range(1, number_of + 1)]
    largest = bound if full else min(bound, max(-(-total // number_of), total * loads[0] // sum(loads)))
    least = 1 if total - largest >= number_of - 1 else 0
    holding, surplus = [largest] + [least] * (number_of - 1), total - largest - least * (number_of - 1)
    while surplus > 0:
        candidates = [i for i in range(1, number_of) if holding[i] < largest] or [i for i in range(1, number_of) if holding[i] < bound]
        pool, remaining = sum([loads[i] for i in candidates]), surplus
        for i in candidates:
            more = min(bound - holding[i], max(1, remaining * loads[i] // pool), surplus)
            holding[i] = holding[i] + more
            surplus = surplus - more
    return np.array(holding)


def scatter_about(rng, dims, deviation, limit, pieces=(), kind=jnp.bfloat16):
    drawn = deviation * jax.random.normal(rng, dims, jnp.float32)
    if pieces:
        drawn = drawn * levels(rng, dims, pieces, -0.22, 0.18)
    return jnp.clip(drawn, -limit, limit).astype(kind)


def setup_inputs(seed: int = 0) -> dict:
    splits = jax.random.split(jax.random.key(seed), 24)
    tokens = scatter_about(splits[0], (TOKENS, D), 1.0, 6.0, ((0, 32),))
    cotangent = scatter_about(splits[1], (TOKENS, D), 1.0, 6.0, ((0, 32),))
    segment = draw_segment(jax.random.fold_in(splits[23], 71), 0)
    ancestry = draw_ancestry(jax.random.fold_in(splits[23], 71), 0)
    position = draw_position(jax.random.fold_in(splits[23], 71), 0)
    routes_keys = jax.random.split(jax.random.fold_in(splits[5], 1), TOKENS // TOK_DEV)
    routes_turns = jax.random.permutation(jax.random.fold_in(splits[5], 3), TOKENS // TOK_DEV)
    routes = jax.vmap(lambda own, number: deal_out(jax.random.fold_in(splits[5], 2), own, number, TOK_DEV, EXPERTS, TOP, CAP, 2))(routes_keys, routes_turns).reshape((TOKENS, TOP))
    attn_gain = jnp.clip(1.0 + 0.1 * jax.random.normal(splits[6], (D,), jnp.float32), 0.5, 1.5).astype(jnp.bfloat16)
    w_query = scatter_about(splits[7], (D, D), D ** -0.5, 0.125, ((0, 4),))
    w_key = scatter_about(splits[8], (D, D), D ** -0.5, 0.125, ((0, 4),))
    w_value = scatter_about(splits[9], (D, D), D ** -0.5, 0.125, ((0, 4),))
    b_query = scatter_about(splits[10], (D,), 0.3, 1.75, ((0, 4),))
    b_key = scatter_about(splits[11], (D,), 0.3, 1.75, ((0, 4),))
    b_value = scatter_about(splits[12], (D,), 0.3, 1.75, ((0, 4),))
    w_output = scatter_about(splits[13], (D, D), (max(D // 64, 4)) ** -0.5, 1.0, ((0, 4),))
    moe_gain = jnp.clip(1.0 + 0.1 * jax.random.normal(splits[14], (D,), jnp.float32), 0.5, 1.5).astype(jnp.bfloat16)
    w_router = scatter_about(splits[15], (D, EXPERTS), (4 * D) ** -0.5, 0.0625, ((0, 4),))
    shared_switch = scatter_about(splits[16], (D,), D ** -0.5, 0.125, ((0, 4),))
    shared_gate = scatter_about(splits[17], (D, FFS), D ** -0.5, 0.125, ((1, 4),))
    shared_up = scatter_about(splits[18], (D, FFS), D ** -0.5, 0.125, ((1, 4),))
    shared_down = scatter_about(splits[19], (FFS, D), (FFS // 8) ** -0.5, 0.21875, ((0, 4),))
    expert_gate = scatter_about(splits[20], (EXPERTS, D, FE), D ** -0.5, 0.125, ((0, 4),))
    routed_up_weight = scatter_about(splits[21], (EXPERTS, D, FE), D ** -0.5, 0.125, ((0, 4),))
    expert_down = scatter_about(splits[22], (EXPERTS, FE, D), (FE // 16) ** -0.5, 0.625, ((0, 4),))
    return {"tokens": tokens, "cotangent": cotangent, "segment": segment, "ancestry": ancestry, "position": position, "routes": routes, "attn_gain": attn_gain, "w_query": w_query, "w_key": w_key, "w_value": w_value, "b_query": b_query, "b_key": b_key, "b_value": b_value, "w_output": w_output, "moe_gain": moe_gain, "w_router": w_router, "shared_switch": shared_switch, "shared_gate": shared_gate, "shared_up": shared_up, "shared_down": shared_down, "expert_gate": expert_gate, "routed_up_weight": routed_up_weight, "expert_down": expert_down}


EPSILON = 1e-06
ROPE_BASE = 1000000.0
MASK_FILL = -1e+30
EXACT_MATMUL = lax.Precision.HIGHEST

@jax.custom_vjp
def low(v):
    return lax.optimization_barrier(v.astype(jnp.bfloat16)).astype(jnp.float32)

@jax.custom_vjp
def low_back(v):
    return v

def low_keep(v):
    return (low(v), None)

def low_pass(kept, grad):
    return (grad,)

def back_keep(v):
    return (v, None)

def back_low(kept, grad):
    return (low(grad),)
low.defvjp(low_keep, low_pass)
low_back.defvjp(back_keep, back_low)

def normalize(values, gain):
    return values * lax.rsqrt(lax.optimization_barrier(jnp.mean(values * values, axis=-1, keepdims=True)) + EPSILON) * gain

def angles(position):
    halfway = HEAD_DIM // 2
    freqs = ROPE_BASE ** (-(jnp.arange(halfway, dtype=jnp.float32) * 2.0 / HEAD_DIM))
    turns = position.astype(jnp.float32)[:, None] * freqs[None, :]
    return (jnp.cos(turns)[:, None, :], jnp.sin(turns)[:, None, :])

def rotate(field, cosine, sine_part):
    halfway = field.shape[-1] // 2
    leading = field[..., :halfway]
    second = field[..., halfway:]
    return jnp.concatenate([leading * cosine - second * sine_part, second * cosine + leading * sine_part], axis=-1)

def tree_block(weights, rows):
    attn_gain, w_query, w_key, w_value, b_query, b_key, b_value, w_output, moe_gain, shared_switch, shared_gate, shared_up, shared_down = weights
    tokens_f, segment, ancestry, position = rows
    count = tokens_f.shape[0]
    normed = low(normalize(tokens_f, attn_gain))
    cosine, sine_part = angles(position)
    query_pre = low_back(jnp.dot(normed, w_query, precision=EXACT_MATMUL) + b_query)
    key_pre = low_back(jnp.dot(normed, w_key, precision=EXACT_MATMUL) + b_key)
    value_pre = jnp.dot(normed, w_value, precision=EXACT_MATMUL) + b_value
    query = low(rotate(query_pre.reshape(count, HEADS, HEAD_DIM), cosine, sine_part))
    keys = low(rotate(key_pre.reshape(count, HEADS, HEAD_DIM), cosine, sine_part))
    values = low(low_back(value_pre)).reshape(count, HEADS, HEAD_DIM)
    visible = ((segment[None, :] == ancestry[:, 0:1]) | (segment[None, :] == ancestry[:, 1:2]) | (segment[None, :] == ancestry[:, 2:3])) & (position[None, :] <= position[:, None])
    scores = low_back(jnp.einsum('qhd,khd->hqk', query, keys, precision=EXACT_MATMUL) * HEAD_DIM ** (-0.5))
    probs = low(jax.nn.softmax(jnp.where(visible[None, :, :], scores, MASK_FILL), axis=-1))
    attended = low(low_back(jnp.einsum('hqk,khd->qhd', probs, values, precision=EXACT_MATMUL).reshape(count, D)))
    branch = low_back(jnp.dot(attended, w_output, precision=EXACT_MATMUL))
    mixed = tokens_f + branch
    moe_in = low(normalize(mixed, moe_gain))
    gate_pre = low_back(jnp.dot(moe_in, shared_gate, precision=EXACT_MATMUL))
    up_pre = low_back(jnp.dot(moe_in, shared_up, precision=EXACT_MATMUL))
    shared_hidden = low(jax.nn.silu(gate_pre) * up_pre)
    shared_out = low_back(jnp.dot(shared_hidden, shared_down, precision=EXACT_MATMUL))
    opener = jax.nn.sigmoid(jnp.dot(moe_in, shared_switch, precision=EXACT_MATMUL))
    return (mixed + opener[:, None] * shared_out, moe_in)

def forward(tokens_f, attn_gain, w_query, w_key, w_value, b_query, b_key, b_value, w_output, moe_gain, w_router, shared_switch, shared_gate, shared_up, shared_down, expert_gate, routed_up_weight, expert_down, segment, ancestry, position, routes):
    weights = (attn_gain, w_query, w_key, w_value, b_query, b_key, b_value, w_output, moe_gain, shared_switch, shared_gate, shared_up, shared_down)
    forest = TOKENS // TREE

    def one_tree(rows):
        return tree_block(weights, rows)
    dense, moe_in = lax.map(jax.checkpoint(one_tree), (tokens_f.reshape(forest, TREE, D), segment.reshape(forest, TREE), ancestry.reshape(forest, TREE, 3), position.reshape(forest, TREE)))
    dense = dense.reshape(TOKENS, D)
    moe_in = moe_in.reshape(TOKENS, D)
    router_probs = jax.nn.softmax(jnp.dot(moe_in, w_router, precision=EXACT_MATMUL), axis=-1)
    gates = jnp.take_along_axis(router_probs, routes, axis=1)
    blocks = TOKENS // TOK_DEV
    chosen = routes.reshape(blocks, TOK_DEV * TOP)
    onehot = (chosen[:, :, None] == jnp.arange(EXPERTS, dtype=jnp.int32)[None, None, :]).astype(jnp.int32)
    slots = lax.optimization_barrier(jnp.sum((jnp.cumsum(onehot, axis=1) - 1) * onehot, axis=2))
    target = ((chosen * blocks + jnp.arange(blocks, dtype=jnp.int32)[:, None]) * CAP + slots).reshape(-1)
    entries = TOKENS * TOP
    source = jnp.full((EXPERTS * blocks * CAP,), entries, jnp.int32).at[target].set(jnp.arange(entries, dtype=jnp.int32)).reshape(EXPERTS, blocks * CAP)
    rows_pad = jnp.concatenate([moe_in, jnp.zeros((1, D), jnp.float32)], axis=0)
    gate_pad = jnp.concatenate([gates.reshape(-1), jnp.zeros((1,), jnp.float32)], axis=0)

    def expert_step(total, item):
        picks, gate_w, up_weight, down_w = item
        owner = picks // TOP
        input_rows = rows_pad[owner]
        expert_gate_rows = low_back(jnp.dot(input_rows, gate_w, precision=EXACT_MATMUL))
        expert_up_rows = low_back(jnp.dot(input_rows, up_weight, precision=EXACT_MATMUL))
        expert_hidden_rows = low(jax.nn.silu(expert_gate_rows) * expert_up_rows)
        eout = low(low_back(jnp.dot(expert_hidden_rows, down_w, precision=EXACT_MATMUL)))
        return (total.at[owner].add(gate_pad[picks][:, None] * eout), None)
    total, unused = lax.scan(jax.checkpoint(expert_step), jnp.zeros((TOKENS + 1, D), jnp.float32), (source, expert_gate, routed_up_weight, expert_down))
    return dense + total[:TOKENS]

def reference(tokens, cotangent, segment, ancestry, position, routes, attn_gain, w_query, w_key, w_value, b_query, b_key, b_value, w_output, moe_gain, w_router, shared_switch, shared_gate, shared_up, shared_down, expert_gate, routed_up_weight, expert_down):
    floats = (tokens, attn_gain, w_query, w_key, w_value, b_query, b_key, b_value, w_output, moe_gain, w_router, shared_switch, shared_gate, shared_up, shared_down, expert_gate, routed_up_weight, expert_down)

    def run(*values):
        return forward(*values, segment, ancestry, position, routes)
    result, pullback = jax.vjp(run, *[value.astype(jnp.float32) for value in floats])
    grads = pullback(cotangent.astype(jnp.float32))
    return (result.astype(jnp.bfloat16), grads[0], grads[1], grads[2], grads[3], grads[4], grads[5], grads[6], grads[7], grads[8], grads[9], grads[10], grads[11], grads[12], grads[13], grads[14], grads[15], grads[16], grads[17])
```

```python
import functools

import jax
import jax.numpy as jnp
from jax import lax
from jax.experimental import pallas as pl
from jax.experimental.pallas import tpu as pltpu
from jax.sharding import PartitionSpec as P

HEADS = 16
HEAD_DIM = 128
EPSILON = 1e-06
ROPE_BASE = 1000000.0
MASK_FILL = -1e30

F32 = jnp.float32
BF16 = jnp.bfloat16
MESH = pl.DeviceIdType.MESH
ANY = pl.BlockSpec(memory_space=pl.ANY)
VMEM = pl.BlockSpec(memory_space=pltpu.VMEM)


def line_kernel(
    parts, stack, out, sib, recv, own_v, sib_v, in_v, more_v, send_v, out_v,
    load_sems, out_sem, sib_send, sib_recv, send_sems, recv_sems,
):
    matrices = stack.shape[0]
    rows = stack.shape[3] // parts
    chunks = matrices * parts
    slots = send_v.shape[0]
    g = lax.axis_index("grp")
    z, core = g // 2, lax.rem(g, 2)
    is_end = (z == 0) | (z == 3)
    is_mid = (z == 1) | (z == 2)

    def at(zz, cc):
        return {"grp": 2 * zz + cc}

    barrier = pltpu.get_barrier_semaphore()
    pl.semaphore_signal(barrier, inc=1, device_id=at(z, 1 - core), device_id_type=MESH)

    @pl.when(z > 0)
    def _():
        pl.semaphore_signal(barrier, inc=1, device_id=at(z - 1, core), device_id_type=MESH)

    @pl.when(z < 3)
    def _():
        pl.semaphore_signal(barrier, inc=1, device_id=at(z + 1, core), device_id_type=MESH)

    @pl.when(is_end)
    def _():
        pl.semaphore_wait(barrier, 2)

    @pl.when(is_mid)
    def _():
        pl.semaphore_wait(barrier, 3)

    def span(q):
        return lax.div(q, parts), pl.ds(pl.multiple_of(lax.rem(q, parts) * rows, rows), rows)

    def swap(q):
        m, r = span(q)
        return pltpu.make_async_remote_copy(
            src_ref=stack.at[m, :, 1 - core, r],
            dst_ref=sib.at[m, :, r],
            send_sem=sib_send.at[q],
            recv_sem=sib_recv.at[q],
            device_id=at(z, 1 - core),
            device_id_type=MESH,
        )

    def begin(q, carry):
        swap(q).start()
        return carry

    lax.fori_loop(0, chunks, begin, 0)

    def out_copy(q):
        m, r = span(q)
        return pltpu.make_async_copy(out_v, out.at[m, r], out_sem)

    def hop(q, slot, p, target, place):
        m, r = span(q)
        return pltpu.make_async_remote_copy(
            src_ref=send_v.at[slot],
            dst_ref=recv.at[m, place, r],
            send_sem=send_sems.at[slot],
            recv_sem=recv_sems.at[q, place],
            device_id=at(target, core),
            device_id_type=MESH,
        )

    def arrived(q, place):
        m, r = span(q)
        hop(q, 0, 0, z, place).wait_recv()

    def base_loads(q, p):
        m, r = span(q)
        return (
            pltpu.make_async_copy(stack.at[m, p, core, r], own_v, load_sems.at[0]),
            pltpu.make_async_copy(sib.at[m, p, r], sib_v, load_sems.at[1]),
        )

    def extra_load(q, place, buf, k):
        m, r = span(q)
        return pltpu.make_async_copy(recv.at[m, place, r], buf, load_sems.at[k])

    def send(t, j, q, p, target, place, more):
        slot = lax.rem(t, slots // 3) * 3 + j

        @pl.when(t >= slots // 3 + (q_first(j)))
        def _():
            hop(q, slot, p, target, place).wait_send()

        loads = base_loads(q, p)
        if more:
            arrived(q, p)
            loads = loads + (extra_load(q, p, in_v, 2),)
        for c in loads:
            c.start()
        for c in loads:
            c.wait()
        total = own_v[...].astype(F32) + sib_v[...].astype(F32)
        if more:
            total = total + in_v[...].astype(F32)
        send_v[slot] = total.astype(BF16)
        hop(q, slot, p, target, place).start()

    def q_first(j):
        return jnp.where(is_end, 0, 1 if j < 2 else 2)

    def turn(t, carry):
        @pl.when(t < chunks)
        def _():
            swap(t).wait_recv()

        @pl.when(is_end & (t < chunks))
        def _():
            for j in range(3):
                p = jnp.where(z == 0, 3 - j, j)
                target = jnp.where(z == 0, 1, 2)
                place = jnp.where((z == 3) & (p == 2), 4, p)
                send(t, j, t, p, target, place, False)

        @pl.when(is_mid & (t >= 1) & (t < chunks + 1))
        def _():
            for j in range(2):
                p = jnp.where(z == 1, 3 - j, j)
                target = jnp.where(z == 1, 2, 1)
                place = jnp.where((z == 2) & (p == 1), 4, p)
                send(t, j, t - 1, p, target, place, True)

        @pl.when(is_mid & (t >= 2) & (t < chunks + 2))
        def _():
            p = jnp.where(z == 2, 3, 0)
            target = p
            place = jnp.where(z == 1, 4, p)
            send(t, 2, t - 2, p, target, place, True)

        @pl.when(t >= 3)
        def _():
            q = t - 3
            loads = base_loads(q, z)
            for c in loads:
                c.start()

            @pl.when(z > 0)
            def _():
                arrived(q, z)
                c = extra_load(q, z, in_v, 2)
                c.start()
                c.wait()

            @pl.when(z < 3)
            def _():
                arrived(q, 4)
                c = extra_load(q, 4, more_v, 3)
                c.start()
                c.wait()

            for c in loads:
                c.wait()

            @pl.when(q >= 1)
            def _():
                out_copy(q - 1).wait()

            total = own_v[...].astype(F32) + sib_v[...].astype(F32)

            @pl.when(z == 0)
            def _():
                out_v[...] = total + more_v[...].astype(F32)

            @pl.when(z == 3)
            def _():
                out_v[...] = total + in_v[...].astype(F32)

            @pl.when(is_mid)
            def _():
                out_v[...] = total + (in_v[...].astype(F32) + more_v[...].astype(F32))

            out_copy(q).start()

        return carry

    lax.fori_loop(0, chunks + 3, turn, 0)
    out_copy(chunks - 1).wait()

    def finish(q, carry):
        swap(q).wait_send()
        return carry

    lax.fori_loop(0, chunks, finish, 0)
    for slot in range(slots):
        hop(0, slot, 0, z, 0).wait_send()


def line_sum(stack, parts, collective_id):
    m, _, _, rows, cols = stack.shape
    r = rows // parts
    chunks = m * parts
    slots = 3 * min(3, chunks)
    buf = (r, cols)
    out, _, _ = pl.pallas_call(
        functools.partial(line_kernel, parts),
        out_shape=(
            jax.ShapeDtypeStruct((m, rows, cols), F32),
            jax.ShapeDtypeStruct((m, 4, rows, cols), BF16),
            jax.ShapeDtypeStruct((m, 5, rows, cols), BF16),
        ),
        in_specs=[ANY],
        out_specs=(ANY, ANY, ANY),
        scratch_shapes=[pltpu.VMEM(buf, BF16)] * 4
        + [
            pltpu.VMEM((slots,) + buf, BF16),
            pltpu.VMEM(buf, F32),
            pltpu.SemaphoreType.DMA((4,)),
            pltpu.SemaphoreType.DMA,
            pltpu.SemaphoreType.DMA((chunks,)),
            pltpu.SemaphoreType.DMA((chunks,)),
            pltpu.SemaphoreType.DMA((slots,)),
            pltpu.SemaphoreType.DMA((chunks, 5)),
        ],
        compiler_params=pltpu.CompilerParams(
            collective_id=collective_id, has_side_effects=True, vmem_limit_bytes=48 * 2**20
        ),
    )(stack)
    return out


def plane_neighbours():
    f = lax.axis_index("fsdp")
    by_x = f + 1 - 2 * lax.rem(f, 2)
    by_y = f + 2 - 4 * (f // 2)
    return {"fsdp": by_x}, {"fsdp": by_y}


def plane_barrier(by_x, by_y):
    barrier = pltpu.get_barrier_semaphore()
    for other in (by_x, by_y):
        pl.semaphore_signal(barrier, inc=1, device_id=other, device_id_type=MESH)
    pl.semaphore_wait(barrier, 2)


def mid_kernel(middle, chunks, gathers, n_in, n_out, *refs):
    partial, ins = refs[0], refs[1 : 1 + n_in]
    refs = refs[1 + n_in :]
    outs, refs = refs[:n_out], refs[n_out:]
    gathered = None
    if gathers:
        gathered, refs = refs[0], refs[1:]
    relay_x, relay_y, got_x, got_y, sum_x, sum_y, own, send_sems, recv_sems, local_sems = refs
    rows = partial.shape[1]
    r = rows // chunks
    h = r // 2
    by_x, by_y = plane_neighbours()
    plane_barrier(by_x, by_y)

    def copy(i, kind, src, dst, target):
        return pltpu.make_async_remote_copy(
            src_ref=src, dst_ref=dst, send_sem=send_sems.at[i, kind], recv_sem=recv_sems.at[i, kind],
            device_id=target, device_id_type=MESH,
        )

    def sends(i):
        lo, hi = pl.ds(i * r, h), pl.ds(i * r + h, h)
        half = pl.ds(i * h, h)
        made = {
            0: lambda: copy(i, 0, partial.at[3, lo], relay_x.at[half], by_x),
            1: lambda: copy(i, 1, partial.at[3, hi], relay_y.at[half], by_y),
            2: lambda: copy(i, 2, partial.at[1, lo], got_x.at[lo], by_x),
            3: lambda: copy(i, 3, partial.at[2, hi], got_y.at[hi], by_y),
            4: lambda: copy(i, 4, sum_y.at[half], got_y.at[lo], by_y),
            5: lambda: copy(i, 5, sum_x.at[half], got_x.at[hi], by_x),
        }
        if gathers:
            made |= {
                6: lambda: copy(i, 6, own.at[lo], gathered.at[1, lo], by_x),
                7: lambda: copy(i, 7, own.at[hi], gathered.at[2, hi], by_y),
                8: lambda: copy(i, 8, own.at[hi], gathered.at[1, hi], by_x),
                9: lambda: copy(i, 9, own.at[lo], gathered.at[2, lo], by_y),
                10: lambda: copy(i, 10, gathered.at[1, lo], gathered.at[3, lo], by_y),
                11: lambda: copy(i, 11, gathered.at[2, hi], gathered.at[3, hi], by_x),
            }
        return made

    def keep(i):
        span = pl.ds(i * r, r)
        return pltpu.make_async_copy(own.at[span], gathered.at[0, span], local_sems.at[i])

    def stage(n, i):
        s = sends(i)
        lo, hi = pl.ds(i * r, h), pl.ds(i * r + h, h)
        half, span = pl.ds(i * h, h), pl.ds(i * r, r)
        if n == 0:
            for kind in (0, 1, 2, 3):
                s[kind]().start()
        elif n == 1:
            s[0]().wait_recv()
            sum_y[half] = (partial[2, lo].astype(F32) + relay_x[half].astype(F32)).astype(BF16)
            s[4]().start()
            s[1]().wait_recv()
            sum_x[half] = (partial[1, hi].astype(F32) + relay_y[half].astype(F32)).astype(BF16)
            s[5]().start()
        elif n == 2:
            for kind in (2, 3, 4, 5):
                s[kind]().wait_recv()
            total = partial[0, span].astype(F32) + (got_x[span].astype(F32) + got_y[span].astype(F32))
            given = middle(total, span, ins, outs)
            if gathers:
                own[span] = given
                for kind in (6, 7, 8, 9):
                    s[kind]().start()
                keep(i).start()
        elif n == 3 and gathers:
            s[6]().wait_recv()
            s[10]().start()
            s[7]().wait_recv()
            s[11]().start()
        elif n == 4:
            if gathers:
                for kind in (8, 9, 10, 11):
                    s[kind]().wait_recv()
                keep(i).wait()
            for kind in s:
                s[kind]().wait_send()

    for t in range(chunks + 4):
        for n in range(5):
            if 0 <= t - n < chunks:
                stage(n, t - n)


def mid_call(middle, partial, ins, out_shapes, gathers, collective_id, chunks=4):
    _, rows, cols = partial.shape
    outs = tuple(out_shapes)
    specs = (VMEM,) * len(outs)
    if gathers:
        outs += (jax.ShapeDtypeStruct((4, rows, cols), BF16),)
        specs += (ANY,)
    return pl.pallas_call(
        functools.partial(mid_kernel, middle, chunks, gathers, len(ins), len(out_shapes)),
        out_shape=outs,
        in_specs=[VMEM] * (1 + len(ins)),
        out_specs=specs,
        scratch_shapes=[
            pltpu.VMEM((rows // 2, cols), BF16),
            pltpu.VMEM((rows // 2, cols), BF16),
            pltpu.VMEM((rows, cols), BF16),
            pltpu.VMEM((rows, cols), BF16),
            pltpu.VMEM((rows // 2, cols), BF16),
            pltpu.VMEM((rows // 2, cols), BF16),
            pltpu.VMEM((rows, cols), BF16),
            pltpu.SemaphoreType.DMA((chunks, 12)),
            pltpu.SemaphoreType.DMA((chunks, 12)),
            pltpu.SemaphoreType.DMA((chunks,)),
        ],
        compiler_params=pltpu.CompilerParams(
            collective_id=collective_id, has_side_effects=True, vmem_limit_bytes=48 * 2**20
        ),
    )(partial, *ins)


def start_kernel(
    tokens, small, marks, w_q, w_k, w_v,
    tokens_all, small_all, marks_all, w_cols, relay,
    send_sems, recv_sems, local_sems,
):
    f = lax.axis_index("fsdp")
    g = lax.axis_index("grp")
    core = lax.rem(g, 2)
    rows = tokens.shape[0]
    depth = w_q.shape[0]
    width = w_q.shape[1] // 4
    by_x, by_y = plane_neighbours()
    fx, fy = by_x["fsdp"], by_y["fsdp"]
    fd = fx + 2 - 4 * (fx // 2)
    by_d, sibling = {"fsdp": fd}, {"grp": g + 1 - 2 * core}
    barrier = pltpu.get_barrier_semaphore()
    for other in (by_x, by_y, by_d, sibling):
        pl.semaphore_signal(barrier, inc=1, device_id=other, device_id_type=MESH)
    pl.semaphore_wait(barrier, 4)

    def copy(n, src, dst, target):
        return pltpu.make_async_remote_copy(
            src_ref=src, dst_ref=dst, send_sem=send_sems.at[n], recv_sem=recv_sems.at[n],
            device_id=target, device_id_type=MESH,
        )

    def columns(j):
        return pl.ds(pl.multiple_of(j * width, width), width)

    def block_rows(owner, c):
        return pl.ds(pl.multiple_of(owner * depth + c * (depth // 2), depth // 2), depth // 2)

    half = depth // 2
    mine = pl.ds(pl.multiple_of(core * half, half), half)
    all_sends = []

    def go(c):
        c.start()
        all_sends.append(c)
        return c

    waits = []
    n = 0
    for k, target in ((1, by_x), (2, by_y), (3, by_d)):
        waits.append(go(copy(n, small, small_all.at[k], target)))
        waits.append(go(copy(n + 1, marks, marks_all.at[k], target)))
        n += 2
    locals_ = [
        pltpu.make_async_copy(small, small_all.at[0], local_sems.at[0]),
        pltpu.make_async_copy(marks, marks_all.at[0], local_sems.at[1]),
        pltpu.make_async_copy(tokens, tokens_all.at[0], local_sems.at[2]),
    ]
    for j, w in enumerate((w_q, w_k, w_v)):
        locals_.append(
            pltpu.make_async_copy(
                w.at[:, columns(f)],
                w_cols.at[pl.ds(pl.multiple_of(f * depth, depth), depth), pl.ds(j * width, width)],
                local_sems.at[3 + j],
            )
        )
    for c in locals_:
        c.start()

    quarter = half // 2
    first = pl.ds(pl.multiple_of(core * half, quarter), quarter)
    second = pl.ds(pl.multiple_of(core * half + quarter, quarter), quarter)
    relays_x, relays_y, direct_x, direct_y = [], [], [], []
    for j, w in enumerate((w_q, w_k, w_v)):
        relays_x.append(go(copy(n, w.at[first, columns(fd)], relay.at[0, j], by_x)))
        relays_y.append(go(copy(n + 1, w.at[second, columns(fd)], relay.at[1, j], by_y)))
        n += 2
    for j, w in enumerate((w_q, w_k, w_v)):
        place = w_cols.at[block_rows(f, core), pl.ds(j * width, width)]
        direct_x.append(go(copy(n, w.at[mine, columns(fx)], place, by_x)))
        direct_y.append(go(copy(n + 1, w.at[mine, columns(fy)], place, by_y)))
        n += 2
    low, high = pl.ds(0, rows // 2), pl.ds(rows // 2, rows // 2)
    t_x0 = go(copy(n, tokens.at[low], tokens_all.at[1, low], by_x))
    t_y1 = go(copy(n + 1, tokens.at[high], tokens_all.at[2, high], by_y))
    t_x1 = go(copy(n + 2, tokens.at[high], tokens_all.at[1, high], by_x))
    t_y0 = go(copy(n + 3, tokens.at[low], tokens_all.at[2, low], by_y))
    n += 4
    forwarded = []
    for j in range(3):
        relays_x[j].wait_recv()
        forwarded.append(
            go(copy(
                n, relay.at[0, j],
                w_cols.at[pl.ds(pl.multiple_of(fx * depth + core * half, quarter), quarter), pl.ds(j * width, width)],
                by_y,
            ))
        )
        relays_y[j].wait_recv()
        forwarded.append(
            go(copy(
                n + 1, relay.at[1, j],
                w_cols.at[pl.ds(pl.multiple_of(fy * depth + core * half + quarter, quarter), quarter), pl.ds(j * width, width)],
                by_x,
            ))
        )
        n += 2
    shares = []

    def share(owner):
        nonlocal n
        place = w_cols.at[block_rows(owner, core)]
        shares.append(go(copy(n, place, place, sibling)))
        n += 1

    for c in direct_x:
        c.wait_recv()
    share(fx)
    for c in direct_y:
        c.wait_recv()
    share(fy)
    t_x0.wait_recv()
    t_d0 = go(copy(n, tokens_all.at[1, low], tokens_all.at[3, low], by_y))
    t_y1.wait_recv()
    t_d1 = go(copy(n + 1, tokens_all.at[2, high], tokens_all.at[3, high], by_x))
    n += 2
    for c in forwarded:
        c.wait_recv()
    share(fd)
    for c in waits + shares + [t_x1, t_y0, t_d0, t_d1]:
        c.wait_recv()
    for c in locals_:
        c.wait()
    for c in all_sends:
        c.wait_send()


def start_call(tokens, small, marks, w_q, w_k, w_v, collective_id):
    depth, features = w_q.shape
    width = features // 4
    n = 6 + 6 + 6 + 4 + 6 + 2 + 3
    return pl.pallas_call(
        start_kernel,
        out_shape=(
            jax.ShapeDtypeStruct((4,) + tokens.shape, tokens.dtype),
            jax.ShapeDtypeStruct((4,) + small.shape, small.dtype),
            jax.ShapeDtypeStruct((4,) + marks.shape, marks.dtype),
            jax.ShapeDtypeStruct((4 * depth, 3 * width), BF16),
            jax.ShapeDtypeStruct((2, 3, depth // 4, width), BF16),
        ),
        in_specs=[ANY] * 6,
        out_specs=(ANY,) * 5,
        scratch_shapes=[
            pltpu.SemaphoreType.DMA((n,)),
            pltpu.SemaphoreType.DMA((n,)),
            pltpu.SemaphoreType.DMA((6,)),
        ],
        compiler_params=pltpu.CompilerParams(
            collective_id=collective_id, has_side_effects=True, vmem_limit_bytes=16 * 2**20
        ),
    )(tokens, small, marks, w_q, w_k, w_v)[:4]


def dot(left, right, dims, out=F32):
    return lax.dot_general(left, right, (dims, ((), ())), preferred_element_type=out)


def rows_dot(left, right):
    return dot(left, right, ((0,), (0,)))


def plain_dot(left, right):
    return dot(left, right, ((1,), (0,)))


def trans_dot(left, right):
    return dot(left, right, ((1,), (1,)))


def silu_pair(value):
    sigma = jax.nn.sigmoid(value)
    return value * sigma, sigma * (1.0 + value * (1.0 - sigma))


def angles(position):
    halfway = HEAD_DIM // 2
    freqs = ROPE_BASE ** (-(jnp.arange(halfway, dtype=F32) * 2.0 / HEAD_DIM))
    turns = position.astype(F32)[:, None] * freqs[None, :]
    return jnp.cos(turns)[:, None, :], jnp.sin(turns)[:, None, :]


def rotate(field, cosine, sine):
    halfway = field.shape[-1] // 2
    first, second = field[..., :halfway], field[..., halfway:]
    return jnp.concatenate(
        [first * cosine - second * sine, second * cosine + first * sine], axis=-1
    )


def two_parts(value):
    high = value.astype(BF16)
    return high, (value - high.astype(F32)).astype(BF16)


class Load:
    def __init__(self, value):
        self.value = value

    def __getitem__(self, place):
        return self.value[place]


class Store:
    def __init__(self, shape):
        self.value = jnp.zeros(shape.shape, shape.dtype)

    def __getitem__(self, place):
        return self.value[place]

    def __setitem__(self, place, value):
        self.value = value.astype(self.value.dtype)


def first_middle(total, span, ins, outs):
    tokens, gain = ins
    mixed = tokens[span].astype(F32) + total
    factor = lax.rsqrt(jnp.mean(mixed * mixed, axis=-1, keepdims=True) + EPSILON)
    outs[0][span] = mixed
    return (mixed * factor * gain[...]).astype(BF16)


def norm_back(values, gain, grad):
    factor = lax.rsqrt(jnp.mean(values * values, axis=-1, keepdims=True) + EPSILON)
    weighted = gain * grad
    back = factor * weighted - values * (factor * factor * factor) * jnp.mean(
        weighted * values, axis=-1, keepdims=True
    )
    return back, jnp.sum(grad * values * factor, axis=0, keepdims=True)


def back_middle(total, span, ins, outs):
    values, gain, base = ins
    back, grad_gain = norm_back(values[span].astype(F32), gain[...], total)
    grad = base[span].astype(F32) + back
    outs[0][span] = grad
    outs[1][span if span == slice(None) else pl.ds(span.start // span.size, 1)] = grad_gain
    return grad.astype(BF16)


class Wires:
    def __init__(self, mesh):
        self.nf = mesh.shape["fsdp"]
        self.ng = mesh.shape["grp"]
        self.nz = self.ng // 2
        self.fast = self.nf == 4 and self.ng == 8
        self.chunks = 4 if self.fast else 1

    def xor(self, value, k):
        return lax.ppermute(value, "fsdp", [(i, i ^ k) for i in range(self.nf)])

    def gather_list(self, value):
        return [value] + [self.xor(value, k) for k in range(1, self.nf)]

    def gather(self, value):
        return jnp.concatenate(self.gather_list(value), axis=0)

    def scatter_sum(self, value):
        rows = value.shape[0] // self.nf
        total = value[:rows]
        for k in range(1, self.nf):
            part = value[k * rows : (k + 1) * rows].astype(BF16)
            total = total + self.xor(part, k).astype(F32)
        return total

    def core_swap(self, value):
        return lax.ppermute(value, "grp", [(i, i ^ 1) for i in range(self.ng)])

    def core_sum(self, partial):
        core = lax.rem(lax.axis_index("grp"), 2)
        mine = lax.dynamic_index_in_dim(partial, core, 1, keepdims=False)
        other = lax.dynamic_index_in_dim(partial, 1 - core, 1, keepdims=False)
        got = self.core_swap(other)
        return (mine.astype(F32) + got.astype(F32)).astype(BF16)

    def line_sum(self, pieces):
        nz = self.nz
        z = lax.axis_index("grp") // 2

        def move(value, up, step):
            pairs = []
            for a in range(nz):
                b = a + 1 if up else a - 1
                sends = a < step if up else a > nz - 1 - step
                if sends and 0 <= b < nz:
                    pairs += [(2 * a + c, 2 * b + c) for c in (0, 1)]
            return lax.ppermute(value, "grp", pairs)

        ups = downs = None
        for step in range(1, nz):
            up_own = pieces(jnp.clip(z + nz - step, 0, nz - 1))
            down_own = pieces(jnp.clip(z - nz + step, 0, nz - 1))
            up_send = up_own if ups is None else (up_own.astype(F32) + ups.astype(F32)).astype(BF16)
            down_send = (
                down_own if downs is None else (down_own.astype(F32) + downs.astype(F32)).astype(BF16)
            )
            ups = move(up_send, True, step)
            downs = move(down_send, False, step)
        return pieces(z).astype(F32) + ups.astype(F32) + downs.astype(F32)

    def reduce_background(self, partial):
        return lax.psum_scatter(
            partial.astype(BF16), "grp", scatter_dimension=0, tiled=True
        ).astype(F32)

    def line_stack(self, stack, parts, number):
        if self.fast:
            return line_sum(stack, parts, number)
        m, nz, _, rows, cols = stack.shape
        flat = stack.reshape(m, nz * 2 * rows, cols)
        return lax.psum_scatter(flat, "grp", scatter_dimension=1, tiled=True).astype(F32)

    def gather_start(self, tokens, small, marks, weights):
        if self.fast:
            return start_call(tokens, small, marks, *weights, 1)
        width = tokens.shape[1] // self.nf
        cols = jnp.concatenate(
            [lax.all_to_all(w, "fsdp", split_axis=1, concat_axis=0, tiled=True) for w in weights],
            axis=1,
        )
        assert cols.shape[1] == 3 * width
        return tuple(jnp.stack(self.gather_list(v)) for v in (tokens, small, marks)) + (cols,)

    def middle(self, body, partial, ins, out_shapes, gathers, number):
        nf = self.nf
        rows, cols = partial.shape[0] // nf, partial.shape[1]
        if self.fast:
            return mid_call(
                body, partial.astype(BF16).reshape(nf, rows, cols), ins, out_shapes, gathers, number
            )
        total = self.scatter_sum(partial)
        outs = [Store(s) for s in out_shapes]
        given = body(total, slice(None), [Load(v) for v in ins], outs)
        results = tuple(o.value for o in outs)
        if gathers:
            results += (jnp.stack(self.gather_list(given)),)
        return results

    def reduce_rows(self, partial):
        rows = partial.shape[0] // self.ng
        partial = partial.astype(BF16).reshape((self.nz, 2, rows) + partial.shape[1:])
        acc = self.core_sum(partial)
        return self.line_sum(lambda i: lax.dynamic_index_in_dim(acc, i, 0, keepdims=False))


def on_device(
    wires,
    tokens,
    cotangent,
    segment,
    ancestry,
    position,
    routes,
    attn_gain,
    w_query,
    w_key,
    w_value,
    b_query,
    b_key,
    b_value,
    w_output,
    moe_gain,
    w_router,
    shared_switch,
    shared_gate,
    shared_up,
    shared_down,
    expert_gate,
    routed_up_weight,
    expert_down,
):
    nf, ng, nz = wires.nf, wires.ng, wires.nz
    me = lax.axis_index("fsdp")
    rows_dev, features = tokens.shape
    count = rows_dev * nf
    width = features // nf
    heads = width // HEAD_DIM
    experts = w_router.shape[1]
    local_experts = experts // nf
    capacity = 5 * rows_dev // 8
    inv_root = HEAD_DIM ** (-0.5)

    small = jnp.concatenate([attn_gain[None], moe_gain[None], w_router.T, shared_switch[None]], axis=0)
    small = jnp.pad(small, ((0, -small.shape[0] % 16), (0, 0)))
    marks = jnp.concatenate([segment[None], ancestry.T, position[None], routes.T], axis=0)
    marks = jnp.pad(marks, ((0, -marks.shape[0] % 16), (0, 0)))
    tokens_all, small_blocks, marks_all, w_cols = wires.gather_start(
        tokens, small, marks, (w_query, w_key, w_value)
    )
    tokens_all = tokens_all.reshape(count, features)
    small_all = jnp.concatenate(
        [lax.dynamic_index_in_dim(small_blocks, me ^ i, 0, keepdims=False) for i in range(nf)], axis=1
    )
    gain_one = small_all[0:1].astype(F32)
    gain_two = small_all[1:2].astype(F32)
    heads_w = small_all[2 : experts + 3].T
    marks_all = jnp.concatenate([marks_all[k] for k in range(nf)], axis=1)
    seg_all, anc_all, pos_all = marks_all[0], marks_all[1:4].T, marks_all[4]
    routes_all = marks_all[5 : 5 + routes.shape[1]].T

    tokens_all, cotangent = lax.optimization_barrier((tokens_all, cotangent))
    cot_all = wires.gather(cotangent)

    tokens_all_f = tokens_all.astype(F32)
    factor_all = lax.rsqrt(jnp.mean(tokens_all_f * tokens_all_f, axis=-1, keepdims=True) + EPSILON)
    normed = (tokens_all_f * factor_all * gain_one).astype(BF16)
    bias = jnp.concatenate([b_query, b_key, b_value]).astype(F32)
    three = plain_dot(normed, w_cols) + bias
    cosine, sine = angles(pos_all)

    def heads_of(x):
        return x.reshape(count, heads, HEAD_DIM)

    query = rotate(heads_of(three[:, :width]), cosine, sine).astype(BF16)
    keys = rotate(heads_of(three[:, width : 2 * width]), cosine, sine).astype(BF16)
    values = heads_of(three[:, 2 * width :]).astype(BF16)
    visible = (
        (seg_all[None, :] == anc_all[:, 0:1])
        | (seg_all[None, :] == anc_all[:, 1:2])
        | (seg_all[None, :] == anc_all[:, 2:3])
    ) & (pos_all[None, :] <= pos_all[:, None])
    scores = jnp.einsum("qhd,khd->hqk", query, keys, preferred_element_type=F32) * inv_root
    masked = jnp.where(visible[None], scores, MASK_FILL)
    peak = jnp.max(masked, axis=-1, keepdims=True)
    expo = jnp.exp(masked - peak)
    total = jnp.sum(expo, axis=-1, keepdims=True)
    log_total = peak + jnp.log(total)
    weights = (expo / total).astype(BF16)
    attended = (
        jnp.einsum("hqk,khd->qhd", weights, values, preferred_element_type=F32)
        .reshape(count, width)
        .astype(BF16)
    )
    mixed, moe_in = wires.middle(
        first_middle,
        plain_dot(attended, w_output),
        (tokens, gain_two),
        (jax.ShapeDtypeStruct((rows_dev, features), F32),),
        True,
        2,
    )
    moe_in = moe_in.reshape(count, features)

    head_pre = plain_dot(moe_in, heads_w)
    router_probs = jax.nn.softmax(head_pre[:, :experts], axis=-1)
    opener = jax.nn.sigmoid(head_pre[:, experts:])
    cot_f = cot_all.astype(F32)

    gate_pre = plain_dot(moe_in, shared_gate)
    up_pre = plain_dot(moe_in, shared_up)
    gate_act, gate_slope = silu_pair(gate_pre)
    shared_hidden = (gate_act * up_pre).astype(BF16)
    shared_grad = (opener * cot_f).astype(BF16)
    grad_shidden = trans_dot(shared_grad, shared_down)
    part_sdown = rows_dot(shared_grad, shared_hidden).astype(BF16)
    grad_sgate_pre = (grad_shidden * up_pre * gate_slope).astype(BF16)
    grad_sup_pre = (grad_shidden * gate_act).astype(BF16)
    part_sgate = rows_dot(moe_in, grad_sgate_pre).astype(BF16)
    part_sup = rows_dot(moe_in, grad_sup_pre).astype(BF16)
    gate_sens = (1.0 - opener) * jnp.sum(
        grad_shidden * shared_hidden.astype(F32), axis=-1, keepdims=True
    )
    out_part = opener * plain_dot(shared_hidden, shared_down)
    moe_part = trans_dot(grad_sgate_pre, shared_gate) + trans_dot(grad_sup_pre, shared_up)

    out_part, part_sdown, part_sgate, part_sup = lax.optimization_barrier(
        (out_part, part_sdown, part_sgate, part_sup)
    )
    final_sdown = wires.reduce_background(part_sdown)
    final_sgate = wires.reduce_background(part_sgate)
    final_sup = wires.reduce_background(part_sup)

    moe_blocks = moe_in.reshape(nf, rows_dev, features)
    cot_blocks = cot_all.reshape(nf, rows_dev, features)
    earlier = (
        jnp.arange(rows_dev)[None, :] < jnp.arange(rows_dev)[:, None]
    ).astype(BF16)
    lanes = jnp.arange(experts, dtype=jnp.int32)[None, :]
    prob_grad = jnp.zeros((count, experts), F32)
    parts = []
    for i in range(local_experts):
        number = me * local_experts + i
        named = jnp.any(routes_all == number, axis=1)
        named_blocks = named.reshape(nf, rows_dev)
        slot = jnp.einsum(
            "ts,bs->bt", earlier, named_blocks.astype(BF16), preferred_element_type=F32
        ).astype(jnp.int32)
        pick = (
            jnp.arange(capacity, dtype=jnp.int32)[None, :, None] == slot[:, None, :]
        ) & named_blocks[:, None, :]
        pick_b = pick.astype(BF16)

        def dispatch(x):
            return (
                jnp.einsum("bst,btd->bsd", pick_b, x, preferred_element_type=F32)
                .astype(BF16)
                .reshape(nf * capacity, features)
            )

        def collect(x):
            return jnp.einsum(
                "bst,bsd->btd", pick_b, x.reshape(nf, capacity, -1), preferred_element_type=F32
            ).reshape(count, -1)

        here = lanes == number
        prob_here = jnp.sum(jnp.where(here, router_probs, 0.0), axis=1)
        gate = jnp.sum(
            jnp.where(pick, prob_here.reshape(nf, 1, rows_dev), 0.0), axis=2
        ).reshape(nf * capacity, 1)
        rows_in = dispatch(moe_blocks)
        cot_rows = dispatch(cot_blocks)
        deout = (gate * cot_rows.astype(F32)).astype(BF16)
        egate = plain_dot(rows_in, expert_gate[i])
        eup = plain_dot(rows_in, routed_up_weight[i])
        act, slope = silu_pair(egate)
        hidden = (act * eup).astype(BF16)
        plain_hidden = trans_dot(cot_rows, expert_down[i])
        grad_hidden = gate * plain_hidden
        part_down = rows_dot(deout, hidden).astype(BF16)
        grad_gate_pre = (grad_hidden * eup * slope).astype(BF16)
        grad_up_pre = (grad_hidden * act).astype(BF16)
        part_gate = rows_dot(rows_in, grad_gate_pre).astype(BF16)
        part_up = rows_dot(rows_in, grad_up_pre).astype(BF16)
        parts += [part_gate, part_up, part_down]
        eout = plain_dot(hidden, expert_down[i]).astype(BF16)
        out_part = out_part + collect((gate * eout.astype(F32)).astype(BF16))
        grad_in = trans_dot(grad_gate_pre, expert_gate[i]) + trans_dot(
            grad_up_pre, routed_up_weight[i]
        )
        moe_part = moe_part + collect(grad_in.astype(BF16))
        gate_grad = jnp.sum(plain_hidden * hidden.astype(F32), axis=-1)
        gate_grad = jnp.sum(
            jnp.where(pick, gate_grad.reshape(nf, capacity, 1), 0.0), axis=1
        ).reshape(count, 1)
        prob_grad = prob_grad + jnp.where(here, gate_grad, 0.0)

    logit_grad = router_probs * (
        prob_grad - jnp.sum(prob_grad * router_probs, axis=-1, keepdims=True)
    )
    high, lower = two_parts(jnp.concatenate([logit_grad, gate_sens], axis=1))
    sens = jnp.concatenate([high, lower], axis=1)
    moe_part = moe_part + trans_dot(sens, jnp.concatenate([heads_w, heads_w], axis=1))
    grad_heads = rows_dot(moe_in, sens)
    grad_heads = grad_heads[:, : experts + 1] + grad_heads[:, experts + 1 :]

    grad_mixed, grad_gain_two, branch_grad = wires.middle(
        back_middle,
        moe_part,
        (mixed, gain_two, cotangent),
        (
            jax.ShapeDtypeStruct((rows_dev, features), F32),
            jax.ShapeDtypeStruct((wires.chunks, features), F32),
        ),
        True,
        3,
    )
    grad_gain_two = jnp.sum(grad_gain_two, axis=0)
    branch_grad = branch_grad.reshape(count, features)

    grad_attended = heads_of(trans_dot(branch_grad, w_output).astype(BF16))
    probs = jnp.exp(masked - log_total)
    weight_grad = jnp.einsum("qhd,khd->hqk", grad_attended, values, preferred_element_type=F32)
    diagonal = jnp.sum(probs * weight_grad, axis=-1, keepdims=True)
    score_grad = (probs * (weight_grad - diagonal)).astype(BF16)
    grad_query = jnp.einsum("hqk,khd->qhd", score_grad, keys, preferred_element_type=F32) * inv_root
    grad_keys = jnp.einsum("hqk,qhd->khd", score_grad, query, preferred_element_type=F32) * inv_root
    grad_values = jnp.einsum("hqk,qhd->khd", weights, grad_attended, preferred_element_type=F32)
    grad_qpre = rotate(grad_query, cosine, -sine).reshape(count, width).astype(BF16)
    grad_kpre = rotate(grad_keys, cosine, -sine).reshape(count, width).astype(BF16)
    grad_vpre = grad_values.reshape(count, width).astype(BF16)
    grad_three = jnp.concatenate([grad_qpre, grad_kpre, grad_vpre], axis=1)
    grad_bias = jnp.sum(grad_three.astype(F32), axis=0)

    grad_tokens, grad_gain_one = wires.middle(
        back_middle,
        trans_dot(grad_three, w_cols),
        (tokens, gain_one, grad_mixed),
        (
            jax.ShapeDtypeStruct((rows_dev, features), F32),
            jax.ShapeDtypeStruct((wires.chunks, features), F32),
        ),
        False,
        4,
    )
    grad_gain_one = jnp.sum(grad_gain_one, axis=0)

    part_output = rows_dot(branch_grad, attended).astype(BF16)
    part_three = rows_dot(grad_three, normed).astype(BF16).reshape(3 * width, nf, width)
    owned = []
    for k in range(nf):
        part = lax.dynamic_index_in_dim(part_three, me ^ k, 1, keepdims=False)
        owned.append(wires.xor(part, k) if k else part)
    out_total = wires.scatter_sum(out_part)

    ngz = (nz, 2, features // ng)
    stack = jnp.stack(parts, axis=0).reshape((3 * local_experts,) + ngz + (-1,))
    stack, final_sdown, final_sgate, final_sup, grad_tokens = lax.optimization_barrier(
        (stack, final_sdown, final_sgate, final_sup, grad_tokens)
    )
    sums = wires.line_stack(stack, 2, 5).reshape((local_experts, 3) + (features // ng, -1))
    output = (mixed + out_total).astype(BF16)
    owned = jnp.stack(owned, axis=0).reshape((nf, 3, 2, width // 2, width))
    owned = jnp.stack(
        [lax.dynamic_index_in_dim(owned, me ^ i, 0, keepdims=False) for i in range(nf)], axis=1
    )
    small_stack = jnp.concatenate(
        [owned, part_output.reshape((1,) + ngz + (width,))], axis=0
    )
    small_stack, sums = lax.optimization_barrier((small_stack, sums))
    attn = wires.line_stack(small_stack, 1, 6).transpose(0, 2, 1)

    vectors = jnp.concatenate(
        [grad_gain_one[:, None], grad_gain_two[:, None], grad_heads], axis=1
    )
    vectors = lax.psum_scatter(vectors, "fsdp", scatter_dimension=0, tiled=True)
    vectors = jnp.concatenate([vectors, grad_bias.reshape(3, width).T], axis=1)
    vectors = lax.psum_scatter(vectors, "grp", scatter_dimension=0, tiled=True)
    return (
        output,
        grad_tokens,
        vectors[:, 0],
        attn[0],
        attn[1],
        attn[2],
        vectors[:, experts + 3],
        vectors[:, experts + 4],
        vectors[:, experts + 5],
        attn[3],
        vectors[:, 1],
        vectors[:, 2 : experts + 2],
        vectors[:, experts + 2],
        final_sgate,
        final_sup,
        final_sdown.T,
        sums[:, 0],
        sums[:, 1],
        sums[:, 2].transpose(0, 2, 1),
    )


def solution(mesh):
    wires = Wires(mesh)

    def step(*args):
        return on_device(wires, *args)

    rows = P(("grp", "fsdp"))
    shard = P("fsdp")
    small = P(("fsdp", "grp"))
    return jax.shard_map(
        step,
        mesh=mesh,
        in_specs=(rows,) * 6
        + (shard,) * 11
        + (P(None, "fsdp"), P(None, "fsdp"), shard, shard, shard, shard),
        out_specs=(
            rows,
            rows,
            small,
            P("fsdp", "grp"),
            P("fsdp", "grp"),
            P("fsdp", "grp"),
            small,
            small,
            small,
            P("fsdp", "grp"),
            small,
            small,
            small,
            P("grp", "fsdp"),
            P("grp", "fsdp"),
            P("fsdp", "grp"),
            P("fsdp", "grp", None),
            P("fsdp", "grp", None),
            P("fsdp", None, "grp"),
        ),
        check_vma=False,
    )
```

```python
import functools

import jax
import jax.numpy as jnp
from jax import lax
from jax.experimental import pallas as pl
from jax.experimental.pallas import tpu as pltpu
from jax.sharding import PartitionSpec as P

HEADS = 16
HEAD_DIM = 128
EPSILON = 1e-06
ROPE_BASE = 1000000.0
MASK_FILL = -1e30

F32 = jnp.float32
BF16 = jnp.bfloat16
MESH = pl.DeviceIdType.MESH
ANY = pl.BlockSpec(memory_space=pl.ANY)
VMEM = pl.BlockSpec(memory_space=pltpu.VMEM)
MIB = 2**20


def dot(left, right, dims, out=F32):
    return lax.dot_general(left, right, (dims, ((), ())), preferred_element_type=out)


def plain_dot(left, right):
    return dot(left, right, ((1,), (0,)))


def trans_dot(left, right):
    return dot(left, right, ((1,), (1,)))


def rows_dot(left, right):
    return dot(left, right, ((0,), (0,)))


def pieces(total, size):
    return [(a, min(size, total - a)) for a in range(0, total, size)]


def hidden_part(x, g, gate, w_gate, w_up, w_down, hidden, d_gate, d_up):
    units = w_gate.shape[1]
    sens = None
    for a, n in pieces(units, 256):
        s = pl.ds(a, n)
        pre = plain_dot(x, w_gate[:, s])
        up = plain_dot(x, w_up[:, s])
        plain = trans_dot(g, w_down[s, :])
        sigma = 1.0 / (1.0 + jnp.exp(-pre))
        act = pre * sigma
        slope = sigma * (1.0 + pre * (1.0 - sigma))
        h = (act * up).astype(BF16)
        hidden[:, s] = h
        grad = gate * plain
        d_gate[:, s] = (grad * up * slope).astype(BF16)
        d_up[:, s] = (grad * act).astype(BF16)
        part = jnp.sum(plain * h.astype(F32), axis=-1, keepdims=True)
        sens = part if sens is None else sens + part
    return sens


def expert_kernel(x_ref, g_ref, gate_ref, wg, wu, wd, hidden, d_gate, d_up, d_out, y_ref, dx_ref, sens_ref):
    blocks, _, slots, features = x_ref.shape
    rows = blocks * slots
    x = x_ref[...].reshape(rows, features)
    g = g_ref[...].reshape(rows, features)
    gate = gate_ref[...].reshape(rows, 1)
    wg, wu, wd = wg.at[0], wu.at[0], wd.at[0]
    hid, dg, du = hidden.at[0], d_gate.at[0], d_up.at[0]
    d_out[...] = (gate * g.astype(F32)).astype(BF16).reshape(d_out.shape)
    sens = hidden_part(x, g, gate, wg, wu, wd, hid, dg, du)
    sens_ref[...] = sens.reshape(sens_ref.shape)
    for a, n in pieces(features, 512):
        s = pl.ds(a, n)
        y = plain_dot(hid[...], wd[:, s]).astype(BF16)
        y_ref[:, :, :, s] = (gate * y.astype(F32)).astype(BF16).reshape(blocks, 1, slots, n)
        dx = trans_dot(dg[...], wg[s, :]) + trans_dot(du[...], wu[s, :])
        dx_ref[:, :, :, s] = dx.astype(BF16).reshape(blocks, 1, slots, n)


def expert_call(rows_in, rows_cot, gate, w_gate, w_up, w_down, tile):
    blocks, experts, slots, features = rows_in.shape
    units = w_gate.shape[2]
    steps = blocks // tile
    rows = tile * slots

    def slot_spec(cols):
        return pl.BlockSpec((tile, 1, slots, cols), lambda i, t: (t, i, 0, 0))

    def unit_spec():
        return pl.BlockSpec((1, rows, units), lambda i, t: (i, t, 0))

    def weight_spec(a, b):
        return pl.BlockSpec((1, a, b), lambda i, t: (i, 0, 0))

    units_shape = jax.ShapeDtypeStruct((experts, blocks * slots, units), BF16)
    slots_shape = jax.ShapeDtypeStruct((blocks, experts, slots, features), BF16)
    return pl.pallas_call(
        expert_kernel,
        grid=(experts, steps),
        in_specs=[
            slot_spec(features),
            slot_spec(features),
            slot_spec(1),
            weight_spec(features, units),
            weight_spec(features, units),
            weight_spec(units, features),
        ],
        out_specs=[unit_spec()] * 3 + [slot_spec(features)] * 3 + [slot_spec(1)],
        out_shape=[units_shape] * 3
        + [slots_shape] * 3
        + [jax.ShapeDtypeStruct((blocks, experts, slots, 1), F32)],
        compiler_params=pltpu.CompilerParams(vmem_limit_bytes=62 * MIB),
    )(rows_in, rows_cot, gate, w_gate, w_up, w_down)


def shared_kernel(
    x_ref, g_ref, head_ref, pick_ref, y_in, dx_in, lane_ref, heads_w, switch_row, wg, wu, wd,
    hidden, d_gate, d_up, d_out, y_ref, dx_ref, sens_ref,
):
    features = x_ref.shape[1]
    x = x_ref[...]
    g = g_ref[...]
    opener = head_ref[...]
    d_out[...] = (opener * g.astype(F32)).astype(BF16)
    sens = hidden_part(x, d_out[...], 1.0, wg, wu, wd, hidden, d_gate, d_up)
    sens = (1.0 - opener) * sens
    sens_ref[...] = sens
    pick = pick_ref[0]
    lanes = lane_ref[...]
    for a, n in pieces(features, 512):
        s = pl.ds(a, n)
        y = opener * plain_dot(hidden[...], wd[:, s]) + rows_dot(pick, y_in[0, :, s])
        y_ref[:, s] = y.astype(BF16)
        dx = trans_dot(d_gate[...], wg[s, :]) + trans_dot(d_up[...], wu[s, :])
        dx = dx + rows_dot(pick, dx_in[0, :, s])
        dx = dx + plain_dot(lanes, heads_w[:, s]) + sens * switch_row[:, s]
        dx_ref[:, s] = dx.astype(BF16)


def shared_call(x, g, opener, pick, y_in, dx_in, lanes, heads_w, switch_row, w_gate, w_up, w_down):
    count, features = x.shape
    units = w_gate.shape[1]
    blocks, taken, tile = pick.shape
    width = lanes.shape[1]

    def rows_spec(cols):
        return pl.BlockSpec((tile, cols), lambda b: (b, 0))

    def block_spec(cols):
        return pl.BlockSpec((1, taken, cols), lambda b: (b, 0, 0))

    def whole(a, b):
        return pl.BlockSpec((a, b), lambda b_: (0, 0), pipeline_mode=pl.Buffered(1))

    def shape(cols, dtype=BF16):
        return jax.ShapeDtypeStruct((count, cols), dtype)

    return pl.pallas_call(
        shared_kernel,
        grid=(blocks,),
        in_specs=[
            rows_spec(features),
            rows_spec(features),
            rows_spec(1),
            block_spec(tile),
            block_spec(features),
            block_spec(features),
            rows_spec(width),
            whole(width, features),
            whole(1, features),
            whole(features, units),
            whole(features, units),
            whole(units, features),
        ],
        out_specs=[rows_spec(units)] * 3 + [rows_spec(features)] * 3 + [rows_spec(1)],
        out_shape=[shape(units)] * 3 + [shape(features)] * 3 + [shape(1, F32)],
        compiler_params=pltpu.CompilerParams(vmem_limit_bytes=62 * MIB),
    )(x, g, opener, pick, y_in, dx_in, lanes, heads_w, switch_row, w_gate, w_up, w_down)


def other_kernel(x_ref, g_ref, heads, wg, wu, wd, hidden, d_gate, d_up, d_out):
    x = x_ref[...]
    pre = trans_dot(x, heads[...])
    opener = 1.0 / (1.0 + jnp.exp(-pre[:, heads.shape[0] - 1 :]))
    d_out[...] = (opener * g_ref[...].astype(F32)).astype(BF16)
    hidden_part(x, d_out[...], 1.0, wg, wu, wd, hidden, d_gate, d_up)


def other_call(x, g, heads, w_gate, w_up, w_down, tile):
    count, features = x.shape
    units = w_gate.shape[1]

    def rows_spec(cols):
        return pl.BlockSpec((tile, cols), lambda b: (b, 0))

    def whole(a, b):
        return pl.BlockSpec((a, b), lambda b_: (0, 0), pipeline_mode=pl.Buffered(1))

    def shape(cols):
        return jax.ShapeDtypeStruct((count, cols), BF16)

    return pl.pallas_call(
        other_kernel,
        grid=(count // tile,),
        in_specs=[
            rows_spec(features),
            rows_spec(features),
            whole(heads.shape[0], features),
            whole(features, units),
            whole(features, units),
            whole(units, features),
        ],
        out_specs=[rows_spec(units)] * 3 + [rows_spec(features)],
        out_shape=[shape(units)] * 3 + [shape(features)],
        compiler_params=pltpu.CompilerParams(vmem_limit_bytes=62 * MIB),
    )(x, g, heads, w_gate, w_up, w_down)


class Line:
    def __init__(self, parts, inner, sources, outs, sib, recv, bufs, sems):
        self.parts, self.inner, self.sources, self.outs = parts, inner, sources, outs
        self.sib, self.recv = sib, recv
        self.own_v, self.sib_v, self.in_v, self.more_v, self.send_v, self.out_v, self.turned_v = bufs
        self.own_sem, self.sib_sem, self.in_sem, self.out_sem, self.sib_send, self.sib_recv, self.sent, self.got = sems
        self.chunks = len(sources) * parts
        self.slots = self.send_v.shape[0]
        self.rows = sources[0].shape[2] // parts
        g = lax.axis_index("grp")
        self.z, self.core = g // 2, lax.rem(g, 2)
        self.is_end = (self.z == 0) | (self.z == 3)
        self.is_mid = (self.z == 1) | (self.z == 2)

    def at(self, z, core):
        return {"grp": 2 * z + core}

    def span(self, q):
        return lax.div(q, self.parts), pl.ds(
            pl.multiple_of(lax.rem(q, self.parts) * self.rows, self.rows), self.rows
        )

    def swap(self, j, m, r, q):
        return pltpu.make_async_remote_copy(
            src_ref=self.sources[j].at[:, 1 - self.core, r],
            dst_ref=self.sib.at[m, :, r],
            send_sem=self.sib_send.at[q],
            recv_sem=self.sib_recv.at[q],
            device_id=self.at(self.z, 1 - self.core),
            device_id_type=MESH,
        )

    def swap_any(self, q):
        m, r = self.span(q)
        return self.swap(0, m, r, q)

    def when_summing(self, condition=None):
        if self.inner:
            condition = self.is_mid if condition is None else self.is_mid & condition
        return (lambda body: body()) if condition is None else pl.when(condition)

    def start_swaps(self):
        @self.when_summing()
        def _():
            for m in range(len(self.sources)):
                for h in range(self.parts):
                    self.swap(m, m, pl.ds(h * self.rows, self.rows), m * self.parts + h).start()

    def out_copy(self, j, r):
        ref, turned = self.outs[j]
        if turned:
            return pltpu.make_async_copy(self.turned_v, ref.at[:, r], self.out_sem)
        return pltpu.make_async_copy(self.out_v, ref.at[r], self.out_sem)

    def each_out(self, q, body):
        m, r = self.span(q)
        for j in range(len(self.sources)):

            @pl.when(m == j)
            def _():
                body(j, r)

    def hop(self, q, slot, target, place):
        m, r = self.span(q)
        return pltpu.make_async_remote_copy(
            src_ref=self.send_v.at[slot],
            dst_ref=self.recv.at[m, place, r],
            send_sem=self.sent.at[slot],
            recv_sem=self.got.at[q, place],
            device_id=self.at(target, self.core),
            device_id_type=MESH,
        )

    def arrived(self, q, place):
        self.hop(q, 0, self.z, place).wait_recv()

    def own_load(self, j, p, r, k):
        return pltpu.make_async_copy(self.sources[j].at[p, self.core, r], self.own_v.at[k], self.own_sem.at[k])

    def sib_load(self, m, p, r, k):
        return pltpu.make_async_copy(self.sib.at[m, p, r], self.sib_v.at[k], self.sib_sem.at[k])

    def start_base(self, q, p, k):
        m, r = self.span(q)
        for j in range(len(self.sources)):

            @pl.when(m == j)
            def _():
                self.own_load(j, p, r, k).start()

        self.sib_load(m, p, r, k).start()

    def base(self, k):
        r = pl.ds(0, self.rows)
        self.own_load(0, 0, r, k).wait()
        self.sib_load(0, 0, r, k).wait()
        return self.own_v[k].astype(F32) + self.sib_v[k].astype(F32)

    def fetch(self, q, place, buf, k):
        self.arrived(q, place)
        m, r = self.span(q)
        c = pltpu.make_async_copy(self.recv.at[m, place, r], buf, self.in_sem.at[k])
        c.start()
        c.wait()
        return buf[...].astype(F32)

    def send(self, t, k, q, p, target, place, more, first):
        depth = self.slots // 3
        slot = lax.rem(t, depth) * 3 + k

        @pl.when(t >= depth + first)
        def _():
            self.hop(q, slot, target, place).wait_send()

        if more:
            extra = self.fetch(q, p, self.in_v, 0)
            total = self.base(k) + extra
        else:
            total = self.base(k)
        self.send_v[slot] = total.astype(BF16)
        self.hop(q, slot, target, place).start()

    def turn(self, t):
        z, chunks = self.z, self.chunks
        to_end = self.is_end & (t >= 0) & (t < chunks)
        to_next = self.is_mid & (t >= 1) & (t < chunks + 1)
        to_last = self.is_mid & (t >= 2) & (t < chunks + 2)
        last = (t >= 3) & (t < chunks + 3)

        @self.when_summing((t >= 0) & (t < chunks))
        def _():
            self.swap_any(t).wait_recv()

        def end_piece(j):
            return jnp.where(z == 0, 3 - j, j)

        def next_piece(j):
            return jnp.where(z == 1, 3 - j, j)

        last_piece = jnp.where(z == 2, 3, 0)
        if not self.inner:

            @pl.when(to_end)
            def _():
                for j in range(3):
                    self.start_base(t, end_piece(j), j)

        @pl.when(to_next)
        def _():
            for j in range(2):
                self.start_base(t - 1, next_piece(j), j)

        @pl.when(to_last)
        def _():
            self.start_base(t - 2, last_piece, 2)

        @self.when_summing(last)
        def _():
            self.start_base(t - 3, z, 3)

        if not self.inner:

            @pl.when(to_end)
            def _():
                for j in range(3):
                    p = end_piece(j)
                    target = jnp.where(z == 0, 1, 2)
                    place = jnp.where((z == 3) & (p == 2), 4, p)
                    self.send(t, j, t, p, target, place, False, 0)

        @pl.when(to_next)
        def _():
            for j in range(2):
                p = next_piece(j)
                target = jnp.where(z == 1, 2, 1)
                place = jnp.where((z == 2) & (p == 1), 4, p)
                self.send(t, j, t - 1, p, target, place, not self.inner, 1)

        @pl.when(to_last)
        def _():
            place = jnp.where(z == 1, 4, last_piece)
            self.send(t, 2, t - 2, last_piece, last_piece, place, True, 2)

        @pl.when(last)
        def _():
            q = t - 3

            @pl.when(q >= 1)
            def _():
                self.each_out(q - 1, lambda j, r: self.out_copy(j, r).wait())

            if self.inner:

                @pl.when(z == 0)
                def _():
                    self.out_v[...] = self.fetch(q, 4, self.more_v, 1)

                @pl.when(z == 3)
                def _():
                    self.out_v[...] = self.fetch(q, 3, self.more_v, 1)

                @pl.when(z == 1)
                def _():
                    got = self.fetch(q, 4, self.more_v, 1)
                    self.out_v[...] = self.base(3) + got

                @pl.when(z == 2)
                def _():
                    got = self.fetch(q, 2, self.more_v, 1)
                    self.out_v[...] = self.base(3) + got

            else:
                self.out_v[...] = self.base(3)

                @pl.when(z > 0)
                def _():
                    self.out_v[...] = self.out_v[...] + self.fetch(q, z, self.in_v, 0)

                @pl.when(z < 3)
                def _():
                    self.out_v[...] = self.out_v[...] + self.fetch(q, 4, self.more_v, 1)

            def put(j, r):
                if self.outs[j][1]:
                    self.turned_v[...] = self.out_v[...].T
                self.out_copy(j, r).start()

            self.each_out(q, put)

    def finish(self):
        self.each_out(self.chunks - 1, lambda j, r: self.out_copy(j, r).wait())

        def body(q, carry):
            self.swap_any(q).wait_send()
            return carry

        @self.when_summing()
        def _():
            lax.fori_loop(0, self.chunks, body, 0)

        assert self.chunks >= self.slots // 3

        @self.when_summing()
        def _():
            for slot in range(self.slots):
                self.hop(0, slot, self.z, 0).wait_send()


def line_bufs(shape, slots, turned):
    return [pltpu.VMEM((4,) + shape, BF16)] * 2 + [
        pltpu.VMEM(shape, BF16),
        pltpu.VMEM(shape, BF16),
        pltpu.VMEM((slots,) + shape, BF16),
        pltpu.VMEM(shape, F32),
        pltpu.VMEM(shape[::-1] if turned else (8, 128), F32),
    ]


def line_sems(q, slots):
    return [
        pltpu.SemaphoreType.DMA((4,)),
        pltpu.SemaphoreType.DMA((4,)),
        pltpu.SemaphoreType.DMA((2,)),
        pltpu.SemaphoreType.DMA,
        pltpu.SemaphoreType.DMA((q,)),
        pltpu.SemaphoreType.DMA((q,)),
        pltpu.SemaphoreType.DMA((slots,)),
        pltpu.SemaphoreType.DMA((q, 5)),
    ]


def line_kernel(n_down, n_shared, parts, shift, *refs):
    def take(n):
        nonlocal refs
        taken, refs = refs[:n], refs[n:]
        return taken

    downs, shared = take(n_down), take(n_shared)
    three, part_out, out_part, mixed, vec, bias_add = take(6)
    out_down, out_gate, out_up, out_sdown, out_four, output, vec_out = take(7)
    sib_a, recv_a, att, sib_b, recv_b, sib_c, recv_c, out_in = take(8)
    bufs_a, bufs_b, bufs_c = take(7), take(7), take(7)
    vec_in, vec_own, vec_sib, vec_line, vec_send, parts_v, mixed_v, sum_v = take(8)
    sems_a, sems_b, sems_c = take(8), take(8), take(8)
    plane_send, plane_recv, local_sems, vec_send_sems, vec_recv_sems, out_send, out_recv = take(7)

    a = Line(parts, False, downs, [(out_down.at[j], True) for j in range(n_down)], sib_a, recv_a, bufs_a, sems_a)
    b = Line(1, False, [att.at[j] for j in range(4)], [(out_four.at[j], True) for j in range(4)], sib_b, recv_b, bufs_b, sems_b)
    c = Line(parts, shift, shared, [(out_gate, False), (out_up, False), (out_sdown, True)], sib_c, recv_c, bufs_c, sems_c)
    z, core = a.z, a.core
    f = lax.axis_index("fsdp")
    fx = f + 1 - 2 * lax.rem(f, 2)
    fy = f + 2 - 4 * (f // 2)
    fd = fx + 2 - 4 * (fx // 2)
    peers = (fx, fy, fd)
    sibling = a.at(z, 1 - core)
    width = three.shape[3] // 4

    barrier = pltpu.get_barrier_semaphore()
    for other in (sibling,) + tuple({"fsdp": p} for p in peers):
        pl.semaphore_signal(barrier, inc=1, device_id=other, device_id_type=MESH)

    @pl.when(z > 0)
    def _():
        pl.semaphore_signal(barrier, inc=1, device_id=a.at(z - 1, core), device_id_type=MESH)

    @pl.when(z < 3)
    def _():
        pl.semaphore_signal(barrier, inc=1, device_id=a.at(z + 1, core), device_id_type=MESH)

    @pl.when(a.is_end)
    def _():
        pl.semaphore_wait(barrier, 5)

    @pl.when(a.is_mid)
    def _():
        pl.semaphore_wait(barrier, 6)

    a.start_swaps()
    c.start_swaps()

    def cols(p):
        return pl.ds(pl.multiple_of(p * width, width), width)

    def to_owner(k, p):
        return pltpu.make_async_remote_copy(
            src_ref=three.at[:, :, :, cols(p)], dst_ref=att.at[pl.ds(0, 3), f],
            send_sem=plane_send.at[k], recv_sem=plane_recv.at[k],
            device_id={"fsdp": p}, device_id_type=MESH,
        )

    def vec_owner(k, p):
        return pltpu.make_async_remote_copy(
            src_ref=vec.at[p], dst_ref=vec_in.at[k],
            send_sem=vec_send_sems.at[k], recv_sem=vec_recv_sems.at[k],
            device_id={"fsdp": p}, device_id_type=MESH,
        )

    def out_owner(k, p):
        return pltpu.make_async_remote_copy(
            src_ref=out_part.at[k + 1], dst_ref=out_in.at[k],
            send_sem=out_send.at[k], recv_sem=out_recv.at[k],
            device_id={"fsdp": p}, device_id_type=MESH,
        )

    for k, p in enumerate(peers):
        vec_owner(k, p).start()
    for k, p in enumerate(peers):
        to_owner(k, p).start()
    keep = (
        pltpu.make_async_copy(three.at[:, :, :, cols(f)], att.at[pl.ds(0, 3), f], local_sems.at[0]),
        pltpu.make_async_copy(part_out, att.at[3], local_sems.at[1]),
    )
    for copy in keep:
        copy.start()

    def vec_swap():
        return pltpu.make_async_remote_copy(
            src_ref=vec_own, dst_ref=vec_sib, send_sem=vec_send_sems.at[3], recv_sem=vec_recv_sems.at[3],
            device_id=sibling, device_id_type=MESH,
        )

    def vec_hop(k, target):
        return pltpu.make_async_remote_copy(
            src_ref=vec_send.at[k], dst_ref=vec_line.at[k], send_sem=vec_send_sems.at[4 + k],
            recv_sem=vec_recv_sems.at[4 + k], device_id=a.at(target, core), device_id_type=MESH,
        )

    def finish_output():
        for k, p in enumerate(peers):
            out_owner(k, p).wait_recv()
        step = parts_v.shape[1]

        def body(i, carry):
            r = pl.ds(pl.multiple_of(i * step, step), step)
            loads = [pltpu.make_async_copy(out_part.at[0, r], parts_v.at[0], local_sems.at[3])]
            loads += [
                pltpu.make_async_copy(out_in.at[k, r], parts_v.at[k + 1], local_sems.at[4 + k]) for k in range(3)
            ]
            loads.append(pltpu.make_async_copy(mixed.at[r], mixed_v, local_sems.at[7]))
            for copy in loads:
                copy.start()
            for copy in loads:
                copy.wait()
            total = (parts_v[0].astype(F32) + parts_v[1].astype(F32)) + (
                parts_v[2].astype(F32) + parts_v[3].astype(F32)
            )
            sum_v[...] = (mixed_v[...] + total).astype(BF16)
            copy = pltpu.make_async_copy(sum_v, output.at[r], local_sems.at[8])
            copy.start()
            copy.wait()
            return carry

        lax.fori_loop(0, mixed.shape[0] // step, body, 0)

    def side_work(t):
        @pl.when(t == 1)
        def _():
            for k, p in enumerate(peers):
                vec_owner(k, p).wait_recv()
            copy = pltpu.make_async_copy(vec.at[f], vec_own, local_sems.at[2])
            copy.start()
            copy.wait()
            vec_own[...] = (vec_own[...] + vec_in[0]) + (vec_in[1] + vec_in[2]) + bias_add[...]
            vec_swap().start()

        @pl.when(t == 2)
        def _():
            vec_swap().wait_recv()
            vec_sib[...] = vec_sib[...] + vec_own[...]

            @pl.when(z == 0)
            def _():
                vec_send[0] = vec_sib[...]
                vec_hop(0, 1).start()

            @pl.when(z == 3)
            def _():
                vec_send[1] = vec_sib[...]
                vec_hop(1, 2).start()

        @pl.when((t == 3) & (z == 1))
        def _():
            vec_hop(0, 1).wait_recv()
            vec_send[0] = vec_sib[...] + vec_line[0]
            vec_hop(0, 2).start()

        @pl.when((t == 3) & (z == 2))
        def _():
            vec_hop(1, 2).wait_recv()
            vec_send[1] = vec_sib[...] + vec_line[1]
            vec_hop(1, 1).start()

        @pl.when(t == 3)
        def _():
            for k, p in enumerate(peers):
                to_owner(k, p).wait_recv()
            for copy in keep:
                copy.wait()
            b.start_swaps()
            for k, p in enumerate(peers):
                out_owner(k, p).start()

        @pl.when((t == 4) & (z == 2))
        def _():
            vec_hop(0, 2).wait_recv()
            vec_send[0] = vec_sib[...] + vec_line[0]
            vec_hop(0, 3).start()
            vec_out[...] = vec_send[0] + vec_line[1]

        @pl.when((t == 4) & (z == 1))
        def _():
            vec_hop(1, 1).wait_recv()
            vec_send[1] = vec_sib[...] + vec_line[1]
            vec_hop(1, 0).start()
            vec_out[...] = vec_send[1] + vec_line[0]

        @pl.when((t == 5) & (z == 3))
        def _():
            vec_hop(0, 3).wait_recv()
            vec_out[...] = vec_sib[...] + vec_line[0]

        @pl.when((t == 5) & (z == 0))
        def _():
            vec_hop(1, 0).wait_recv()
            vec_out[...] = vec_sib[...] + vec_line[1]

        @pl.when(t == 6)
        def _():
            finish_output()

    def slower(t):
        if a.chunks + b.chunks < c.chunks + 2:
            c.turn(t)
            return

        @pl.when((t != 2) & (t != 5))
        def _():
            c.turn(t - jnp.where(t > 2, 1, 0) - jnp.where(t > 5, 1, 0))

    def first_loop(t, carry):
        a.turn(t)
        b.turn(t - a.chunks)
        slower(t)
        side_work(t)
        return carry

    def last_loop(t, carry):
        b.turn(t - a.chunks)
        slower(t)
        return carry

    turns = max(a.chunks + b.chunks, c.chunks + 2) + 3
    lax.fori_loop(0, max(7, a.chunks + 3), first_loop, 0)
    lax.fori_loop(max(7, a.chunks + 3), turns, last_loop, 0)
    a.finish()
    b.finish()
    c.finish()
    for k, p in enumerate(peers):
        vec_owner(k, p).wait_send()
        to_owner(k, p).wait_send()
        out_owner(k, p).wait_send()
    vec_swap().wait_send()

    @pl.when(z < 3)
    def _():
        vec_hop(0, 3).wait_send()

    @pl.when(z > 0)
    def _():
        vec_hop(1, 0).wait_send()


def line_call(downs, shared, three, part_out, out_part, mixed, vec, bias_add, parts, shift, collective_id):
    _, _, rows, cols = shared[0].shape
    m, s = len(downs), len(shared)
    _, _, share, features = three.shape
    width = features // 4
    own_rows = mixed.shape[0]
    r = rows // parts
    slots = 9
    small = (16, width)
    step = own_rows // 4

    def shape(*dims, dtype=BF16):
        return jax.ShapeDtypeStruct(dims, dtype)

    outs = pl.pallas_call(
        functools.partial(line_kernel, m, s, parts, shift),
        out_shape=(
            shape(m, cols, rows, dtype=F32),
            shape(rows, cols, dtype=F32),
            shape(rows, cols, dtype=F32),
            shape(cols, rows, dtype=F32),
            shape(4, width, share, dtype=F32),
            shape(own_rows, features),
            shape(*small, dtype=F32),
            shape(m, 4, rows, cols),
            shape(m, 5, rows, cols),
            shape(4, 4, 2, share, width),
            shape(4, 4, share, width),
            shape(4, 5, share, width),
            shape(s, 4, rows, cols),
            shape(s, 5, rows, cols),
            shape(3, own_rows, features),
        ),
        in_specs=[ANY] * (m + s + 5) + [VMEM],
        out_specs=(ANY,) * 6 + (VMEM,) + (ANY,) * 8,
        scratch_shapes=line_bufs((r, cols), slots, True)
        + line_bufs((share, width), slots, True)
        + line_bufs((r, cols), slots, True)
        + [
            pltpu.VMEM((3,) + small, F32),
            pltpu.VMEM(small, F32),
            pltpu.VMEM(small, F32),
            pltpu.VMEM((2,) + small, F32),
            pltpu.VMEM((2,) + small, F32),
            pltpu.VMEM((4, step, features), BF16),
            pltpu.VMEM((step, features), F32),
            pltpu.VMEM((step, features), BF16),
        ]
        + line_sems(m * parts, slots)
        + line_sems(4, slots)
        + line_sems(s * parts, slots)
        + [
            pltpu.SemaphoreType.DMA((3,)),
            pltpu.SemaphoreType.DMA((3,)),
            pltpu.SemaphoreType.DMA((9,)),
            pltpu.SemaphoreType.DMA((6,)),
            pltpu.SemaphoreType.DMA((6,)),
            pltpu.SemaphoreType.DMA((3,)),
            pltpu.SemaphoreType.DMA((3,)),
        ],
        compiler_params=pltpu.CompilerParams(
            collective_id=collective_id, has_side_effects=True, vmem_limit_bytes=60 * MIB
        ),
    )(*downs, *shared, three, part_out, out_part, mixed, vec, bias_add)
    return outs[:7]


def plane_neighbours():
    f = lax.axis_index("fsdp")
    by_x = f + 1 - 2 * lax.rem(f, 2)
    by_y = f + 2 - 4 * (f // 2)
    return {"fsdp": by_x}, {"fsdp": by_y}


def plane_barrier(by_x, by_y):
    barrier = pltpu.get_barrier_semaphore()
    for other in (by_x, by_y):
        pl.semaphore_signal(barrier, inc=1, device_id=other, device_id_type=MESH)
    pl.semaphore_wait(barrier, 2)


class Side:
    block = 512

    def __init__(self, arrays, jobs):
        self.arrays, self.jobs = list(arrays), list(jobs)
        self.operands = sorted({o for job in self.jobs for pair in job for o in pair}, key=str)

    def shape(self, operand):
        number, axis, _ = operand
        full = self.arrays[number].shape
        return full if axis is None else full[:axis] + full[axis + 1 :]

    def out_shapes(self):
        return [
            jax.ShapeDtypeStruct((self.shape(job[0][0])[-1], self.shape(job[0][1])[-1]), BF16)
            for job in self.jobs
        ]

    def scratch(self):
        stages = sorted({self.shape(job[0][1])[-1] for job in self.jobs})
        self.stage_of = {n: k for k, n in enumerate(stages)}
        return (
            [pltpu.VMEM(self.shape(o), BF16) for o in self.operands]
            + [pltpu.VMEM((2, self.block, n), BF16) for n in stages]
            + [
                pltpu.SemaphoreType.DMA((max(1, len(self.operands)),)),
                pltpu.SemaphoreType.DMA((max(1, 2 * len(stages)),)),
            ]
        )

    def bind(self, ins, outs, scratch):
        n = len(self.operands)
        self.ins, self.outs = ins, outs
        self.bufs, self.stages = scratch[:n], scratch[n:-2]
        self.load_sems, self.out_sems = scratch[-2:]
        self.loaded, self.pending, self.turn_of = set(), {}, {}
        self.units = [
            (j, k)
            for j, job in enumerate(self.jobs)
            for k in range(self.shape(job[0][0])[-1] // self.block)
        ]

    def load(self, k):
        number, axis, entry = self.operands[k]
        ref = self.ins[number]
        if axis is not None:
            ref = ref.at[(slice(None),) * axis + (entry,)]
        return pltpu.make_async_copy(ref, self.bufs[k], self.load_sems.at[k])

    def begin(self):
        for o in [o for job in self.jobs for pair in job for o in pair]:
            k = self.operands.index(o)
            if k not in self.loaded:
                self.loaded.add(k)
                self.load(k).start()
        self.loaded = set()

    def step(self, number):
        for _ in range(number):
            if not self.units:
                return
            j, block = self.units.pop(0)
            pairs = [tuple(self.operands.index(o) for o in pair) for pair in self.jobs[j]]
            for k in [k for pair in pairs for k in pair]:
                if k not in self.loaded:
                    self.loaded.add(k)
                    self.load(k).wait()
            n = self.shape(self.jobs[j][0][1])[-1]
            stage = self.stage_of[n]
            slot = self.turn_of.get(stage, 0)
            self.turn_of[stage] = 1 - slot
            if (stage, slot) in self.pending:
                self.pending.pop((stage, slot)).wait()
            rows = pl.ds(block * self.block, self.block)
            total = None
            for ka, kb in pairs:
                left = self.bufs[ka][..., rows].reshape(-1, self.block)
                part = rows_dot(left, self.bufs[kb][...].reshape(-1, n))
                total = part if total is None else total + part
            self.stages[stage][slot] = total.astype(BF16)
            copy = pltpu.make_async_copy(
                self.stages[stage].at[slot], self.outs[j].at[rows], self.out_sems.at[2 * stage + slot]
            )
            copy.start()
            self.pending[(stage, slot)] = copy

    def end(self):
        self.step(len(self.units))
        for copy in self.pending.values():
            copy.wait()


def mid_kernel(middle, chunks, gathers, n_in, n_out, side, *refs):
    n_side, n_jobs = len(side.arrays), len(side.jobs)
    partial, ins = refs[0], refs[1 : 1 + n_in]
    side_ins, refs = refs[1 + n_in : 1 + n_in + n_side], refs[1 + n_in + n_side :]
    outs, refs = refs[:n_out], refs[n_out:]
    gathered = None
    if gathers:
        gathered, refs = refs[0], refs[1:]
    side_outs, refs = refs[:n_jobs], refs[n_jobs:]
    relay_x, relay_y, got_x, got_y, sum_x, sum_y, own, send_sems, recv_sems, local_sems = refs[:10]
    if n_jobs:
        side.bind(side_ins, side_outs, refs[10:])
    rows = partial.shape[1]
    r = rows // chunks
    h = r // 2
    by_x, by_y = plane_neighbours()
    plane_barrier(by_x, by_y)

    def copy(i, kind, src, dst, target):
        return pltpu.make_async_remote_copy(
            src_ref=src, dst_ref=dst, send_sem=send_sems.at[i, kind], recv_sem=recv_sems.at[i, kind],
            device_id=target, device_id_type=MESH,
        )

    def sends(i):
        lo, hi = pl.ds(i * r, h), pl.ds(i * r + h, h)
        half = pl.ds(i * h, h)
        made = {
            0: lambda: copy(i, 0, partial.at[3, lo], relay_x.at[half], by_x),
            1: lambda: copy(i, 1, partial.at[3, hi], relay_y.at[half], by_y),
            2: lambda: copy(i, 2, partial.at[1, lo], got_x.at[lo], by_x),
            3: lambda: copy(i, 3, partial.at[2, hi], got_y.at[hi], by_y),
            4: lambda: copy(i, 4, sum_y.at[half], got_y.at[lo], by_y),
            5: lambda: copy(i, 5, sum_x.at[half], got_x.at[hi], by_x),
        }
        if gathers:
            made |= {
                6: lambda: copy(i, 6, own.at[lo], gathered.at[1, lo], by_x),
                7: lambda: copy(i, 7, own.at[hi], gathered.at[2, hi], by_y),
                8: lambda: copy(i, 8, own.at[hi], gathered.at[1, hi], by_x),
                9: lambda: copy(i, 9, own.at[lo], gathered.at[2, lo], by_y),
                10: lambda: copy(i, 10, gathered.at[1, lo], gathered.at[3, lo], by_y),
                11: lambda: copy(i, 11, gathered.at[2, hi], gathered.at[3, hi], by_x),
            }
        return made

    def keep(i):
        span = pl.ds(i * r, r)
        return pltpu.make_async_copy(own.at[span], gathered.at[0, span], local_sems.at[i])

    def stage(n, i):
        s = sends(i)
        lo, hi = pl.ds(i * r, h), pl.ds(i * r + h, h)
        half, span = pl.ds(i * h, h), pl.ds(i * r, r)
        if n == 0:
            for kind in (0, 1, 2, 3):
                s[kind]().start()
        elif n == 1:
            s[0]().wait_recv()
            sum_y[half] = (partial[2, lo].astype(F32) + relay_x[half].astype(F32)).astype(BF16)
            s[4]().start()
            s[1]().wait_recv()
            sum_x[half] = (partial[1, hi].astype(F32) + relay_y[half].astype(F32)).astype(BF16)
            s[5]().start()
        elif n == 2:
            for kind in (2, 3, 4, 5):
                s[kind]().wait_recv()
            total = partial[0, span].astype(F32) + (got_x[span].astype(F32) + got_y[span].astype(F32))
            given = middle(total, span, ins, outs)
            if gathers:
                own[span] = given
                for kind in (6, 7, 8, 9):
                    s[kind]().start()
                keep(i).start()
        elif n == 3 and gathers:
            s[6]().wait_recv()
            s[10]().start()
            s[7]().wait_recv()
            s[11]().start()
        elif n == 4:
            if gathers:
                for kind in (8, 9, 10, 11):
                    s[kind]().wait_recv()
                keep(i).wait()
            for kind in s:
                s[kind]().wait_send()

    turns = chunks + 4
    if n_jobs:
        side.begin()
        each = -(-len(side.units) // turns)
    for t in range(turns):
        for n in range(5):
            if 0 <= t - n < chunks:
                stage(n, t - n)
        if n_jobs:
            side.step(each)
    if n_jobs:
        side.end()


def mid_call(middle, partial, ins, out_shapes, gathers, side, collective_id, chunks=4):
    _, rows, cols = partial.shape
    outs = tuple(out_shapes)
    specs = (VMEM,) * len(outs)
    if gathers:
        outs += (jax.ShapeDtypeStruct((4, rows, cols), BF16),)
        specs += (ANY,)
    outs += tuple(side.out_shapes())
    specs += (ANY,) * len(side.jobs)
    return pl.pallas_call(
        functools.partial(mid_kernel, middle, chunks, gathers, len(ins), len(out_shapes), side),
        out_shape=outs,
        in_specs=[VMEM] * (1 + len(ins)) + [ANY] * len(side.arrays),
        out_specs=specs,
        scratch_shapes=[
            pltpu.VMEM((rows // 2, cols), BF16),
            pltpu.VMEM((rows // 2, cols), BF16),
            pltpu.VMEM((rows, cols), BF16),
            pltpu.VMEM((rows, cols), BF16),
            pltpu.VMEM((rows // 2, cols), BF16),
            pltpu.VMEM((rows // 2, cols), BF16),
            pltpu.VMEM((rows, cols), BF16),
            pltpu.SemaphoreType.DMA((chunks, 12)),
            pltpu.SemaphoreType.DMA((chunks, 12)),
            pltpu.SemaphoreType.DMA((chunks,)),
        ]
        + (side.scratch() if side.jobs else []),
        compiler_params=pltpu.CompilerParams(
            collective_id=collective_id, has_side_effects=True, vmem_limit_bytes=60 * MIB
        ),
    )(partial, *ins, *side.arrays)


def start_kernel(
    tokens, small, marks, w_q, w_k, w_v,
    tokens_all, small_all, marks_all, w_cols, relay,
    send_sems, recv_sems, local_sems,
):
    f = lax.axis_index("fsdp")
    g = lax.axis_index("grp")
    core = lax.rem(g, 2)
    rows = tokens.shape[0]
    depth = w_q.shape[0]
    width = w_q.shape[1] // 4
    by_x, by_y = plane_neighbours()
    fx, fy = by_x["fsdp"], by_y["fsdp"]
    fd = fx + 2 - 4 * (fx // 2)
    by_d, sibling = {"fsdp": fd}, {"grp": g + 1 - 2 * core}
    barrier = pltpu.get_barrier_semaphore()
    for other in (by_x, by_y, by_d, sibling):
        pl.semaphore_signal(barrier, inc=1, device_id=other, device_id_type=MESH)
    pl.semaphore_wait(barrier, 4)

    def copy(n, src, dst, target):
        return pltpu.make_async_remote_copy(
            src_ref=src, dst_ref=dst, send_sem=send_sems.at[n], recv_sem=recv_sems.at[n],
            device_id=target, device_id_type=MESH,
        )

    def columns(j):
        return pl.ds(pl.multiple_of(j * width, width), width)

    def block_rows(owner, c):
        return pl.ds(pl.multiple_of(owner * depth + c * (depth // 2), depth // 2), depth // 2)

    half = depth // 2
    mine = pl.ds(pl.multiple_of(core * half, half), half)
    all_sends = []

    def go(c):
        c.start()
        all_sends.append(c)
        return c

    waits = []
    n = 0
    for k, target in ((1, by_x), (2, by_y), (3, by_d)):
        waits.append(go(copy(n, small, small_all.at[k], target)))
        waits.append(go(copy(n + 1, marks, marks_all.at[k], target)))
        n += 2
    locals_ = [
        pltpu.make_async_copy(small, small_all.at[0], local_sems.at[0]),
        pltpu.make_async_copy(marks, marks_all.at[0], local_sems.at[1]),
        pltpu.make_async_copy(tokens, tokens_all.at[0], local_sems.at[2]),
    ]
    for j, w in enumerate((w_q, w_k, w_v)):
        locals_.append(
            pltpu.make_async_copy(
                w.at[:, columns(f)],
                w_cols.at[pl.ds(pl.multiple_of(f * depth, depth), depth), pl.ds(j * width, width)],
                local_sems.at[3 + j],
            )
        )
    for c in locals_:
        c.start()

    quarter = half // 2
    first = pl.ds(pl.multiple_of(core * half, quarter), quarter)
    second = pl.ds(pl.multiple_of(core * half + quarter, quarter), quarter)
    relays_x, relays_y, direct_x, direct_y = [], [], [], []
    for j, w in enumerate((w_q, w_k, w_v)):
        relays_x.append(go(copy(n, w.at[first, columns(fd)], relay.at[0, j], by_x)))
        relays_y.append(go(copy(n + 1, w.at[second, columns(fd)], relay.at[1, j], by_y)))
        n += 2
    for j, w in enumerate((w_q, w_k, w_v)):
        place = w_cols.at[block_rows(f, core), pl.ds(j * width, width)]
        direct_x.append(go(copy(n, w.at[mine, columns(fx)], place, by_x)))
        direct_y.append(go(copy(n + 1, w.at[mine, columns(fy)], place, by_y)))
        n += 2
    low, high = pl.ds(0, rows // 2), pl.ds(rows // 2, rows // 2)
    t_x0 = go(copy(n, tokens.at[low], tokens_all.at[1, low], by_x))
    t_y1 = go(copy(n + 1, tokens.at[high], tokens_all.at[2, high], by_y))
    t_x1 = go(copy(n + 2, tokens.at[high], tokens_all.at[1, high], by_x))
    t_y0 = go(copy(n + 3, tokens.at[low], tokens_all.at[2, low], by_y))
    n += 4
    forwarded = []
    for j in range(3):
        relays_x[j].wait_recv()
        forwarded.append(
            go(copy(
                n, relay.at[0, j],
                w_cols.at[pl.ds(pl.multiple_of(fx * depth + core * half, quarter), quarter), pl.ds(j * width, width)],
                by_y,
            ))
        )
        relays_y[j].wait_recv()
        forwarded.append(
            go(copy(
                n + 1, relay.at[1, j],
                w_cols.at[pl.ds(pl.multiple_of(fy * depth + core * half + quarter, quarter), quarter), pl.ds(j * width, width)],
                by_x,
            ))
        )
        n += 2
    shares = []

    def share(owner):
        nonlocal n
        place = w_cols.at[block_rows(owner, core)]
        shares.append(go(copy(n, place, place, sibling)))
        n += 1

    for c in direct_x:
        c.wait_recv()
    share(fx)
    for c in direct_y:
        c.wait_recv()
    share(fy)
    t_x0.wait_recv()
    t_d0 = go(copy(n, tokens_all.at[1, low], tokens_all.at[3, low], by_y))
    t_y1.wait_recv()
    t_d1 = go(copy(n + 1, tokens_all.at[2, high], tokens_all.at[3, high], by_x))
    n += 2
    for c in forwarded:
        c.wait_recv()
    share(fd)
    for c in waits + shares + [t_x1, t_y0, t_d0, t_d1]:
        c.wait_recv()
    for c in locals_:
        c.wait()
    for c in all_sends:
        c.wait_send()


def start_call(tokens, small, marks, w_q, w_k, w_v, collective_id):
    depth, features = w_q.shape
    width = features // 4
    n = 6 + 6 + 6 + 4 + 6 + 2 + 3
    return pl.pallas_call(
        start_kernel,
        out_shape=(
            jax.ShapeDtypeStruct((4,) + tokens.shape, tokens.dtype),
            jax.ShapeDtypeStruct((4,) + small.shape, small.dtype),
            jax.ShapeDtypeStruct((4,) + marks.shape, marks.dtype),
            jax.ShapeDtypeStruct((4 * depth, 3 * width), BF16),
            jax.ShapeDtypeStruct((2, 3, depth // 4, width), BF16),
        ),
        in_specs=[ANY] * 6,
        out_specs=(ANY,) * 5,
        scratch_shapes=[
            pltpu.SemaphoreType.DMA((n,)),
            pltpu.SemaphoreType.DMA((n,)),
            pltpu.SemaphoreType.DMA((6,)),
        ],
        compiler_params=pltpu.CompilerParams(
            collective_id=collective_id, has_side_effects=True, vmem_limit_bytes=16 * MIB
        ),
    )(tokens, small, marks, w_q, w_k, w_v)[:4]


def turn_half(x):
    return pltpu.roll(x, HEAD_DIM // 2, 1)


def hidden_bias(of_keys, of_queries):
    key_segment, key_position = of_keys[0], of_keys[4]
    seen = (
        (key_segment == of_queries[1]) | (key_segment == of_queries[2]) | (key_segment == of_queries[3])
    ) & (key_position <= of_queries[4])
    return jnp.where(seen, 0.0, MASK_FILL)


def attend_kernel(
    tokens, gain, w_cols, bias, w_out, cosine, sine, mark_cols, mark_rows,
    normed, three, attended, branch, mask,
):
    count = tokens.shape[0]
    width = w_out.shape[0]
    scale = HEAD_DIM**-0.5
    step = 256
    rows_of = [mark_rows[j : j + 1, :] for j in range(5)]
    for a, n in pieces(count, step):
        s = pl.ds(a, n)
        x = tokens[s, :].astype(F32)
        factor = lax.rsqrt(jnp.mean(x * x, axis=-1, keepdims=True) + EPSILON)
        normed[s, :] = (x * factor * gain[...]).astype(BF16)
        cols_of = [mark_cols[s, j : j + 1] for j in range(5)]
        mask[s, :] = hidden_bias(rows_of, cols_of)
    for b, m in pieces(3 * width, 256):
        c = pl.ds(b, m)
        pre = plain_dot(normed[...], w_cols[:, c]) + bias[:, c]
        if b < 2 * width:
            for d in range(0, m, HEAD_DIM):
                x = pre[:, d : d + HEAD_DIM]
                three[:, b + d : b + d + HEAD_DIM] = (
                    x * cosine[...] + turn_half(x) * sine[...]
                ).astype(BF16)
        else:
            three[:, c] = pre.astype(BF16)
    for h in range(width // HEAD_DIM):
        q_cols = pl.ds(h * HEAD_DIM, HEAD_DIM)
        k_cols = pl.ds(width + h * HEAD_DIM, HEAD_DIM)
        v_cols = pl.ds(2 * width + h * HEAD_DIM, HEAD_DIM)
        for a, n in pieces(count, step):
            s = pl.ds(a, n)
            scores = trans_dot(three[s, q_cols], three[:, k_cols]) + mask[s, :]
            peak = jnp.max(scores, axis=-1, keepdims=True)
            expo = jnp.exp((scores - peak) * scale)
            total = jnp.sum(expo, axis=-1, keepdims=True)
            weights = (expo * (1.0 / total)).astype(BF16)
            attended[s, q_cols] = plain_dot(weights, three[:, v_cols]).astype(BF16)
    for b, m in pieces(w_out.shape[1], 512):
        c = pl.ds(b, m)
        branch[:, c] = plain_dot(attended[...], w_out[:, c]).astype(BF16)


def attend_call(tokens, gain, w_cols, bias, w_out, cosine, sine, mark_cols, mark_rows):
    count, features = tokens.shape
    width = w_out.shape[0]

    def shape(cols):
        return jax.ShapeDtypeStruct((count, cols), BF16)

    return pl.pallas_call(
        attend_kernel,
        in_specs=[VMEM] * 9,
        out_specs=(VMEM,) * 4,
        out_shape=(shape(features), shape(3 * width), shape(width), shape(features)),
        scratch_shapes=[pltpu.VMEM((count, count), F32)],
        compiler_params=pltpu.CompilerParams(vmem_limit_bytes=60 * MIB),
    )(tokens, gain, w_cols, bias, w_out, cosine, sine, mark_cols, mark_rows)


def attend_back_kernel(
    grad, w_out, three, w_cols, cosine, sine, mark_cols, mark_rows,
    grad_three, partial, grad_bias, mask, grad_att,
):
    count = grad.shape[0]
    width = w_out.shape[0]
    scale = HEAD_DIM**-0.5
    step = 256
    for b, m in pieces(width, 256):
        c = pl.ds(b, m)
        grad_att[:, c] = trans_dot(grad[...], w_out[c, :]).astype(BF16)
    rows_of = [mark_rows[j : j + 1, :] for j in range(5)]
    for a, n in pieces(count, step):
        s = pl.ds(a, n)
        mask[s, :] = hidden_bias([mark_cols[s, j : j + 1] for j in range(5)], rows_of)
    for h in range(width // HEAD_DIM):
        q_cols = pl.ds(h * HEAD_DIM, HEAD_DIM)
        k_cols = pl.ds(width + h * HEAD_DIM, HEAD_DIM)
        v_cols = pl.ds(2 * width + h * HEAD_DIM, HEAD_DIM)
        grad_k = grad_v = None
        for a, n in pieces(count, step):
            s = pl.ds(a, n)
            query, g = three[s, q_cols], grad_att[s, q_cols]
            scores = trans_dot(three[:, k_cols], query) + mask[:, s]
            peak = jnp.max(scores, axis=0, keepdims=True)
            expo = jnp.exp((scores - peak) * scale)
            probs = expo * (1.0 / jnp.sum(expo, axis=0, keepdims=True))
            weight_grad = trans_dot(three[:, v_cols], g)
            diagonal = jnp.sum(probs * weight_grad, axis=0, keepdims=True)
            score_grad = (probs * (weight_grad - diagonal)).astype(BF16)
            part_v = plain_dot(probs.astype(BF16), g)
            part_k = plain_dot(score_grad, query)
            grad_v = part_v if grad_v is None else grad_v + part_v
            grad_k = part_k if grad_k is None else grad_k + part_k
            grad_q = rows_dot(score_grad, three[:, k_cols]) * scale
            grad_three[s, q_cols] = (
                grad_q * cosine[s, :] - turn_half(grad_q) * sine[s, :]
            ).astype(BF16)
        grad_k = grad_k * scale
        grad_three[:, k_cols] = (grad_k * cosine[...] - turn_half(grad_k) * sine[...]).astype(BF16)
        grad_three[:, v_cols] = grad_v.astype(BF16)
    for b, m in pieces(3 * width, 512):
        c = pl.ds(b, m)
        grad_bias[:, c] = jnp.sum(grad_three[:, c].astype(F32), axis=0, keepdims=True)
    for b, m in pieces(w_cols.shape[0], 512):
        c = pl.ds(b, m)
        partial[:, c] = trans_dot(grad_three[...], w_cols[c, :]).astype(BF16)


def attend_back_call(grad, w_out, three, w_cols, cosine, sine, mark_cols, mark_rows):
    count, features = grad.shape
    width = w_out.shape[0]

    def shape(rows, cols, dtype=BF16):
        return jax.ShapeDtypeStruct((rows, cols), dtype)

    return pl.pallas_call(
        attend_back_kernel,
        in_specs=[VMEM] * 8,
        out_specs=(VMEM,) * 3,
        out_shape=(shape(count, 3 * width), shape(count, features), shape(1, 3 * width, F32)),
        scratch_shapes=[pltpu.VMEM((count, count), F32), pltpu.VMEM((count, width), BF16)],
        compiler_params=pltpu.CompilerParams(vmem_limit_bytes=60 * MIB),
    )(grad, w_out, three, w_cols, cosine, sine, mark_cols, mark_rows)


class Load:
    def __init__(self, value):
        self.value = value

    def __getitem__(self, place):
        return self.value[place]


class Store:
    def __init__(self, shape):
        self.value = jnp.zeros(shape.shape, shape.dtype)

    def __getitem__(self, place):
        return self.value[place]

    def __setitem__(self, place, value):
        self.value = value.astype(self.value.dtype)


def first_middle(total, span, ins, outs):
    tokens, gain = ins
    mixed = tokens[span].astype(F32) + total
    factor = lax.rsqrt(jnp.mean(mixed * mixed, axis=-1, keepdims=True) + EPSILON)
    outs[0][span] = mixed
    return (mixed * factor * gain[...]).astype(BF16)


def norm_back(values, gain, grad):
    factor = lax.rsqrt(jnp.mean(values * values, axis=-1, keepdims=True) + EPSILON)
    weighted = gain * grad
    back = factor * weighted - values * (factor * factor * factor) * jnp.mean(
        weighted * values, axis=-1, keepdims=True
    )
    return back, jnp.sum(grad * values * factor, axis=0, keepdims=True)


def back_middle(total, span, ins, outs):
    values, gain, base = ins
    back, grad_gain = norm_back(values[span].astype(F32), gain[...], total)
    grad = base[span].astype(F32) + back
    outs[0][span] = grad
    outs[1][span if span == slice(None) else pl.ds(span.start // span.size, 1)] = grad_gain
    return grad.astype(BF16)


class Wires:
    def __init__(self, mesh):
        self.nf = mesh.shape["fsdp"]
        self.ng = mesh.shape["grp"]
        self.nz = self.ng // 2
        self.fast = self.nf == 4 and self.ng == 8
        self.chunks = 4 if self.fast else 1

    def xor(self, value, k):
        return lax.ppermute(value, "fsdp", [(i, i ^ k) for i in range(self.nf)])

    def inwards(self, value):
        if not self.fast:
            return None
        return lax.ppermute(value, "grp", [(0, 2), (1, 3), (6, 4), (7, 5)])

    def gather_list(self, value):
        return [value] + [self.xor(value, k) for k in range(1, self.nf)]

    def gather(self, value):
        return jnp.concatenate(self.gather_list(value), axis=0)

    def scatter_sum(self, value):
        rows = value.shape[0] // self.nf
        total = value[:rows].astype(F32)
        for k in range(1, self.nf):
            part = value[k * rows : (k + 1) * rows].astype(BF16)
            total = total + self.xor(part, k).astype(F32)
        return total

    def reduce_background(self, partial):
        return lax.psum_scatter(partial, "grp", scatter_dimension=0, tiled=True)

    def gather_start(self, tokens, small, marks, weights):
        if self.fast:
            return start_call(tokens, small, marks, *weights, 1)
        cols = jnp.concatenate(
            [lax.all_to_all(w, "fsdp", split_axis=1, concat_axis=0, tiled=True) for w in weights],
            axis=1,
        )
        return tuple(jnp.stack(self.gather_list(v)) for v in (tokens, small, marks)) + (cols,)

    def middle(self, body, partial, ins, out_shapes, gathers, number, arrays=(), jobs=()):
        nf = self.nf
        rows, cols = partial.shape[0] // nf, partial.shape[1]
        if self.fast:
            side = Side(arrays, jobs)
            return mid_call(body, partial.reshape(nf, rows, cols), ins, out_shapes, gathers, side, number)
        total = self.scatter_sum(partial)
        outs = [Store(s) for s in out_shapes]
        given = body(total, slice(None), [Load(v) for v in ins], outs)
        results = tuple(o.value for o in outs)
        if gathers:
            results += (jnp.stack(self.gather_list(given)),)

        def operand(o):
            number, axis, entry = o
            v = arrays[number] if axis is None else lax.index_in_dim(arrays[number], entry, axis, False)
            return v.reshape(-1, v.shape[-1])

        return results + tuple(
            sum(rows_dot(operand(a), operand(b)) for a, b in job).astype(BF16) for job in jobs
        )

    def last_sums(self, downs, shared, part_three, part_output, out_part, mixed, vec, bias_add, number):
        nf, ng, nz = self.nf, self.ng, self.nz
        features, width = part_output.shape
        share = features // ng
        if self.fast:
            outs = line_call(
                [v.reshape(nz, 2, share, -1) for v in downs],
                [v.reshape(nz, 2, share, -1) for v in shared],
                part_three.reshape(3, 2, share, features),
                part_output.reshape(nz, 2, share, width),
                out_part.reshape(nf, -1, features),
                mixed,
                vec.reshape(16, nf, width).transpose(1, 0, 2),
                bias_add,
                2,
                True,
                number,
            )
            return outs[0], outs[1:4], outs[4], outs[5], outs[6]
        down = jnp.stack([self.reduce_background(v).astype(F32).T for v in downs], axis=0)
        sums = [self.reduce_background(v).astype(F32) for v in shared]
        three = lax.all_to_all(
            part_three.reshape(3, width, features), "fsdp", split_axis=2, concat_axis=1, tiled=True
        )
        four = jnp.concatenate([three, part_output[None]], axis=0)
        four = lax.psum_scatter(four, "grp", scatter_dimension=1, tiled=True).astype(F32)
        vec = lax.psum_scatter(vec, "fsdp", scatter_dimension=1, tiled=True) + bias_add
        output = (mixed + self.scatter_sum(out_part)).astype(BF16)
        return down, (sums[0], sums[1], sums[2].T), four.transpose(0, 2, 1), output, lax.psum(vec, "grp")


def on_device(
    wires,
    tokens,
    cotangent,
    segment,
    ancestry,
    position,
    routes,
    attn_gain,
    w_query,
    w_key,
    w_value,
    b_query,
    b_key,
    b_value,
    w_output,
    moe_gain,
    w_router,
    shared_switch,
    shared_gate,
    shared_up,
    shared_down,
    expert_gate,
    routed_up_weight,
    expert_down,
):
    nf, ng = wires.nf, wires.ng
    me = lax.axis_index("fsdp")
    rows_dev, features = tokens.shape
    count = rows_dev * nf
    width = features // nf
    experts = w_router.shape[1]
    local_experts = experts // nf
    capacity = 5 * rows_dev // 8
    choose = routes.shape[1]

    small = jnp.concatenate([attn_gain[None], moe_gain[None], w_router.T, shared_switch[None]], axis=0)
    small = jnp.pad(small, ((0, -small.shape[0] % 16), (0, 0)))
    marks = jnp.concatenate([segment[None], ancestry.T, position[None], routes.T], axis=0)
    marks = jnp.pad(marks, ((0, -marks.shape[0] % 16), (0, 0)))
    tokens_all, small_blocks, marks_all, w_cols = wires.gather_start(
        tokens, small, marks, (w_query, w_key, w_value)
    )
    tokens_all = tokens_all.reshape(count, features)
    small_all = jnp.concatenate(
        [lax.dynamic_index_in_dim(small_blocks, me ^ i, 0, keepdims=False) for i in range(nf)], axis=1
    )
    gain_one = small_all[0:1].astype(F32)
    gain_two = small_all[1:2].astype(F32)
    heads_rows = small_all[2 : experts + 3]
    mark_rows = jnp.concatenate([marks_all[k] for k in range(nf)], axis=1)
    mark_cols = mark_rows.T
    routes_rows = mark_rows[5 : 5 + choose]

    tokens_all, cotangent = lax.optimization_barrier((tokens_all, cotangent))
    cot_all = wires.gather(cotangent)

    halfway = HEAD_DIM // 2
    freqs = ROPE_BASE ** (-(jnp.arange(halfway, dtype=F32) * 2.0 / HEAD_DIM))
    turns = mark_cols[:, 4:5].astype(F32) * jnp.concatenate([freqs, freqs])[None, :]
    cosine = jnp.cos(turns)
    sine = jnp.sin(turns) * jnp.where(jnp.arange(HEAD_DIM) < halfway, -1.0, 1.0)[None, :]
    bias = jnp.concatenate([b_query, b_key, b_value]).astype(F32)[None]
    normed, three, attended, branch = attend_call(
        tokens_all, gain_one, w_cols, bias, w_output, cosine, sine, mark_cols, mark_rows
    )

    numbers = me * local_experts + jnp.arange(local_experts, dtype=jnp.int32)
    named = jnp.any(routes_rows[None] == numbers[:, None, None], axis=1)
    named = named.reshape(local_experts, nf, rows_dev)
    earlier = (jnp.arange(rows_dev)[None, :] < jnp.arange(rows_dev)[:, None]).astype(BF16)
    slot = jnp.einsum("ts,ebs->bet", earlier, named.astype(BF16), preferred_element_type=F32)
    slot = jnp.where(named.transpose(1, 0, 2), slot.astype(jnp.int32), -1)
    pick = jnp.arange(capacity, dtype=jnp.int32)[None, None, :, None] == slot[:, :, None, :]
    pick_b = pick.astype(BF16).reshape(nf, local_experts * capacity, rows_dev)

    branch, cot_all = lax.optimization_barrier((branch, cot_all))
    cot_other = wires.inwards(cot_all)
    mixed, moe_blocks = wires.middle(
        first_middle,
        branch,
        (tokens, gain_two),
        (jax.ShapeDtypeStruct((rows_dev, features), F32),),
        True,
        2,
    )
    moe_in = moe_blocks.reshape(count, features)
    moe_other = wires.inwards(moe_in)

    head_pre = trans_dot(moe_in, heads_rows)
    router_probs = jax.nn.softmax(head_pre[:, :experts], axis=-1)
    opener = jax.nn.sigmoid(head_pre[:, experts:])
    local = jnp.stack(
        [
            jnp.sum(jnp.where(jnp.arange(experts)[None] == numbers[i], router_probs, 0.0), axis=1)
            for i in range(local_experts)
        ],
        axis=0,
    )
    local = local.reshape(local_experts, nf, rows_dev).transpose(1, 0, 2)
    gate = jnp.sum(jnp.where(pick, local[:, :, None, :], 0.0), axis=3, keepdims=True)

    def dispatch(x):
        return jnp.einsum(
            "bst,btd->bsd", pick_b, x.reshape(nf, rows_dev, -1), preferred_element_type=F32
        ).astype(BF16)

    shape = (nf, local_experts, capacity, -1)
    rows_in = dispatch(moe_in).reshape(shape)
    rows_cot = dispatch(cot_all).reshape(shape)
    if wires.fast:
        rows_cot, cot_other = lax.optimization_barrier((rows_cot, cot_other))
    hidden, d_gate, d_up, d_out, y_rows, dx_rows, sens_rows = expert_call(
        rows_in, rows_cot, gate, expert_gate, routed_up_weight, expert_down, nf // 2
    )

    def slot_rows(x, i):
        return x[:, i].reshape(nf * capacity, features)

    gate_parts = [rows_dot(slot_rows(rows_in, i), d_gate[i]).astype(BF16) for i in range(local_experts)]
    up_part = rows_dot(slot_rows(rows_in, 0), d_up[0]).astype(BF16)
    gate_parts, up_part, hidden, sens_rows, y_rows, moe_other = lax.optimization_barrier(
        (gate_parts, up_part, hidden, sens_rows, y_rows, moe_other)
    )
    gate_sums = [wires.reduce_background(v) for v in gate_parts]
    up_sums = [wires.reduce_background(up_part)]

    gate_grad = jnp.sum(jnp.where(pick, sens_rows, 0.0), axis=2)
    gate_grad = gate_grad.transpose(1, 0, 2).reshape(local_experts, count)
    prob_grad = sum(
        jnp.where(jnp.arange(experts)[None] == numbers[i], gate_grad[i][:, None], 0.0)
        for i in range(local_experts)
    )
    logit_grad = router_probs * (
        prob_grad - jnp.sum(prob_grad * router_probs, axis=-1, keepdims=True)
    )
    high = logit_grad.astype(BF16)
    lanes = jnp.concatenate([high, (logit_grad - high.astype(F32)).astype(BF16)], axis=1)
    router_rows = heads_rows[:experts]
    taken = (nf, local_experts * capacity, features)
    s_hidden, sd_gate, sd_up, sd_out, out_part, moe_part, gate_sens = shared_call(
        moe_in,
        cot_all,
        opener,
        pick_b,
        y_rows.reshape(taken),
        dx_rows.reshape(taken),
        lanes,
        jnp.concatenate([router_rows, router_rows], axis=0),
        heads_rows[experts:].astype(F32),
        shared_gate,
        shared_up,
        shared_down,
    )
    sens_high = gate_sens.astype(BF16)
    sens_low = (gate_sens - sens_high.astype(F32)).astype(BF16)
    grad_heads = rows_dot(jnp.concatenate([lanes, sens_high, sens_low], axis=1), moe_in)
    grad_heads = jnp.concatenate(
        [
            grad_heads[:experts] + grad_heads[experts : 2 * experts],
            grad_heads[2 * experts : 2 * experts + 1] + grad_heads[2 * experts + 1 :],
        ],
        axis=0,
    )
    arrays = (rows_in, d_gate, d_up, moe_in, sd_gate, sd_up, sd_out)
    if wires.fast:
        o_hidden, od_gate, od_up, od_out = other_call(
            moe_other, cot_other, heads_rows, shared_gate, shared_up, shared_down, rows_dev
        )
        arrays += (moe_other, od_gate, od_up, s_hidden, od_out, o_hidden)
    else:
        arrays += (None, None, None, s_hidden)
    jobs = []
    for i in range(1, local_experts):
        jobs += [(((0, 1, i), (2, 0, i)),)]

    def whole(*numbers):
        return tuple((n, None, 0) for n in numbers)

    if wires.fast:
        jobs += [(whole(3, 4), whole(7, 8)), (whole(3, 5), whole(7, 9)), (whole(6, 10), whole(11, 12))]
    else:
        jobs += [(whole(3, 4),), (whole(3, 5),), (whole(6, 10),)]
    grad_mixed, grad_gain_two, branch_grad, *parts = wires.middle(
        back_middle,
        moe_part,
        (mixed, gain_two, cotangent),
        (
            jax.ShapeDtypeStruct((rows_dev, features), F32),
            jax.ShapeDtypeStruct((wires.chunks, features), F32),
        ),
        True,
        3,
        arrays,
        jobs,
    )
    late = local_experts - 1
    parts, up_sums = lax.optimization_barrier((parts, up_sums))
    up_sums += [wires.reduce_background(v) for v in parts[:late]]
    shared_parts = parts[late:]
    branch_grad = branch_grad.reshape(count, features)
    grad_three, normed_part, grad_bias = attend_back_call(
        branch_grad, w_output, three, w_cols, cosine, sine, mark_cols, mark_rows
    )
    grad_tokens, grad_gain_one, part_output, part_three, *down_parts = wires.middle(
        back_middle,
        normed_part,
        (tokens, gain_one, grad_mixed),
        (
            jax.ShapeDtypeStruct((rows_dev, features), F32),
            jax.ShapeDtypeStruct((wires.chunks, features), F32),
        ),
        False,
        4,
        (branch_grad, attended, grad_three, normed, d_out, hidden),
        [(whole(0, 1),), (whole(2, 3),)] + [(((4, 1, i), (5, 0, i)),) for i in range(local_experts)],
    )

    vec = jnp.concatenate(
        [
            jnp.sum(grad_gain_one, axis=0, keepdims=True),
            jnp.sum(grad_gain_two, axis=0, keepdims=True),
            grad_heads,
        ],
        axis=0,
    )
    vec = jnp.pad(vec, ((0, 16 - vec.shape[0]), (0, 0)))
    bias_add = jnp.pad(grad_bias.reshape(3, width), ((experts + 3, 16 - experts - 6), (0, 0)))
    down_sums, shared_sums, four, output, vec = wires.last_sums(
        down_parts, shared_parts, part_three, part_output, out_part, mixed, vec, bias_add, 5
    )
    own = width // ng
    vec = lax.dynamic_slice_in_dim(vec, lax.axis_index("grp") * own, own, 1)
    return (
        output,
        grad_tokens,
        vec[0],
        four[0],
        four[1],
        four[2],
        vec[experts + 3],
        vec[experts + 4],
        vec[experts + 5],
        four[3],
        vec[1],
        vec[2 : experts + 2].T,
        vec[experts + 2],
        shared_sums[0],
        shared_sums[1],
        shared_sums[2],
        jnp.stack(gate_sums, axis=0).astype(F32),
        jnp.stack(up_sums, axis=0).astype(F32),
        down_sums,
    )


def solution(mesh):
    wires = Wires(mesh)

    def step(*args):
        return on_device(wires, *args)

    rows = P(("grp", "fsdp"))
    shard = P("fsdp")
    small = P(("fsdp", "grp"))
    return jax.shard_map(
        step,
        mesh=mesh,
        in_specs=(rows,) * 6
        + (shard,) * 11
        + (P(None, "fsdp"), P(None, "fsdp"), shard, shard, shard, shard),
        out_specs=(
            rows,
            rows,
            small,
            P("fsdp", "grp"),
            P("fsdp", "grp"),
            P("fsdp", "grp"),
            small,
            small,
            small,
            P("fsdp", "grp"),
            small,
            small,
            small,
            P("grp", "fsdp"),
            P("grp", "fsdp"),
            P("fsdp", "grp"),
            P("fsdp", "grp", None),
            P("fsdp", "grp", None),
            P("fsdp", None, "grp"),
        ),
        check_vma=False,
    )
```

```python
import functools

import jax
import jax.numpy as jnp
from jax import lax
from jax.experimental import pallas as pl
from jax.experimental.pallas import tpu as pltpu
from jax.sharding import PartitionSpec as P

HEADS = 16
HEAD_DIM = 128
EPSILON = 1e-06
ROPE_BASE = 1000000.0
MASK_FILL = -1e30

F32 = jnp.float32
BF16 = jnp.bfloat16
MESH = pl.DeviceIdType.MESH
ANY = pl.BlockSpec(memory_space=pl.ANY)
VMEM = pl.BlockSpec(memory_space=pltpu.VMEM)
MIB = 2**20


def dot(left, right, dims, out=F32):
    return lax.dot_general(left, right, (dims, ((), ())), preferred_element_type=out)


def plain_dot(left, right):
    return dot(left, right, ((1,), (0,)))


def trans_dot(left, right):
    return dot(left, right, ((1,), (1,)))


def rows_dot(left, right):
    return dot(left, right, ((0,), (0,)))


def pieces(total, size):
    return [(a, min(size, total - a)) for a in range(0, total, size)]


def hidden_part(x, g, gate, w_gate, w_up, w_down, hidden, d_gate, d_up):
    units = w_gate.shape[1]
    sens = None
    for a, n in pieces(units, 256):
        s = pl.ds(a, n)
        pre = plain_dot(x, w_gate[:, s])
        up = plain_dot(x, w_up[:, s])
        plain = trans_dot(g, w_down[s, :])
        sigma = 1.0 / (1.0 + jnp.exp(-pre))
        act = pre * sigma
        slope = sigma * (1.0 + pre * (1.0 - sigma))
        h = (act * up).astype(BF16)
        hidden[:, s] = h
        grad = gate * plain
        d_gate[:, s] = (grad * up * slope).astype(BF16)
        d_up[:, s] = (grad * act).astype(BF16)
        part = jnp.sum(plain * h.astype(F32), axis=-1, keepdims=True)
        sens = part if sens is None else sens + part
    return sens


def expert_kernel(x_ref, g_ref, gate_ref, wg, wu, wd, hidden, d_gate, d_up, d_out, y_ref, dx_ref, sens_ref):
    blocks, _, slots, features = x_ref.shape
    rows = blocks * slots
    x = x_ref[...].reshape(rows, features)
    g = g_ref[...].reshape(rows, features)
    gate = gate_ref[...].reshape(rows, 1)
    wg, wu, wd = wg.at[0], wu.at[0], wd.at[0]
    hid, dg, du = hidden.at[0], d_gate.at[0], d_up.at[0]
    d_out[...] = (gate * g.astype(F32)).astype(BF16).reshape(d_out.shape)
    sens = hidden_part(x, g, gate, wg, wu, wd, hid, dg, du)
    sens_ref[...] = sens.reshape(sens_ref.shape)
    for a, n in pieces(features, 512):
        s = pl.ds(a, n)
        y = plain_dot(hid[...], wd[:, s]).astype(BF16)
        y_ref[:, :, :, s] = (gate * y.astype(F32)).astype(BF16).reshape(blocks, 1, slots, n)
        dx = trans_dot(dg[...], wg[s, :]) + trans_dot(du[...], wu[s, :])
        dx_ref[:, :, :, s] = dx.astype(BF16).reshape(blocks, 1, slots, n)


def expert_call(rows_in, rows_cot, gate, w_gate, w_up, w_down, tile):
    blocks, experts, slots, features = rows_in.shape
    units = w_gate.shape[2]
    steps = blocks // tile
    rows = tile * slots

    def slot_spec(cols):
        return pl.BlockSpec((tile, 1, slots, cols), lambda i, t: (t, i, 0, 0))

    def unit_spec():
        return pl.BlockSpec((1, rows, units), lambda i, t: (i, t, 0))

    def weight_spec(a, b):
        return pl.BlockSpec((1, a, b), lambda i, t: (i, 0, 0))

    units_shape = jax.ShapeDtypeStruct((experts, blocks * slots, units), BF16)
    slots_shape = jax.ShapeDtypeStruct((blocks, experts, slots, features), BF16)
    return pl.pallas_call(
        expert_kernel,
        grid=(experts, steps),
        in_specs=[
            slot_spec(features),
            slot_spec(features),
            slot_spec(1),
            weight_spec(features, units),
            weight_spec(features, units),
            weight_spec(units, features),
        ],
        out_specs=[unit_spec()] * 3 + [slot_spec(features)] * 3 + [slot_spec(1)],
        out_shape=[units_shape] * 3
        + [slots_shape] * 3
        + [jax.ShapeDtypeStruct((blocks, experts, slots, 1), F32)],
        compiler_params=pltpu.CompilerParams(vmem_limit_bytes=62 * MIB),
    )(rows_in, rows_cot, gate, w_gate, w_up, w_down)


def shared_kernel(
    x_ref, g_ref, head_ref, pick_ref, y_in, dx_in, lane_ref, heads_w, switch_row, wg, wu, wd,
    hidden, d_gate, d_up, d_out, y_ref, dx_ref, sens_ref,
):
    features = x_ref.shape[1]
    x = x_ref[...]
    g = g_ref[...]
    opener = head_ref[...]
    d_out[...] = (opener * g.astype(F32)).astype(BF16)
    sens = hidden_part(x, d_out[...], 1.0, wg, wu, wd, hidden, d_gate, d_up)
    sens = (1.0 - opener) * sens
    sens_ref[...] = sens
    pick = pick_ref[0]
    lanes = lane_ref[...]
    for a, n in pieces(features, 512):
        s = pl.ds(a, n)
        y = opener * plain_dot(hidden[...], wd[:, s]) + rows_dot(pick, y_in[0, :, s])
        y_ref[:, s] = y.astype(BF16)
        dx = trans_dot(d_gate[...], wg[s, :]) + trans_dot(d_up[...], wu[s, :])
        dx = dx + rows_dot(pick, dx_in[0, :, s])
        dx = dx + plain_dot(lanes, heads_w[:, s]) + sens * switch_row[:, s]
        dx_ref[:, s] = dx.astype(BF16)


def shared_call(x, g, opener, pick, y_in, dx_in, lanes, heads_w, switch_row, w_gate, w_up, w_down):
    count, features = x.shape
    units = w_gate.shape[1]
    blocks, taken, tile = pick.shape
    width = lanes.shape[1]

    def rows_spec(cols):
        return pl.BlockSpec((tile, cols), lambda b: (b, 0))

    def block_spec(cols):
        return pl.BlockSpec((1, taken, cols), lambda b: (b, 0, 0))

    def whole(a, b):
        return pl.BlockSpec((a, b), lambda b_: (0, 0), pipeline_mode=pl.Buffered(1))

    def shape(cols, dtype=BF16):
        return jax.ShapeDtypeStruct((count, cols), dtype)

    return pl.pallas_call(
        shared_kernel,
        grid=(blocks,),
        in_specs=[
            rows_spec(features),
            rows_spec(features),
            rows_spec(1),
            block_spec(tile),
            block_spec(features),
            block_spec(features),
            rows_spec(width),
            whole(width, features),
            whole(1, features),
            whole(features, units),
            whole(features, units),
            whole(units, features),
        ],
        out_specs=[rows_spec(units)] * 3 + [rows_spec(features)] * 3 + [rows_spec(1)],
        out_shape=[shape(units)] * 3 + [shape(features)] * 3 + [shape(1, F32)],
        compiler_params=pltpu.CompilerParams(vmem_limit_bytes=62 * MIB),
    )(x, g, opener, pick, y_in, dx_in, lanes, heads_w, switch_row, w_gate, w_up, w_down)


def other_kernel(x_ref, g_ref, heads, wg, wu, wd, hidden, d_gate, d_up, d_out):
    x = x_ref[...]
    pre = trans_dot(x, heads[...])
    opener = 1.0 / (1.0 + jnp.exp(-pre[:, heads.shape[0] - 1 :]))
    d_out[...] = (opener * g_ref[...].astype(F32)).astype(BF16)
    hidden_part(x, d_out[...], 1.0, wg, wu, wd, hidden, d_gate, d_up)


def other_call(x, g, heads, w_gate, w_up, w_down, tile):
    count, features = x.shape
    units = w_gate.shape[1]

    def rows_spec(cols):
        return pl.BlockSpec((tile, cols), lambda b: (b, 0))

    def whole(a, b):
        return pl.BlockSpec((a, b), lambda b_: (0, 0), pipeline_mode=pl.Buffered(1))

    def shape(cols):
        return jax.ShapeDtypeStruct((count, cols), BF16)

    return pl.pallas_call(
        other_kernel,
        grid=(count // tile,),
        in_specs=[
            rows_spec(features),
            rows_spec(features),
            whole(heads.shape[0], features),
            whole(features, units),
            whole(features, units),
            whole(units, features),
        ],
        out_specs=[rows_spec(units)] * 3 + [rows_spec(features)],
        out_shape=[shape(units)] * 3 + [shape(features)],
        compiler_params=pltpu.CompilerParams(vmem_limit_bytes=62 * MIB),
    )(x, g, heads, w_gate, w_up, w_down)


def dispatch_kernel(x_ref, g_ref, slot_ref, heads, rows_in, rows_cot, gate_ref, pick_ref, probs_ref, opener_ref):
    x, g = x_ref[...], g_ref[...]
    local, slots = rows_in.shape[1], rows_in.shape[2]
    count = heads.shape[0] - 1
    pre = trans_dot(x, heads[...])
    opener_ref[...] = 1.0 / (1.0 + jnp.exp(-pre[:, count:]))
    pre = pre[:, :count]
    expo = jnp.exp(pre - jnp.max(pre, axis=-1, keepdims=True))
    probs = expo / jnp.sum(expo, axis=-1, keepdims=True)
    probs_ref[...] = probs
    parts, rest = [], probs
    for _ in range(3):
        parts.append(rest.astype(BF16))
        rest = rest - parts[-1].astype(F32)
    numbers = lax.broadcasted_iota(jnp.int32, (slots, count), 1)
    places = lax.broadcasted_iota(jnp.int32, (slots, x.shape[0]), 0)
    for i in range(local):
        pick = jnp.where(places == slot_ref[0, i : i + 1, :], 1.0, 0.0).astype(BF16)
        pick_ref[0, i * slots : (i + 1) * slots, :] = pick
        rows_in[0, i] = plain_dot(pick, x).astype(BF16)
        rows_cot[0, i] = plain_dot(pick, g).astype(BF16)
        found = plain_dot(pick, parts[0]) + (plain_dot(pick, parts[1]) + plain_dot(pick, parts[2]))
        number = lax.axis_index("fsdp") * local + i
        gate_ref[0, i] = jnp.sum(jnp.where(numbers == number, found, 0.0), axis=-1, keepdims=True)


def dispatch_call(x, g, slot, heads, slots):
    count, features = x.shape
    blocks, local, rows = slot.shape
    experts = heads.shape[0] - 1

    def rows_spec(cols):
        return pl.BlockSpec((rows, cols), lambda b: (b, 0))

    def slots_spec(cols):
        return pl.BlockSpec((1, local, slots, cols), lambda b: (b, 0, 0, 0))

    def slots_shape(cols, dtype=BF16):
        return jax.ShapeDtypeStruct((blocks, local, slots, cols), dtype)

    return pl.pallas_call(
        dispatch_kernel,
        grid=(blocks,),
        in_specs=[
            rows_spec(features),
            rows_spec(features),
            pl.BlockSpec((1, local, rows), lambda b: (b, 0, 0)),
            pl.BlockSpec(heads.shape, lambda b: (0, 0)),
        ],
        out_specs=[
            slots_spec(features),
            slots_spec(features),
            slots_spec(1),
            pl.BlockSpec((1, local * slots, rows), lambda b: (b, 0, 0)),
            rows_spec(experts),
            rows_spec(1),
        ],
        out_shape=[
            slots_shape(features),
            slots_shape(features),
            slots_shape(1, F32),
            jax.ShapeDtypeStruct((blocks, local * slots, rows), BF16),
            jax.ShapeDtypeStruct((count, experts), F32),
            jax.ShapeDtypeStruct((count, 1), F32),
        ],
        compiler_params=pltpu.CompilerParams(vmem_limit_bytes=60 * MIB),
    )(x, g, slot, heads)


class Line:
    def __init__(self, parts, inner, sources, outs, sib, recv, bufs, sems):
        self.parts, self.inner, self.sources, self.outs = parts, inner, sources, outs
        self.sib, self.recv = sib, recv
        self.own_v, self.sib_v, self.send_v, self.out_v, self.turned_v = bufs
        self.own_sem, self.sib_sem, self.out_sem, self.sib_send, self.sib_recv, self.sent, self.got = sems
        self.chunks = len(sources) * parts
        self.slots = self.send_v.shape[0]
        self.rows = sources[0].shape[2] // parts
        g = lax.axis_index("grp")
        self.z, self.core = g // 2, lax.rem(g, 2)
        self.is_end = (self.z == 0) | (self.z == 3)
        self.is_mid = (self.z == 1) | (self.z == 2)

    def at(self, z, core):
        return {"grp": 2 * z + core}

    def span(self, q):
        return lax.div(q, self.parts), pl.ds(
            pl.multiple_of(lax.rem(q, self.parts) * self.rows, self.rows), self.rows
        )

    def swap(self, j, m, r, q):
        return pltpu.make_async_remote_copy(
            src_ref=self.sources[j].at[:, 1 - self.core, r],
            dst_ref=self.sib.at[m, :, r],
            send_sem=self.sib_send.at[q],
            recv_sem=self.sib_recv.at[q],
            device_id=self.at(self.z, 1 - self.core),
            device_id_type=MESH,
        )

    def swap_any(self, q):
        m, r = self.span(q)
        return self.swap(0, m, r, q)

    def when_summing(self, condition=None):
        if self.inner:
            condition = self.is_mid if condition is None else self.is_mid & condition
        return (lambda body: body()) if condition is None else pl.when(condition)

    def start_swaps(self):
        @self.when_summing()
        def _():
            for m in range(len(self.sources)):
                for h in range(self.parts):
                    self.swap(m, m, pl.ds(h * self.rows, self.rows), m * self.parts + h).start()

    def out_copy(self, j, r):
        ref, turned = self.outs[j]
        if turned:
            return pltpu.make_async_copy(self.turned_v, ref.at[:, r], self.out_sem)
        return pltpu.make_async_copy(self.out_v, ref.at[r], self.out_sem)

    def each_out(self, q, body):
        m, r = self.span(q)
        for j in range(len(self.sources)):

            @pl.when(m == j)
            def _():
                body(j, r)

    def hop(self, q, slot, target, place):
        m, r = self.span(q)
        return pltpu.make_async_remote_copy(
            src_ref=self.send_v.at[slot],
            dst_ref=self.recv.at[m, place, r],
            send_sem=self.sent.at[slot],
            recv_sem=self.got.at[q, place],
            device_id=self.at(target, self.core),
            device_id_type=MESH,
        )

    def arrived(self, q, place):
        self.hop(q, 0, self.z, place).wait_recv()

    def own_load(self, j, p, r, k):
        return pltpu.make_async_copy(self.sources[j].at[p, self.core, r], self.own_v.at[k], self.own_sem.at[k])

    def sib_load(self, m, p, r, k):
        return pltpu.make_async_copy(self.sib.at[m, p, r], self.sib_v.at[k], self.sib_sem.at[k])

    def start_base(self, q, p, k):
        m, r = self.span(q)
        for j in range(len(self.sources)):

            @pl.when(m == j)
            def _():
                self.own_load(j, p, r, k).start()

        self.sib_load(m, p, r, k).start()

    def base(self, k):
        r = pl.ds(0, self.rows)
        self.own_load(0, 0, r, k).wait()
        self.sib_load(0, 0, r, k).wait()
        return self.own_v[k].astype(F32) + self.sib_v[k].astype(F32)

    def fetch(self, q, place):
        self.arrived(q, place)
        m, r = self.span(q)
        return self.recv[m, place, r].astype(F32)

    def send(self, t, k, q, p, target, place, more, first):
        depth = self.slots // 3
        slot = lax.rem(t, depth) * 3 + k

        @pl.when(t >= depth + first)
        def _():
            self.hop(q, slot, target, place).wait_send()

        if more:
            extra = self.fetch(q, p)
            total = self.base(k) + extra
        else:
            total = self.base(k)
        self.send_v[slot] = total.astype(BF16)
        self.hop(q, slot, target, place).start()

    def turn(self, t):
        z, chunks = self.z, self.chunks
        to_end = self.is_end & (t >= 0) & (t < chunks)
        to_next = self.is_mid & (t >= 1) & (t < chunks + 1)
        to_last = self.is_mid & (t >= 2) & (t < chunks + 2)
        last = (t >= 3) & (t < chunks + 3)

        @self.when_summing((t >= 0) & (t < chunks))
        def _():
            self.swap_any(t).wait_recv()

        def end_piece(j):
            return jnp.where(z == 0, 3 - j, j)

        def next_piece(j):
            return jnp.where(z == 1, 3 - j, j)

        last_piece = jnp.where(z == 2, 3, 0)
        if not self.inner:

            @pl.when(to_end)
            def _():
                for j in range(3):
                    self.start_base(t, end_piece(j), j)

        @pl.when(to_next)
        def _():
            for j in range(2):
                self.start_base(t - 1, next_piece(j), j)

        @pl.when(to_last)
        def _():
            self.start_base(t - 2, last_piece, 2)

        @self.when_summing(last)
        def _():
            self.start_base(t - 3, z, 3)

        if not self.inner:

            @pl.when(to_end)
            def _():
                for j in range(3):
                    p = end_piece(j)
                    target = jnp.where(z == 0, 1, 2)
                    place = jnp.where((z == 3) & (p == 2), 4, p)
                    self.send(t, j, t, p, target, place, False, 0)

        @pl.when(to_next)
        def _():
            for j in range(2):
                p = next_piece(j)
                target = jnp.where(z == 1, 2, 1)
                place = jnp.where((z == 2) & (p == 1), 4, p)
                self.send(t, j, t - 1, p, target, place, not self.inner, 1)

        @pl.when(to_last)
        def _():
            place = jnp.where(z == 1, 4, last_piece)
            self.send(t, 2, t - 2, last_piece, last_piece, place, True, 2)

        @pl.when(last)
        def _():
            q = t - 3

            @pl.when(q >= 1)
            def _():
                self.each_out(q - 1, lambda j, r: self.out_copy(j, r).wait())

            if self.inner:

                @pl.when(z == 0)
                def _():
                    self.out_v[...] = self.fetch(q, 4)

                @pl.when(z == 3)
                def _():
                    self.out_v[...] = self.fetch(q, 3)

                @pl.when(z == 1)
                def _():
                    got = self.fetch(q, 4)
                    self.out_v[...] = self.base(3) + got

                @pl.when(z == 2)
                def _():
                    got = self.fetch(q, 2)
                    self.out_v[...] = self.base(3) + got

            else:
                self.out_v[...] = self.base(3)

                @pl.when(z > 0)
                def _():
                    self.out_v[...] = self.out_v[...] + self.fetch(q, z)

                @pl.when(z < 3)
                def _():
                    self.out_v[...] = self.out_v[...] + self.fetch(q, 4)

            def put(j, r):
                if self.outs[j][1]:
                    self.turned_v[...] = self.out_v[...].T
                self.out_copy(j, r).start()

            self.each_out(q, put)

    def finish(self):
        self.each_out(self.chunks - 1, lambda j, r: self.out_copy(j, r).wait())

        def body(q, carry):
            self.swap_any(q).wait_send()
            return carry

        @self.when_summing()
        def _():
            lax.fori_loop(0, self.chunks, body, 0)

        assert self.chunks >= self.slots // 3

        @self.when_summing()
        def _():
            for slot in range(self.slots):
                self.hop(0, slot, self.z, 0).wait_send()


def line_bufs(shape, slots, turned):
    return [pltpu.VMEM((4,) + shape, BF16)] * 2 + [
        pltpu.VMEM((slots,) + shape, BF16),
        pltpu.VMEM(shape, F32),
        pltpu.VMEM(shape[::-1] if turned else (8, 128), F32),
    ]


def line_sems(q, slots):
    return [
        pltpu.SemaphoreType.DMA((4,)),
        pltpu.SemaphoreType.DMA((4,)),
        pltpu.SemaphoreType.DMA,
        pltpu.SemaphoreType.DMA((q,)),
        pltpu.SemaphoreType.DMA((q,)),
        pltpu.SemaphoreType.DMA((slots,)),
        pltpu.SemaphoreType.DMA((q, 5)),
    ]


def line_kernel(n_down, n_shared, parts, shift, *refs):
    def take(n):
        nonlocal refs
        taken, refs = refs[:n], refs[n:]
        return taken

    downs, shared = take(n_down), take(n_shared)
    three, part_out, out_part, mixed, vec, bias_add = take(6)
    out_down, out_gate, out_up, out_sdown = take(4)
    out_four = take(4)
    output, vec_out = take(2)
    sib_a, att, sib_b, sib_c, out_in = take(5)
    bufs_a, bufs_b, bufs_c = take(5), take(5), take(5)
    recv_a, recv_b, recv_c = take(3)
    vec_in, vec_own, vec_sib, vec_line, vec_send, parts_v, mixed_v, sum_v = take(8)
    sems_a, sems_b, sems_c = take(7), take(7), take(7)
    plane_send, plane_recv, local_sems, vec_send_sems, vec_recv_sems, out_send, out_recv = take(7)

    a = Line(parts, False, downs, [(out_down.at[j], True) for j in range(n_down)], sib_a, recv_a, bufs_a, sems_a)
    b = Line(1, False, [att.at[j] for j in range(4)], [(v, True) for v in out_four], sib_b, recv_b, bufs_b, sems_b)
    c = Line(parts, shift, shared, [(out_gate, False), (out_up, False), (out_sdown, True)], sib_c, recv_c, bufs_c, sems_c)
    z, core = a.z, a.core
    f = lax.axis_index("fsdp")
    fx = f + 1 - 2 * lax.rem(f, 2)
    fy = f + 2 - 4 * (f // 2)
    fd = fx + 2 - 4 * (fx // 2)
    peers = (fx, fy, fd)
    sibling = a.at(z, 1 - core)
    width = three.shape[3] // 4

    barrier = pltpu.get_barrier_semaphore()
    for other in (sibling,) + tuple({"fsdp": p} for p in peers):
        pl.semaphore_signal(barrier, inc=1, device_id=other, device_id_type=MESH)

    @pl.when(z > 0)
    def _():
        pl.semaphore_signal(barrier, inc=1, device_id=a.at(z - 1, core), device_id_type=MESH)

    @pl.when(z < 3)
    def _():
        pl.semaphore_signal(barrier, inc=1, device_id=a.at(z + 1, core), device_id_type=MESH)

    @pl.when(a.is_end)
    def _():
        pl.semaphore_wait(barrier, 5)

    @pl.when(a.is_mid)
    def _():
        pl.semaphore_wait(barrier, 6)

    a.start_swaps()
    c.start_swaps()

    def cols(p):
        return pl.ds(pl.multiple_of(p * width, width), width)

    def to_owner(k, p):
        return pltpu.make_async_remote_copy(
            src_ref=three.at[:, :, :, cols(p)], dst_ref=att.at[pl.ds(0, 3), f],
            send_sem=plane_send.at[k], recv_sem=plane_recv.at[k],
            device_id={"fsdp": p}, device_id_type=MESH,
        )

    def vec_owner(k, p):
        return pltpu.make_async_remote_copy(
            src_ref=vec.at[p], dst_ref=vec_in.at[k],
            send_sem=vec_send_sems.at[k], recv_sem=vec_recv_sems.at[k],
            device_id={"fsdp": p}, device_id_type=MESH,
        )

    def out_owner(k, p):
        return pltpu.make_async_remote_copy(
            src_ref=out_part.at[k + 1], dst_ref=out_in.at[k],
            send_sem=out_send.at[k], recv_sem=out_recv.at[k],
            device_id={"fsdp": p}, device_id_type=MESH,
        )

    for k, p in enumerate(peers):
        vec_owner(k, p).start()
    for k, p in enumerate(peers):
        to_owner(k, p).start()
    keep = (
        pltpu.make_async_copy(three.at[:, :, :, cols(f)], att.at[pl.ds(0, 3), f], local_sems.at[0]),
        pltpu.make_async_copy(part_out, att.at[3], local_sems.at[1]),
    )
    for copy in keep:
        copy.start()

    def vec_swap():
        return pltpu.make_async_remote_copy(
            src_ref=vec_own, dst_ref=vec_sib, send_sem=vec_send_sems.at[3], recv_sem=vec_recv_sems.at[3],
            device_id=sibling, device_id_type=MESH,
        )

    def vec_hop(k, target):
        return pltpu.make_async_remote_copy(
            src_ref=vec_send.at[k], dst_ref=vec_line.at[k], send_sem=vec_send_sems.at[4 + k],
            recv_sem=vec_recv_sems.at[4 + k], device_id=a.at(target, core), device_id_type=MESH,
        )

    def finish_output():
        for k, p in enumerate(peers):
            out_owner(k, p).wait_recv()
        step = parts_v.shape[1]

        def body(i, carry):
            r = pl.ds(pl.multiple_of(i * step, step), step)
            loads = [pltpu.make_async_copy(out_part.at[0, r], parts_v.at[0], local_sems.at[3])]
            loads += [
                pltpu.make_async_copy(out_in.at[k, r], parts_v.at[k + 1], local_sems.at[4 + k]) for k in range(3)
            ]
            loads.append(pltpu.make_async_copy(mixed.at[r], mixed_v, local_sems.at[7]))
            for copy in loads:
                copy.start()
            for copy in loads:
                copy.wait()
            total = (parts_v[0].astype(F32) + parts_v[1].astype(F32)) + (
                parts_v[2].astype(F32) + parts_v[3].astype(F32)
            )
            sum_v[...] = (mixed_v[...] + total).astype(BF16)
            copy = pltpu.make_async_copy(sum_v, output.at[r], local_sems.at[8])
            copy.start()
            copy.wait()
            return carry

        lax.fori_loop(0, mixed.shape[0] // step, body, 0)

    def side_work(t):
        @pl.when(t == 1)
        def _():
            for k, p in enumerate(peers):
                vec_owner(k, p).wait_recv()
            copy = pltpu.make_async_copy(vec.at[f], vec_own, local_sems.at[2])
            copy.start()
            copy.wait()
            vec_own[...] = (vec_own[...] + vec_in[0]) + (vec_in[1] + vec_in[2]) + bias_add[...]
            vec_swap().start()

        @pl.when(t == 2)
        def _():
            vec_swap().wait_recv()
            vec_sib[...] = vec_sib[...] + vec_own[...]

            @pl.when(z == 0)
            def _():
                vec_send[0] = vec_sib[...]
                vec_hop(0, 1).start()

            @pl.when(z == 3)
            def _():
                vec_send[1] = vec_sib[...]
                vec_hop(1, 2).start()

        @pl.when((t == 3) & (z == 1))
        def _():
            vec_hop(0, 1).wait_recv()
            vec_send[0] = vec_sib[...] + vec_line[0]
            vec_hop(0, 2).start()

        @pl.when((t == 3) & (z == 2))
        def _():
            vec_hop(1, 2).wait_recv()
            vec_send[1] = vec_sib[...] + vec_line[1]
            vec_hop(1, 1).start()

        @pl.when(t == 3)
        def _():
            for k, p in enumerate(peers):
                to_owner(k, p).wait_recv()
            for copy in keep:
                copy.wait()
            b.start_swaps()
            for k, p in enumerate(peers):
                out_owner(k, p).start()

        @pl.when((t == 4) & (z == 2))
        def _():
            vec_hop(0, 2).wait_recv()
            vec_send[0] = vec_sib[...] + vec_line[0]
            vec_hop(0, 3).start()
            vec_out[...] = vec_send[0] + vec_line[1]

        @pl.when((t == 4) & (z == 1))
        def _():
            vec_hop(1, 1).wait_recv()
            vec_send[1] = vec_sib[...] + vec_line[1]
            vec_hop(1, 0).start()
            vec_out[...] = vec_send[1] + vec_line[0]

        @pl.when((t == 5) & (z == 3))
        def _():
            vec_hop(0, 3).wait_recv()
            vec_out[...] = vec_sib[...] + vec_line[0]

        @pl.when((t == 5) & (z == 0))
        def _():
            vec_hop(1, 0).wait_recv()
            vec_out[...] = vec_sib[...] + vec_line[1]

        @pl.when(t == 6)
        def _():
            finish_output()

    def first_loop(t, carry):
        a.turn(t)
        b.turn(t - a.chunks)
        c.turn(t)
        side_work(t)
        return carry

    def last_loop(t, carry):
        b.turn(t - a.chunks)
        c.turn(t)
        return carry

    turns = max(a.chunks + b.chunks, c.chunks) + 3
    lax.fori_loop(0, max(7, a.chunks + 3), first_loop, 0)
    lax.fori_loop(max(7, a.chunks + 3), turns, last_loop, 0)
    a.finish()
    b.finish()
    c.finish()
    for k, p in enumerate(peers):
        vec_owner(k, p).wait_send()
        to_owner(k, p).wait_send()
        out_owner(k, p).wait_send()
    vec_swap().wait_send()

    @pl.when(z < 3)
    def _():
        vec_hop(0, 3).wait_send()

    @pl.when(z > 0)
    def _():
        vec_hop(1, 0).wait_send()


def line_call(downs, shared, three, part_out, out_part, mixed, vec, bias_add, parts, shift, collective_id):
    _, _, rows, cols = shared[0].shape
    m, s = len(downs), len(shared)
    _, _, share, features = three.shape
    width = features // 4
    own_rows = mixed.shape[0]
    r = rows // parts
    slots = 9
    small = (16, width)
    step = own_rows // 4

    def shape(*dims, dtype=BF16):
        return jax.ShapeDtypeStruct(dims, dtype)

    outs = pl.pallas_call(
        functools.partial(line_kernel, m, s, parts, shift),
        out_shape=(
            shape(m, cols, rows, dtype=F32),
            shape(rows, cols, dtype=F32),
            shape(rows, cols, dtype=F32),
            shape(cols, rows, dtype=F32),
            shape(width, share, dtype=F32),
            shape(width, share, dtype=F32),
            shape(width, share, dtype=F32),
            shape(width, share, dtype=F32),
            shape(own_rows, features),
            shape(*small, dtype=F32),
            shape(m, 4, rows, cols),
            shape(4, 4, 2, share, width),
            shape(4, 4, share, width),
            shape(s, 4, rows, cols),
            shape(3, own_rows, features),
        ),
        in_specs=[ANY] * (m + s + 5) + [VMEM],
        out_specs=(ANY,) * 9 + (VMEM,) + (ANY,) * 5,
        scratch_shapes=line_bufs((r, cols), slots, True)
        + line_bufs((share, width), slots, True)
        + line_bufs((r, cols), slots, True)
        + [
            pltpu.VMEM((m, 5, rows, cols), BF16),
            pltpu.VMEM((4, 5, share, width), BF16),
            pltpu.VMEM((s, 5, rows, cols), BF16),
            pltpu.VMEM((3,) + small, F32),
            pltpu.VMEM(small, F32),
            pltpu.VMEM(small, F32),
            pltpu.VMEM((2,) + small, F32),
            pltpu.VMEM((2,) + small, F32),
            pltpu.VMEM((4, step, features), BF16),
            pltpu.VMEM((step, features), F32),
            pltpu.VMEM((step, features), BF16),
        ]
        + line_sems(m * parts, slots)
        + line_sems(4, slots)
        + line_sems(s * parts, slots)
        + [
            pltpu.SemaphoreType.DMA((3,)),
            pltpu.SemaphoreType.DMA((3,)),
            pltpu.SemaphoreType.DMA((9,)),
            pltpu.SemaphoreType.DMA((6,)),
            pltpu.SemaphoreType.DMA((6,)),
            pltpu.SemaphoreType.DMA((3,)),
            pltpu.SemaphoreType.DMA((3,)),
        ],
        compiler_params=pltpu.CompilerParams(
            collective_id=collective_id, has_side_effects=True, vmem_limit_bytes=60 * MIB
        ),
    )(*downs, *shared, three, part_out, out_part, mixed, vec, bias_add)
    return outs[0], outs[1:4], outs[4:8], outs[8], outs[9]


def plane_neighbours():
    f = lax.axis_index("fsdp")
    by_x = f + 1 - 2 * lax.rem(f, 2)
    by_y = f + 2 - 4 * (f // 2)
    return {"fsdp": by_x}, {"fsdp": by_y}


def plane_barrier(by_x, by_y):
    barrier = pltpu.get_barrier_semaphore()
    for other in (by_x, by_y):
        pl.semaphore_signal(barrier, inc=1, device_id=other, device_id_type=MESH)
    pl.semaphore_wait(barrier, 2)


class Side:
    block = 512

    def __init__(self, arrays, jobs):
        self.arrays, self.jobs = list(arrays), list(jobs)
        self.operands = sorted({o for job in self.jobs for pair in job for o in pair}, key=str)

    def shape(self, operand):
        number, axis, _ = operand
        full = self.arrays[number].shape
        return full if axis is None else full[:axis] + full[axis + 1 :]

    def out_shapes(self):
        return [
            jax.ShapeDtypeStruct((self.shape(job[0][0])[-1], self.shape(job[0][1])[-1]), BF16)
            for job in self.jobs
        ]

    def scratch(self):
        stages = sorted({self.shape(job[0][1])[-1] for job in self.jobs})
        self.stage_of = {n: k for k, n in enumerate(stages)}
        return (
            [pltpu.VMEM(self.shape(o), BF16) for o in self.operands]
            + [pltpu.VMEM((2, self.block, n), BF16) for n in stages]
            + [
                pltpu.SemaphoreType.DMA((max(1, len(self.operands)),)),
                pltpu.SemaphoreType.DMA((max(1, 2 * len(stages)),)),
            ]
        )

    def bind(self, ins, outs, scratch):
        n = len(self.operands)
        self.ins, self.outs = ins, outs
        self.bufs, self.stages = scratch[:n], scratch[n:-2]
        self.load_sems, self.out_sems = scratch[-2:]
        self.loaded, self.pending, self.turn_of = set(), {}, {}
        self.units = [
            (j, k)
            for j, job in enumerate(self.jobs)
            for k in range(self.shape(job[0][0])[-1] // self.block)
        ]

    def load(self, k):
        number, axis, entry = self.operands[k]
        ref = self.ins[number]
        if axis is not None:
            ref = ref.at[(slice(None),) * axis + (entry,)]
        return pltpu.make_async_copy(ref, self.bufs[k], self.load_sems.at[k])

    def begin(self):
        for o in [o for job in self.jobs for pair in job for o in pair]:
            k = self.operands.index(o)
            if k not in self.loaded:
                self.loaded.add(k)
                self.load(k).start()
        self.loaded = set()

    def step(self, number):
        for _ in range(number):
            if not self.units:
                return
            j, block = self.units.pop(0)
            pairs = [tuple(self.operands.index(o) for o in pair) for pair in self.jobs[j]]
            for k in [k for pair in pairs for k in pair]:
                if k not in self.loaded:
                    self.loaded.add(k)
                    self.load(k).wait()
            n = self.shape(self.jobs[j][0][1])[-1]
            stage = self.stage_of[n]
            slot = self.turn_of.get(stage, 0)
            self.turn_of[stage] = 1 - slot
            if (stage, slot) in self.pending:
                self.pending.pop((stage, slot)).wait()
            rows = pl.ds(block * self.block, self.block)
            total = None
            for ka, kb in pairs:
                left = self.bufs[ka][..., rows].reshape(-1, self.block)
                part = rows_dot(left, self.bufs[kb][...].reshape(-1, n))
                total = part if total is None else total + part
            self.stages[stage][slot] = total.astype(BF16)
            copy = pltpu.make_async_copy(
                self.stages[stage].at[slot], self.outs[j].at[rows], self.out_sems.at[2 * stage + slot]
            )
            copy.start()
            self.pending[(stage, slot)] = copy

    def end(self):
        self.step(len(self.units))
        for copy in self.pending.values():
            copy.wait()


def mid_kernel(middle, chunks, gathers, n_in, n_out, side, *refs):
    n_side, n_jobs = len(side.arrays), len(side.jobs)
    partial, ins = refs[0], refs[1 : 1 + n_in]
    side_ins, refs = refs[1 + n_in : 1 + n_in + n_side], refs[1 + n_in + n_side :]
    outs, refs = refs[:n_out], refs[n_out:]
    gathered = None
    if gathers:
        gathered, refs = refs[0], refs[1:]
    side_outs, refs = refs[:n_jobs], refs[n_jobs:]
    relay_x, relay_y, got_x, got_y, sum_x, sum_y, own, send_sems, recv_sems, local_sems = refs[:10]
    if n_jobs:
        side.bind(side_ins, side_outs, refs[10:])
    rows = partial.shape[1]
    r = rows // chunks
    h = r // 2
    by_x, by_y = plane_neighbours()
    plane_barrier(by_x, by_y)

    def copy(i, kind, src, dst, target):
        return pltpu.make_async_remote_copy(
            src_ref=src, dst_ref=dst, send_sem=send_sems.at[i, kind], recv_sem=recv_sems.at[i, kind],
            device_id=target, device_id_type=MESH,
        )

    def sends(i):
        lo, hi = pl.ds(i * r, h), pl.ds(i * r + h, h)
        half = pl.ds(i * h, h)
        made = {
            0: lambda: copy(i, 0, partial.at[3, lo], relay_x.at[half], by_x),
            1: lambda: copy(i, 1, partial.at[3, hi], relay_y.at[half], by_y),
            2: lambda: copy(i, 2, partial.at[1, lo], got_x.at[lo], by_x),
            3: lambda: copy(i, 3, partial.at[2, hi], got_y.at[hi], by_y),
            4: lambda: copy(i, 4, sum_y.at[half], got_y.at[lo], by_y),
            5: lambda: copy(i, 5, sum_x.at[half], got_x.at[hi], by_x),
        }
        if gathers:
            made |= {
                6: lambda: copy(i, 6, own.at[lo], gathered.at[1, lo], by_x),
                7: lambda: copy(i, 7, own.at[hi], gathered.at[2, hi], by_y),
                8: lambda: copy(i, 8, own.at[hi], gathered.at[1, hi], by_x),
                9: lambda: copy(i, 9, own.at[lo], gathered.at[2, lo], by_y),
                10: lambda: copy(i, 10, gathered.at[1, lo], gathered.at[3, lo], by_y),
                11: lambda: copy(i, 11, gathered.at[2, hi], gathered.at[3, hi], by_x),
            }
        return made

    def keep(i):
        span = pl.ds(i * r, r)
        return pltpu.make_async_copy(own.at[span], gathered.at[0, span], local_sems.at[i])

    def stage(n, i):
        s = sends(i)
        lo, hi = pl.ds(i * r, h), pl.ds(i * r + h, h)
        half, span = pl.ds(i * h, h), pl.ds(i * r, r)
        if n == 0:
            for kind in (0, 1, 2, 3):
                s[kind]().start()
        elif n == 1:
            s[0]().wait_recv()
            sum_y[half] = (partial[2, lo].astype(F32) + relay_x[half].astype(F32)).astype(BF16)
            s[4]().start()
            s[1]().wait_recv()
            sum_x[half] = (partial[1, hi].astype(F32) + relay_y[half].astype(F32)).astype(BF16)
            s[5]().start()
        elif n == 2:
            for kind in (2, 3, 4, 5):
                s[kind]().wait_recv()
            total = partial[0, span].astype(F32) + (got_x[span].astype(F32) + got_y[span].astype(F32))
            given = middle(total, span, ins, outs)
            if gathers:
                own[span] = given
                for kind in (6, 7, 8, 9):
                    s[kind]().start()
                keep(i).start()
        elif n == 3 and gathers:
            s[6]().wait_recv()
            s[10]().start()
            s[7]().wait_recv()
            s[11]().start()
        elif n == 4:
            if gathers:
                for kind in (8, 9, 10, 11):
                    s[kind]().wait_recv()
                keep(i).wait()
            for kind in s:
                s[kind]().wait_send()

    turns = chunks + 4
    if n_jobs:
        side.begin()
        each = len(side.units) / (5 * chunks)
    steps = done = 0
    for t in range(turns):
        for n in range(5):
            if 0 <= t - n < chunks:
                stage(n, t - n)
                steps += 1
                if n_jobs and int(steps * each) > done:
                    side.step(int(steps * each) - done)
                    done = int(steps * each)
    if n_jobs:
        side.end()


def mid_call(middle, partial, ins, out_shapes, gathers, side, collective_id, chunks=4):
    _, rows, cols = partial.shape
    outs = tuple(out_shapes)
    specs = (VMEM,) * len(outs)
    if gathers:
        outs += (jax.ShapeDtypeStruct((4, rows, cols), BF16),)
        specs += (ANY,)
    outs += tuple(side.out_shapes())
    specs += (ANY,) * len(side.jobs)
    return pl.pallas_call(
        functools.partial(mid_kernel, middle, chunks, gathers, len(ins), len(out_shapes), side),
        out_shape=outs,
        in_specs=[VMEM] * (1 + len(ins)) + [ANY] * len(side.arrays),
        out_specs=specs,
        scratch_shapes=[
            pltpu.VMEM((rows // 2, cols), BF16),
            pltpu.VMEM((rows // 2, cols), BF16),
            pltpu.VMEM((rows, cols), BF16),
            pltpu.VMEM((rows, cols), BF16),
            pltpu.VMEM((rows // 2, cols), BF16),
            pltpu.VMEM((rows // 2, cols), BF16),
            pltpu.VMEM((rows, cols), BF16),
            pltpu.SemaphoreType.DMA((chunks, 12)),
            pltpu.SemaphoreType.DMA((chunks, 12)),
            pltpu.SemaphoreType.DMA((chunks,)),
        ]
        + (side.scratch() if side.jobs else []),
        compiler_params=pltpu.CompilerParams(
            collective_id=collective_id, has_side_effects=True, vmem_limit_bytes=60 * MIB
        ),
    )(partial, *ins, *side.arrays)


def start_kernel(
    tokens, small, marks, w_q, w_k, w_v,
    tokens_all, small_all, marks_all, w_cols, relay,
    send_sems, recv_sems, local_sems,
):
    f = lax.axis_index("fsdp")
    g = lax.axis_index("grp")
    core = lax.rem(g, 2)
    rows = tokens.shape[0]
    depth = w_q.shape[0]
    width = w_q.shape[1] // 4
    by_x, by_y = plane_neighbours()
    fx, fy = by_x["fsdp"], by_y["fsdp"]
    fd = fx + 2 - 4 * (fx // 2)
    z = g // 2
    odd = lax.rem(z, 2)
    by_d, sibling = {"fsdp": fd}, {"grp": g + 1 - 2 * core}
    by_z = {"grp": g + 2 - 4 * odd}
    barrier = pltpu.get_barrier_semaphore()
    for other in (by_x, by_y, by_d, sibling, by_z):
        pl.semaphore_signal(barrier, inc=1, device_id=other, device_id_type=MESH)
    pl.semaphore_wait(barrier, 5)

    def copy(n, src, dst, target):
        return pltpu.make_async_remote_copy(
            src_ref=src, dst_ref=dst, send_sem=send_sems.at[n], recv_sem=recv_sems.at[n],
            device_id=target, device_id_type=MESH,
        )

    def columns(j):
        return pl.ds(pl.multiple_of(j * width, width), width)

    quarter = depth // 4
    eighth = quarter // 2
    here, there = 2 * odd + core, 2 * (1 - odd) + core

    def block_rows(owner, q):
        return pl.ds(pl.multiple_of(owner * depth + q * quarter, quarter), quarter)

    mine = pl.ds(pl.multiple_of(here * quarter, quarter), quarter)
    all_sends = []

    def go(c):
        c.start()
        all_sends.append(c)
        return c

    waits = []
    n = 0
    for k, target in ((1, by_x), (2, by_y), (3, by_d)):
        waits.append(go(copy(n, small, small_all.at[k], target)))
        waits.append(go(copy(n + 1, marks, marks_all.at[k], target)))
        n += 2
    locals_ = [
        pltpu.make_async_copy(small, small_all.at[0], local_sems.at[0]),
        pltpu.make_async_copy(marks, marks_all.at[0], local_sems.at[1]),
        pltpu.make_async_copy(tokens, tokens_all.at[0], local_sems.at[2]),
    ]
    for j, w in enumerate((w_q, w_k, w_v)):
        locals_.append(
            pltpu.make_async_copy(
                w.at[:, columns(f)],
                w_cols.at[pl.ds(pl.multiple_of(f * depth, depth), depth), pl.ds(j * width, width)],
                local_sems.at[3 + j],
            )
        )
    for c in locals_:
        c.start()

    first = pl.ds(pl.multiple_of(here * quarter, eighth), eighth)
    second = pl.ds(pl.multiple_of(here * quarter + eighth, eighth), eighth)
    relays_x, relays_y, direct_x, direct_y = [], [], [], []
    for j, w in enumerate((w_q, w_k, w_v)):
        relays_x.append(go(copy(n, w.at[first, columns(fd)], relay.at[0, j], by_x)))
        relays_y.append(go(copy(n + 1, w.at[second, columns(fd)], relay.at[1, j], by_y)))
        n += 2
    for j, w in enumerate((w_q, w_k, w_v)):
        place = w_cols.at[block_rows(f, here), pl.ds(j * width, width)]
        direct_x.append(go(copy(n, w.at[mine, columns(fx)], place, by_x)))
        direct_y.append(go(copy(n + 1, w.at[mine, columns(fy)], place, by_y)))
        n += 2
    low, high = pl.ds(0, rows // 2), pl.ds(rows // 2, rows // 2)
    t_x0 = go(copy(n, tokens.at[low], tokens_all.at[1, low], by_x))
    t_y1 = go(copy(n + 1, tokens.at[high], tokens_all.at[2, high], by_y))
    t_x1 = go(copy(n + 2, tokens.at[high], tokens_all.at[1, high], by_x))
    t_y0 = go(copy(n + 3, tokens.at[low], tokens_all.at[2, low], by_y))
    n += 4
    forwarded = []
    for j in range(3):
        relays_x[j].wait_recv()
        forwarded.append(
            go(copy(
                n, relay.at[0, j],
                w_cols.at[pl.ds(pl.multiple_of(fx * depth + here * quarter, eighth), eighth), pl.ds(j * width, width)],
                by_y,
            ))
        )
        relays_y[j].wait_recv()
        forwarded.append(
            go(copy(
                n + 1, relay.at[1, j],
                w_cols.at[
                    pl.ds(pl.multiple_of(fy * depth + here * quarter + eighth, eighth), eighth), pl.ds(j * width, width)
                ],
                by_x,
            ))
        )
        n += 2
    shares, lent = [], []

    def share(owner, q, target):
        nonlocal n
        place = w_cols.at[block_rows(owner, q)]
        c = go(copy(n, place, place, target))
        n += 1
        return c

    def fetched(owner):
        lent.append(share(owner, here, by_z))
        shares.append(share(owner, here, sibling))

    for c in direct_x:
        c.wait_recv()
    fetched(fx)
    for c in direct_y:
        c.wait_recv()
    fetched(fy)
    t_x0.wait_recv()
    t_d0 = go(copy(n, tokens_all.at[1, low], tokens_all.at[3, low], by_y))
    t_y1.wait_recv()
    t_d1 = go(copy(n + 1, tokens_all.at[2, high], tokens_all.at[3, high], by_x))
    n += 2
    for c in forwarded:
        c.wait_recv()
    fetched(fd)
    for owner, c in zip((fx, fy, fd), lent):
        c.wait_recv()
        shares.append(share(owner, there, sibling))
    for c in waits + shares + [t_x1, t_y0, t_d0, t_d1]:
        c.wait_recv()
    for c in locals_:
        c.wait()
    for c in all_sends:
        c.wait_send()


def start_call(tokens, small, marks, w_q, w_k, w_v, collective_id):
    depth, features = w_q.shape
    width = features // 4
    n = 6 + 6 + 6 + 4 + 6 + 2 + 9
    return pl.pallas_call(
        start_kernel,
        out_shape=(
            jax.ShapeDtypeStruct((4,) + tokens.shape, tokens.dtype),
            jax.ShapeDtypeStruct((4,) + small.shape, small.dtype),
            jax.ShapeDtypeStruct((4,) + marks.shape, marks.dtype),
            jax.ShapeDtypeStruct((4 * depth, 3 * width), BF16),
            jax.ShapeDtypeStruct((2, 3, depth // 8, width), BF16),
        ),
        in_specs=[ANY] * 6,
        out_specs=(ANY,) * 5,
        scratch_shapes=[
            pltpu.SemaphoreType.DMA((n,)),
            pltpu.SemaphoreType.DMA((n,)),
            pltpu.SemaphoreType.DMA((6,)),
        ],
        compiler_params=pltpu.CompilerParams(
            collective_id=collective_id, has_side_effects=True, vmem_limit_bytes=16 * MIB
        ),
    )(tokens, small, marks, w_q, w_k, w_v)[:4]


def turn_half(x):
    return pltpu.roll(x, HEAD_DIM // 2, 1)


def hidden_bias(of_keys, of_queries):
    key_segment, key_position = of_keys[0], of_keys[4]
    seen = (
        (key_segment == of_queries[1]) | (key_segment == of_queries[2]) | (key_segment == of_queries[3])
    ) & (key_position <= of_queries[4])
    return jnp.where(seen, 0.0, MASK_FILL)


class Spread:
    def __init__(self, own, everyone, send_sems, recv_sems, local_sem):
        self.everyone, self.send_sems, self.recv_sems = everyone, send_sems, recv_sems
        self.by_x, self.by_y = plane_neighbours()
        rows = own.shape[0]
        low, high = pl.ds(0, rows // 2), pl.ds(rows // 2, rows // 2)
        self.kept = pltpu.make_async_copy(own, everyone.at[0], local_sem)
        self.first = [
            self.copy(0, own.at[low], (1, low), self.by_x),
            self.copy(1, own.at[high], (2, high), self.by_y),
            self.copy(2, own.at[high], (1, high), self.by_x),
            self.copy(3, own.at[low], (2, low), self.by_y),
        ]
        self.second = [
            self.copy(4, everyone.at[1, low], (3, low), self.by_y),
            self.copy(5, everyone.at[2, high], (3, high), self.by_x),
        ]

    def copy(self, n, src, place, target):
        return pltpu.make_async_remote_copy(
            src_ref=src, dst_ref=self.everyone.at[place], send_sem=self.send_sems.at[n],
            recv_sem=self.recv_sems.at[n], device_id=target, device_id_type=MESH,
        )

    def begin(self):
        plane_barrier(self.by_x, self.by_y)
        for c in self.first:
            c.start()
        self.kept.start()

    def middle(self):
        for got, onward in zip(self.first[:2], self.second):
            got.wait_recv()
            onward.start()

    def end(self):
        for c in self.first[2:] + self.second:
            c.wait_recv()
        for c in self.first + self.second:
            c.wait_send()
        self.kept.wait()


def attend_kernel(
    tokens, gain, w_cols, bias, w_out, cosine, sine, mark_cols, mark_rows, *refs
):
    spread = None
    if len(refs) > 5:
        own, refs = refs[0], refs[1:]
        normed, three, attended, branch, everyone, mask = refs[:6]
        spread = Spread(own, everyone, *refs[6:])
        spread.begin()
    else:
        normed, three, attended, branch, mask = refs
    count = tokens.shape[0]
    width = w_out.shape[0]
    scale = HEAD_DIM**-0.5
    step = 256
    rows_of = [mark_rows[j : j + 1, :] for j in range(5)]
    for a, n in pieces(count, step):
        s = pl.ds(a, n)
        x = tokens[s, :].astype(F32)
        factor = lax.rsqrt(jnp.mean(x * x, axis=-1, keepdims=True) + EPSILON)
        normed[s, :] = (x * factor * gain[...]).astype(BF16)
        cols_of = [mark_cols[s, j : j + 1] for j in range(5)]
        mask[s, :] = hidden_bias(rows_of, cols_of)
    for b, m in pieces(3 * width, 256):
        c = pl.ds(b, m)
        pre = plain_dot(normed[...], w_cols[:, c]) + bias[:, c]
        if b < 2 * width:
            for d in range(0, m, HEAD_DIM):
                x = pre[:, d : d + HEAD_DIM]
                three[:, b + d : b + d + HEAD_DIM] = (
                    x * cosine[...] + turn_half(x) * sine[...]
                ).astype(BF16)
        else:
            three[:, c] = pre.astype(BF16)
    if spread:
        spread.middle()
    for h in range(width // HEAD_DIM):
        q_cols = pl.ds(h * HEAD_DIM, HEAD_DIM)
        k_cols = pl.ds(width + h * HEAD_DIM, HEAD_DIM)
        v_cols = pl.ds(2 * width + h * HEAD_DIM, HEAD_DIM)
        for a, n in pieces(count, step):
            s = pl.ds(a, n)
            scores = trans_dot(three[s, q_cols], three[:, k_cols]) + mask[s, :]
            peak = jnp.max(scores, axis=-1, keepdims=True)
            expo = jnp.exp((scores - peak) * scale)
            total = jnp.sum(expo, axis=-1, keepdims=True)
            weights = (expo * (1.0 / total)).astype(BF16)
            attended[s, q_cols] = plain_dot(weights, three[:, v_cols]).astype(BF16)
    for b, m in pieces(w_out.shape[1], 512):
        c = pl.ds(b, m)
        branch[:, c] = plain_dot(attended[...], w_out[:, c]).astype(BF16)
    if spread:
        spread.end()


def attend_call(tokens, gain, w_cols, bias, w_out, cosine, sine, mark_cols, mark_rows, own=None, collective_id=None):
    count, features = tokens.shape
    width = w_out.shape[0]

    def shape(cols):
        return jax.ShapeDtypeStruct((count, cols), BF16)

    ins = [tokens, gain, w_cols, bias, w_out, cosine, sine, mark_cols, mark_rows]
    in_specs, out_specs = [VMEM] * 9, (VMEM,) * 4
    out_shape = (shape(features), shape(3 * width), shape(width), shape(features))
    scratch = [pltpu.VMEM((count, count), F32)]
    params = {}
    if own is not None:
        ins.append(own)
        in_specs.append(ANY)
        out_specs += (ANY,)
        out_shape += (jax.ShapeDtypeStruct((4,) + own.shape, own.dtype),)
        scratch += [pltpu.SemaphoreType.DMA((6,)), pltpu.SemaphoreType.DMA((6,)), pltpu.SemaphoreType.DMA]
        params = {"collective_id": collective_id, "has_side_effects": True}
    return pl.pallas_call(
        attend_kernel,
        in_specs=in_specs,
        out_specs=out_specs,
        out_shape=out_shape,
        scratch_shapes=scratch,
        compiler_params=pltpu.CompilerParams(vmem_limit_bytes=60 * MIB, **params),
    )(*ins)


def attend_back_kernel(
    grad, w_out, three, w_cols, cosine, sine, mark_cols, mark_rows,
    grad_three, partial, grad_bias, mask, grad_att,
):
    count = grad.shape[0]
    width = w_out.shape[0]
    scale = HEAD_DIM**-0.5
    step = 256
    for b, m in pieces(width, 256):
        c = pl.ds(b, m)
        grad_att[:, c] = trans_dot(grad[...], w_out[c, :]).astype(BF16)
    rows_of = [mark_rows[j : j + 1, :] for j in range(5)]
    for a, n in pieces(count, step):
        s = pl.ds(a, n)
        mask[s, :] = hidden_bias([mark_cols[s, j : j + 1] for j in range(5)], rows_of)
    for h in range(width // HEAD_DIM):
        q_cols = pl.ds(h * HEAD_DIM, HEAD_DIM)
        k_cols = pl.ds(width + h * HEAD_DIM, HEAD_DIM)
        v_cols = pl.ds(2 * width + h * HEAD_DIM, HEAD_DIM)
        grad_k = grad_v = None
        for a, n in pieces(count, step):
            s = pl.ds(a, n)
            query, g = three[s, q_cols], grad_att[s, q_cols]
            scores = trans_dot(three[:, k_cols], query) + mask[:, s]
            peak = jnp.max(scores, axis=0, keepdims=True)
            expo = jnp.exp((scores - peak) * scale)
            probs = expo * (1.0 / jnp.sum(expo, axis=0, keepdims=True))
            weight_grad = trans_dot(three[:, v_cols], g)
            diagonal = jnp.sum(probs * weight_grad, axis=0, keepdims=True)
            score_grad = (probs * (weight_grad - diagonal)).astype(BF16)
            part_v = plain_dot(probs.astype(BF16), g)
            part_k = plain_dot(score_grad, query)
            grad_v = part_v if grad_v is None else grad_v + part_v
            grad_k = part_k if grad_k is None else grad_k + part_k
            grad_q = rows_dot(score_grad, three[:, k_cols]) * scale
            grad_three[s, q_cols] = (
                grad_q * cosine[s, :] - turn_half(grad_q) * sine[s, :]
            ).astype(BF16)
        grad_k = grad_k * scale
        grad_three[:, k_cols] = (grad_k * cosine[...] - turn_half(grad_k) * sine[...]).astype(BF16)
        grad_three[:, v_cols] = grad_v.astype(BF16)
    for b, m in pieces(3 * width, 512):
        c = pl.ds(b, m)
        grad_bias[:, c] = jnp.sum(grad_three[:, c].astype(F32), axis=0, keepdims=True)
    for b, m in pieces(w_cols.shape[0], 512):
        c = pl.ds(b, m)
        partial[:, c] = trans_dot(grad_three[...], w_cols[c, :]).astype(BF16)


def attend_back_call(grad, w_out, three, w_cols, cosine, sine, mark_cols, mark_rows):
    count, features = grad.shape
    width = w_out.shape[0]

    def shape(rows, cols, dtype=BF16):
        return jax.ShapeDtypeStruct((rows, cols), dtype)

    return pl.pallas_call(
        attend_back_kernel,
        in_specs=[VMEM] * 8,
        out_specs=(VMEM,) * 3,
        out_shape=(shape(count, 3 * width), shape(count, features), shape(1, 3 * width, F32)),
        scratch_shapes=[pltpu.VMEM((count, count), F32), pltpu.VMEM((count, width), BF16)],
        compiler_params=pltpu.CompilerParams(vmem_limit_bytes=60 * MIB),
    )(grad, w_out, three, w_cols, cosine, sine, mark_cols, mark_rows)


class Load:
    def __init__(self, value):
        self.value = value

    def __getitem__(self, place):
        return self.value[place]


class Store:
    def __init__(self, shape):
        self.value = jnp.zeros(shape.shape, shape.dtype)

    def __getitem__(self, place):
        return self.value[place]

    def __setitem__(self, place, value):
        self.value = value.astype(self.value.dtype)


def first_middle(total, span, ins, outs):
    tokens, gain = ins
    mixed = tokens[span].astype(F32) + total
    factor = lax.rsqrt(jnp.mean(mixed * mixed, axis=-1, keepdims=True) + EPSILON)
    outs[0][span] = mixed
    return (mixed * factor * gain[...]).astype(BF16)


def norm_back(values, gain, grad):
    factor = lax.rsqrt(jnp.mean(values * values, axis=-1, keepdims=True) + EPSILON)
    weighted = gain * grad
    back = factor * weighted - values * (factor * factor * factor) * jnp.mean(
        weighted * values, axis=-1, keepdims=True
    )
    return back, jnp.sum(grad * values * factor, axis=0, keepdims=True)


def back_middle(total, span, ins, outs):
    values, gain, base = ins
    back, grad_gain = norm_back(values[span].astype(F32), gain[...], total)
    grad = base[span].astype(F32) + back
    outs[0][span] = grad
    outs[1][span if span == slice(None) else pl.ds(span.start // span.size, 1)] = grad_gain
    return grad.astype(BF16)


class Wires:
    def __init__(self, mesh):
        self.nf = mesh.shape["fsdp"]
        self.ng = mesh.shape["grp"]
        self.nz = self.ng // 2
        self.fast = self.nf == 4 and self.ng == 8
        self.chunks = 4 if self.fast else 1

    def xor(self, value, k):
        return lax.ppermute(value, "fsdp", [(i, i ^ k) for i in range(self.nf)])

    def inwards(self, value):
        if not self.fast:
            return None
        return lax.ppermute(value, "grp", [(0, 2), (1, 3), (6, 4), (7, 5)])

    def gather_list(self, value):
        return [value] + [self.xor(value, k) for k in range(1, self.nf)]

    def gather(self, value):
        return jnp.concatenate(self.gather_list(value), axis=0)

    def scatter_sum(self, value):
        rows = value.shape[0] // self.nf
        total = value[:rows].astype(F32)
        for k in range(1, self.nf):
            part = value[k * rows : (k + 1) * rows].astype(BF16)
            total = total + self.xor(part, k).astype(F32)
        return total

    def reduce_background(self, partial):
        return lax.psum_scatter(partial, "grp", scatter_dimension=0, tiled=True)

    def gather_start(self, tokens, small, marks, weights):
        if self.fast:
            return start_call(tokens, small, marks, *weights, 1)
        cols = jnp.concatenate(
            [lax.all_to_all(w, "fsdp", split_axis=1, concat_axis=0, tiled=True) for w in weights],
            axis=1,
        )
        return tuple(jnp.stack(self.gather_list(v)) for v in (tokens, small, marks)) + (cols,)

    def middle(self, body, partial, ins, out_shapes, gathers, number, arrays=(), jobs=()):
        nf = self.nf
        rows, cols = partial.shape[0] // nf, partial.shape[1]
        if self.fast:
            side = Side(arrays, jobs)
            return mid_call(body, partial.reshape(nf, rows, cols), ins, out_shapes, gathers, side, number)
        total = self.scatter_sum(partial)
        outs = [Store(s) for s in out_shapes]
        given = body(total, slice(None), [Load(v) for v in ins], outs)
        results = tuple(o.value for o in outs)
        if gathers:
            results += (jnp.stack(self.gather_list(given)),)

        def operand(o):
            number, axis, entry = o
            v = arrays[number] if axis is None else lax.index_in_dim(arrays[number], entry, axis, False)
            return v.reshape(-1, v.shape[-1])

        return results + tuple(
            sum(rows_dot(operand(a), operand(b)) for a, b in job).astype(BF16) for job in jobs
        )

    def last_sums(self, downs, shared, part_three, part_output, out_part, mixed, vec, bias_add, number):
        nf, ng, nz = self.nf, self.ng, self.nz
        features, width = part_output.shape
        share = features // ng
        if self.fast:
            outs = line_call(
                [v.reshape(nz, 2, share, -1) for v in downs],
                [v.reshape(nz, 2, share, -1) for v in shared],
                part_three.reshape(3, 2, share, features),
                part_output.reshape(nz, 2, share, width),
                out_part.reshape(nf, -1, features),
                mixed,
                vec.reshape(16, nf, width).transpose(1, 0, 2),
                bias_add,
                2,
                True,
                number,
            )
            return outs
        down = jnp.stack([self.reduce_background(v).astype(F32).T for v in downs], axis=0)
        sums = [self.reduce_background(v).astype(F32) for v in shared]
        three = lax.all_to_all(
            part_three.reshape(3, width, features), "fsdp", split_axis=2, concat_axis=1, tiled=True
        )
        four = jnp.concatenate([three, part_output[None]], axis=0)
        four = lax.psum_scatter(four, "grp", scatter_dimension=1, tiled=True).astype(F32)
        vec = lax.psum_scatter(vec, "fsdp", scatter_dimension=1, tiled=True) + bias_add
        output = (mixed + self.scatter_sum(out_part)).astype(BF16)
        return down, (sums[0], sums[1], sums[2].T), four.transpose(0, 2, 1), output, lax.psum(vec, "grp")


def on_device(
    wires,
    tokens,
    cotangent,
    segment,
    ancestry,
    position,
    routes,
    attn_gain,
    w_query,
    w_key,
    w_value,
    b_query,
    b_key,
    b_value,
    w_output,
    moe_gain,
    w_router,
    shared_switch,
    shared_gate,
    shared_up,
    shared_down,
    expert_gate,
    routed_up_weight,
    expert_down,
):
    nf, ng = wires.nf, wires.ng
    me = lax.axis_index("fsdp")
    rows_dev, features = tokens.shape
    count = rows_dev * nf
    width = features // nf
    experts = w_router.shape[1]
    local_experts = experts // nf
    capacity = 5 * rows_dev // 8
    choose = routes.shape[1]

    small = jnp.concatenate([attn_gain[None], moe_gain[None], w_router.T, shared_switch[None]], axis=0)
    small = jnp.pad(small, ((0, -small.shape[0] % 16), (0, 0)))
    marks = jnp.concatenate([segment[None], ancestry.T, position[None], routes.T], axis=0)
    marks = jnp.pad(marks, ((0, -marks.shape[0] % 16), (0, 0)))
    tokens_all, small_blocks, marks_all, w_cols = wires.gather_start(
        tokens, small, marks, (w_query, w_key, w_value)
    )
    tokens_all = tokens_all.reshape(count, features)
    small_all = jnp.concatenate(
        [lax.dynamic_index_in_dim(small_blocks, me ^ i, 0, keepdims=False) for i in range(nf)], axis=1
    )
    gain_one = small_all[0:1].astype(F32)
    gain_two = small_all[1:2].astype(F32)
    heads_rows = small_all[2 : experts + 3]
    mark_rows = jnp.concatenate([marks_all[k] for k in range(nf)], axis=1)
    mark_cols = mark_rows.T
    routes_rows = mark_rows[5 : 5 + choose]


    halfway = HEAD_DIM // 2
    freqs = ROPE_BASE ** (-(jnp.arange(halfway, dtype=F32) * 2.0 / HEAD_DIM))
    turns = mark_cols[:, 4:5].astype(F32) * jnp.concatenate([freqs, freqs])[None, :]
    cosine = jnp.cos(turns)
    sine = jnp.sin(turns) * jnp.where(jnp.arange(HEAD_DIM) < halfway, -1.0, 1.0)[None, :]
    bias = jnp.concatenate([b_query, b_key, b_value]).astype(F32)[None]
    operands = (tokens_all, gain_one, w_cols, bias, w_output, cosine, sine, mark_cols, mark_rows)
    if wires.fast:
        normed, three, attended, branch, cot_all = attend_call(*operands, cotangent, 6)
        cot_all = cot_all.reshape(count, features)
    else:
        normed, three, attended, branch = attend_call(*operands)
        cot_all = wires.gather(cotangent)

    numbers = me * local_experts + jnp.arange(local_experts, dtype=jnp.int32)
    named = jnp.any(routes_rows[None] == numbers[:, None, None], axis=1)
    named = named.reshape(local_experts, nf, rows_dev)
    earlier = (jnp.arange(rows_dev)[None, :] < jnp.arange(rows_dev)[:, None]).astype(BF16)
    slot = jnp.einsum("ts,ebs->bet", earlier, named.astype(BF16), preferred_element_type=F32)
    slot = jnp.where(named.transpose(1, 0, 2), slot.astype(jnp.int32), -1)
    pick = jnp.arange(capacity, dtype=jnp.int32)[None, None, :, None] == slot[:, :, None, :]

    cot_other = wires.inwards(cot_all)
    mixed, moe_blocks = wires.middle(
        first_middle,
        branch,
        (tokens, gain_two),
        (jax.ShapeDtypeStruct((rows_dev, features), F32),),
        True,
        2,
    )
    moe_in = moe_blocks.reshape(count, features)
    moe_other = wires.inwards(moe_in)

    rows_in, rows_cot, gate, pick_b, router_probs, opener = dispatch_call(
        moe_in, cot_all, slot, heads_rows, capacity
    )
    if wires.fast:
        rows_cot, cot_other = lax.optimization_barrier((rows_cot, cot_other))
    hidden, d_gate, d_up, d_out, y_rows, dx_rows, sens_rows = expert_call(
        rows_in, rows_cot, gate, expert_gate, routed_up_weight, expert_down, nf // 2
    )

    def slot_rows(x, i):
        return x[:, i].reshape(nf * capacity, features)

    gate_parts = [rows_dot(slot_rows(rows_in, i), d_gate[i]).astype(BF16) for i in range(local_experts)]
    up_part = rows_dot(slot_rows(rows_in, 0), d_up[0]).astype(BF16)
    gate_parts, up_part, hidden, sens_rows, y_rows, moe_other = lax.optimization_barrier(
        (gate_parts, up_part, hidden, sens_rows, y_rows, moe_other)
    )
    gate_sums = [wires.reduce_background(v) for v in gate_parts]
    up_sums = [wires.reduce_background(up_part)]

    gate_grad = jnp.sum(jnp.where(pick, sens_rows, 0.0), axis=2)
    gate_grad = gate_grad.transpose(1, 0, 2).reshape(local_experts, count)
    prob_grad = sum(
        jnp.where(jnp.arange(experts)[None] == numbers[i], gate_grad[i][:, None], 0.0)
        for i in range(local_experts)
    )
    logit_grad = router_probs * (
        prob_grad - jnp.sum(prob_grad * router_probs, axis=-1, keepdims=True)
    )
    high = logit_grad.astype(BF16)
    lanes = jnp.concatenate([high, (logit_grad - high.astype(F32)).astype(BF16)], axis=1)
    router_rows = heads_rows[:experts]
    taken = (nf, local_experts * capacity, features)
    s_hidden, sd_gate, sd_up, sd_out, out_part, moe_part, gate_sens = shared_call(
        moe_in,
        cot_all,
        opener,
        pick_b,
        y_rows.reshape(taken),
        dx_rows.reshape(taken),
        lanes,
        jnp.concatenate([router_rows, router_rows], axis=0),
        heads_rows[experts:].astype(F32),
        shared_gate,
        shared_up,
        shared_down,
    )
    sens_high = gate_sens.astype(BF16)
    sens_low = (gate_sens - sens_high.astype(F32)).astype(BF16)
    grad_heads = rows_dot(jnp.concatenate([lanes, sens_high, sens_low], axis=1), moe_in)
    grad_heads = jnp.concatenate(
        [
            grad_heads[:experts] + grad_heads[experts : 2 * experts],
            grad_heads[2 * experts : 2 * experts + 1] + grad_heads[2 * experts + 1 :],
        ],
        axis=0,
    )
    arrays = (rows_in, d_gate, d_up, moe_in, sd_gate, sd_up, sd_out)
    if wires.fast:
        o_hidden, od_gate, od_up, od_out = other_call(
            moe_other, cot_other, heads_rows, shared_gate, shared_up, shared_down, rows_dev
        )
        arrays += (moe_other, od_gate, od_up, s_hidden, od_out, o_hidden)
    else:
        arrays += (None, None, None, s_hidden)
    jobs = []
    for i in range(1, local_experts):
        jobs += [(((0, 1, i), (2, 0, i)),)]

    def whole(*numbers):
        return tuple((n, None, 0) for n in numbers)

    if wires.fast:
        jobs += [(whole(3, 4), whole(7, 8)), (whole(3, 5), whole(7, 9)), (whole(6, 10), whole(11, 12))]
    else:
        jobs += [(whole(3, 4),), (whole(3, 5),), (whole(6, 10),)]
    grad_mixed, grad_gain_two, branch_grad, *parts = wires.middle(
        back_middle,
        moe_part,
        (mixed, gain_two, cotangent),
        (
            jax.ShapeDtypeStruct((rows_dev, features), F32),
            jax.ShapeDtypeStruct((wires.chunks, features), F32),
        ),
        True,
        3,
        arrays,
        jobs,
    )
    late = local_experts - 1
    parts, up_sums = lax.optimization_barrier((parts, up_sums))
    up_sums += [wires.reduce_background(v) for v in parts[:late]]
    shared_parts = parts[late:]
    branch_grad = branch_grad.reshape(count, features)
    grad_three, normed_part, grad_bias = attend_back_call(
        branch_grad, w_output, three, w_cols, cosine, sine, mark_cols, mark_rows
    )
    grad_tokens, grad_gain_one, part_output, part_three, *down_parts = wires.middle(
        back_middle,
        normed_part,
        (tokens, gain_one, grad_mixed),
        (
            jax.ShapeDtypeStruct((rows_dev, features), F32),
            jax.ShapeDtypeStruct((wires.chunks, features), F32),
        ),
        False,
        4,
        (branch_grad, attended, grad_three, normed, d_out, hidden),
        [(whole(0, 1),), (whole(2, 3),)] + [(((4, 1, i), (5, 0, i)),) for i in range(local_experts)],
    )

    vec = jnp.concatenate(
        [
            jnp.sum(grad_gain_one, axis=0, keepdims=True),
            jnp.sum(grad_gain_two, axis=0, keepdims=True),
            grad_heads,
        ],
        axis=0,
    )
    vec = jnp.pad(vec, ((0, 16 - vec.shape[0]), (0, 0)))
    bias_add = jnp.pad(grad_bias.reshape(3, width), ((experts + 3, 16 - experts - 6), (0, 0)))
    down_sums, shared_sums, four, output, vec = wires.last_sums(
        down_parts, shared_parts, part_three, part_output, out_part, mixed, vec, bias_add, 5
    )
    own = width // ng
    vec = lax.dynamic_slice_in_dim(vec, lax.axis_index("grp") * own, own, 1)
    return (
        output,
        grad_tokens,
        vec[0],
        four[0],
        four[1],
        four[2],
        vec[experts + 3],
        vec[experts + 4],
        vec[experts + 5],
        four[3],
        vec[1],
        vec[2 : experts + 2].T,
        vec[experts + 2],
        shared_sums[0],
        shared_sums[1],
        shared_sums[2],
        jnp.stack(gate_sums, axis=0).astype(F32),
        jnp.stack(up_sums, axis=0).astype(F32),
        down_sums,
    )


def solution(mesh):
    wires = Wires(mesh)

    def step(*args):
        return on_device(wires, *args)

    rows = P(("grp", "fsdp"))
    shard = P("fsdp")
    small = P(("fsdp", "grp"))
    return jax.shard_map(
        step,
        mesh=mesh,
        in_specs=(rows,) * 6
        + (shard,) * 11
        + (P(None, "fsdp"), P(None, "fsdp"), shard, shard, shard, shard),
        out_specs=(
            rows,
            rows,
            small,
            P("fsdp", "grp"),
            P("fsdp", "grp"),
            P("fsdp", "grp"),
            small,
            small,
            small,
            P("fsdp", "grp"),
            small,
            small,
            small,
            P("grp", "fsdp"),
            P("grp", "fsdp"),
            P("fsdp", "grp"),
            P("fsdp", "grp", None),
            P("fsdp", "grp", None),
            P("fsdp", None, "grp"),
        ),
        check_vma=False,
    )
```

```python
import functools

import jax
import jax.numpy as jnp
from jax import lax
from jax.experimental import pallas as pl
from jax.experimental.pallas import tpu as pltpu
from jax.sharding import PartitionSpec as P

HEADS = 16
HEAD_DIM = 128
EPSILON = 1e-06
ROPE_BASE = 1000000.0
MASK_FILL = -1e30

F32 = jnp.float32
BF16 = jnp.bfloat16
MESH = pl.DeviceIdType.MESH
ANY = pl.BlockSpec(memory_space=pl.ANY)
VMEM = pl.BlockSpec(memory_space=pltpu.VMEM)
MIB = 2**20


def dot(left, right, dims, out=F32):
    return lax.dot_general(left, right, (dims, ((), ())), preferred_element_type=out)


def plain_dot(left, right):
    return dot(left, right, ((1,), (0,)))


def trans_dot(left, right):
    return dot(left, right, ((1,), (1,)))


def rows_dot(left, right):
    return dot(left, right, ((0,), (0,)))


def pieces(total, size):
    return [(a, min(size, total - a)) for a in range(0, total, size)]


def hidden_part(x, g, gate, w_gate, w_up, w_down, hidden, d_gate, d_up):
    units = w_gate.shape[1]
    sens = None
    for a, n in pieces(units, 256):
        s = pl.ds(a, n)
        pre = plain_dot(x, w_gate[:, s])
        up = plain_dot(x, w_up[:, s])
        plain = trans_dot(g, w_down[s, :])
        sigma = 1.0 / (1.0 + jnp.exp(-pre))
        act = pre * sigma
        slope = sigma * (1.0 + pre * (1.0 - sigma))
        h = (act * up).astype(BF16)
        hidden[:, s] = h
        grad = gate * plain
        d_gate[:, s] = (grad * up * slope).astype(BF16)
        d_up[:, s] = (grad * act).astype(BF16)
        part = jnp.sum(plain * h.astype(F32), axis=-1, keepdims=True)
        sens = part if sens is None else sens + part
    return sens


def expert_kernel(x_ref, g_ref, gate_ref, wg, wu, wd, hidden, d_gate, d_up, d_out, y_ref, dx_ref, sens_ref):
    blocks, _, slots, features = x_ref.shape
    rows = blocks * slots
    x = x_ref[...].reshape(rows, features)
    g = g_ref[...].reshape(rows, features)
    gate = gate_ref[...].reshape(rows, 1)
    wg, wu, wd = wg.at[0], wu.at[0], wd.at[0]
    hid, dg, du = hidden.at[0], d_gate.at[0], d_up.at[0]
    d_out[...] = (gate * g.astype(F32)).astype(BF16).reshape(d_out.shape)
    sens = hidden_part(x, g, gate, wg, wu, wd, hid, dg, du)
    sens_ref[...] = sens.reshape(sens_ref.shape)
    for a, n in pieces(features, 512):
        s = pl.ds(a, n)
        y = plain_dot(hid[...], wd[:, s]).astype(BF16)
        y_ref[:, :, :, s] = (gate * y.astype(F32)).astype(BF16).reshape(blocks, 1, slots, n)
        dx = trans_dot(dg[...], wg[s, :]) + trans_dot(du[...], wu[s, :])
        dx_ref[:, :, :, s] = dx.astype(BF16).reshape(blocks, 1, slots, n)


def expert_call(rows_in, rows_cot, gate, w_gate, w_up, w_down, tile):
    blocks, experts, slots, features = rows_in.shape
    units = w_gate.shape[2]
    steps = blocks // tile
    rows = tile * slots

    def slot_spec(cols):
        return pl.BlockSpec((tile, 1, slots, cols), lambda i, t: (t, i, 0, 0))

    def unit_spec():
        return pl.BlockSpec((1, rows, units), lambda i, t: (i, t, 0))

    def weight_spec(a, b):
        return pl.BlockSpec((1, a, b), lambda i, t: (i, 0, 0))

    units_shape = jax.ShapeDtypeStruct((experts, blocks * slots, units), BF16)
    slots_shape = jax.ShapeDtypeStruct((blocks, experts, slots, features), BF16)
    return pl.pallas_call(
        expert_kernel,
        grid=(experts, steps),
        in_specs=[
            slot_spec(features),
            slot_spec(features),
            slot_spec(1),
            weight_spec(features, units),
            weight_spec(features, units),
            weight_spec(units, features),
        ],
        out_specs=[unit_spec()] * 3 + [slot_spec(features)] * 3 + [slot_spec(1)],
        out_shape=[units_shape] * 3
        + [slots_shape] * 3
        + [jax.ShapeDtypeStruct((blocks, experts, slots, 1), F32)],
        compiler_params=pltpu.CompilerParams(vmem_limit_bytes=62 * MIB),
    )(rows_in, rows_cot, gate, w_gate, w_up, w_down)


def shared_kernel(
    x_ref, g_ref, head_ref, pick_ref, y_in, dx_in, lane_ref, heads_w, switch_row, wg, wu, wd,
    hidden, d_gate, d_up, d_out, y_ref, dx_ref, sens_ref,
):
    features = x_ref.shape[1]
    x = x_ref[...]
    g = g_ref[...]
    opener = head_ref[...]
    d_out[...] = (opener * g.astype(F32)).astype(BF16)
    sens = hidden_part(x, d_out[...], 1.0, wg, wu, wd, hidden, d_gate, d_up)
    sens = (1.0 - opener) * sens
    sens_ref[...] = sens
    pick = pick_ref[0]
    lanes = lane_ref[...]
    for a, n in pieces(features, 512):
        s = pl.ds(a, n)
        y = opener * plain_dot(hidden[...], wd[:, s]) + rows_dot(pick, y_in[0, :, s])
        y_ref[:, s] = y.astype(BF16)
        dx = trans_dot(d_gate[...], wg[s, :]) + trans_dot(d_up[...], wu[s, :])
        dx = dx + rows_dot(pick, dx_in[0, :, s])
        dx = dx + plain_dot(lanes, heads_w[:, s]) + sens * switch_row[:, s]
        dx_ref[:, s] = dx.astype(BF16)


def shared_call(x, g, opener, pick, y_in, dx_in, lanes, heads_w, switch_row, w_gate, w_up, w_down):
    count, features = x.shape
    units = w_gate.shape[1]
    blocks, taken, tile = pick.shape
    width = lanes.shape[1]

    def rows_spec(cols):
        return pl.BlockSpec((tile, cols), lambda b: (b, 0))

    def block_spec(cols):
        return pl.BlockSpec((1, taken, cols), lambda b: (b, 0, 0))

    def whole(a, b):
        return pl.BlockSpec((a, b), lambda b_: (0, 0), pipeline_mode=pl.Buffered(1))

    def shape(cols, dtype=BF16):
        return jax.ShapeDtypeStruct((count, cols), dtype)

    return pl.pallas_call(
        shared_kernel,
        grid=(blocks,),
        in_specs=[
            rows_spec(features),
            rows_spec(features),
            rows_spec(1),
            block_spec(tile),
            block_spec(features),
            block_spec(features),
            rows_spec(width),
            whole(width, features),
            whole(1, features),
            whole(features, units),
            whole(features, units),
            whole(units, features),
        ],
        out_specs=[rows_spec(units)] * 3 + [rows_spec(features)] * 3 + [rows_spec(1)],
        out_shape=[shape(units)] * 3 + [shape(features)] * 3 + [shape(1, F32)],
        compiler_params=pltpu.CompilerParams(vmem_limit_bytes=62 * MIB),
    )(x, g, opener, pick, y_in, dx_in, lanes, heads_w, switch_row, w_gate, w_up, w_down)


def other_kernel(x_ref, g_ref, heads, wg, wu, wd, hidden, d_gate, d_up, d_out):
    x = x_ref[...]
    pre = trans_dot(x, heads[...])
    opener = 1.0 / (1.0 + jnp.exp(-pre[:, heads.shape[0] - 1 :]))
    d_out[...] = (opener * g_ref[...].astype(F32)).astype(BF16)
    hidden_part(x, d_out[...], 1.0, wg, wu, wd, hidden, d_gate, d_up)


def other_call(x, g, heads, w_gate, w_up, w_down, tile):
    count, features = x.shape
    units = w_gate.shape[1]

    def rows_spec(cols):
        return pl.BlockSpec((tile, cols), lambda b: (b, 0))

    def whole(a, b):
        return pl.BlockSpec((a, b), lambda b_: (0, 0), pipeline_mode=pl.Buffered(1))

    def shape(cols):
        return jax.ShapeDtypeStruct((count, cols), BF16)

    return pl.pallas_call(
        other_kernel,
        grid=(count // tile,),
        in_specs=[
            rows_spec(features),
            rows_spec(features),
            whole(heads.shape[0], features),
            whole(features, units),
            whole(features, units),
            whole(units, features),
        ],
        out_specs=[rows_spec(units)] * 3 + [rows_spec(features)],
        out_shape=[shape(units)] * 3 + [shape(features)],
        compiler_params=pltpu.CompilerParams(vmem_limit_bytes=62 * MIB),
    )(x, g, heads, w_gate, w_up, w_down)


def dispatch_kernel(x_ref, g_ref, slot_ref, heads, rows_in, rows_cot, gate_ref, pick_ref, probs_ref, opener_ref):
    x, g = x_ref[...], g_ref[...]
    local, slots = rows_in.shape[1], rows_in.shape[2]
    count = heads.shape[0] - 1
    pre = trans_dot(x, heads[...])
    opener_ref[...] = 1.0 / (1.0 + jnp.exp(-pre[:, count:]))
    pre = pre[:, :count]
    expo = jnp.exp(pre - jnp.max(pre, axis=-1, keepdims=True))
    probs = expo / jnp.sum(expo, axis=-1, keepdims=True)
    probs_ref[...] = probs
    parts, rest = [], probs
    for _ in range(3):
        parts.append(rest.astype(BF16))
        rest = rest - parts[-1].astype(F32)
    numbers = lax.broadcasted_iota(jnp.int32, (slots, count), 1)
    places = lax.broadcasted_iota(jnp.int32, (slots, x.shape[0]), 0)
    for i in range(local):
        pick = jnp.where(places == slot_ref[0, i : i + 1, :], 1.0, 0.0).astype(BF16)
        pick_ref[0, i * slots : (i + 1) * slots, :] = pick
        rows_in[0, i] = plain_dot(pick, x).astype(BF16)
        rows_cot[0, i] = plain_dot(pick, g).astype(BF16)
        found = plain_dot(pick, parts[0]) + (plain_dot(pick, parts[1]) + plain_dot(pick, parts[2]))
        number = lax.axis_index("fsdp") * local + i
        gate_ref[0, i] = jnp.sum(jnp.where(numbers == number, found, 0.0), axis=-1, keepdims=True)


def dispatch_call(x, g, slot, heads, slots):
    count, features = x.shape
    blocks, local, rows = slot.shape
    experts = heads.shape[0] - 1

    def rows_spec(cols):
        return pl.BlockSpec((rows, cols), lambda b: (b, 0))

    def slots_spec(cols):
        return pl.BlockSpec((1, local, slots, cols), lambda b: (b, 0, 0, 0))

    def slots_shape(cols, dtype=BF16):
        return jax.ShapeDtypeStruct((blocks, local, slots, cols), dtype)

    return pl.pallas_call(
        dispatch_kernel,
        grid=(blocks,),
        in_specs=[
            rows_spec(features),
            rows_spec(features),
            pl.BlockSpec((1, local, rows), lambda b: (b, 0, 0)),
            pl.BlockSpec(heads.shape, lambda b: (0, 0)),
        ],
        out_specs=[
            slots_spec(features),
            slots_spec(features),
            slots_spec(1),
            pl.BlockSpec((1, local * slots, rows), lambda b: (b, 0, 0)),
            rows_spec(experts),
            rows_spec(1),
        ],
        out_shape=[
            slots_shape(features),
            slots_shape(features),
            slots_shape(1, F32),
            jax.ShapeDtypeStruct((blocks, local * slots, rows), BF16),
            jax.ShapeDtypeStruct((count, experts), F32),
            jax.ShapeDtypeStruct((count, 1), F32),
        ],
        compiler_params=pltpu.CompilerParams(vmem_limit_bytes=60 * MIB),
    )(x, g, slot, heads)


def outer_kernel(a_ref, b_ref, out_ref):
    out_ref[...] = rows_dot(a_ref[...].reshape(-1, a_ref.shape[-1]), b_ref[0]).astype(BF16)


def outer_call(rows, i, units):
    blocks, _, slots, features = rows.shape
    _, depth, n = units.shape
    tile = 512
    return pl.pallas_call(
        outer_kernel,
        grid=(features // tile,),
        in_specs=[
            pl.BlockSpec((blocks, 1, slots, tile), lambda j: (0, i, 0, j)),
            pl.BlockSpec((1, depth, n), lambda j: (i, 0, 0)),
        ],
        out_specs=pl.BlockSpec((tile, n), lambda j: (j, 0)),
        out_shape=jax.ShapeDtypeStruct((features, n), BF16),
        compiler_params=pltpu.CompilerParams(vmem_limit_bytes=40 * MIB),
    )(rows, units)


class Line:
    def __init__(self, parts, inner, sources, outs, sib, recv, bufs, sems):
        self.parts, self.inner, self.sources, self.outs = parts, inner, sources, outs
        self.sib, self.recv = sib, recv
        self.own_v, self.sib_v, self.send_v, self.out_v, self.turned_v = bufs
        self.own_sem, self.sib_sem, self.out_sem, self.sib_send, self.sib_recv, self.sent, self.got = sems
        self.chunks = len(sources) * parts
        self.slots = self.send_v.shape[0]
        self.rows = sources[0].shape[2] // parts
        g = lax.axis_index("grp")
        self.z, self.core = g // 2, lax.rem(g, 2)
        self.is_end = (self.z == 0) | (self.z == 3)
        self.is_mid = (self.z == 1) | (self.z == 2)

    def at(self, z, core):
        return {"grp": 2 * z + core}

    def span(self, q):
        return lax.div(q, self.parts), pl.ds(
            pl.multiple_of(lax.rem(q, self.parts) * self.rows, self.rows), self.rows
        )

    def swap(self, j, m, r, q):
        return pltpu.make_async_remote_copy(
            src_ref=self.sources[j].at[:, 1 - self.core, r],
            dst_ref=self.sib.at[m, :, r],
            send_sem=self.sib_send.at[q],
            recv_sem=self.sib_recv.at[q],
            device_id=self.at(self.z, 1 - self.core),
            device_id_type=MESH,
        )

    def swap_any(self, q):
        m, r = self.span(q)
        return self.swap(0, m, r, q)

    def when_summing(self, condition=None):
        if self.inner:
            condition = self.is_mid if condition is None else self.is_mid & condition
        return (lambda body: body()) if condition is None else pl.when(condition)

    def start_swaps(self):
        @self.when_summing()
        def _():
            for m in range(len(self.sources)):
                for h in range(self.parts):
                    self.swap(m, m, pl.ds(h * self.rows, self.rows), m * self.parts + h).start()

    def out_copy(self, j, r):
        ref, turned = self.outs[j]
        if turned:
            return pltpu.make_async_copy(self.turned_v, ref.at[:, r], self.out_sem)
        return pltpu.make_async_copy(self.out_v, ref.at[r], self.out_sem)

    def each_out(self, q, body):
        m, r = self.span(q)
        for j in range(len(self.sources)):

            @pl.when(m == j)
            def _():
                body(j, r)

    def hop(self, q, slot, target, place):
        m, r = self.span(q)
        return pltpu.make_async_remote_copy(
            src_ref=self.send_v.at[slot],
            dst_ref=self.recv.at[m, place, r],
            send_sem=self.sent.at[slot],
            recv_sem=self.got.at[q, place],
            device_id=self.at(target, self.core),
            device_id_type=MESH,
        )

    def arrived(self, q, place):
        self.hop(q, 0, self.z, place).wait_recv()

    def own_load(self, j, p, r, k):
        return pltpu.make_async_copy(self.sources[j].at[p, self.core, r], self.own_v.at[k], self.own_sem.at[k])

    def sib_load(self, m, p, r, k):
        return pltpu.make_async_copy(self.sib.at[m, p, r], self.sib_v.at[k], self.sib_sem.at[k])

    def start_base(self, q, p, k):
        m, r = self.span(q)
        for j in range(len(self.sources)):

            @pl.when(m == j)
            def _():
                self.own_load(j, p, r, k).start()

        self.sib_load(m, p, r, k).start()

    def base(self, k):
        r = pl.ds(0, self.rows)
        self.own_load(0, 0, r, k).wait()
        self.sib_load(0, 0, r, k).wait()
        return self.own_v[k].astype(F32) + self.sib_v[k].astype(F32)

    def fetch(self, q, place):
        self.arrived(q, place)
        m, r = self.span(q)
        return self.recv[m, place, r].astype(F32)

    def send(self, t, k, q, p, target, place, more, first):
        depth = self.slots // 3
        slot = lax.rem(t, depth) * 3 + k

        @pl.when(t >= depth + first)
        def _():
            self.hop(q, slot, target, place).wait_send()

        if more:
            extra = self.fetch(q, p)
            total = self.base(k) + extra
        else:
            total = self.base(k)
        self.send_v[slot] = total.astype(BF16)
        self.hop(q, slot, target, place).start()

    def turn(self, t):
        z, chunks = self.z, self.chunks
        to_end = self.is_end & (t >= 0) & (t < chunks)
        to_next = self.is_mid & (t >= 1) & (t < chunks + 1)
        to_last = self.is_mid & (t >= 2) & (t < chunks + 2)
        last = (t >= 3) & (t < chunks + 3)

        @self.when_summing((t >= 0) & (t < chunks))
        def _():
            self.swap_any(t).wait_recv()

        def end_piece(j):
            return jnp.where(z == 0, 3 - j, j)

        def next_piece(j):
            return jnp.where(z == 1, 3 - j, j)

        last_piece = jnp.where(z == 2, 3, 0)
        if not self.inner:

            @pl.when(to_end)
            def _():
                for j in range(3):
                    self.start_base(t, end_piece(j), j)

        @pl.when(to_next)
        def _():
            for j in range(2):
                self.start_base(t - 1, next_piece(j), j)

        @pl.when(to_last)
        def _():
            self.start_base(t - 2, last_piece, 2)

        @self.when_summing(last)
        def _():
            self.start_base(t - 3, z, 3)

        if not self.inner:

            @pl.when(to_end)
            def _():
                for j in range(3):
                    p = end_piece(j)
                    target = jnp.where(z == 0, 1, 2)
                    place = jnp.where((z == 3) & (p == 2), 4, p)
                    self.send(t, j, t, p, target, place, False, 0)

        @pl.when(to_next)
        def _():
            for j in range(2):
                p = next_piece(j)
                target = jnp.where(z == 1, 2, 1)
                place = jnp.where((z == 2) & (p == 1), 4, p)
                self.send(t, j, t - 1, p, target, place, not self.inner, 1)

        @pl.when(to_last)
        def _():
            place = jnp.where(z == 1, 4, last_piece)
            self.send(t, 2, t - 2, last_piece, last_piece, place, True, 2)

        @pl.when(last)
        def _():
            q = t - 3

            @pl.when(q >= 1)
            def _():
                self.each_out(q - 1, lambda j, r: self.out_copy(j, r).wait())

            if self.inner:

                @pl.when(z == 0)
                def _():
                    self.out_v[...] = self.fetch(q, 4)

                @pl.when(z == 3)
                def _():
                    self.out_v[...] = self.fetch(q, 3)

                @pl.when(z == 1)
                def _():
                    got = self.fetch(q, 4)
                    self.out_v[...] = self.base(3) + got

                @pl.when(z == 2)
                def _():
                    got = self.fetch(q, 2)
                    self.out_v[...] = self.base(3) + got

            else:
                self.out_v[...] = self.base(3)

                @pl.when(z > 0)
                def _():
                    self.out_v[...] = self.out_v[...] + self.fetch(q, z)

                @pl.when(z < 3)
                def _():
                    self.out_v[...] = self.out_v[...] + self.fetch(q, 4)

            def put(j, r):
                if self.outs[j][1]:
                    self.turned_v[...] = self.out_v[...].T
                self.out_copy(j, r).start()

            self.each_out(q, put)

    def finish(self):
        self.each_out(self.chunks - 1, lambda j, r: self.out_copy(j, r).wait())

        def body(q, carry):
            self.swap_any(q).wait_send()
            return carry

        @self.when_summing()
        def _():
            lax.fori_loop(0, self.chunks, body, 0)

        assert self.chunks >= self.slots // 3

        @self.when_summing()
        def _():
            for slot in range(self.slots):
                self.hop(0, slot, self.z, 0).wait_send()


def line_bufs(shape, slots, turned):
    return [pltpu.VMEM((4,) + shape, BF16)] * 2 + [
        pltpu.VMEM((slots,) + shape, BF16),
        pltpu.VMEM(shape, F32),
        pltpu.VMEM(shape[::-1] if turned else (8, 128), F32),
    ]


def line_sems(q, slots):
    return [
        pltpu.SemaphoreType.DMA((4,)),
        pltpu.SemaphoreType.DMA((4,)),
        pltpu.SemaphoreType.DMA,
        pltpu.SemaphoreType.DMA((q,)),
        pltpu.SemaphoreType.DMA((q,)),
        pltpu.SemaphoreType.DMA((slots,)),
        pltpu.SemaphoreType.DMA((q, 5)),
    ]


def line_kernel(n_down, n_shared, parts, shift, *refs):
    def take(n):
        nonlocal refs
        taken, refs = refs[:n], refs[n:]
        return taken

    downs, shared = take(n_down), take(n_shared)
    three, part_out, out_part, mixed, normed_part, tokens, base, vec, gain, bias_add = take(10)
    out_down, out_gate, out_up, out_sdown = take(4)
    out_four = take(4)
    output, grad_tokens, vec_out = take(3)
    sib_a, att, sib_b, sib_c, out_in = take(5)
    bufs_a, bufs_b, bufs_c = take(5), take(5), take(5)
    recv_a, recv_b, recv_c = take(3)
    vec_in, vec_own, vec_sib, vec_line, vec_send, parts_v, mixed_v, sum_v = take(8)
    relay_x, relay_y, got_x, got_y, sum_x, sum_y, gain_v, grad_v, vec_v = take(9)
    sems_a, sems_b, sems_c = take(7), take(7), take(7)
    plane_send, plane_recv, local_sems, vec_send_sems, vec_recv_sems, out_send, out_recv, norm_send, norm_recv = take(9)

    a = Line(parts, False, downs, [(out_down.at[j], True) for j in range(n_down)], sib_a, recv_a, bufs_a, sems_a)
    b = Line(1, False, [att.at[j] for j in range(4)], [(v, True) for v in out_four], sib_b, recv_b, bufs_b, sems_b)
    c = Line(parts, shift, shared, [(out_gate, False), (out_up, False), (out_sdown, True)], sib_c, recv_c, bufs_c, sems_c)
    z, core = a.z, a.core
    f = lax.axis_index("fsdp")
    fx = f + 1 - 2 * lax.rem(f, 2)
    fy = f + 2 - 4 * (f // 2)
    fd = fx + 2 - 4 * (fx // 2)
    peers = (fx, fy, fd)
    sibling = a.at(z, 1 - core)
    width = three.shape[3] // 4

    barrier = pltpu.get_barrier_semaphore()
    for other in (sibling,) + tuple({"fsdp": p} for p in peers):
        pl.semaphore_signal(barrier, inc=1, device_id=other, device_id_type=MESH)

    @pl.when(z > 0)
    def _():
        pl.semaphore_signal(barrier, inc=1, device_id=a.at(z - 1, core), device_id_type=MESH)

    @pl.when(z < 3)
    def _():
        pl.semaphore_signal(barrier, inc=1, device_id=a.at(z + 1, core), device_id_type=MESH)

    @pl.when(a.is_end)
    def _():
        pl.semaphore_wait(barrier, 5)

    @pl.when(a.is_mid)
    def _():
        pl.semaphore_wait(barrier, 6)

    a.start_swaps()
    c.start_swaps()

    def cols(p):
        return pl.ds(pl.multiple_of(p * width, width), width)

    def to_owner(k, p):
        return pltpu.make_async_remote_copy(
            src_ref=three.at[:, :, :, cols(p)], dst_ref=att.at[pl.ds(0, 3), f],
            send_sem=plane_send.at[k], recv_sem=plane_recv.at[k],
            device_id={"fsdp": p}, device_id_type=MESH,
        )

    def vec_owner(k, p):
        return pltpu.make_async_remote_copy(
            src_ref=vec_v.at[p], dst_ref=vec_in.at[k],
            send_sem=vec_send_sems.at[k], recv_sem=vec_recv_sems.at[k],
            device_id={"fsdp": p}, device_id_type=MESH,
        )

    def out_owner(k, p):
        return pltpu.make_async_remote_copy(
            src_ref=out_part.at[k + 1], dst_ref=out_in.at[k],
            send_sem=out_send.at[k], recv_sem=out_recv.at[k],
            device_id={"fsdp": p}, device_id_type=MESH,
        )

    for k, p in enumerate(peers):
        to_owner(k, p).start()

    rows_half = mixed.shape[0] // 2
    low, high = pl.ds(0, rows_half), pl.ds(rows_half, rows_half)

    def norm_copy(n, src, dst, target):
        return pltpu.make_async_remote_copy(
            src_ref=src, dst_ref=dst, send_sem=norm_send.at[n], recv_sem=norm_recv.at[n],
            device_id={"fsdp": target}, device_id_type=MESH,
        )

    norm_copies = [
        norm_copy(0, normed_part.at[3, low], relay_x, fx),
        norm_copy(1, normed_part.at[3, high], relay_y, fy),
        norm_copy(2, normed_part.at[1, low], got_x.at[low], fx),
        norm_copy(3, normed_part.at[2, high], got_y.at[high], fy),
        norm_copy(4, sum_y, got_y.at[low], fy),
        norm_copy(5, sum_x, got_x.at[high], fx),
    ]
    for copy in norm_copies[:4]:
        copy.start()

    def relay():
        loads = [
            pltpu.make_async_copy(normed_part.at[2, low], sum_y, local_sems.at[3]),
            pltpu.make_async_copy(normed_part.at[1, high], sum_x, local_sems.at[4]),
        ]
        for copy in loads:
            copy.start()
        for copy in loads:
            copy.wait()
        norm_copies[0].wait_recv()
        sum_y[...] = (sum_y[...].astype(F32) + relay_x[...].astype(F32)).astype(BF16)
        norm_copies[4].start()
        norm_copies[1].wait_recv()
        sum_x[...] = (sum_x[...].astype(F32) + relay_y[...].astype(F32)).astype(BF16)
        norm_copies[5].start()

    def finish_norm():
        for copy in norm_copies[2:]:
            copy.wait_recv()
        step = parts_v.shape[1]
        gain_v[...] = jnp.zeros_like(gain_v)

        def body(i, carry):
            r = pl.ds(pl.multiple_of(i * step, step), step)
            loads = [
                pltpu.make_async_copy(normed_part.at[0, r], parts_v.at[0], local_sems.at[3]),
                pltpu.make_async_copy(tokens.at[r], parts_v.at[1], local_sems.at[4]),
                pltpu.make_async_copy(base.at[r], mixed_v, local_sems.at[5]),
            ]
            for copy in loads:
                copy.start()
            for copy in loads:
                copy.wait()
            total = parts_v[0].astype(F32) + (got_x[r].astype(F32) + got_y[r].astype(F32))
            back, grad_gain = norm_back(parts_v[1].astype(F32), gain[...], total)
            gain_v[...] = gain_v[...] + grad_gain
            grad_v[...] = mixed_v[...] + back
            copy = pltpu.make_async_copy(grad_v, grad_tokens.at[r], local_sems.at[6])
            copy.start()
            copy.wait()
            return carry

        lax.fori_loop(0, mixed.shape[0] // step, body, 0)
        copy = pltpu.make_async_copy(vec, vec_v, local_sems.at[2])
        copy.start()
        copy.wait()
        for k in range(4):
            vec_v[k, 0:1, :] = gain_v[:, k * width : (k + 1) * width]
        for k, p in enumerate(peers):
            vec_owner(k, p).start()

    keep = (
        pltpu.make_async_copy(three.at[:, :, :, cols(f)], att.at[pl.ds(0, 3), f], local_sems.at[0]),
        pltpu.make_async_copy(part_out, att.at[3], local_sems.at[1]),
    )
    for copy in keep:
        copy.start()

    def vec_swap():
        return pltpu.make_async_remote_copy(
            src_ref=vec_own, dst_ref=vec_sib, send_sem=vec_send_sems.at[3], recv_sem=vec_recv_sems.at[3],
            device_id=sibling, device_id_type=MESH,
        )

    def vec_hop(k, target):
        return pltpu.make_async_remote_copy(
            src_ref=vec_send.at[k], dst_ref=vec_line.at[k], send_sem=vec_send_sems.at[4 + k],
            recv_sem=vec_recv_sems.at[4 + k], device_id=a.at(target, core), device_id_type=MESH,
        )

    def finish_output():
        for k, p in enumerate(peers):
            out_owner(k, p).wait_recv()
        step = parts_v.shape[1]

        def body(i, carry):
            r = pl.ds(pl.multiple_of(i * step, step), step)
            loads = [pltpu.make_async_copy(out_part.at[0, r], parts_v.at[0], local_sems.at[3])]
            loads += [
                pltpu.make_async_copy(out_in.at[k, r], parts_v.at[k + 1], local_sems.at[4 + k]) for k in range(3)
            ]
            loads.append(pltpu.make_async_copy(mixed.at[r], mixed_v, local_sems.at[7]))
            for copy in loads:
                copy.start()
            for copy in loads:
                copy.wait()
            total = (parts_v[0].astype(F32) + parts_v[1].astype(F32)) + (
                parts_v[2].astype(F32) + parts_v[3].astype(F32)
            )
            sum_v[...] = (mixed_v[...] + total).astype(BF16)
            copy = pltpu.make_async_copy(sum_v, output.at[r], local_sems.at[8])
            copy.start()
            copy.wait()
            return carry

        lax.fori_loop(0, mixed.shape[0] // step, body, 0)

    def side_work(t):
        @pl.when(t == 3)
        def _():
            for k, p in enumerate(peers):
                to_owner(k, p).wait_recv()
            for copy in keep:
                copy.wait()
            b.start_swaps()

        @pl.when(t == 4)
        def _():
            relay()
            for k, p in enumerate(peers):
                out_owner(k, p).start()

        @pl.when(t == 5)
        def _():
            finish_norm()

        @pl.when(t == 6)
        def _():
            for k, p in enumerate(peers):
                vec_owner(k, p).wait_recv()
            vec_own[...] = (vec_v[f] + vec_in[0]) + (vec_in[1] + vec_in[2]) + bias_add[...]
            vec_swap().start()

        @pl.when(t == 7)
        def _():
            vec_swap().wait_recv()
            vec_sib[...] = vec_sib[...] + vec_own[...]

            @pl.when(z == 0)
            def _():
                vec_send[0] = vec_sib[...]
                vec_hop(0, 1).start()

            @pl.when(z == 3)
            def _():
                vec_send[1] = vec_sib[...]
                vec_hop(1, 2).start()

        @pl.when((t == 8) & (z == 1))
        def _():
            vec_hop(0, 1).wait_recv()
            vec_send[0] = vec_sib[...] + vec_line[0]
            vec_hop(0, 2).start()

        @pl.when((t == 8) & (z == 2))
        def _():
            vec_hop(1, 2).wait_recv()
            vec_send[1] = vec_sib[...] + vec_line[1]
            vec_hop(1, 1).start()

        @pl.when(t == 8)
        def _():
            finish_output()

        @pl.when((t == 9) & (z == 2))
        def _():
            vec_hop(0, 2).wait_recv()
            vec_send[0] = vec_sib[...] + vec_line[0]
            vec_hop(0, 3).start()
            vec_out[...] = vec_send[0] + vec_line[1]

        @pl.when((t == 9) & (z == 1))
        def _():
            vec_hop(1, 1).wait_recv()
            vec_send[1] = vec_sib[...] + vec_line[1]
            vec_hop(1, 0).start()
            vec_out[...] = vec_send[1] + vec_line[0]

        @pl.when((t == 10) & (z == 3))
        def _():
            vec_hop(0, 3).wait_recv()
            vec_out[...] = vec_sib[...] + vec_line[0]

        @pl.when((t == 10) & (z == 0))
        def _():
            vec_hop(1, 0).wait_recv()
            vec_out[...] = vec_sib[...] + vec_line[1]

    def loop(t, carry):
        a.turn(t)
        b.turn(t - a.chunks)
        c.turn(t)
        side_work(t)
        return carry

    turns = max(a.chunks + b.chunks, c.chunks) + 3
    assert turns == 11
    lax.fori_loop(0, turns, loop, 0)
    for copy in norm_copies:
        copy.wait_send()
    a.finish()
    b.finish()
    c.finish()
    for k, p in enumerate(peers):
        vec_owner(k, p).wait_send()
        to_owner(k, p).wait_send()
        out_owner(k, p).wait_send()
    vec_swap().wait_send()

    @pl.when(z < 3)
    def _():
        vec_hop(0, 3).wait_send()

    @pl.when(z > 0)
    def _():
        vec_hop(1, 0).wait_send()


def line_call(
    downs, shared, three, part_out, out_part, mixed, normed_part, tokens, base, vec, gain, bias_add, parts, shift, collective_id
):
    _, _, rows, cols = shared[0].shape
    m, s = len(downs), len(shared)
    _, _, share, features = three.shape
    width = features // 4
    own_rows = mixed.shape[0]
    r = rows // parts
    slots = 9
    small = (16, width)
    step = own_rows // 4

    def shape(*dims, dtype=BF16):
        return jax.ShapeDtypeStruct(dims, dtype)

    outs = pl.pallas_call(
        functools.partial(line_kernel, m, s, parts, shift),
        out_shape=(
            shape(m, cols, rows, dtype=F32),
            shape(rows, cols, dtype=F32),
            shape(rows, cols, dtype=F32),
            shape(cols, rows, dtype=F32),
            shape(width, share, dtype=F32),
            shape(width, share, dtype=F32),
            shape(width, share, dtype=F32),
            shape(width, share, dtype=F32),
            shape(own_rows, features),
            shape(own_rows, features, dtype=F32),
            shape(*small, dtype=F32),
            shape(m, 4, rows, cols),
            shape(4, 4, 2, share, width),
            shape(4, 4, share, width),
            shape(s, 4, rows, cols),
            shape(3, own_rows, features),
        ),
        in_specs=[ANY] * (m + s + 8) + [VMEM] * 2,
        out_specs=(ANY,) * 10 + (VMEM,) + (ANY,) * 5,
        scratch_shapes=line_bufs((r, cols), slots, True)
        + line_bufs((share, width), slots, True)
        + line_bufs((r, cols), slots, True)
        + [
            pltpu.VMEM((m, 5, rows, cols), BF16),
            pltpu.VMEM((4, 5, share, width), BF16),
            pltpu.VMEM((s, 5, rows, cols), BF16),
            pltpu.VMEM((3,) + small, F32),
            pltpu.VMEM(small, F32),
            pltpu.VMEM(small, F32),
            pltpu.VMEM((2,) + small, F32),
            pltpu.VMEM((2,) + small, F32),
            pltpu.VMEM((4, step, features), BF16),
            pltpu.VMEM((step, features), F32),
            pltpu.VMEM((step, features), BF16),
            pltpu.VMEM((own_rows // 2, features), BF16),
            pltpu.VMEM((own_rows // 2, features), BF16),
            pltpu.VMEM((own_rows, features), BF16),
            pltpu.VMEM((own_rows, features), BF16),
            pltpu.VMEM((own_rows // 2, features), BF16),
            pltpu.VMEM((own_rows // 2, features), BF16),
            pltpu.VMEM((1, features), F32),
            pltpu.VMEM((step, features), F32),
            pltpu.VMEM((4,) + small, F32),
        ]
        + line_sems(m * parts, slots)
        + line_sems(4, slots)
        + line_sems(s * parts, slots)
        + [
            pltpu.SemaphoreType.DMA((3,)),
            pltpu.SemaphoreType.DMA((3,)),
            pltpu.SemaphoreType.DMA((9,)),
            pltpu.SemaphoreType.DMA((6,)),
            pltpu.SemaphoreType.DMA((6,)),
            pltpu.SemaphoreType.DMA((3,)),
            pltpu.SemaphoreType.DMA((3,)),
            pltpu.SemaphoreType.DMA((6,)),
            pltpu.SemaphoreType.DMA((6,)),
        ],
        compiler_params=pltpu.CompilerParams(
            collective_id=collective_id, has_side_effects=True, vmem_limit_bytes=60 * MIB
        ),
    )(*downs, *shared, three, part_out, out_part, mixed, normed_part, tokens, base, vec, gain, bias_add)
    return outs[0], outs[1:4], outs[4:8], outs[8], outs[9], outs[10]


def plane_neighbours():
    f = lax.axis_index("fsdp")
    by_x = f + 1 - 2 * lax.rem(f, 2)
    by_y = f + 2 - 4 * (f // 2)
    return {"fsdp": by_x}, {"fsdp": by_y}


def plane_barrier(by_x, by_y):
    barrier = pltpu.get_barrier_semaphore()
    for other in (by_x, by_y):
        pl.semaphore_signal(barrier, inc=1, device_id=other, device_id_type=MESH)
    pl.semaphore_wait(barrier, 2)


class Side:
    block = 512

    def __init__(self, arrays, jobs, later=()):
        self.arrays, self.jobs, self.later = list(arrays), list(jobs), dict(later)
        self.operands = sorted({o for job in self.jobs for pair in job for o in pair}, key=str)

    def shape(self, operand):
        number, axis, _ = operand
        full = self.arrays[number].shape
        return full if axis is None else full[:axis] + full[axis + 1 :]

    def out_shapes(self):
        return [
            jax.ShapeDtypeStruct((self.shape(job[0][0])[-1], self.shape(job[0][1])[-1]), BF16)
            for job in self.jobs
        ]

    def scratch(self):
        stages = sorted({self.shape(job[0][1])[-1] for job in self.jobs})
        self.stage_of = {n: k for k, n in enumerate(stages)}
        return (
            [pltpu.VMEM(self.shape(o), BF16) for o in self.operands if o not in self.later]
            + [pltpu.VMEM((2, self.block, n), BF16) for n in stages]
            + [
                pltpu.SemaphoreType.DMA((max(1, len(self.operands)),)),
                pltpu.SemaphoreType.DMA((max(1, 2 * len(stages)),)),
            ]
        )

    def bind(self, ins, outs, scratch):
        holders = [o for o in self.operands if o not in self.later]
        n = len(holders)
        self.ins, self.outs = ins, outs
        self.bufs = [scratch[holders.index(self.later.get(o, o))] for o in self.operands]
        self.stages = scratch[n:-2]
        self.load_sems, self.out_sems = scratch[-2:]
        self.loaded, self.pending, self.turn_of = set(), {}, {}
        self.units = [
            (j, k)
            for j, job in enumerate(self.jobs)
            for k in range(self.shape(job[0][0])[-1] // self.block)
        ]

    def load(self, k):
        number, axis, entry = self.operands[k]
        ref = self.ins[number]
        if axis is not None:
            ref = ref.at[(slice(None),) * axis + (entry,)]
        return pltpu.make_async_copy(ref, self.bufs[k], self.load_sems.at[k])

    def begin(self):
        for o in [o for job in self.jobs for pair in job for o in pair]:
            k = self.operands.index(o)
            if k not in self.loaded and o not in self.later:
                self.loaded.add(k)
                self.load(k).start()
        self.loaded = set()

    def step(self, number):
        for _ in range(number):
            if not self.units:
                return
            j, block = self.units.pop(0)
            pairs = [tuple(self.operands.index(o) for o in pair) for pair in self.jobs[j]]
            for k in [k for pair in pairs for k in pair]:
                if k not in self.loaded:
                    self.loaded.add(k)
                    self.load(k).wait()
            n = self.shape(self.jobs[j][0][1])[-1]
            stage = self.stage_of[n]
            slot = self.turn_of.get(stage, 0)
            self.turn_of[stage] = 1 - slot
            if (stage, slot) in self.pending:
                self.pending.pop((stage, slot)).wait()
            rows = pl.ds(block * self.block, self.block)
            total = None
            for ka, kb in pairs:
                left = self.bufs[ka][..., rows].reshape(-1, self.block)
                part = rows_dot(left, self.bufs[kb][...].reshape(-1, n))
                total = part if total is None else total + part
            self.stages[stage][slot] = total.astype(BF16)
            copy = pltpu.make_async_copy(
                self.stages[stage].at[slot], self.outs[j].at[rows], self.out_sems.at[2 * stage + slot]
            )
            copy.start()
            self.pending[(stage, slot)] = copy
            if not self.units or self.units[0][0] != j:
                for o in [o for pair in self.jobs[j] for o in pair]:
                    for k, heir in enumerate(self.operands):
                        if self.later.get(heir) == o:
                            self.load(k).start()

    def end(self):
        self.step(len(self.units))
        for copy in self.pending.values():
            copy.wait()


def mid_kernel(middle, chunks, gathers, n_in, n_out, side, *refs):
    n_side, n_jobs = len(side.arrays), len(side.jobs)
    partial, ins = refs[0], refs[1 : 1 + n_in]
    side_ins, refs = refs[1 + n_in : 1 + n_in + n_side], refs[1 + n_in + n_side :]
    outs, refs = refs[:n_out], refs[n_out:]
    gathered = None
    if gathers:
        gathered, refs = refs[0], refs[1:]
    side_outs, refs = refs[:n_jobs], refs[n_jobs:]
    relay_x, relay_y, got_x, got_y, sum_x, sum_y, own, send_sems, recv_sems, local_sems = refs[:10]
    if n_jobs:
        side.bind(side_ins, side_outs, refs[10:])
    rows = partial.shape[1]
    r = rows // chunks
    h = r // 2
    by_x, by_y = plane_neighbours()
    plane_barrier(by_x, by_y)

    def copy(i, kind, src, dst, target):
        return pltpu.make_async_remote_copy(
            src_ref=src, dst_ref=dst, send_sem=send_sems.at[i, kind], recv_sem=recv_sems.at[i, kind],
            device_id=target, device_id_type=MESH,
        )

    def sends(i):
        lo, hi = pl.ds(i * r, h), pl.ds(i * r + h, h)
        half = pl.ds(i * h, h)
        made = {
            0: lambda: copy(i, 0, partial.at[3, lo], relay_x.at[half], by_x),
            1: lambda: copy(i, 1, partial.at[3, hi], relay_y.at[half], by_y),
            2: lambda: copy(i, 2, partial.at[1, lo], got_x.at[lo], by_x),
            3: lambda: copy(i, 3, partial.at[2, hi], got_y.at[hi], by_y),
            4: lambda: copy(i, 4, sum_y.at[half], got_y.at[lo], by_y),
            5: lambda: copy(i, 5, sum_x.at[half], got_x.at[hi], by_x),
        }
        if gathers:
            made |= {
                6: lambda: copy(i, 6, own.at[lo], gathered.at[1, lo], by_x),
                7: lambda: copy(i, 7, own.at[hi], gathered.at[2, hi], by_y),
                8: lambda: copy(i, 8, own.at[hi], gathered.at[1, hi], by_x),
                9: lambda: copy(i, 9, own.at[lo], gathered.at[2, lo], by_y),
                10: lambda: copy(i, 10, gathered.at[1, lo], gathered.at[3, lo], by_y),
                11: lambda: copy(i, 11, gathered.at[2, hi], gathered.at[3, hi], by_x),
            }
        return made

    def keep(i):
        span = pl.ds(i * r, r)
        return pltpu.make_async_copy(own.at[span], gathered.at[0, span], local_sems.at[i])

    def stage(n, i):
        s = sends(i)
        lo, hi = pl.ds(i * r, h), pl.ds(i * r + h, h)
        half, span = pl.ds(i * h, h), pl.ds(i * r, r)
        if n == 0:
            for kind in (0, 1, 2, 3):
                s[kind]().start()
        elif n == 1:
            s[0]().wait_recv()
            sum_y[half] = (partial[2, lo].astype(F32) + relay_x[half].astype(F32)).astype(BF16)
            s[4]().start()
            s[1]().wait_recv()
            sum_x[half] = (partial[1, hi].astype(F32) + relay_y[half].astype(F32)).astype(BF16)
            s[5]().start()
        elif n == 2:
            for kind in (2, 3, 4, 5):
                s[kind]().wait_recv()
            total = partial[0, span].astype(F32) + (got_x[span].astype(F32) + got_y[span].astype(F32))
            given = middle(total, span, ins, outs)
            if gathers:
                own[span] = given
                for kind in (6, 7, 8, 9):
                    s[kind]().start()
                keep(i).start()
        elif n == 3 and gathers:
            s[6]().wait_recv()
            s[10]().start()
            s[7]().wait_recv()
            s[11]().start()
        elif n == 4:
            if gathers:
                for kind in (8, 9, 10, 11):
                    s[kind]().wait_recv()
                keep(i).wait()
            for kind in s:
                s[kind]().wait_send()

    turns = chunks + 4
    if n_jobs:
        side.begin()
        each = len(side.units) / (5 * chunks)
    steps = done = 0
    for t in range(turns):
        for n in range(5):
            if 0 <= t - n < chunks:
                stage(n, t - n)
                steps += 1
                if n_jobs and int(steps * each) > done:
                    side.step(int(steps * each) - done)
                    done = int(steps * each)
    if n_jobs:
        side.end()


def mid_call(middle, partial, ins, out_shapes, gathers, side, collective_id, chunks=4):
    _, rows, cols = partial.shape
    outs = tuple(out_shapes)
    specs = (VMEM,) * len(outs)
    if gathers:
        outs += (jax.ShapeDtypeStruct((4, rows, cols), BF16),)
        specs += (ANY,)
    outs += tuple(side.out_shapes())
    specs += (ANY,) * len(side.jobs)
    return pl.pallas_call(
        functools.partial(mid_kernel, middle, chunks, gathers, len(ins), len(out_shapes), side),
        out_shape=outs,
        in_specs=[VMEM] * (1 + len(ins)) + [ANY] * len(side.arrays),
        out_specs=specs,
        scratch_shapes=[
            pltpu.VMEM((rows // 2, cols), BF16),
            pltpu.VMEM((rows // 2, cols), BF16),
            pltpu.VMEM((rows, cols), BF16),
            pltpu.VMEM((rows, cols), BF16),
            pltpu.VMEM((rows // 2, cols), BF16),
            pltpu.VMEM((rows // 2, cols), BF16),
            pltpu.VMEM((rows, cols), BF16),
            pltpu.SemaphoreType.DMA((chunks, 12)),
            pltpu.SemaphoreType.DMA((chunks, 12)),
            pltpu.SemaphoreType.DMA((chunks,)),
        ]
        + (side.scratch() if side.jobs else []),
        compiler_params=pltpu.CompilerParams(
            collective_id=collective_id, has_side_effects=True, vmem_limit_bytes=60 * MIB
        ),
    )(partial, *ins, *side.arrays)


def start_kernel(
    tokens, small, marks, w_q, w_k, w_v,
    tokens_all, small_all, marks_all, w_cols, relay,
    send_sems, recv_sems, local_sems,
):
    f = lax.axis_index("fsdp")
    g = lax.axis_index("grp")
    core = lax.rem(g, 2)
    rows = tokens.shape[0]
    depth = w_q.shape[0]
    width = w_q.shape[1] // 4
    by_x, by_y = plane_neighbours()
    fx, fy = by_x["fsdp"], by_y["fsdp"]
    fd = fx + 2 - 4 * (fx // 2)
    z = g // 2
    odd = lax.rem(z, 2)
    by_d, sibling = {"fsdp": fd}, {"grp": g + 1 - 2 * core}
    by_z = {"grp": g + 2 - 4 * odd}
    barrier = pltpu.get_barrier_semaphore()
    for other in (by_x, by_y, by_d, sibling, by_z):
        pl.semaphore_signal(barrier, inc=1, device_id=other, device_id_type=MESH)
    pl.semaphore_wait(barrier, 5)

    def copy(n, src, dst, target):
        return pltpu.make_async_remote_copy(
            src_ref=src, dst_ref=dst, send_sem=send_sems.at[n], recv_sem=recv_sems.at[n],
            device_id=target, device_id_type=MESH,
        )

    def columns(j):
        return pl.ds(pl.multiple_of(j * width, width), width)

    quarter = depth // 4
    eighth = quarter // 2
    here, there = 2 * odd + core, 2 * (1 - odd) + core

    def block_rows(owner, q):
        return pl.ds(pl.multiple_of(owner * depth + q * quarter, quarter), quarter)

    mine = pl.ds(pl.multiple_of(here * quarter, quarter), quarter)
    all_sends = []

    def go(c):
        c.start()
        all_sends.append(c)
        return c

    waits = []
    n = 0
    for k, target in ((1, by_x), (2, by_y), (3, by_d)):
        waits.append(go(copy(n, small, small_all.at[k], target)))
        waits.append(go(copy(n + 1, marks, marks_all.at[k], target)))
        n += 2
    locals_ = [
        pltpu.make_async_copy(small, small_all.at[0], local_sems.at[0]),
        pltpu.make_async_copy(marks, marks_all.at[0], local_sems.at[1]),
        pltpu.make_async_copy(tokens, tokens_all.at[0], local_sems.at[2]),
    ]
    for j, w in enumerate((w_q, w_k, w_v)):
        locals_.append(
            pltpu.make_async_copy(
                w.at[:, columns(f)],
                w_cols.at[pl.ds(pl.multiple_of(f * depth, depth), depth), pl.ds(j * width, width)],
                local_sems.at[3 + j],
            )
        )
    for c in locals_:
        c.start()

    first = pl.ds(pl.multiple_of(here * quarter, eighth), eighth)
    second = pl.ds(pl.multiple_of(here * quarter + eighth, eighth), eighth)
    relays_x, relays_y, direct_x, direct_y = [], [], [], []
    for j, w in enumerate((w_q, w_k, w_v)):
        relays_x.append(go(copy(n, w.at[first, columns(fd)], relay.at[0, j], by_x)))
        relays_y.append(go(copy(n + 1, w.at[second, columns(fd)], relay.at[1, j], by_y)))
        n += 2
    for j, w in enumerate((w_q, w_k, w_v)):
        place = w_cols.at[block_rows(f, here), pl.ds(j * width, width)]
        direct_x.append(go(copy(n, w.at[mine, columns(fx)], place, by_x)))
        direct_y.append(go(copy(n + 1, w.at[mine, columns(fy)], place, by_y)))
        n += 2
    low, high = pl.ds(0, rows // 2), pl.ds(rows // 2, rows // 2)
    t_x0 = go(copy(n, tokens.at[low], tokens_all.at[1, low], by_x))
    t_y1 = go(copy(n + 1, tokens.at[high], tokens_all.at[2, high], by_y))
    t_x1 = go(copy(n + 2, tokens.at[high], tokens_all.at[1, high], by_x))
    t_y0 = go(copy(n + 3, tokens.at[low], tokens_all.at[2, low], by_y))
    n += 4
    forwarded = []
    for j in range(3):
        relays_x[j].wait_recv()
        forwarded.append(
            go(copy(
                n, relay.at[0, j],
                w_cols.at[pl.ds(pl.multiple_of(fx * depth + here * quarter, eighth), eighth), pl.ds(j * width, width)],
                by_y,
            ))
        )
        relays_y[j].wait_recv()
        forwarded.append(
            go(copy(
                n + 1, relay.at[1, j],
                w_cols.at[
                    pl.ds(pl.multiple_of(fy * depth + here * quarter + eighth, eighth), eighth), pl.ds(j * width, width)
                ],
                by_x,
            ))
        )
        n += 2
    shares, lent = [], []

    def share(owner, q, target):
        nonlocal n
        place = w_cols.at[block_rows(owner, q)]
        c = go(copy(n, place, place, target))
        n += 1
        return c

    def fetched(owner):
        lent.append(share(owner, here, by_z))
        shares.append(share(owner, here, sibling))

    for c in direct_x:
        c.wait_recv()
    fetched(fx)
    for c in direct_y:
        c.wait_recv()
    fetched(fy)
    t_x0.wait_recv()
    t_d0 = go(copy(n, tokens_all.at[1, low], tokens_all.at[3, low], by_y))
    t_y1.wait_recv()
    t_d1 = go(copy(n + 1, tokens_all.at[2, high], tokens_all.at[3, high], by_x))
    n += 2
    for c in forwarded:
        c.wait_recv()
    fetched(fd)
    for owner, c in zip((fx, fy, fd), lent):
        c.wait_recv()
        shares.append(share(owner, there, sibling))
    for c in waits + shares + [t_x1, t_y0, t_d0, t_d1]:
        c.wait_recv()
    for c in locals_:
        c.wait()
    for c in all_sends:
        c.wait_send()


def start_call(tokens, small, marks, w_q, w_k, w_v, collective_id):
    depth, features = w_q.shape
    width = features // 4
    n = 6 + 6 + 6 + 4 + 6 + 2 + 9
    return pl.pallas_call(
        start_kernel,
        out_shape=(
            jax.ShapeDtypeStruct((4,) + tokens.shape, tokens.dtype),
            jax.ShapeDtypeStruct((4,) + small.shape, small.dtype),
            jax.ShapeDtypeStruct((4,) + marks.shape, marks.dtype),
            jax.ShapeDtypeStruct((4 * depth, 3 * width), BF16),
            jax.ShapeDtypeStruct((2, 3, depth // 8, width), BF16),
        ),
        in_specs=[ANY] * 6,
        out_specs=(ANY,) * 5,
        scratch_shapes=[
            pltpu.SemaphoreType.DMA((n,)),
            pltpu.SemaphoreType.DMA((n,)),
            pltpu.SemaphoreType.DMA((6,)),
        ],
        compiler_params=pltpu.CompilerParams(
            collective_id=collective_id, has_side_effects=True, vmem_limit_bytes=16 * MIB
        ),
    )(tokens, small, marks, w_q, w_k, w_v)[:4]


def turn_half(x):
    return pltpu.roll(x, HEAD_DIM // 2, 1)


def hidden_bias(of_keys, of_queries):
    key_segment, key_position = of_keys[0], of_keys[4]
    seen = (
        (key_segment == of_queries[1]) | (key_segment == of_queries[2]) | (key_segment == of_queries[3])
    ) & (key_position <= of_queries[4])
    return jnp.where(seen, 0.0, MASK_FILL)


class Spread:
    def __init__(self, own, everyone, send_sems, recv_sems, local_sem):
        self.everyone, self.send_sems, self.recv_sems = everyone, send_sems, recv_sems
        self.by_x, self.by_y = plane_neighbours()
        rows = own.shape[0]
        low, high = pl.ds(0, rows // 2), pl.ds(rows // 2, rows // 2)
        self.kept = pltpu.make_async_copy(own, everyone.at[0], local_sem)
        self.first = [
            self.copy(0, own.at[low], (1, low), self.by_x),
            self.copy(1, own.at[high], (2, high), self.by_y),
            self.copy(2, own.at[high], (1, high), self.by_x),
            self.copy(3, own.at[low], (2, low), self.by_y),
        ]
        self.second = [
            self.copy(4, everyone.at[1, low], (3, low), self.by_y),
            self.copy(5, everyone.at[2, high], (3, high), self.by_x),
        ]

    def copy(self, n, src, place, target):
        return pltpu.make_async_remote_copy(
            src_ref=src, dst_ref=self.everyone.at[place], send_sem=self.send_sems.at[n],
            recv_sem=self.recv_sems.at[n], device_id=target, device_id_type=MESH,
        )

    def begin(self):
        plane_barrier(self.by_x, self.by_y)
        for c in self.first:
            c.start()
        self.kept.start()

    def middle(self):
        for got, onward in zip(self.first[:2], self.second):
            got.wait_recv()
            onward.start()

    def end(self):
        for c in self.first[2:] + self.second:
            c.wait_recv()
        for c in self.first + self.second:
            c.wait_send()
        self.kept.wait()


def attend_kernel(
    tokens, gain, w_cols, bias, w_out, cosine, sine, mark_cols, mark_rows, *refs
):
    spread = None
    if len(refs) > 5:
        own, refs = refs[0], refs[1:]
        normed, three, attended, branch, everyone, mask = refs[:6]
        spread = Spread(own, everyone, *refs[6:])
        spread.begin()
    else:
        normed, three, attended, branch, mask = refs
    count = tokens.shape[0]
    width = w_out.shape[0]
    scale = HEAD_DIM**-0.5
    step = 256
    rows_of = [mark_rows[j : j + 1, :] for j in range(5)]
    for a, n in pieces(count, step):
        s = pl.ds(a, n)
        x = tokens[s, :].astype(F32)
        factor = lax.rsqrt(jnp.mean(x * x, axis=-1, keepdims=True) + EPSILON)
        normed[s, :] = (x * factor * gain[...]).astype(BF16)
        cols_of = [mark_cols[s, j : j + 1] for j in range(5)]
        mask[s, :] = hidden_bias(rows_of, cols_of)
    for b, m in pieces(3 * width, 256):
        c = pl.ds(b, m)
        pre = plain_dot(normed[...], w_cols[:, c]) + bias[:, c]
        if b < 2 * width:
            for d in range(0, m, HEAD_DIM):
                x = pre[:, d : d + HEAD_DIM]
                three[:, b + d : b + d + HEAD_DIM] = (
                    x * cosine[...] + turn_half(x) * sine[...]
                ).astype(BF16)
        else:
            three[:, c] = pre.astype(BF16)
    if spread:
        spread.middle()
    for h in range(width // HEAD_DIM):
        q_cols = pl.ds(h * HEAD_DIM, HEAD_DIM)
        k_cols = pl.ds(width + h * HEAD_DIM, HEAD_DIM)
        v_cols = pl.ds(2 * width + h * HEAD_DIM, HEAD_DIM)
        for a, n in pieces(count, step):
            s = pl.ds(a, n)
            scores = trans_dot(three[s, q_cols], three[:, k_cols]) + mask[s, :]
            peak = jnp.max(scores, axis=-1, keepdims=True)
            expo = jnp.exp((scores - peak) * scale)
            total = jnp.sum(expo, axis=-1, keepdims=True)
            weights = (expo * (1.0 / total)).astype(BF16)
            attended[s, q_cols] = plain_dot(weights, three[:, v_cols]).astype(BF16)
    for b, m in pieces(w_out.shape[1], 512):
        c = pl.ds(b, m)
        branch[:, c] = plain_dot(attended[...], w_out[:, c]).astype(BF16)
    if spread:
        spread.end()


def attend_call(tokens, gain, w_cols, bias, w_out, cosine, sine, mark_cols, mark_rows, own=None, collective_id=None):
    count, features = tokens.shape
    width = w_out.shape[0]

    def shape(cols):
        return jax.ShapeDtypeStruct((count, cols), BF16)

    ins = [tokens, gain, w_cols, bias, w_out, cosine, sine, mark_cols, mark_rows]
    in_specs, out_specs = [VMEM] * 9, (VMEM,) * 4
    out_shape = (shape(features), shape(3 * width), shape(width), shape(features))
    scratch = [pltpu.VMEM((count, count), F32)]
    params = {}
    if own is not None:
        ins.append(own)
        in_specs.append(VMEM)
        out_specs += (VMEM,)
        out_shape += (jax.ShapeDtypeStruct((4,) + own.shape, own.dtype),)
        scratch += [pltpu.SemaphoreType.DMA((6,)), pltpu.SemaphoreType.DMA((6,)), pltpu.SemaphoreType.DMA]
        params = {"collective_id": collective_id, "has_side_effects": True}
    return pl.pallas_call(
        attend_kernel,
        in_specs=in_specs,
        out_specs=out_specs,
        out_shape=out_shape,
        scratch_shapes=scratch,
        compiler_params=pltpu.CompilerParams(vmem_limit_bytes=60 * MIB, **params),
    )(*ins)


def attend_back_kernel(
    grad, w_out, three, w_cols, cosine, sine, mark_cols, mark_rows,
    grad_three, partial, grad_bias, mask, grad_att,
):
    count = grad.shape[0]
    width = w_out.shape[0]
    scale = HEAD_DIM**-0.5
    step = 256
    for b, m in pieces(width, 256):
        c = pl.ds(b, m)
        grad_att[:, c] = trans_dot(grad[...], w_out[c, :]).astype(BF16)
    rows_of = [mark_rows[j : j + 1, :] for j in range(5)]
    for a, n in pieces(count, step):
        s = pl.ds(a, n)
        mask[s, :] = hidden_bias([mark_cols[s, j : j + 1] for j in range(5)], rows_of)
    for h in range(width // HEAD_DIM):
        q_cols = pl.ds(h * HEAD_DIM, HEAD_DIM)
        k_cols = pl.ds(width + h * HEAD_DIM, HEAD_DIM)
        v_cols = pl.ds(2 * width + h * HEAD_DIM, HEAD_DIM)
        grad_k = grad_v = None
        for a, n in pieces(count, step):
            s = pl.ds(a, n)
            query, g = three[s, q_cols], grad_att[s, q_cols]
            scores = trans_dot(three[:, k_cols], query) + mask[:, s]
            peak = jnp.max(scores, axis=0, keepdims=True)
            expo = jnp.exp((scores - peak) * scale)
            probs = expo * (1.0 / jnp.sum(expo, axis=0, keepdims=True))
            weight_grad = trans_dot(three[:, v_cols], g)
            diagonal = jnp.sum(probs * weight_grad, axis=0, keepdims=True)
            score_grad = (probs * (weight_grad - diagonal)).astype(BF16)
            part_v = plain_dot(probs.astype(BF16), g)
            part_k = plain_dot(score_grad, query)
            grad_v = part_v if grad_v is None else grad_v + part_v
            grad_k = part_k if grad_k is None else grad_k + part_k
            grad_q = rows_dot(score_grad, three[:, k_cols]) * scale
            grad_three[s, q_cols] = (
                grad_q * cosine[s, :] - turn_half(grad_q) * sine[s, :]
            ).astype(BF16)
        grad_k = grad_k * scale
        grad_three[:, k_cols] = (grad_k * cosine[...] - turn_half(grad_k) * sine[...]).astype(BF16)
        grad_three[:, v_cols] = grad_v.astype(BF16)
    for b, m in pieces(3 * width, 512):
        c = pl.ds(b, m)
        grad_bias[:, c] = jnp.sum(grad_three[:, c].astype(F32), axis=0, keepdims=True)
    for b, m in pieces(w_cols.shape[0], 512):
        c = pl.ds(b, m)
        partial[:, c] = trans_dot(grad_three[...], w_cols[c, :]).astype(BF16)


def attend_back_call(grad, w_out, three, w_cols, cosine, sine, mark_cols, mark_rows):
    count, features = grad.shape
    width = w_out.shape[0]

    def shape(rows, cols, dtype=BF16):
        return jax.ShapeDtypeStruct((rows, cols), dtype)

    return pl.pallas_call(
        attend_back_kernel,
        in_specs=[VMEM] * 8,
        out_specs=(VMEM,) * 3,
        out_shape=(shape(count, 3 * width), shape(count, features), shape(1, 3 * width, F32)),
        scratch_shapes=[pltpu.VMEM((count, count), F32), pltpu.VMEM((count, width), BF16)],
        compiler_params=pltpu.CompilerParams(vmem_limit_bytes=60 * MIB),
    )(grad, w_out, three, w_cols, cosine, sine, mark_cols, mark_rows)


class Load:
    def __init__(self, value):
        self.value = value

    def __getitem__(self, place):
        return self.value[place]


class Store:
    def __init__(self, shape):
        self.value = jnp.zeros(shape.shape, shape.dtype)

    def __getitem__(self, place):
        return self.value[place]

    def __setitem__(self, place, value):
        self.value = value.astype(self.value.dtype)


def first_middle(total, span, ins, outs):
    tokens, gain = ins
    mixed = tokens[span].astype(F32) + total
    factor = lax.rsqrt(jnp.mean(mixed * mixed, axis=-1, keepdims=True) + EPSILON)
    outs[0][span] = mixed
    return (mixed * factor * gain[...]).astype(BF16)


def norm_back(values, gain, grad):
    factor = lax.rsqrt(jnp.mean(values * values, axis=-1, keepdims=True) + EPSILON)
    weighted = gain * grad
    back = factor * weighted - values * (factor * factor * factor) * jnp.mean(
        weighted * values, axis=-1, keepdims=True
    )
    return back, jnp.sum(grad * values * factor, axis=0, keepdims=True)


def back_middle(total, span, ins, outs):
    values, gain, base = ins
    back, grad_gain = norm_back(values[span].astype(F32), gain[...], total)
    grad = base[span].astype(F32) + back
    outs[0][span] = grad
    outs[1][span if span == slice(None) else pl.ds(span.start // span.size, 1)] = grad_gain
    return grad.astype(BF16)


class Wires:
    def __init__(self, mesh):
        self.nf = mesh.shape["fsdp"]
        self.ng = mesh.shape["grp"]
        self.nz = self.ng // 2
        self.fast = self.nf == 4 and self.ng == 8
        self.chunks = 4 if self.fast else 1

    def xor(self, value, k):
        return lax.ppermute(value, "fsdp", [(i, i ^ k) for i in range(self.nf)])

    def inwards(self, value):
        if not self.fast:
            return None
        return lax.ppermute(value, "grp", [(0, 2), (1, 3), (6, 4), (7, 5)])

    def gather_list(self, value):
        return [value] + [self.xor(value, k) for k in range(1, self.nf)]

    def gather(self, value):
        return jnp.concatenate(self.gather_list(value), axis=0)

    def scatter_sum(self, value):
        rows = value.shape[0] // self.nf
        total = value[:rows].astype(F32)
        for k in range(1, self.nf):
            part = value[k * rows : (k + 1) * rows].astype(BF16)
            total = total + self.xor(part, k).astype(F32)
        return total

    def reduce_background(self, partial):
        return lax.psum_scatter(partial, "grp", scatter_dimension=0, tiled=True)

    def gather_start(self, tokens, small, marks, weights):
        if self.fast:
            return start_call(tokens, small, marks, *weights, 1)
        cols = jnp.concatenate(
            [lax.all_to_all(w, "fsdp", split_axis=1, concat_axis=0, tiled=True) for w in weights],
            axis=1,
        )
        return tuple(jnp.stack(self.gather_list(v)) for v in (tokens, small, marks)) + (cols,)

    def middle(self, body, partial, ins, out_shapes, gathers, number, arrays=(), jobs=(), later=()):
        nf = self.nf
        rows, cols = partial.shape[0] // nf, partial.shape[1]
        if self.fast:
            side = Side(arrays, jobs, later)
            return mid_call(body, partial.reshape(nf, rows, cols), ins, out_shapes, gathers, side, number)
        total = self.scatter_sum(partial)
        outs = [Store(s) for s in out_shapes]
        given = body(total, slice(None), [Load(v) for v in ins], outs)
        results = tuple(o.value for o in outs)
        if gathers:
            results += (jnp.stack(self.gather_list(given)),)

        def operand(o):
            number, axis, entry = o
            v = arrays[number] if axis is None else lax.index_in_dim(arrays[number], entry, axis, False)
            return v.reshape(-1, v.shape[-1])

        return results + tuple(
            sum(rows_dot(operand(a), operand(b)) for a, b in job).astype(BF16) for job in jobs
        )

    def last_sums(
        self, downs, shared, part_three, part_output, out_part, mixed, normed_part, tokens, base, vec, gain, bias_add, number
    ):
        nf, ng, nz = self.nf, self.ng, self.nz
        features, width = part_output.shape
        share = features // ng
        if self.fast:
            outs = line_call(
                [v.reshape(nz, 2, share, -1) for v in downs],
                [v.reshape(nz, 2, share, -1) for v in shared],
                part_three.reshape(3, 2, share, features),
                part_output.reshape(nz, 2, share, width),
                out_part.reshape(nf, -1, features),
                mixed,
                normed_part.reshape(nf, -1, features),
                tokens,
                base,
                vec.reshape(16, nf, width).transpose(1, 0, 2),
                gain,
                bias_add,
                2,
                True,
                number,
            )
            return outs
        down = jnp.stack([self.reduce_background(v).astype(F32).T for v in downs], axis=0)
        sums = [self.reduce_background(v).astype(F32) for v in shared]
        three = lax.all_to_all(
            part_three.reshape(3, width, features), "fsdp", split_axis=2, concat_axis=1, tiled=True
        )
        four = jnp.concatenate([three, part_output[None]], axis=0)
        four = lax.psum_scatter(four, "grp", scatter_dimension=1, tiled=True).astype(F32)
        back, grad_gain = norm_back(tokens.astype(F32), gain, self.scatter_sum(normed_part))
        vec = jnp.concatenate([grad_gain, vec[1:]], axis=0)
        vec = lax.psum_scatter(vec, "fsdp", scatter_dimension=1, tiled=True) + bias_add
        output = (mixed + self.scatter_sum(out_part)).astype(BF16)
        return down, (sums[0], sums[1], sums[2].T), four.transpose(0, 2, 1), output, base + back, lax.psum(vec, "grp")


def on_device(
    wires,
    tokens,
    cotangent,
    segment,
    ancestry,
    position,
    routes,
    attn_gain,
    w_query,
    w_key,
    w_value,
    b_query,
    b_key,
    b_value,
    w_output,
    moe_gain,
    w_router,
    shared_switch,
    shared_gate,
    shared_up,
    shared_down,
    expert_gate,
    routed_up_weight,
    expert_down,
):
    nf, ng = wires.nf, wires.ng
    me = lax.axis_index("fsdp")
    rows_dev, features = tokens.shape
    count = rows_dev * nf
    width = features // nf
    experts = w_router.shape[1]
    local_experts = experts // nf
    capacity = 5 * rows_dev // 8
    choose = routes.shape[1]

    small = jnp.concatenate([attn_gain[None], moe_gain[None], w_router.T, shared_switch[None]], axis=0)
    small = jnp.pad(small, ((0, -small.shape[0] % 16), (0, 0)))
    marks = jnp.concatenate([segment[None], ancestry.T, position[None], routes.T], axis=0)
    marks = jnp.pad(marks, ((0, -marks.shape[0] % 16), (0, 0)))
    tokens_all, small_blocks, marks_all, w_cols = wires.gather_start(
        tokens, small, marks, (w_query, w_key, w_value)
    )
    tokens_all = tokens_all.reshape(count, features)
    small_all = jnp.concatenate(
        [lax.dynamic_index_in_dim(small_blocks, me ^ i, 0, keepdims=False) for i in range(nf)], axis=1
    )
    gain_one = small_all[0:1].astype(F32)
    gain_two = small_all[1:2].astype(F32)
    heads_rows = small_all[2 : experts + 3]
    mark_rows = jnp.concatenate([marks_all[k] for k in range(nf)], axis=1)
    mark_cols = mark_rows.T
    routes_rows = mark_rows[5 : 5 + choose]


    halfway = HEAD_DIM // 2
    freqs = ROPE_BASE ** (-(jnp.arange(halfway, dtype=F32) * 2.0 / HEAD_DIM))
    turns = mark_cols[:, 4:5].astype(F32) * jnp.concatenate([freqs, freqs])[None, :]
    cosine = jnp.cos(turns)
    sine = jnp.sin(turns) * jnp.where(jnp.arange(HEAD_DIM) < halfway, -1.0, 1.0)[None, :]
    bias = jnp.concatenate([b_query, b_key, b_value]).astype(F32)[None]
    operands = (tokens_all, gain_one, w_cols, bias, w_output, cosine, sine, mark_cols, mark_rows)
    if wires.fast:
        normed, three, attended, branch, cot_all = attend_call(*operands, cotangent, 6)
        cot_all = cot_all.reshape(count, features)
    else:
        normed, three, attended, branch = attend_call(*operands)
        cot_all = wires.gather(cotangent)

    numbers = me * local_experts + jnp.arange(local_experts, dtype=jnp.int32)
    named = jnp.any(routes_rows[None] == numbers[:, None, None], axis=1)
    named = named.reshape(local_experts, nf, rows_dev)
    earlier = (jnp.arange(rows_dev)[None, :] < jnp.arange(rows_dev)[:, None]).astype(BF16)
    slot = jnp.einsum("ts,ebs->bet", earlier, named.astype(BF16), preferred_element_type=F32)
    slot = jnp.where(named.transpose(1, 0, 2), slot.astype(jnp.int32), -1)
    pick = jnp.arange(capacity, dtype=jnp.int32)[None, None, :, None] == slot[:, :, None, :]

    cot_other = wires.inwards(cot_all)
    mixed, moe_blocks = wires.middle(
        first_middle,
        branch,
        (tokens, gain_two),
        (jax.ShapeDtypeStruct((rows_dev, features), F32),),
        True,
        2,
    )
    moe_in = moe_blocks.reshape(count, features)
    moe_other = wires.inwards(moe_in)

    rows_in, rows_cot, gate, pick_b, router_probs, opener = dispatch_call(
        moe_in, cot_all, slot, heads_rows, capacity
    )
    if wires.fast:
        rows_cot, cot_other = lax.optimization_barrier((rows_cot, cot_other))
    hidden, d_gate, d_up, d_out, y_rows, dx_rows, sens_rows = expert_call(
        rows_in, rows_cot, gate, expert_gate, routed_up_weight, expert_down, nf // 2
    )

    gate_parts = [outer_call(rows_in, i, d_gate) for i in range(local_experts)]
    up_part = outer_call(rows_in, 0, d_up)
    gate_parts, up_part, hidden, sens_rows, y_rows, moe_other = lax.optimization_barrier(
        (gate_parts, up_part, hidden, sens_rows, y_rows, moe_other)
    )
    gate_sums = [wires.reduce_background(v) for v in gate_parts]
    up_sums = [wires.reduce_background(up_part)]

    gate_grad = jnp.sum(jnp.where(pick, sens_rows, 0.0), axis=2)
    gate_grad = gate_grad.transpose(1, 0, 2).reshape(local_experts, count)
    prob_grad = sum(
        jnp.where(jnp.arange(experts)[None] == numbers[i], gate_grad[i][:, None], 0.0)
        for i in range(local_experts)
    )
    logit_grad = router_probs * (
        prob_grad - jnp.sum(prob_grad * router_probs, axis=-1, keepdims=True)
    )
    high = logit_grad.astype(BF16)
    lanes = jnp.concatenate([high, (logit_grad - high.astype(F32)).astype(BF16)], axis=1)
    router_rows = heads_rows[:experts]
    taken = (nf, local_experts * capacity, features)
    s_hidden, sd_gate, sd_up, sd_out, out_part, moe_part, gate_sens = shared_call(
        moe_in,
        cot_all,
        opener,
        pick_b,
        y_rows.reshape(taken),
        dx_rows.reshape(taken),
        lanes,
        jnp.concatenate([router_rows, router_rows], axis=0),
        heads_rows[experts:].astype(F32),
        shared_gate,
        shared_up,
        shared_down,
    )
    sens_high = gate_sens.astype(BF16)
    sens_low = (gate_sens - sens_high.astype(F32)).astype(BF16)
    grad_heads = rows_dot(jnp.concatenate([lanes, sens_high, sens_low], axis=1), moe_in)
    grad_heads = jnp.concatenate(
        [
            grad_heads[:experts] + grad_heads[experts : 2 * experts],
            grad_heads[2 * experts : 2 * experts + 1] + grad_heads[2 * experts + 1 :],
        ],
        axis=0,
    )
    arrays = (rows_in, d_up, hidden, moe_in, sd_gate, sd_up, sd_out)
    if wires.fast:
        o_hidden, od_gate, od_up, od_out = other_call(
            moe_other, cot_other, heads_rows, shared_gate, shared_up, shared_down, rows_dev
        )
        arrays += (moe_other, od_gate, od_up, s_hidden, od_out, o_hidden, d_out)
        later = {(13, 1, 1): (0, 1, 1), (2, 0, 1): (1, 0, 1)}
    else:
        arrays += (None, None, None, s_hidden, None, None, d_out)
        later = {}
    jobs = []
    for i in range(1, local_experts):
        jobs += [(((0, 1, i), (1, 0, i)),)]
    jobs += [(((13, 1, i), (2, 0, i)),) for i in range(local_experts)]

    def whole(*numbers):
        return tuple((n, None, 0) for n in numbers)

    if wires.fast:
        jobs += [(whole(3, 4), whole(7, 8)), (whole(3, 5), whole(7, 9)), (whole(6, 10), whole(11, 12))]
    else:
        jobs += [(whole(3, 4),), (whole(3, 5),), (whole(6, 10),)]
    grad_mixed, grad_gain_two, branch_grad, *parts = wires.middle(
        back_middle,
        moe_part,
        (mixed, gain_two, cotangent),
        (
            jax.ShapeDtypeStruct((rows_dev, features), F32),
            jax.ShapeDtypeStruct((wires.chunks, features), F32),
        ),
        True,
        3,
        arrays,
        jobs,
        later,
    )
    late = local_experts - 1
    parts, up_sums = lax.optimization_barrier((parts, up_sums))
    up_sums += [wires.reduce_background(v) for v in parts[:late]]
    down_parts, shared_parts = parts[late : late + local_experts], parts[late + local_experts :]
    branch_grad = branch_grad.reshape(count, features)
    grad_three, normed_part, grad_bias = attend_back_call(
        branch_grad, w_output, three, w_cols, cosine, sine, mark_cols, mark_rows
    )
    part_output = rows_dot(branch_grad, attended).astype(BF16)
    part_three = rows_dot(grad_three, normed).astype(BF16)

    vec = jnp.concatenate(
        [
            jnp.zeros_like(gain_one),
            jnp.sum(grad_gain_two, axis=0, keepdims=True),
            grad_heads,
        ],
        axis=0,
    )
    vec = jnp.pad(vec, ((0, 16 - vec.shape[0]), (0, 0)))
    bias_add = jnp.pad(grad_bias.reshape(3, width), ((experts + 3, 16 - experts - 6), (0, 0)))
    down_sums, shared_sums, four, output, grad_tokens, vec = wires.last_sums(
        down_parts,
        shared_parts,
        part_three,
        part_output,
        out_part,
        mixed,
        normed_part,
        tokens,
        grad_mixed,
        vec,
        gain_one,
        bias_add,
        5,
    )
    own = width // ng
    vec = lax.dynamic_slice_in_dim(vec, lax.axis_index("grp") * own, own, 1)
    return (
        output,
        grad_tokens,
        vec[0],
        four[0],
        four[1],
        four[2],
        vec[experts + 3],
        vec[experts + 4],
        vec[experts + 5],
        four[3],
        vec[1],
        vec[2 : experts + 2].T,
        vec[experts + 2],
        shared_sums[0],
        shared_sums[1],
        shared_sums[2],
        jnp.stack(gate_sums, axis=0).astype(F32),
        jnp.stack(up_sums, axis=0).astype(F32),
        down_sums,
    )


def solution(mesh):
    wires = Wires(mesh)

    def step(*args):
        return on_device(wires, *args)

    rows = P(("grp", "fsdp"))
    shard = P("fsdp")
    small = P(("fsdp", "grp"))
    return jax.shard_map(
        step,
        mesh=mesh,
        in_specs=(rows,) * 6
        + (shard,) * 11
        + (P(None, "fsdp"), P(None, "fsdp"), shard, shard, shard, shard),
        out_specs=(
            rows,
            rows,
            small,
            P("fsdp", "grp"),
            P("fsdp", "grp"),
            P("fsdp", "grp"),
            small,
            small,
            small,
            P("fsdp", "grp"),
            small,
            small,
            small,
            P("grp", "fsdp"),
            P("grp", "fsdp"),
            P("fsdp", "grp"),
            P("fsdp", "grp", None),
            P("fsdp", "grp", None),
            P("fsdp", None, "grp"),
        ),
        check_vma=False,
    )
```

```python
import functools

import jax
import jax.numpy as jnp
from jax import lax
from jax.experimental import pallas as pl
from jax.experimental.pallas import tpu as pltpu
from jax.sharding import PartitionSpec as P

HEADS = 16
HEAD_DIM = 128
EPSILON = 1e-06
ROPE_BASE = 1000000.0
MASK_FILL = -1e30

F32 = jnp.float32
BF16 = jnp.bfloat16
MESH = pl.DeviceIdType.MESH
ANY = pl.BlockSpec(memory_space=pl.ANY)
VMEM = pl.BlockSpec(memory_space=pltpu.VMEM)
MIB = 2**20


def dot(left, right, dims, out=F32):
    return lax.dot_general(left, right, (dims, ((), ())), preferred_element_type=out)


def plain_dot(left, right):
    return dot(left, right, ((1,), (0,)))


def trans_dot(left, right):
    return dot(left, right, ((1,), (1,)))


def rows_dot(left, right):
    return dot(left, right, ((0,), (0,)))


def pieces(total, size):
    return [(a, min(size, total - a)) for a in range(0, total, size)]


def hidden_part(x, g, gate, w_gate, w_up, w_down, hidden, d_gate, d_up):
    units = w_gate.shape[1]
    sens = None
    for a, n in pieces(units, 256):
        s = pl.ds(a, n)
        pre = plain_dot(x, w_gate[:, s])
        up = plain_dot(x, w_up[:, s])
        plain = trans_dot(g, w_down[s, :])
        sigma = 1.0 / (1.0 + jnp.exp(-pre))
        act = pre * sigma
        slope = sigma * (1.0 + pre * (1.0 - sigma))
        h = (act * up).astype(BF16)
        hidden[:, s] = h
        grad = gate * plain
        d_gate[:, s] = (grad * up * slope).astype(BF16)
        d_up[:, s] = (grad * act).astype(BF16)
        part = jnp.sum(plain * h.astype(F32), axis=-1, keepdims=True)
        sens = part if sens is None else sens + part
    return sens


def expert_kernel(x_ref, g_ref, gate_ref, wg, wu, wd, hidden, d_gate, d_up, d_out, y_ref, dx_ref, sens_ref):
    blocks, _, slots, features = x_ref.shape
    rows = blocks * slots
    x = x_ref[...].reshape(rows, features)
    g = g_ref[...].reshape(rows, features)
    gate = gate_ref[...].reshape(rows, 1)
    wg, wu, wd = wg.at[0], wu.at[0], wd.at[0]
    hid, dg, du = hidden.at[0], d_gate.at[0], d_up.at[0]
    d_out[...] = (gate * g.astype(F32)).astype(BF16).reshape(d_out.shape)
    sens = hidden_part(x, g, gate, wg, wu, wd, hid, dg, du)
    sens_ref[...] = sens.reshape(sens_ref.shape)
    for a, n in pieces(features, 512):
        s = pl.ds(a, n)
        y = plain_dot(hid[...], wd[:, s]).astype(BF16)
        y_ref[:, :, :, s] = (gate * y.astype(F32)).astype(BF16).reshape(blocks, 1, slots, n)
        dx = trans_dot(dg[...], wg[s, :]) + trans_dot(du[...], wu[s, :])
        dx_ref[:, :, :, s] = dx.astype(BF16).reshape(blocks, 1, slots, n)


def expert_call(rows_in, rows_cot, gate, w_gate, w_up, w_down, tile):
    blocks, experts, slots, features = rows_in.shape
    units = w_gate.shape[2]
    steps = blocks // tile
    rows = tile * slots

    def slot_spec(cols):
        return pl.BlockSpec((tile, 1, slots, cols), lambda i, t: (t, i, 0, 0))

    def unit_spec():
        return pl.BlockSpec((1, rows, units), lambda i, t: (i, t, 0))

    def weight_spec(a, b):
        return pl.BlockSpec((1, a, b), lambda i, t: (i, 0, 0))

    units_shape = jax.ShapeDtypeStruct((experts, blocks * slots, units), BF16)
    slots_shape = jax.ShapeDtypeStruct((blocks, experts, slots, features), BF16)
    return pl.pallas_call(
        expert_kernel,
        grid=(experts, steps),
        in_specs=[
            slot_spec(features),
            slot_spec(features),
            slot_spec(1),
            weight_spec(features, units),
            weight_spec(features, units),
            weight_spec(units, features),
        ],
        out_specs=[unit_spec()] * 3 + [slot_spec(features)] * 3 + [slot_spec(1)],
        out_shape=[units_shape] * 3
        + [slots_shape] * 3
        + [jax.ShapeDtypeStruct((blocks, experts, slots, 1), F32)],
        compiler_params=pltpu.CompilerParams(vmem_limit_bytes=62 * MIB),
    )(rows_in, rows_cot, gate, w_gate, w_up, w_down)


def own_kernel(
    x_ref, g_ref, head_ref, pick_ref, y_in, dx_in, lane_ref, heads_w, switch_row, wg, wu, wd,
    hidden, d_gate, d_up, d_out, y_ref, dx_ref, sens_ref,
):
    features = x_ref.shape[1]
    x = x_ref[...]
    g = g_ref[...]
    opener = head_ref[...]
    d_out[...] = (opener * g.astype(F32)).astype(BF16)
    sens = hidden_part(x, d_out[...], 1.0, wg, wu, wd, hidden, d_gate, d_up)
    sens = (1.0 - opener) * sens
    sens_ref[...] = sens
    pick = pick_ref[0]
    lanes = lane_ref[...]
    for a, n in pieces(features, 512):
        s = pl.ds(a, n)
        y = opener * plain_dot(hidden[...], wd[:, s]) + rows_dot(pick, y_in[0, :, s])
        y_ref[:, s] = y.astype(BF16)
        dx = trans_dot(d_gate[...], wg[s, :]) + trans_dot(d_up[...], wu[s, :])
        dx = dx + rows_dot(pick, dx_in[0, :, s])
        dx = dx + plain_dot(lanes, heads_w[:, s]) + sens * switch_row[:, s]
        dx_ref[:, s] = dx.astype(BF16)


def other_kernel(x_ref, g_ref, heads, wg, wu, wd, hidden, d_gate, d_up, d_out):
    x = x_ref[...]
    pre = trans_dot(x, heads[...])
    opener = 1.0 / (1.0 + jnp.exp(-pre[:, heads.shape[0] - 1 :]))
    d_out[...] = (opener * g_ref[...].astype(F32)).astype(BF16)
    hidden_part(x, d_out[...], 1.0, wg, wu, wd, hidden, d_gate, d_up)


def shared_kernel(blocks, others, *refs):
    if not others:
        own_kernel(*refs)
        return
    ins, outs = refs[:15], refs[15:]
    weights = ins[9:12]
    step = pl.program_id(0)

    @pl.when(step < blocks)
    def _():
        own_kernel(*ins[:12], *outs[:7])

    @pl.when(step >= blocks)
    def _():
        other_kernel(*ins[12:15], *weights, *outs[7:])


def shared_call(x, g, opener, pick, y_in, dx_in, lanes, heads_w, switch_row, w_gate, w_up, w_down, others=None):
    count, features = x.shape
    units = w_gate.shape[1]
    blocks, taken, tile = pick.shape
    width = lanes.shape[1]

    def own(b):
        return jnp.minimum(b, blocks - 1)

    def other(b):
        return jnp.maximum(b - blocks, 0)

    def rows_spec(cols, place=own):
        return pl.BlockSpec((tile, cols), lambda b: (place(b), 0))

    def block_spec(cols):
        return pl.BlockSpec((1, taken, cols), lambda b: (own(b), 0, 0))

    def whole(a, b):
        return pl.BlockSpec((a, b), lambda b_: (0, 0), pipeline_mode=pl.Buffered(1))

    def shape(cols, dtype=BF16):
        return jax.ShapeDtypeStruct((count, cols), dtype)

    ins = [x, g, opener, pick, y_in, dx_in, lanes, heads_w, switch_row, w_gate, w_up, w_down]
    in_specs = [
        rows_spec(features),
        rows_spec(features),
        rows_spec(1),
        block_spec(tile),
        block_spec(features),
        block_spec(features),
        rows_spec(width),
        whole(width, features),
        whole(1, features),
        whole(features, units),
        whole(features, units),
        whole(units, features),
    ]
    out_specs = [rows_spec(units)] * 3 + [rows_spec(features)] * 3 + [rows_spec(1)]
    out_shape = [shape(units)] * 3 + [shape(features)] * 3 + [shape(1, F32)]
    if others:
        ins += others
        in_specs += [rows_spec(features, other)] * 2 + [whole(others[2].shape[0], features)]
        out_specs += [rows_spec(units, other)] * 3 + [rows_spec(features, other)]
        out_shape += [shape(units)] * 3 + [shape(features)]
    return pl.pallas_call(
        functools.partial(shared_kernel, blocks, bool(others)),
        grid=(2 * blocks if others else blocks,),
        in_specs=in_specs,
        out_specs=out_specs,
        out_shape=out_shape,
        compiler_params=pltpu.CompilerParams(vmem_limit_bytes=62 * MIB),
    )(*ins)


def dispatch_kernel(x_ref, g_ref, slot_ref, heads, rows_in, rows_cot, gate_ref, pick_ref, probs_ref, opener_ref):
    x, g = x_ref[...], g_ref[...]
    local, slots = rows_in.shape[1], rows_in.shape[2]
    count = heads.shape[0] - 1
    pre = trans_dot(x, heads[...])
    opener_ref[...] = 1.0 / (1.0 + jnp.exp(-pre[:, count:]))
    pre = pre[:, :count]
    expo = jnp.exp(pre - jnp.max(pre, axis=-1, keepdims=True))
    probs = expo / jnp.sum(expo, axis=-1, keepdims=True)
    probs_ref[...] = probs
    parts, rest = [], probs
    for _ in range(3):
        parts.append(rest.astype(BF16))
        rest = rest - parts[-1].astype(F32)
    numbers = lax.broadcasted_iota(jnp.int32, (slots, count), 1)
    places = lax.broadcasted_iota(jnp.int32, (slots, x.shape[0]), 0)
    for i in range(local):
        pick = jnp.where(places == slot_ref[0, i : i + 1, :], 1.0, 0.0).astype(BF16)
        pick_ref[0, i * slots : (i + 1) * slots, :] = pick
        rows_in[0, i] = plain_dot(pick, x).astype(BF16)
        rows_cot[0, i] = plain_dot(pick, g).astype(BF16)
        found = plain_dot(pick, parts[0]) + (plain_dot(pick, parts[1]) + plain_dot(pick, parts[2]))
        number = lax.axis_index("fsdp") * local + i
        gate_ref[0, i] = jnp.sum(jnp.where(numbers == number, found, 0.0), axis=-1, keepdims=True)


def dispatch_call(x, g, slot, heads, slots):
    count, features = x.shape
    blocks, local, rows = slot.shape
    experts = heads.shape[0] - 1

    def rows_spec(cols):
        return pl.BlockSpec((rows, cols), lambda b: (b, 0))

    def slots_spec(cols):
        return pl.BlockSpec((1, local, slots, cols), lambda b: (b, 0, 0, 0))

    def slots_shape(cols, dtype=BF16):
        return jax.ShapeDtypeStruct((blocks, local, slots, cols), dtype)

    return pl.pallas_call(
        dispatch_kernel,
        grid=(blocks,),
        in_specs=[
            rows_spec(features),
            rows_spec(features),
            pl.BlockSpec((1, local, rows), lambda b: (b, 0, 0)),
            pl.BlockSpec(heads.shape, lambda b: (0, 0)),
        ],
        out_specs=[
            slots_spec(features),
            slots_spec(features),
            slots_spec(1),
            pl.BlockSpec((1, local * slots, rows), lambda b: (b, 0, 0)),
            rows_spec(experts),
            rows_spec(1),
        ],
        out_shape=[
            slots_shape(features),
            slots_shape(features),
            slots_shape(1, F32),
            jax.ShapeDtypeStruct((blocks, local * slots, rows), BF16),
            jax.ShapeDtypeStruct((count, experts), F32),
            jax.ShapeDtypeStruct((count, 1), F32),
        ],
        compiler_params=pltpu.CompilerParams(vmem_limit_bytes=60 * MIB),
    )(x, g, slot, heads)


def outer_kernel(a_ref, b_ref, out_ref):
    out_ref[...] = rows_dot(a_ref[...].reshape(-1, a_ref.shape[-1]), b_ref[0]).astype(BF16)


def outer_call(rows, i, units):
    blocks, _, slots, features = rows.shape
    _, depth, n = units.shape
    tile = 512
    return pl.pallas_call(
        outer_kernel,
        grid=(features // tile,),
        in_specs=[
            pl.BlockSpec((blocks, 1, slots, tile), lambda j: (0, i, 0, j)),
            pl.BlockSpec((1, depth, n), lambda j: (i, 0, 0)),
        ],
        out_specs=pl.BlockSpec((tile, n), lambda j: (j, 0)),
        out_shape=jax.ShapeDtypeStruct((features, n), BF16),
        compiler_params=pltpu.CompilerParams(vmem_limit_bytes=62 * MIB),
    )(rows, units)


class Line:
    def __init__(self, parts, inner, sources, outs, sib, recv, bufs, sems):
        self.parts, self.inner, self.sources, self.outs = parts, inner, sources, outs
        self.sib, self.recv = sib, recv
        self.own_v, self.sib_v, self.send_v, self.out_v, self.turned_v = bufs
        self.own_sem, self.sib_sem, self.out_sem, self.sib_send, self.sib_recv, self.sent, self.got = sems
        self.chunks = len(sources) * parts
        self.slots = self.send_v.shape[0]
        self.rows = sources[0].shape[2] // parts
        g = lax.axis_index("grp")
        self.z, self.core = g // 2, lax.rem(g, 2)
        self.is_end = (self.z == 0) | (self.z == 3)
        self.is_mid = (self.z == 1) | (self.z == 2)

    def at(self, z, core):
        return {"grp": 2 * z + core}

    def span(self, q):
        return lax.div(q, self.parts), pl.ds(
            pl.multiple_of(lax.rem(q, self.parts) * self.rows, self.rows), self.rows
        )

    def swap(self, j, m, r, q):
        return pltpu.make_async_remote_copy(
            src_ref=self.sources[j].at[:, 1 - self.core, r],
            dst_ref=self.sib.at[m, :, r],
            send_sem=self.sib_send.at[q],
            recv_sem=self.sib_recv.at[q],
            device_id=self.at(self.z, 1 - self.core),
            device_id_type=MESH,
        )

    def swap_any(self, q):
        m, r = self.span(q)
        return self.swap(0, m, r, q)

    def when_summing(self, condition=None):
        if self.inner:
            condition = self.is_mid if condition is None else self.is_mid & condition
        return (lambda body: body()) if condition is None else pl.when(condition)

    def start_swaps(self):
        @self.when_summing()
        def _():
            for m in range(len(self.sources)):
                for h in range(self.parts):
                    self.swap(m, m, pl.ds(h * self.rows, self.rows), m * self.parts + h).start()

    def out_copy(self, j, r):
        ref, turned = self.outs[j]
        if turned:
            return pltpu.make_async_copy(self.turned_v, ref.at[:, r], self.out_sem)
        return pltpu.make_async_copy(self.out_v, ref.at[r], self.out_sem)

    def each_out(self, q, body):
        m, r = self.span(q)
        for j in range(len(self.sources)):

            @pl.when(m == j)
            def _():
                body(j, r)

    def hop(self, q, slot, target, place):
        m, r = self.span(q)
        return pltpu.make_async_remote_copy(
            src_ref=self.send_v.at[slot],
            dst_ref=self.recv.at[m, place, r],
            send_sem=self.sent.at[slot],
            recv_sem=self.got.at[q, place],
            device_id=self.at(target, self.core),
            device_id_type=MESH,
        )

    def arrived(self, q, place):
        self.hop(q, 0, self.z, place).wait_recv()

    def own_load(self, j, p, r, k):
        return pltpu.make_async_copy(self.sources[j].at[p, self.core, r], self.own_v.at[k], self.own_sem.at[k])

    def sib_load(self, m, p, r, k):
        return pltpu.make_async_copy(self.sib.at[m, p, r], self.sib_v.at[k], self.sib_sem.at[k])

    def start_base(self, q, p, k):
        m, r = self.span(q)
        for j in range(len(self.sources)):

            @pl.when(m == j)
            def _():
                self.own_load(j, p, r, k).start()

        self.sib_load(m, p, r, k).start()

    def base(self, k):
        r = pl.ds(0, self.rows)
        self.own_load(0, 0, r, k).wait()
        self.sib_load(0, 0, r, k).wait()
        return self.own_v[k].astype(F32) + self.sib_v[k].astype(F32)

    def fetch(self, q, place):
        self.arrived(q, place)
        m, r = self.span(q)
        return self.recv[m, place, r].astype(F32)

    def send(self, t, k, q, p, target, place, more, first):
        depth = self.slots // 3
        slot = lax.rem(t, depth) * 3 + k

        @pl.when(t >= depth + first)
        def _():
            self.hop(q, slot, target, place).wait_send()

        if more:
            extra = self.fetch(q, p)
            total = self.base(k) + extra
        else:
            total = self.base(k)
        self.send_v[slot] = total.astype(BF16)
        self.hop(q, slot, target, place).start()

    def turn(self, t):
        z, chunks = self.z, self.chunks
        to_end = self.is_end & (t >= 0) & (t < chunks)
        to_next = self.is_mid & (t >= 1) & (t < chunks + 1)
        to_last = self.is_mid & (t >= 2) & (t < chunks + 2)
        last = (t >= 3) & (t < chunks + 3)

        @self.when_summing((t >= 0) & (t < chunks))
        def _():
            self.swap_any(t).wait_recv()

        def end_piece(j):
            return jnp.where(z == 0, 3 - j, j)

        def next_piece(j):
            return jnp.where(z == 1, 3 - j, j)

        last_piece = jnp.where(z == 2, 3, 0)
        if not self.inner:

            @pl.when(to_end)
            def _():
                for j in range(3):
                    self.start_base(t, end_piece(j), j)

        @pl.when(to_next)
        def _():
            for j in range(2):
                self.start_base(t - 1, next_piece(j), j)

        @pl.when(to_last)
        def _():
            self.start_base(t - 2, last_piece, 2)

        @self.when_summing(last)
        def _():
            self.start_base(t - 3, z, 3)

        if not self.inner:

            @pl.when(to_end)
            def _():
                for j in range(3):
                    p = end_piece(j)
                    target = jnp.where(z == 0, 1, 2)
                    place = jnp.where((z == 3) & (p == 2), 4, p)
                    self.send(t, j, t, p, target, place, False, 0)

        @pl.when(to_next)
        def _():
            for j in range(2):
                p = next_piece(j)
                target = jnp.where(z == 1, 2, 1)
                place = jnp.where((z == 2) & (p == 1), 4, p)
                self.send(t, j, t - 1, p, target, place, not self.inner, 1)

        @pl.when(to_last)
        def _():
            place = jnp.where(z == 1, 4, last_piece)
            self.send(t, 2, t - 2, last_piece, last_piece, place, True, 2)

        @pl.when(last)
        def _():
            q = t - 3

            @pl.when(q >= 1)
            def _():
                self.each_out(q - 1, lambda j, r: self.out_copy(j, r).wait())

            if self.inner:

                @pl.when(z == 0)
                def _():
                    self.out_v[...] = self.fetch(q, 4)

                @pl.when(z == 3)
                def _():
                    self.out_v[...] = self.fetch(q, 3)

                @pl.when(z == 1)
                def _():
                    got = self.fetch(q, 4)
                    self.out_v[...] = self.base(3) + got

                @pl.when(z == 2)
                def _():
                    got = self.fetch(q, 2)
                    self.out_v[...] = self.base(3) + got

            else:
                self.out_v[...] = self.base(3)

                @pl.when(z > 0)
                def _():
                    self.out_v[...] = self.out_v[...] + self.fetch(q, z)

                @pl.when(z < 3)
                def _():
                    self.out_v[...] = self.out_v[...] + self.fetch(q, 4)

            def put(j, r):
                if self.outs[j][1]:
                    self.turned_v[...] = self.out_v[...].T
                self.out_copy(j, r).start()

            self.each_out(q, put)

    def finish(self):
        self.each_out(self.chunks - 1, lambda j, r: self.out_copy(j, r).wait())

        def body(q, carry):
            self.swap_any(q).wait_send()
            return carry

        @self.when_summing()
        def _():
            lax.fori_loop(0, self.chunks, body, 0)

        assert self.chunks >= self.slots // 3

        @self.when_summing()
        def _():
            for slot in range(self.slots):
                self.hop(0, slot, self.z, 0).wait_send()


def line_bufs(shape, slots, turned):
    return [pltpu.VMEM((4,) + shape, BF16)] * 2 + [
        pltpu.VMEM((slots,) + shape, BF16),
        pltpu.VMEM(shape, F32),
        pltpu.VMEM(shape[::-1] if turned else (8, 128), F32),
    ]


def line_sems(q, slots):
    return [
        pltpu.SemaphoreType.DMA((4,)),
        pltpu.SemaphoreType.DMA((4,)),
        pltpu.SemaphoreType.DMA,
        pltpu.SemaphoreType.DMA((q,)),
        pltpu.SemaphoreType.DMA((q,)),
        pltpu.SemaphoreType.DMA((slots,)),
        pltpu.SemaphoreType.DMA((q, 5)),
    ]


def line_kernel(n_down, n_shared, parts, shift, *refs):
    def take(n):
        nonlocal refs
        taken, refs = refs[:n], refs[n:]
        return taken

    downs, shared = take(n_down), take(n_shared)
    three, part_out, out_part, mixed, normed_part, tokens, base, vec, gain, bias_add = take(10)
    out_down, out_gate, out_up, out_sdown = take(4)
    out_four = take(4)
    output, grad_tokens, vec_out = take(3)
    sib_a, att, sib_b, sib_c, out_in = take(5)
    bufs_a, bufs_b, bufs_c = take(5), take(5), take(5)
    recv_a, recv_b, recv_c = take(3)
    vec_in, vec_own, vec_sib, vec_line, vec_send, parts_v, mixed_v, sum_v = take(8)
    relay_x, relay_y, got_x, got_y, sum_x, sum_y, gain_v, grad_v, vec_v = take(9)
    sems_a, sems_b, sems_c = take(7), take(7), take(7)
    plane_send, plane_recv, local_sems, vec_send_sems, vec_recv_sems, out_send, out_recv, norm_send, norm_recv = take(9)

    a = Line(parts, False, downs, [(out_down.at[j], True) for j in range(n_down)], sib_a, recv_a, bufs_a, sems_a)
    b = Line(1, False, [att.at[j] for j in range(4)], [(v, True) for v in out_four], sib_b, recv_b, bufs_b, sems_b)
    c = Line(parts, shift, shared, [(out_gate, False), (out_up, False), (out_sdown, True)], sib_c, recv_c, bufs_c, sems_c)
    z, core = a.z, a.core
    f = lax.axis_index("fsdp")
    fx = f + 1 - 2 * lax.rem(f, 2)
    fy = f + 2 - 4 * (f // 2)
    fd = fx + 2 - 4 * (fx // 2)
    peers = (fx, fy, fd)
    sibling = a.at(z, 1 - core)
    width = three.shape[3] // 4

    barrier = pltpu.get_barrier_semaphore()
    for other in (sibling,) + tuple({"fsdp": p} for p in peers):
        pl.semaphore_signal(barrier, inc=1, device_id=other, device_id_type=MESH)

    @pl.when(z > 0)
    def _():
        pl.semaphore_signal(barrier, inc=1, device_id=a.at(z - 1, core), device_id_type=MESH)

    @pl.when(z < 3)
    def _():
        pl.semaphore_signal(barrier, inc=1, device_id=a.at(z + 1, core), device_id_type=MESH)

    @pl.when(a.is_end)
    def _():
        pl.semaphore_wait(barrier, 5)

    @pl.when(a.is_mid)
    def _():
        pl.semaphore_wait(barrier, 6)

    a.start_swaps()
    c.start_swaps()

    def cols(p):
        return pl.ds(pl.multiple_of(p * width, width), width)

    def to_owner(k, p):
        return pltpu.make_async_remote_copy(
            src_ref=three.at[:, :, :, cols(p)], dst_ref=att.at[pl.ds(0, 3), f],
            send_sem=plane_send.at[k], recv_sem=plane_recv.at[k],
            device_id={"fsdp": p}, device_id_type=MESH,
        )

    def vec_owner(k, p):
        return pltpu.make_async_remote_copy(
            src_ref=vec_v.at[p], dst_ref=vec_in.at[k],
            send_sem=vec_send_sems.at[k], recv_sem=vec_recv_sems.at[k],
            device_id={"fsdp": p}, device_id_type=MESH,
        )

    def out_owner(k, p):
        return pltpu.make_async_remote_copy(
            src_ref=out_part.at[k + 1], dst_ref=out_in.at[k],
            send_sem=out_send.at[k], recv_sem=out_recv.at[k],
            device_id={"fsdp": p}, device_id_type=MESH,
        )

    for k, p in enumerate(peers):
        to_owner(k, p).start()

    rows_half = mixed.shape[0] // 2
    low, high = pl.ds(0, rows_half), pl.ds(rows_half, rows_half)

    def norm_copy(n, src, dst, target):
        return pltpu.make_async_remote_copy(
            src_ref=src, dst_ref=dst, send_sem=norm_send.at[n], recv_sem=norm_recv.at[n],
            device_id={"fsdp": target}, device_id_type=MESH,
        )

    norm_copies = [
        norm_copy(0, normed_part.at[3, low], relay_x, fx),
        norm_copy(1, normed_part.at[3, high], relay_y, fy),
        norm_copy(2, normed_part.at[1, low], got_x.at[low], fx),
        norm_copy(3, normed_part.at[2, high], got_y.at[high], fy),
        norm_copy(4, sum_y, got_y.at[low], fy),
        norm_copy(5, sum_x, got_x.at[high], fx),
    ]
    for copy in norm_copies[:4]:
        copy.start()

    def relay():
        loads = [
            pltpu.make_async_copy(normed_part.at[2, low], sum_y, local_sems.at[3]),
            pltpu.make_async_copy(normed_part.at[1, high], sum_x, local_sems.at[4]),
        ]
        for copy in loads:
            copy.start()
        for copy in loads:
            copy.wait()
        norm_copies[0].wait_recv()
        sum_y[...] = (sum_y[...].astype(F32) + relay_x[...].astype(F32)).astype(BF16)
        norm_copies[4].start()
        norm_copies[1].wait_recv()
        sum_x[...] = (sum_x[...].astype(F32) + relay_y[...].astype(F32)).astype(BF16)
        norm_copies[5].start()

    def finish_norm():
        for copy in norm_copies[2:]:
            copy.wait_recv()
        step = parts_v.shape[1]
        gain_v[...] = jnp.zeros_like(gain_v)

        def body(i, carry):
            r = pl.ds(pl.multiple_of(i * step, step), step)
            loads = [
                pltpu.make_async_copy(normed_part.at[0, r], parts_v.at[0], local_sems.at[3]),
                pltpu.make_async_copy(tokens.at[r], parts_v.at[1], local_sems.at[4]),
                pltpu.make_async_copy(base.at[r], mixed_v, local_sems.at[5]),
            ]
            for copy in loads:
                copy.start()
            for copy in loads:
                copy.wait()
            total = parts_v[0].astype(F32) + (got_x[r].astype(F32) + got_y[r].astype(F32))
            back, grad_gain = norm_back(parts_v[1].astype(F32), gain[...], total)
            gain_v[...] = gain_v[...] + grad_gain
            grad_v[...] = mixed_v[...] + back
            copy = pltpu.make_async_copy(grad_v, grad_tokens.at[r], local_sems.at[6])
            copy.start()
            copy.wait()
            return carry

        lax.fori_loop(0, mixed.shape[0] // step, body, 0)
        copy = pltpu.make_async_copy(vec, vec_v, local_sems.at[2])
        copy.start()
        copy.wait()
        for k in range(4):
            vec_v[k, 0:1, :] = gain_v[:, k * width : (k + 1) * width]
        for k, p in enumerate(peers):
            vec_owner(k, p).start()

    keep = (
        pltpu.make_async_copy(three.at[:, :, :, cols(f)], att.at[pl.ds(0, 3), f], local_sems.at[0]),
        pltpu.make_async_copy(part_out, att.at[3], local_sems.at[1]),
    )
    for copy in keep:
        copy.start()

    def vec_swap():
        return pltpu.make_async_remote_copy(
            src_ref=vec_own, dst_ref=vec_sib, send_sem=vec_send_sems.at[3], recv_sem=vec_recv_sems.at[3],
            device_id=sibling, device_id_type=MESH,
        )

    def vec_hop(k, target):
        return pltpu.make_async_remote_copy(
            src_ref=vec_send.at[k], dst_ref=vec_line.at[k], send_sem=vec_send_sems.at[4 + k],
            recv_sem=vec_recv_sems.at[4 + k], device_id=a.at(target, core), device_id_type=MESH,
        )

    def finish_output():
        for k, p in enumerate(peers):
            out_owner(k, p).wait_recv()
        step = parts_v.shape[1]

        def body(i, carry):
            r = pl.ds(pl.multiple_of(i * step, step), step)
            loads = [pltpu.make_async_copy(out_part.at[0, r], parts_v.at[0], local_sems.at[3])]
            loads += [
                pltpu.make_async_copy(out_in.at[k, r], parts_v.at[k + 1], local_sems.at[4 + k]) for k in range(3)
            ]
            loads.append(pltpu.make_async_copy(mixed.at[r], mixed_v, local_sems.at[7]))
            for copy in loads:
                copy.start()
            for copy in loads:
                copy.wait()
            total = (parts_v[0].astype(F32) + parts_v[1].astype(F32)) + (
                parts_v[2].astype(F32) + parts_v[3].astype(F32)
            )
            sum_v[...] = (mixed_v[...] + total).astype(BF16)
            copy = pltpu.make_async_copy(sum_v, output.at[r], local_sems.at[8])
            copy.start()
            copy.wait()
            return carry

        lax.fori_loop(0, mixed.shape[0] // step, body, 0)

    def side_work(t):
        @pl.when(t == 3)
        def _():
            for k, p in enumerate(peers):
                to_owner(k, p).wait_recv()
            for copy in keep:
                copy.wait()
            b.start_swaps()

        @pl.when(t == 4)
        def _():
            relay()
            for k, p in enumerate(peers):
                out_owner(k, p).start()

        @pl.when(t == 5)
        def _():
            finish_norm()

        @pl.when(t == 6)
        def _():
            for k, p in enumerate(peers):
                vec_owner(k, p).wait_recv()
            vec_own[...] = (vec_v[f] + vec_in[0]) + (vec_in[1] + vec_in[2]) + bias_add[...]
            vec_swap().start()

        @pl.when(t == 7)
        def _():
            vec_swap().wait_recv()
            vec_sib[...] = vec_sib[...] + vec_own[...]

            @pl.when(z == 0)
            def _():
                vec_send[0] = vec_sib[...]
                vec_hop(0, 1).start()

            @pl.when(z == 3)
            def _():
                vec_send[1] = vec_sib[...]
                vec_hop(1, 2).start()

        @pl.when((t == 8) & (z == 1))
        def _():
            vec_hop(0, 1).wait_recv()
            vec_send[0] = vec_sib[...] + vec_line[0]
            vec_hop(0, 2).start()

        @pl.when((t == 8) & (z == 2))
        def _():
            vec_hop(1, 2).wait_recv()
            vec_send[1] = vec_sib[...] + vec_line[1]
            vec_hop(1, 1).start()

        @pl.when(t == 8)
        def _():
            finish_output()

        @pl.when((t == 9) & (z == 2))
        def _():
            vec_hop(0, 2).wait_recv()
            vec_send[0] = vec_sib[...] + vec_line[0]
            vec_hop(0, 3).start()
            vec_out[...] = vec_send[0] + vec_line[1]

        @pl.when((t == 9) & (z == 1))
        def _():
            vec_hop(1, 1).wait_recv()
            vec_send[1] = vec_sib[...] + vec_line[1]
            vec_hop(1, 0).start()
            vec_out[...] = vec_send[1] + vec_line[0]

        @pl.when((t == 10) & (z == 3))
        def _():
            vec_hop(0, 3).wait_recv()
            vec_out[...] = vec_sib[...] + vec_line[0]

        @pl.when((t == 10) & (z == 0))
        def _():
            vec_hop(1, 0).wait_recv()
            vec_out[...] = vec_sib[...] + vec_line[1]

    def loop(t, carry):
        a.turn(t)
        b.turn(t - a.chunks)
        c.turn(t)
        side_work(t)
        return carry

    turns = max(a.chunks + b.chunks, c.chunks) + 3
    assert turns == 11
    lax.fori_loop(0, turns, loop, 0)
    for copy in norm_copies:
        copy.wait_send()
    a.finish()
    b.finish()
    c.finish()
    for k, p in enumerate(peers):
        vec_owner(k, p).wait_send()
        to_owner(k, p).wait_send()
        out_owner(k, p).wait_send()
    vec_swap().wait_send()

    @pl.when(z < 3)
    def _():
        vec_hop(0, 3).wait_send()

    @pl.when(z > 0)
    def _():
        vec_hop(1, 0).wait_send()


def line_call(
    downs, shared, three, part_out, out_part, mixed, normed_part, tokens, base, vec, gain, bias_add, parts, shift, collective_id
):
    _, _, rows, cols = shared[0].shape
    m, s = len(downs), len(shared)
    _, _, share, features = three.shape
    width = features // 4
    own_rows = mixed.shape[0]
    r = rows // parts
    slots = 9
    small = (16, width)
    step = own_rows // 4

    def shape(*dims, dtype=BF16):
        return jax.ShapeDtypeStruct(dims, dtype)

    outs = pl.pallas_call(
        functools.partial(line_kernel, m, s, parts, shift),
        out_shape=(
            shape(m, cols, rows, dtype=F32),
            shape(rows, cols, dtype=F32),
            shape(rows, cols, dtype=F32),
            shape(cols, rows, dtype=F32),
            shape(width, share, dtype=F32),
            shape(width, share, dtype=F32),
            shape(width, share, dtype=F32),
            shape(width, share, dtype=F32),
            shape(own_rows, features),
            shape(own_rows, features, dtype=F32),
            shape(*small, dtype=F32),
            shape(m, 4, rows, cols),
            shape(4, 4, 2, share, width),
            shape(4, 4, share, width),
            shape(s, 4, rows, cols),
            shape(3, own_rows, features),
        ),
        in_specs=[ANY] * (m + s + 8) + [VMEM] * 2,
        out_specs=(ANY,) * 10 + (VMEM,) + (ANY,) * 5,
        scratch_shapes=line_bufs((r, cols), slots, True)
        + line_bufs((share, width), slots, True)
        + line_bufs((r, cols), slots, True)
        + [
            pltpu.VMEM((m, 5, rows, cols), BF16),
            pltpu.VMEM((4, 5, share, width), BF16),
            pltpu.VMEM((s, 5, rows, cols), BF16),
            pltpu.VMEM((3,) + small, F32),
            pltpu.VMEM(small, F32),
            pltpu.VMEM(small, F32),
            pltpu.VMEM((2,) + small, F32),
            pltpu.VMEM((2,) + small, F32),
            pltpu.VMEM((4, step, features), BF16),
            pltpu.VMEM((step, features), F32),
            pltpu.VMEM((step, features), BF16),
            pltpu.VMEM((own_rows // 2, features), BF16),
            pltpu.VMEM((own_rows // 2, features), BF16),
            pltpu.VMEM((own_rows, features), BF16),
            pltpu.VMEM((own_rows, features), BF16),
            pltpu.VMEM((own_rows // 2, features), BF16),
            pltpu.VMEM((own_rows // 2, features), BF16),
            pltpu.VMEM((1, features), F32),
            pltpu.VMEM((step, features), F32),
            pltpu.VMEM((4,) + small, F32),
        ]
        + line_sems(m * parts, slots)
        + line_sems(4, slots)
        + line_sems(s * parts, slots)
        + [
            pltpu.SemaphoreType.DMA((3,)),
            pltpu.SemaphoreType.DMA((3,)),
            pltpu.SemaphoreType.DMA((9,)),
            pltpu.SemaphoreType.DMA((6,)),
            pltpu.SemaphoreType.DMA((6,)),
            pltpu.SemaphoreType.DMA((3,)),
            pltpu.SemaphoreType.DMA((3,)),
            pltpu.SemaphoreType.DMA((6,)),
            pltpu.SemaphoreType.DMA((6,)),
        ],
        compiler_params=pltpu.CompilerParams(
            collective_id=collective_id, has_side_effects=True, vmem_limit_bytes=60 * MIB
        ),
    )(*downs, *shared, three, part_out, out_part, mixed, normed_part, tokens, base, vec, gain, bias_add)
    return outs[0], outs[1:4], outs[4:8], outs[8], outs[9], outs[10]


def plane_neighbours():
    f = lax.axis_index("fsdp")
    by_x = f + 1 - 2 * lax.rem(f, 2)
    by_y = f + 2 - 4 * (f // 2)
    return {"fsdp": by_x}, {"fsdp": by_y}


def plane_barrier(by_x, by_y):
    barrier = pltpu.get_barrier_semaphore()
    for other in (by_x, by_y):
        pl.semaphore_signal(barrier, inc=1, device_id=other, device_id_type=MESH)
    pl.semaphore_wait(barrier, 2)


class Side:
    block = 512

    def __init__(self, arrays, jobs, later=()):
        self.arrays, self.jobs, self.later = list(arrays), list(jobs), dict(later)
        self.operands = sorted({o for job in self.jobs for pair in job for o in pair}, key=str)

    def shape(self, operand):
        number, axis, _ = operand
        full = self.arrays[number].shape
        return full if axis is None else full[:axis] + full[axis + 1 :]

    def out_shapes(self):
        return [
            jax.ShapeDtypeStruct((self.shape(job[0][0])[-1], self.shape(job[0][1])[-1]), BF16)
            for job in self.jobs
        ]

    def scratch(self):
        stages = sorted({self.shape(job[0][1])[-1] for job in self.jobs})
        self.stage_of = {n: k for k, n in enumerate(stages)}
        return (
            [pltpu.VMEM(self.shape(o), BF16) for o in self.operands if o not in self.later]
            + [pltpu.VMEM((2, self.block, n), BF16) for n in stages]
            + [
                pltpu.SemaphoreType.DMA((max(1, len(self.operands)),)),
                pltpu.SemaphoreType.DMA((max(1, 2 * len(stages)),)),
            ]
        )

    def bind(self, ins, outs, scratch):
        holders = [o for o in self.operands if o not in self.later]
        n = len(holders)
        self.ins, self.outs = ins, outs
        self.bufs = [scratch[holders.index(self.later.get(o, o))] for o in self.operands]
        self.stages = scratch[n:-2]
        self.load_sems, self.out_sems = scratch[-2:]
        self.loaded, self.pending, self.turn_of = set(), {}, {}
        self.units = [
            (j, k)
            for j, job in enumerate(self.jobs)
            for k in range(self.shape(job[0][0])[-1] // self.block)
        ]

    def load(self, k):
        number, axis, entry = self.operands[k]
        ref = self.ins[number]
        if axis is not None:
            ref = ref.at[(slice(None),) * axis + (entry,)]
        return pltpu.make_async_copy(ref, self.bufs[k], self.load_sems.at[k])

    def begin(self):
        for o in [o for job in self.jobs for pair in job for o in pair]:
            k = self.operands.index(o)
            if k not in self.loaded and o not in self.later:
                self.loaded.add(k)
                self.load(k).start()
        self.loaded = set()

    def step(self, number):
        for _ in range(number):
            if not self.units:
                return
            j, block = self.units.pop(0)
            pairs = [tuple(self.operands.index(o) for o in pair) for pair in self.jobs[j]]
            for k in [k for pair in pairs for k in pair]:
                if k not in self.loaded:
                    self.loaded.add(k)
                    self.load(k).wait()
            n = self.shape(self.jobs[j][0][1])[-1]
            stage = self.stage_of[n]
            slot = self.turn_of.get(stage, 0)
            self.turn_of[stage] = 1 - slot
            if (stage, slot) in self.pending:
                self.pending.pop((stage, slot)).wait()
            rows = pl.ds(block * self.block, self.block)
            total = None
            for ka, kb in pairs:
                left = self.bufs[ka][..., rows].reshape(-1, self.block)
                part = rows_dot(left, self.bufs[kb][...].reshape(-1, n))
                total = part if total is None else total + part
            self.stages[stage][slot] = total.astype(BF16)
            copy = pltpu.make_async_copy(
                self.stages[stage].at[slot], self.outs[j].at[rows], self.out_sems.at[2 * stage + slot]
            )
            copy.start()
            self.pending[(stage, slot)] = copy
            if not self.units or self.units[0][0] != j:
                for o in [o for pair in self.jobs[j] for o in pair]:
                    for k, heir in enumerate(self.operands):
                        if self.later.get(heir) == o:
                            self.load(k).start()

    def end(self):
        self.step(len(self.units))
        for copy in self.pending.values():
            copy.wait()


def mid_kernel(middle, chunks, gathers, n_in, n_out, side, *refs):
    n_side, n_jobs = len(side.arrays), len(side.jobs)
    partial, ins = refs[0], refs[1 : 1 + n_in]
    side_ins, refs = refs[1 + n_in : 1 + n_in + n_side], refs[1 + n_in + n_side :]
    outs, refs = refs[:n_out], refs[n_out:]
    gathered = None
    if gathers:
        gathered, refs = refs[0], refs[1:]
    side_outs, refs = refs[:n_jobs], refs[n_jobs:]
    relay_x, relay_y, got_x, got_y, sum_x, sum_y, own, send_sems, recv_sems, local_sems = refs[:10]
    if n_jobs:
        side.bind(side_ins, side_outs, refs[10:])
    rows = partial.shape[1]
    r = rows // chunks
    h = r // 2
    by_x, by_y = plane_neighbours()
    plane_barrier(by_x, by_y)

    def copy(i, kind, src, dst, target):
        return pltpu.make_async_remote_copy(
            src_ref=src, dst_ref=dst, send_sem=send_sems.at[i, kind], recv_sem=recv_sems.at[i, kind],
            device_id=target, device_id_type=MESH,
        )

    def sends(i):
        lo, hi = pl.ds(i * r, h), pl.ds(i * r + h, h)
        half = pl.ds(i * h, h)
        made = {
            0: lambda: copy(i, 0, partial.at[3, lo], relay_x.at[half], by_x),
            1: lambda: copy(i, 1, partial.at[3, hi], relay_y.at[half], by_y),
            2: lambda: copy(i, 2, partial.at[1, lo], got_x.at[lo], by_x),
            3: lambda: copy(i, 3, partial.at[2, hi], got_y.at[hi], by_y),
            4: lambda: copy(i, 4, sum_y.at[half], got_y.at[lo], by_y),
            5: lambda: copy(i, 5, sum_x.at[half], got_x.at[hi], by_x),
        }
        if gathers:
            made |= {
                6: lambda: copy(i, 6, own.at[lo], gathered.at[1, lo], by_x),
                7: lambda: copy(i, 7, own.at[hi], gathered.at[2, hi], by_y),
                8: lambda: copy(i, 8, own.at[hi], gathered.at[1, hi], by_x),
                9: lambda: copy(i, 9, own.at[lo], gathered.at[2, lo], by_y),
                10: lambda: copy(i, 10, gathered.at[1, lo], gathered.at[3, lo], by_y),
                11: lambda: copy(i, 11, gathered.at[2, hi], gathered.at[3, hi], by_x),
            }
        return made

    def keep(i):
        span = pl.ds(i * r, r)
        return pltpu.make_async_copy(own.at[span], gathered.at[0, span], local_sems.at[i])

    def stage(n, i):
        s = sends(i)
        lo, hi = pl.ds(i * r, h), pl.ds(i * r + h, h)
        half, span = pl.ds(i * h, h), pl.ds(i * r, r)
        if n == 0:
            for kind in (0, 1, 2, 3):
                s[kind]().start()
        elif n == 1:
            s[0]().wait_recv()
            sum_y[half] = (partial[2, lo].astype(F32) + relay_x[half].astype(F32)).astype(BF16)
            s[4]().start()
            s[1]().wait_recv()
            sum_x[half] = (partial[1, hi].astype(F32) + relay_y[half].astype(F32)).astype(BF16)
            s[5]().start()
        elif n == 2:
            for kind in (2, 3, 4, 5):
                s[kind]().wait_recv()
            total = partial[0, span].astype(F32) + (got_x[span].astype(F32) + got_y[span].astype(F32))
            given = middle(total, span, ins, outs)
            if gathers:
                own[span] = given
                for kind in (6, 7, 8, 9):
                    s[kind]().start()
                keep(i).start()
        elif n == 3 and gathers:
            s[6]().wait_recv()
            s[10]().start()
            s[7]().wait_recv()
            s[11]().start()
        elif n == 4:
            if gathers:
                for kind in (8, 9, 10, 11):
                    s[kind]().wait_recv()
                keep(i).wait()
            for kind in s:
                s[kind]().wait_send()

    turns = chunks + 4
    if n_jobs:
        side.begin()
        each = len(side.units) / (5 * chunks)
    steps = done = 0
    for t in range(turns):
        for n in range(5):
            if 0 <= t - n < chunks:
                stage(n, t - n)
                steps += 1
                if n_jobs and int(steps * each) > done:
                    side.step(int(steps * each) - done)
                    done = int(steps * each)
    if n_jobs:
        side.end()


def mid_call(middle, partial, ins, out_shapes, gathers, side, collective_id, chunks=4):
    _, rows, cols = partial.shape
    outs = tuple(out_shapes)
    specs = (VMEM,) * len(outs)
    if gathers:
        outs += (jax.ShapeDtypeStruct((4, rows, cols), BF16),)
        specs += (ANY,)
    outs += tuple(side.out_shapes())
    specs += (ANY,) * len(side.jobs)
    return pl.pallas_call(
        functools.partial(mid_kernel, middle, chunks, gathers, len(ins), len(out_shapes), side),
        out_shape=outs,
        in_specs=[VMEM] * (1 + len(ins)) + [ANY] * len(side.arrays),
        out_specs=specs,
        scratch_shapes=[
            pltpu.VMEM((rows // 2, cols), BF16),
            pltpu.VMEM((rows // 2, cols), BF16),
            pltpu.VMEM((rows, cols), BF16),
            pltpu.VMEM((rows, cols), BF16),
            pltpu.VMEM((rows // 2, cols), BF16),
            pltpu.VMEM((rows // 2, cols), BF16),
            pltpu.VMEM((rows, cols), BF16),
            pltpu.SemaphoreType.DMA((chunks, 12)),
            pltpu.SemaphoreType.DMA((chunks, 12)),
            pltpu.SemaphoreType.DMA((chunks,)),
        ]
        + (side.scratch() if side.jobs else []),
        compiler_params=pltpu.CompilerParams(
            collective_id=collective_id, has_side_effects=True, vmem_limit_bytes=60 * MIB
        ),
    )(partial, *ins, *side.arrays)


def start_kernel(
    tokens, small, marks, w_q, w_k, w_v,
    tokens_all, small_all, marks_all, w_cols, relay,
    send_sems, recv_sems, local_sems,
):
    f = lax.axis_index("fsdp")
    g = lax.axis_index("grp")
    core = lax.rem(g, 2)
    rows = tokens.shape[0]
    depth = w_q.shape[0]
    width = w_q.shape[1] // 4
    by_x, by_y = plane_neighbours()
    fx, fy = by_x["fsdp"], by_y["fsdp"]
    fd = fx + 2 - 4 * (fx // 2)
    z = g // 2
    odd = lax.rem(z, 2)
    by_d, sibling = {"fsdp": fd}, {"grp": g + 1 - 2 * core}
    by_z = {"grp": g + 2 - 4 * odd}
    barrier = pltpu.get_barrier_semaphore()
    for other in (by_x, by_y, by_d, sibling, by_z):
        pl.semaphore_signal(barrier, inc=1, device_id=other, device_id_type=MESH)
    pl.semaphore_wait(barrier, 5)

    def copy(n, src, dst, target):
        return pltpu.make_async_remote_copy(
            src_ref=src, dst_ref=dst, send_sem=send_sems.at[n], recv_sem=recv_sems.at[n],
            device_id=target, device_id_type=MESH,
        )

    def columns(j):
        return pl.ds(pl.multiple_of(j * width, width), width)

    quarter = depth // 4
    eighth = quarter // 2
    here, there = 2 * odd + core, 2 * (1 - odd) + core

    def block_rows(owner, q):
        return pl.ds(pl.multiple_of(owner * depth + q * quarter, quarter), quarter)

    mine = pl.ds(pl.multiple_of(here * quarter, quarter), quarter)
    all_sends = []

    def go(c):
        c.start()
        all_sends.append(c)
        return c

    waits = []
    n = 0
    for k, target in ((1, by_x), (2, by_y), (3, by_d)):
        waits.append(go(copy(n, small, small_all.at[k], target)))
        waits.append(go(copy(n + 1, marks, marks_all.at[k], target)))
        n += 2
    locals_ = [
        pltpu.make_async_copy(small, small_all.at[0], local_sems.at[0]),
        pltpu.make_async_copy(marks, marks_all.at[0], local_sems.at[1]),
        pltpu.make_async_copy(tokens, tokens_all.at[0], local_sems.at[2]),
    ]
    for j, w in enumerate((w_q, w_k, w_v)):
        locals_.append(
            pltpu.make_async_copy(
                w.at[:, columns(f)],
                w_cols.at[pl.ds(pl.multiple_of(f * depth, depth), depth), pl.ds(j * width, width)],
                local_sems.at[3 + j],
            )
        )
    for c in locals_:
        c.start()

    first = pl.ds(pl.multiple_of(here * quarter, eighth), eighth)
    second = pl.ds(pl.multiple_of(here * quarter + eighth, eighth), eighth)
    relays_x, relays_y, direct_x, direct_y = [], [], [], []
    for j, w in enumerate((w_q, w_k, w_v)):
        relays_x.append(go(copy(n, w.at[first, columns(fd)], relay.at[0, j], by_x)))
        relays_y.append(go(copy(n + 1, w.at[second, columns(fd)], relay.at[1, j], by_y)))
        n += 2
    for j, w in enumerate((w_q, w_k, w_v)):
        place = w_cols.at[block_rows(f, here), pl.ds(j * width, width)]
        direct_x.append(go(copy(n, w.at[mine, columns(fx)], place, by_x)))
        direct_y.append(go(copy(n + 1, w.at[mine, columns(fy)], place, by_y)))
        n += 2
    low, high = pl.ds(0, rows // 2), pl.ds(rows // 2, rows // 2)
    t_x0 = go(copy(n, tokens.at[low], tokens_all.at[1, low], by_x))
    t_y1 = go(copy(n + 1, tokens.at[high], tokens_all.at[2, high], by_y))
    t_x1 = go(copy(n + 2, tokens.at[high], tokens_all.at[1, high], by_x))
    t_y0 = go(copy(n + 3, tokens.at[low], tokens_all.at[2, low], by_y))
    n += 4
    forwarded = []
    for j in range(3):
        relays_x[j].wait_recv()
        forwarded.append(
            go(copy(
                n, relay.at[0, j],
                w_cols.at[pl.ds(pl.multiple_of(fx * depth + here * quarter, eighth), eighth), pl.ds(j * width, width)],
                by_y,
            ))
        )
        relays_y[j].wait_recv()
        forwarded.append(
            go(copy(
                n + 1, relay.at[1, j],
                w_cols.at[
                    pl.ds(pl.multiple_of(fy * depth + here * quarter + eighth, eighth), eighth), pl.ds(j * width, width)
                ],
                by_x,
            ))
        )
        n += 2
    shares, lent = [], []

    def share(owner, q, target):
        nonlocal n
        place = w_cols.at[block_rows(owner, q)]
        c = go(copy(n, place, place, target))
        n += 1
        return c

    def fetched(owner):
        lent.append(share(owner, here, by_z))
        shares.append(share(owner, here, sibling))

    for c in direct_x:
        c.wait_recv()
    fetched(fx)
    for c in direct_y:
        c.wait_recv()
    fetched(fy)
    t_x0.wait_recv()
    t_d0 = go(copy(n, tokens_all.at[1, low], tokens_all.at[3, low], by_y))
    t_y1.wait_recv()
    t_d1 = go(copy(n + 1, tokens_all.at[2, high], tokens_all.at[3, high], by_x))
    n += 2
    for c in forwarded:
        c.wait_recv()
    fetched(fd)
    for owner, c in zip((fx, fy, fd), lent):
        c.wait_recv()
        shares.append(share(owner, there, sibling))
    for c in waits + shares + [t_x1, t_y0, t_d0, t_d1]:
        c.wait_recv()
    for c in locals_:
        c.wait()
    for c in all_sends:
        c.wait_send()


def start_call(tokens, small, marks, w_q, w_k, w_v, collective_id):
    depth, features = w_q.shape
    width = features // 4
    n = 6 + 6 + 6 + 4 + 6 + 2 + 9
    return pl.pallas_call(
        start_kernel,
        out_shape=(
            jax.ShapeDtypeStruct((4,) + tokens.shape, tokens.dtype),
            jax.ShapeDtypeStruct((4,) + small.shape, small.dtype),
            jax.ShapeDtypeStruct((4,) + marks.shape, marks.dtype),
            jax.ShapeDtypeStruct((4 * depth, 3 * width), BF16),
            jax.ShapeDtypeStruct((2, 3, depth // 8, width), BF16),
        ),
        in_specs=[ANY] * 6,
        out_specs=(ANY,) * 5,
        scratch_shapes=[
            pltpu.SemaphoreType.DMA((n,)),
            pltpu.SemaphoreType.DMA((n,)),
            pltpu.SemaphoreType.DMA((6,)),
        ],
        compiler_params=pltpu.CompilerParams(
            collective_id=collective_id, has_side_effects=True, vmem_limit_bytes=16 * MIB
        ),
    )(tokens, small, marks, w_q, w_k, w_v)[:4]


def turn_half(x):
    return pltpu.roll(x, HEAD_DIM // 2, 1)


def hidden_bias(of_keys, of_queries):
    key_segment, key_position = of_keys[0], of_keys[4]
    seen = (
        (key_segment == of_queries[1]) | (key_segment == of_queries[2]) | (key_segment == of_queries[3])
    ) & (key_position <= of_queries[4])
    return jnp.where(seen, 0.0, MASK_FILL)


class Spread:
    def __init__(self, own, everyone, send_sems, recv_sems, local_sem):
        self.everyone, self.send_sems, self.recv_sems = everyone, send_sems, recv_sems
        self.by_x, self.by_y = plane_neighbours()
        rows = own.shape[0]
        low, high = pl.ds(0, rows // 2), pl.ds(rows // 2, rows // 2)
        self.kept = pltpu.make_async_copy(own, everyone.at[0], local_sem)
        self.first = [
            self.copy(0, own.at[low], (1, low), self.by_x),
            self.copy(1, own.at[high], (2, high), self.by_y),
            self.copy(2, own.at[high], (1, high), self.by_x),
            self.copy(3, own.at[low], (2, low), self.by_y),
        ]
        self.second = [
            self.copy(4, everyone.at[1, low], (3, low), self.by_y),
            self.copy(5, everyone.at[2, high], (3, high), self.by_x),
        ]

    def copy(self, n, src, place, target):
        return pltpu.make_async_remote_copy(
            src_ref=src, dst_ref=self.everyone.at[place], send_sem=self.send_sems.at[n],
            recv_sem=self.recv_sems.at[n], device_id=target, device_id_type=MESH,
        )

    def begin(self):
        plane_barrier(self.by_x, self.by_y)
        for c in self.first:
            c.start()
        self.kept.start()

    def middle(self):
        for got, onward in zip(self.first[:2], self.second):
            got.wait_recv()
            onward.start()

    def end(self):
        for c in self.first[2:] + self.second:
            c.wait_recv()
        for c in self.first + self.second:
            c.wait_send()
        self.kept.wait()


def attend_kernel(
    tokens, gain, w_cols, bias, w_out, cosine, sine, mark_cols, mark_rows, *refs
):
    spread = None
    if len(refs) > 5:
        own, refs = refs[0], refs[1:]
        normed, three, attended, branch, everyone, mask = refs[:6]
        spread = Spread(own, everyone, *refs[6:])
        spread.begin()
    else:
        normed, three, attended, branch, mask = refs
    count = tokens.shape[0]
    width = w_out.shape[0]
    scale = HEAD_DIM**-0.5
    step = 256
    rows_of = [mark_rows[j : j + 1, :] for j in range(5)]
    for a, n in pieces(count, step):
        s = pl.ds(a, n)
        x = tokens[s, :].astype(F32)
        factor = lax.rsqrt(jnp.mean(x * x, axis=-1, keepdims=True) + EPSILON)
        normed[s, :] = (x * factor * gain[...]).astype(BF16)
        cols_of = [mark_cols[s, j : j + 1] for j in range(5)]
        mask[s, :] = hidden_bias(rows_of, cols_of)
    for b, m in pieces(3 * width, 256):
        c = pl.ds(b, m)
        pre = plain_dot(normed[...], w_cols[:, c]) + bias[:, c]
        if b < 2 * width:
            for d in range(0, m, HEAD_DIM):
                x = pre[:, d : d + HEAD_DIM]
                three[:, b + d : b + d + HEAD_DIM] = (
                    x * cosine[...] + turn_half(x) * sine[...]
                ).astype(BF16)
        else:
            three[:, c] = pre.astype(BF16)
    if spread:
        spread.middle()
    for h in range(width // HEAD_DIM):
        q_cols = pl.ds(h * HEAD_DIM, HEAD_DIM)
        k_cols = pl.ds(width + h * HEAD_DIM, HEAD_DIM)
        v_cols = pl.ds(2 * width + h * HEAD_DIM, HEAD_DIM)
        for a, n in pieces(count, step):
            s = pl.ds(a, n)
            scores = trans_dot(three[s, q_cols], three[:, k_cols]) + mask[s, :]
            peak = jnp.max(scores, axis=-1, keepdims=True)
            expo = jnp.exp((scores - peak) * scale)
            total = jnp.sum(expo, axis=-1, keepdims=True)
            weights = (expo * (1.0 / total)).astype(BF16)
            attended[s, q_cols] = plain_dot(weights, three[:, v_cols]).astype(BF16)
    for b, m in pieces(w_out.shape[1], 512):
        c = pl.ds(b, m)
        branch[:, c] = plain_dot(attended[...], w_out[:, c]).astype(BF16)
    if spread:
        spread.end()


def attend_call(tokens, gain, w_cols, bias, w_out, cosine, sine, mark_cols, mark_rows, own=None, collective_id=None):
    count, features = tokens.shape
    width = w_out.shape[0]

    def shape(cols):
        return jax.ShapeDtypeStruct((count, cols), BF16)

    ins = [tokens, gain, w_cols, bias, w_out, cosine, sine, mark_cols, mark_rows]
    in_specs, out_specs = [VMEM] * 9, (VMEM,) * 4
    out_shape = (shape(features), shape(3 * width), shape(width), shape(features))
    scratch = [pltpu.VMEM((count, count), F32)]
    params = {}
    if own is not None:
        ins.append(own)
        in_specs.append(VMEM)
        out_specs += (VMEM,)
        out_shape += (jax.ShapeDtypeStruct((4,) + own.shape, own.dtype),)
        scratch += [pltpu.SemaphoreType.DMA((6,)), pltpu.SemaphoreType.DMA((6,)), pltpu.SemaphoreType.DMA]
        params = {"collective_id": collective_id, "has_side_effects": True}
    return pl.pallas_call(
        attend_kernel,
        in_specs=in_specs,
        out_specs=out_specs,
        out_shape=out_shape,
        scratch_shapes=scratch,
        compiler_params=pltpu.CompilerParams(vmem_limit_bytes=60 * MIB, **params),
    )(*ins)


def attend_back_kernel(
    grad, w_out, three, w_cols, cosine, sine, mark_cols, mark_rows,
    grad_three, partial, grad_bias, mask, grad_att,
):
    count = grad.shape[0]
    width = w_out.shape[0]
    scale = HEAD_DIM**-0.5
    step = 256
    for b, m in pieces(width, 256):
        c = pl.ds(b, m)
        grad_att[:, c] = trans_dot(grad[...], w_out[c, :]).astype(BF16)
    rows_of = [mark_rows[j : j + 1, :] for j in range(5)]
    for a, n in pieces(count, step):
        s = pl.ds(a, n)
        mask[s, :] = hidden_bias([mark_cols[s, j : j + 1] for j in range(5)], rows_of)
    for h in range(width // HEAD_DIM):
        q_cols = pl.ds(h * HEAD_DIM, HEAD_DIM)
        k_cols = pl.ds(width + h * HEAD_DIM, HEAD_DIM)
        v_cols = pl.ds(2 * width + h * HEAD_DIM, HEAD_DIM)
        grad_k = grad_v = None
        for a, n in pieces(count, step):
            s = pl.ds(a, n)
            query, g = three[s, q_cols], grad_att[s, q_cols]
            scores = trans_dot(three[:, k_cols], query) + mask[:, s]
            peak = jnp.max(scores, axis=0, keepdims=True)
            expo = jnp.exp((scores - peak) * scale)
            probs = expo * (1.0 / jnp.sum(expo, axis=0, keepdims=True))
            weight_grad = trans_dot(three[:, v_cols], g)
            diagonal = jnp.sum(probs * weight_grad, axis=0, keepdims=True)
            score_grad = (probs * (weight_grad - diagonal)).astype(BF16)
            part_v = plain_dot(probs.astype(BF16), g)
            part_k = plain_dot(score_grad, query)
            grad_v = part_v if grad_v is None else grad_v + part_v
            grad_k = part_k if grad_k is None else grad_k + part_k
            grad_q = rows_dot(score_grad, three[:, k_cols]) * scale
            grad_three[s, q_cols] = (
                grad_q * cosine[s, :] - turn_half(grad_q) * sine[s, :]
            ).astype(BF16)
        grad_k = grad_k * scale
        grad_three[:, k_cols] = (grad_k * cosine[...] - turn_half(grad_k) * sine[...]).astype(BF16)
        grad_three[:, v_cols] = grad_v.astype(BF16)
    for b, m in pieces(3 * width, 512):
        c = pl.ds(b, m)
        grad_bias[:, c] = jnp.sum(grad_three[:, c].astype(F32), axis=0, keepdims=True)
    for b, m in pieces(w_cols.shape[0], 512):
        c = pl.ds(b, m)
        partial[:, c] = trans_dot(grad_three[...], w_cols[c, :]).astype(BF16)


def attend_back_call(grad, w_out, three, w_cols, cosine, sine, mark_cols, mark_rows):
    count, features = grad.shape
    width = w_out.shape[0]

    def shape(rows, cols, dtype=BF16):
        return jax.ShapeDtypeStruct((rows, cols), dtype)

    return pl.pallas_call(
        attend_back_kernel,
        in_specs=[VMEM] * 8,
        out_specs=(VMEM,) * 3,
        out_shape=(shape(count, 3 * width), shape(count, features), shape(1, 3 * width, F32)),
        scratch_shapes=[pltpu.VMEM((count, count), F32), pltpu.VMEM((count, width), BF16)],
        compiler_params=pltpu.CompilerParams(vmem_limit_bytes=60 * MIB),
    )(grad, w_out, three, w_cols, cosine, sine, mark_cols, mark_rows)


class Load:
    def __init__(self, value):
        self.value = value

    def __getitem__(self, place):
        return self.value[place]


class Store:
    def __init__(self, shape):
        self.value = jnp.zeros(shape.shape, shape.dtype)

    def __getitem__(self, place):
        return self.value[place]

    def __setitem__(self, place, value):
        self.value = value.astype(self.value.dtype)


def first_middle(total, span, ins, outs):
    tokens, gain = ins
    mixed = tokens[span].astype(F32) + total
    factor = lax.rsqrt(jnp.mean(mixed * mixed, axis=-1, keepdims=True) + EPSILON)
    outs[0][span] = mixed
    return (mixed * factor * gain[...]).astype(BF16)


def norm_back(values, gain, grad):
    factor = lax.rsqrt(jnp.mean(values * values, axis=-1, keepdims=True) + EPSILON)
    weighted = gain * grad
    back = factor * weighted - values * (factor * factor * factor) * jnp.mean(
        weighted * values, axis=-1, keepdims=True
    )
    return back, jnp.sum(grad * values * factor, axis=0, keepdims=True)


def back_middle(total, span, ins, outs):
    values, gain, base = ins
    back, grad_gain = norm_back(values[span].astype(F32), gain[...], total)
    grad = base[span].astype(F32) + back
    outs[0][span] = grad
    outs[1][span if span == slice(None) else pl.ds(span.start // span.size, 1)] = grad_gain
    return grad.astype(BF16)


class Wires:
    def __init__(self, mesh):
        self.nf = mesh.shape["fsdp"]
        self.ng = mesh.shape["grp"]
        self.nz = self.ng // 2
        self.fast = self.nf == 4 and self.ng == 8
        self.chunks = 4 if self.fast else 1

    def xor(self, value, k):
        return lax.ppermute(value, "fsdp", [(i, i ^ k) for i in range(self.nf)])

    def inwards(self, value):
        if not self.fast:
            return None
        return lax.ppermute(value, "grp", [(0, 2), (1, 3), (6, 4), (7, 5)])

    def gather_list(self, value):
        return [value] + [self.xor(value, k) for k in range(1, self.nf)]

    def gather(self, value):
        return jnp.concatenate(self.gather_list(value), axis=0)

    def scatter_sum(self, value):
        rows = value.shape[0] // self.nf
        total = value[:rows].astype(F32)
        for k in range(1, self.nf):
            part = value[k * rows : (k + 1) * rows].astype(BF16)
            total = total + self.xor(part, k).astype(F32)
        return total

    def reduce_background(self, partial):
        return lax.psum_scatter(partial, "grp", scatter_dimension=0, tiled=True)

    def gather_start(self, tokens, small, marks, weights):
        if self.fast:
            return start_call(tokens, small, marks, *weights, 1)
        cols = jnp.concatenate(
            [lax.all_to_all(w, "fsdp", split_axis=1, concat_axis=0, tiled=True) for w in weights],
            axis=1,
        )
        return tuple(jnp.stack(self.gather_list(v)) for v in (tokens, small, marks)) + (cols,)

    def middle(self, body, partial, ins, out_shapes, gathers, number, arrays=(), jobs=(), later=()):
        nf = self.nf
        rows, cols = partial.shape[0] // nf, partial.shape[1]
        if self.fast:
            side = Side(arrays, jobs, later)
            return mid_call(body, partial.reshape(nf, rows, cols), ins, out_shapes, gathers, side, number)
        total = self.scatter_sum(partial)
        outs = [Store(s) for s in out_shapes]
        given = body(total, slice(None), [Load(v) for v in ins], outs)
        results = tuple(o.value for o in outs)
        if gathers:
            results += (jnp.stack(self.gather_list(given)),)

        def operand(o):
            number, axis, entry = o
            v = arrays[number] if axis is None else lax.index_in_dim(arrays[number], entry, axis, False)
            return v.reshape(-1, v.shape[-1])

        return results + tuple(
            sum(rows_dot(operand(a), operand(b)) for a, b in job).astype(BF16) for job in jobs
        )

    def last_sums(
        self, downs, shared, part_three, part_output, out_part, mixed, normed_part, tokens, base, vec, gain, bias_add, number
    ):
        nf, ng, nz = self.nf, self.ng, self.nz
        features, width = part_output.shape
        share = features // ng
        if self.fast:
            outs = line_call(
                [v.reshape(nz, 2, share, -1) for v in downs],
                [v.reshape(nz, 2, share, -1) for v in shared],
                part_three.reshape(3, 2, share, features),
                part_output.reshape(nz, 2, share, width),
                out_part.reshape(nf, -1, features),
                mixed,
                normed_part.reshape(nf, -1, features),
                tokens,
                base,
                vec.reshape(16, nf, width).transpose(1, 0, 2),
                gain,
                bias_add,
                2,
                True,
                number,
            )
            return outs
        down = jnp.stack([self.reduce_background(v).astype(F32).T for v in downs], axis=0)
        sums = [self.reduce_background(v).astype(F32) for v in shared]
        three = lax.all_to_all(
            part_three.reshape(3, width, features), "fsdp", split_axis=2, concat_axis=1, tiled=True
        )
        four = jnp.concatenate([three, part_output[None]], axis=0)
        four = lax.psum_scatter(four, "grp", scatter_dimension=1, tiled=True).astype(F32)
        back, grad_gain = norm_back(tokens.astype(F32), gain, self.scatter_sum(normed_part))
        vec = jnp.concatenate([grad_gain, vec[1:]], axis=0)
        vec = lax.psum_scatter(vec, "fsdp", scatter_dimension=1, tiled=True) + bias_add
        output = (mixed + self.scatter_sum(out_part)).astype(BF16)
        return down, (sums[0], sums[1], sums[2].T), four.transpose(0, 2, 1), output, base + back, lax.psum(vec, "grp")


def on_device(
    wires,
    tokens,
    cotangent,
    segment,
    ancestry,
    position,
    routes,
    attn_gain,
    w_query,
    w_key,
    w_value,
    b_query,
    b_key,
    b_value,
    w_output,
    moe_gain,
    w_router,
    shared_switch,
    shared_gate,
    shared_up,
    shared_down,
    expert_gate,
    routed_up_weight,
    expert_down,
):
    nf, ng = wires.nf, wires.ng
    me = lax.axis_index("fsdp")
    rows_dev, features = tokens.shape
    count = rows_dev * nf
    width = features // nf
    experts = w_router.shape[1]
    local_experts = experts // nf
    capacity = 5 * rows_dev // 8
    choose = routes.shape[1]

    small = jnp.concatenate([attn_gain[None], moe_gain[None], w_router.T, shared_switch[None]], axis=0)
    small = jnp.pad(small, ((0, -small.shape[0] % 16), (0, 0)))
    marks = jnp.concatenate([segment[None], ancestry.T, position[None], routes.T], axis=0)
    marks = jnp.pad(marks, ((0, -marks.shape[0] % 16), (0, 0)))
    tokens_all, small_blocks, marks_all, w_cols = wires.gather_start(
        tokens, small, marks, (w_query, w_key, w_value)
    )
    tokens_all = tokens_all.reshape(count, features)
    small_all = jnp.concatenate(
        [lax.dynamic_index_in_dim(small_blocks, me ^ i, 0, keepdims=False) for i in range(nf)], axis=1
    )
    gain_one = small_all[0:1].astype(F32)
    gain_two = small_all[1:2].astype(F32)
    heads_rows = small_all[2 : experts + 3]
    mark_rows = jnp.concatenate([marks_all[k] for k in range(nf)], axis=1)
    mark_cols = mark_rows.T
    routes_rows = mark_rows[5 : 5 + choose]


    halfway = HEAD_DIM // 2
    freqs = ROPE_BASE ** (-(jnp.arange(halfway, dtype=F32) * 2.0 / HEAD_DIM))
    turns = mark_cols[:, 4:5].astype(F32) * jnp.concatenate([freqs, freqs])[None, :]
    cosine = jnp.cos(turns)
    sine = jnp.sin(turns) * jnp.where(jnp.arange(HEAD_DIM) < halfway, -1.0, 1.0)[None, :]
    bias = jnp.concatenate([b_query, b_key, b_value]).astype(F32)[None]
    operands = (tokens_all, gain_one, w_cols, bias, w_output, cosine, sine, mark_cols, mark_rows)
    if wires.fast:
        normed, three, attended, branch, cot_all = attend_call(*operands, cotangent, 6)
        cot_all = cot_all.reshape(count, features)
    else:
        normed, three, attended, branch = attend_call(*operands)
        cot_all = wires.gather(cotangent)

    numbers = me * local_experts + jnp.arange(local_experts, dtype=jnp.int32)
    named = jnp.any(routes_rows[None] == numbers[:, None, None], axis=1)
    named = named.reshape(local_experts, nf, rows_dev)
    earlier = (jnp.arange(rows_dev)[None, :] < jnp.arange(rows_dev)[:, None]).astype(BF16)
    slot = jnp.einsum("ts,ebs->bet", earlier, named.astype(BF16), preferred_element_type=F32)
    slot = jnp.where(named.transpose(1, 0, 2), slot.astype(jnp.int32), -1)
    pick = jnp.arange(capacity, dtype=jnp.int32)[None, None, :, None] == slot[:, :, None, :]

    cot_other = wires.inwards(cot_all)
    mixed, moe_blocks = wires.middle(
        first_middle,
        branch,
        (tokens, gain_two),
        (jax.ShapeDtypeStruct((rows_dev, features), F32),),
        True,
        2,
    )
    moe_in = moe_blocks.reshape(count, features)
    moe_other = wires.inwards(moe_in)

    rows_in, rows_cot, gate, pick_b, router_probs, opener = dispatch_call(
        moe_in, cot_all, slot, heads_rows, capacity
    )
    if wires.fast:
        rows_cot, cot_other = lax.optimization_barrier((rows_cot, cot_other))
    hidden, d_gate, d_up, d_out, y_rows, dx_rows, sens_rows = expert_call(
        rows_in, rows_cot, gate, expert_gate, routed_up_weight, expert_down, nf // 2
    )

    gate_part = outer_call(rows_in, 0, d_gate)
    gate_sums = [wires.reduce_background(gate_part)]
    late_gates = [outer_call(rows_in, i, d_gate) for i in range(1, local_experts)]
    up_part = outer_call(rows_in, 0, d_up)
    gate_part, late_gates, up_part, hidden, sens_rows, y_rows, moe_other = lax.optimization_barrier(
        (gate_part, late_gates, up_part, hidden, sens_rows, y_rows, moe_other)
    )
    gate_sums += [wires.reduce_background(v) for v in late_gates]
    up_sums = [wires.reduce_background(up_part)]

    gate_grad = jnp.sum(jnp.where(pick, sens_rows, 0.0), axis=2)
    gate_grad = gate_grad.transpose(1, 0, 2).reshape(local_experts, count)
    prob_grad = sum(
        jnp.where(jnp.arange(experts)[None] == numbers[i], gate_grad[i][:, None], 0.0)
        for i in range(local_experts)
    )
    logit_grad = router_probs * (
        prob_grad - jnp.sum(prob_grad * router_probs, axis=-1, keepdims=True)
    )
    high = logit_grad.astype(BF16)
    lanes = jnp.concatenate([high, (logit_grad - high.astype(F32)).astype(BF16)], axis=1)
    router_rows = heads_rows[:experts]
    taken = (nf, local_experts * capacity, features)
    s_hidden, sd_gate, sd_up, sd_out, out_part, moe_part, gate_sens, *of_other = shared_call(
        moe_in,
        cot_all,
        opener,
        pick_b,
        y_rows.reshape(taken),
        dx_rows.reshape(taken),
        lanes,
        jnp.concatenate([router_rows, router_rows], axis=0),
        heads_rows[experts:].astype(F32),
        shared_gate,
        shared_up,
        shared_down,
        [moe_other, cot_other, heads_rows] if wires.fast else None,
    )
    sens_high = gate_sens.astype(BF16)
    sens_low = (gate_sens - sens_high.astype(F32)).astype(BF16)
    grad_heads = rows_dot(jnp.concatenate([lanes, sens_high, sens_low], axis=1), moe_in)
    grad_heads = jnp.concatenate(
        [
            grad_heads[:experts] + grad_heads[experts : 2 * experts],
            grad_heads[2 * experts : 2 * experts + 1] + grad_heads[2 * experts + 1 :],
        ],
        axis=0,
    )
    arrays = (rows_in, d_up, hidden, moe_in, sd_gate, sd_up, sd_out)
    if wires.fast:
        o_hidden, od_gate, od_up, od_out = of_other
        arrays += (moe_other, od_gate, od_up, s_hidden, od_out, o_hidden, d_out)
        later = {(13, 1, 1): (0, 1, 1), (2, 0, 1): (1, 0, 1)}
    else:
        arrays += (None, None, None, s_hidden, None, None, d_out)
        later = {}
    jobs = []
    for i in range(1, local_experts):
        jobs += [(((0, 1, i), (1, 0, i)),)]
    jobs += [(((13, 1, i), (2, 0, i)),) for i in range(local_experts)]

    def whole(*numbers):
        return tuple((n, None, 0) for n in numbers)

    if wires.fast:
        jobs += [(whole(3, 4), whole(7, 8)), (whole(3, 5), whole(7, 9)), (whole(6, 10), whole(11, 12))]
    else:
        jobs += [(whole(3, 4),), (whole(3, 5),), (whole(6, 10),)]
    grad_mixed, grad_gain_two, branch_grad, *parts = wires.middle(
        back_middle,
        moe_part,
        (mixed, gain_two, cotangent),
        (
            jax.ShapeDtypeStruct((rows_dev, features), F32),
            jax.ShapeDtypeStruct((wires.chunks, features), F32),
        ),
        True,
        3,
        arrays,
        jobs,
        later,
    )
    late = local_experts - 1
    parts, up_sums = lax.optimization_barrier((parts, up_sums))
    up_sums += [wires.reduce_background(v) for v in parts[:late]]
    down_parts, shared_parts = parts[late : late + local_experts], parts[late + local_experts :]
    branch_grad = branch_grad.reshape(count, features)
    grad_three, normed_part, grad_bias = attend_back_call(
        branch_grad, w_output, three, w_cols, cosine, sine, mark_cols, mark_rows
    )
    part_output = rows_dot(branch_grad, attended).astype(BF16)
    part_three = rows_dot(grad_three, normed).astype(BF16)

    vec = jnp.concatenate(
        [
            jnp.zeros_like(gain_one),
            jnp.sum(grad_gain_two, axis=0, keepdims=True),
            grad_heads,
        ],
        axis=0,
    )
    vec = jnp.pad(vec, ((0, 16 - vec.shape[0]), (0, 0)))
    bias_add = jnp.pad(grad_bias.reshape(3, width), ((experts + 3, 16 - experts - 6), (0, 0)))
    down_sums, shared_sums, four, output, grad_tokens, vec = wires.last_sums(
        down_parts,
        shared_parts,
        part_three,
        part_output,
        out_part,
        mixed,
        normed_part,
        tokens,
        grad_mixed,
        vec,
        gain_one,
        bias_add,
        5,
    )
    own = width // ng
    vec = lax.dynamic_slice_in_dim(vec, lax.axis_index("grp") * own, own, 1)
    return (
        output,
        grad_tokens,
        vec[0],
        four[0],
        four[1],
        four[2],
        vec[experts + 3],
        vec[experts + 4],
        vec[experts + 5],
        four[3],
        vec[1],
        vec[2 : experts + 2].T,
        vec[experts + 2],
        shared_sums[0],
        shared_sums[1],
        shared_sums[2],
        jnp.stack(gate_sums, axis=0).astype(F32),
        jnp.stack(up_sums, axis=0).astype(F32),
        down_sums,
    )


def solution(mesh):
    wires = Wires(mesh)

    def step(*args):
        return on_device(wires, *args)

    rows = P(("grp", "fsdp"))
    shard = P("fsdp")
    small = P(("fsdp", "grp"))
    return jax.shard_map(
        step,
        mesh=mesh,
        in_specs=(rows,) * 6
        + (shard,) * 11
        + (P(None, "fsdp"), P(None, "fsdp"), shard, shard, shard, shard),
        out_specs=(
            rows,
            rows,
            small,
            P("fsdp", "grp"),
            P("fsdp", "grp"),
            P("fsdp", "grp"),
            small,
            small,
            small,
            P("fsdp", "grp"),
            small,
            small,
            small,
            P("grp", "fsdp"),
            P("grp", "fsdp"),
            P("fsdp", "grp"),
            P("fsdp", "grp", None),
            P("fsdp", "grp", None),
            P("fsdp", None, "grp"),
        ),
        check_vma=False,
    )
```

```python
import functools

import jax
import jax.numpy as jnp
from jax import lax
from jax.experimental import pallas as pl
from jax.experimental.pallas import tpu as pltpu
from jax.sharding import PartitionSpec as P

HEADS = 16
HEAD_DIM = 128
EPSILON = 1e-06
ROPE_BASE = 1000000.0
MASK_FILL = -1e30

F32 = jnp.float32
BF16 = jnp.bfloat16
MESH = pl.DeviceIdType.MESH
ANY = pl.BlockSpec(memory_space=pl.ANY)
VMEM = pl.BlockSpec(memory_space=pltpu.VMEM)
MIB = 2**20


def dot(left, right, dims, out=F32):
    return lax.dot_general(left, right, (dims, ((), ())), preferred_element_type=out)


def plain_dot(left, right):
    return dot(left, right, ((1,), (0,)))


def trans_dot(left, right):
    return dot(left, right, ((1,), (1,)))


def rows_dot(left, right):
    return dot(left, right, ((0,), (0,)))


def pieces(total, size):
    return [(a, min(size, total - a)) for a in range(0, total, size)]


def hidden_part(x, g, gate, w_gate, w_up, w_down, hidden, d_gate, d_up):
    units = w_gate.shape[1]
    sens = None
    for a, n in pieces(units, 256):
        s = pl.ds(a, n)
        pre = plain_dot(x, w_gate[:, s])
        up = plain_dot(x, w_up[:, s])
        plain = trans_dot(g, w_down[s, :])
        sigma = 1.0 / (1.0 + jnp.exp(-pre))
        act = pre * sigma
        slope = sigma * (1.0 + pre * (1.0 - sigma))
        h = (act * up).astype(BF16)
        hidden[:, s] = h
        grad = gate * plain
        d_gate[:, s] = (grad * up * slope).astype(BF16)
        d_up[:, s] = (grad * act).astype(BF16)
        part = jnp.sum(plain * h.astype(F32), axis=-1, keepdims=True)
        sens = part if sens is None else sens + part
    return sens


def expert_kernel(x_ref, g_ref, gate_ref, wg, wu, wd, hidden, d_gate, d_up, d_out, y_ref, dx_ref, sens_ref):
    blocks, _, slots, features = x_ref.shape
    rows = blocks * slots
    x = x_ref[...].reshape(rows, features)
    g = g_ref[...].reshape(rows, features)
    gate = gate_ref[...].reshape(rows, 1)
    wg, wu, wd = wg.at[0], wu.at[0], wd.at[0]
    hid, dg, du = hidden.at[0], d_gate.at[0], d_up.at[0]
    d_out[...] = (gate * g.astype(F32)).astype(BF16).reshape(d_out.shape)
    sens = hidden_part(x, g, gate, wg, wu, wd, hid, dg, du)
    sens_ref[...] = sens.reshape(sens_ref.shape)
    for a, n in pieces(features, 512):
        s = pl.ds(a, n)
        y = plain_dot(hid[...], wd[:, s]).astype(BF16)
        y_ref[:, :, :, s] = (gate * y.astype(F32)).astype(BF16).reshape(blocks, 1, slots, n)
        dx = trans_dot(dg[...], wg[s, :]) + trans_dot(du[...], wu[s, :])
        dx_ref[:, :, :, s] = dx.astype(BF16).reshape(blocks, 1, slots, n)


def expert_call(rows_in, rows_cot, gate, w_gate, w_up, w_down, tile):
    blocks, experts, slots, features = rows_in.shape
    units = w_gate.shape[2]
    steps = blocks // tile
    rows = tile * slots

    def slot_spec(cols):
        return pl.BlockSpec((tile, 1, slots, cols), lambda i, t: (t, i, 0, 0))

    def unit_spec():
        return pl.BlockSpec((1, rows, units), lambda i, t: (i, t, 0))

    def weight_spec(a, b):
        return pl.BlockSpec((1, a, b), lambda i, t: (i, 0, 0))

    units_shape = jax.ShapeDtypeStruct((experts, blocks * slots, units), BF16)
    slots_shape = jax.ShapeDtypeStruct((blocks, experts, slots, features), BF16)
    return pl.pallas_call(
        expert_kernel,
        grid=(experts, steps),
        in_specs=[
            slot_spec(features),
            slot_spec(features),
            slot_spec(1),
            weight_spec(features, units),
            weight_spec(features, units),
            weight_spec(units, features),
        ],
        out_specs=[unit_spec()] * 3 + [slot_spec(features)] * 3 + [slot_spec(1)],
        out_shape=[units_shape] * 3
        + [slots_shape] * 3
        + [jax.ShapeDtypeStruct((blocks, experts, slots, 1), F32)],
        compiler_params=pltpu.CompilerParams(vmem_limit_bytes=62 * MIB),
    )(rows_in, rows_cot, gate, w_gate, w_up, w_down)


def own_kernel(
    x_ref, g_ref, head_ref, pick_ref, y_in, dx_in, lane_ref, heads_w, switch_row, wg, wu, wd,
    hidden, d_gate, d_up, d_out, y_ref, dx_ref, sens_ref,
):
    features = x_ref.shape[1]
    x = x_ref[...]
    g = g_ref[...]
    opener = head_ref[...]
    d_out[...] = (opener * g.astype(F32)).astype(BF16)
    sens = hidden_part(x, d_out[...], 1.0, wg, wu, wd, hidden, d_gate, d_up)
    sens = (1.0 - opener) * sens
    sens_ref[...] = sens
    pick = pick_ref[0]
    lanes = lane_ref[...]
    for a, n in pieces(features, 512):
        s = pl.ds(a, n)
        y = opener * plain_dot(hidden[...], wd[:, s]) + rows_dot(pick, y_in[0, :, s])
        y_ref[:, s] = y.astype(BF16)
        dx = trans_dot(d_gate[...], wg[s, :]) + trans_dot(d_up[...], wu[s, :])
        dx = dx + rows_dot(pick, dx_in[0, :, s])
        dx = dx + plain_dot(lanes, heads_w[:, s]) + sens * switch_row[:, s]
        dx_ref[:, s] = dx.astype(BF16)


def other_kernel(x_ref, g_ref, heads, wg, wu, wd, hidden, d_gate, d_up, d_out):
    x = x_ref[...]
    pre = trans_dot(x, heads[...])
    opener = 1.0 / (1.0 + jnp.exp(-pre[:, heads.shape[0] - 1 :]))
    d_out[...] = (opener * g_ref[...].astype(F32)).astype(BF16)
    hidden_part(x, d_out[...], 1.0, wg, wu, wd, hidden, d_gate, d_up)


def shared_kernel(blocks, others, *refs):
    if not others:
        own_kernel(*refs)
        return
    ins, outs = refs[:15], refs[15:]
    weights = ins[9:12]
    step = pl.program_id(0)

    @pl.when(step < blocks)
    def _():
        own_kernel(*ins[:12], *outs[:7])

    @pl.when(step >= blocks)
    def _():
        other_kernel(*ins[12:15], *weights, *outs[7:])


def shared_call(x, g, opener, pick, y_in, dx_in, lanes, heads_w, switch_row, w_gate, w_up, w_down, others=None):
    count, features = x.shape
    units = w_gate.shape[1]
    blocks, taken, tile = pick.shape
    width = lanes.shape[1]

    def own(b):
        return jnp.minimum(b, blocks - 1)

    def other(b):
        return jnp.maximum(b - blocks, 0)

    def rows_spec(cols, place=own):
        return pl.BlockSpec((tile, cols), lambda b: (place(b), 0))

    def block_spec(cols):
        return pl.BlockSpec((1, taken, cols), lambda b: (own(b), 0, 0))

    def whole(a, b):
        return pl.BlockSpec((a, b), lambda b_: (0, 0), pipeline_mode=pl.Buffered(1))

    def shape(cols, dtype=BF16):
        return jax.ShapeDtypeStruct((count, cols), dtype)

    ins = [x, g, opener, pick, y_in, dx_in, lanes, heads_w, switch_row, w_gate, w_up, w_down]
    in_specs = [
        rows_spec(features),
        rows_spec(features),
        rows_spec(1),
        block_spec(tile),
        block_spec(features),
        block_spec(features),
        rows_spec(width),
        whole(width, features),
        whole(1, features),
        whole(features, units),
        whole(features, units),
        whole(units, features),
    ]
    out_specs = [rows_spec(units)] * 3 + [rows_spec(features)] * 3 + [rows_spec(1)]
    out_shape = [shape(units)] * 3 + [shape(features)] * 3 + [shape(1, F32)]
    if others:
        ins += others
        in_specs += [rows_spec(features, other)] * 2 + [whole(others[2].shape[0], features)]
        out_specs += [rows_spec(units, other)] * 3 + [rows_spec(features, other)]
        out_shape += [shape(units)] * 3 + [shape(features)]
    return pl.pallas_call(
        functools.partial(shared_kernel, blocks, bool(others)),
        grid=(2 * blocks if others else blocks,),
        in_specs=in_specs,
        out_specs=out_specs,
        out_shape=out_shape,
        compiler_params=pltpu.CompilerParams(vmem_limit_bytes=62 * MIB),
    )(*ins)


def dispatch_kernel(x_ref, g_ref, slot_ref, heads, rows_in, rows_cot, gate_ref, pick_ref, probs_ref, opener_ref):
    x, g = x_ref[...], g_ref[...]
    local, slots = rows_in.shape[1], rows_in.shape[2]
    count = heads.shape[0] - 1
    pre = trans_dot(x, heads[...])
    opener_ref[...] = 1.0 / (1.0 + jnp.exp(-pre[:, count:]))
    pre = pre[:, :count]
    expo = jnp.exp(pre - jnp.max(pre, axis=-1, keepdims=True))
    probs = expo / jnp.sum(expo, axis=-1, keepdims=True)
    probs_ref[...] = probs
    parts, rest = [], probs
    for _ in range(3):
        parts.append(rest.astype(BF16))
        rest = rest - parts[-1].astype(F32)
    numbers = lax.broadcasted_iota(jnp.int32, (slots, count), 1)
    places = lax.broadcasted_iota(jnp.int32, (slots, x.shape[0]), 0)
    for i in range(local):
        pick = jnp.where(places == slot_ref[0, i : i + 1, :], 1.0, 0.0).astype(BF16)
        pick_ref[0, i * slots : (i + 1) * slots, :] = pick
        rows_in[0, i] = plain_dot(pick, x).astype(BF16)
        rows_cot[0, i] = plain_dot(pick, g).astype(BF16)
        found = plain_dot(pick, parts[0]) + (plain_dot(pick, parts[1]) + plain_dot(pick, parts[2]))
        number = lax.axis_index("fsdp") * local + i
        gate_ref[0, i] = jnp.sum(jnp.where(numbers == number, found, 0.0), axis=-1, keepdims=True)


def dispatch_call(x, g, slot, heads, slots):
    count, features = x.shape
    blocks, local, rows = slot.shape
    experts = heads.shape[0] - 1

    def rows_spec(cols):
        return pl.BlockSpec((rows, cols), lambda b: (b, 0))

    def slots_spec(cols):
        return pl.BlockSpec((1, local, slots, cols), lambda b: (b, 0, 0, 0))

    def slots_shape(cols, dtype=BF16):
        return jax.ShapeDtypeStruct((blocks, local, slots, cols), dtype)

    return pl.pallas_call(
        dispatch_kernel,
        grid=(blocks,),
        in_specs=[
            rows_spec(features),
            rows_spec(features),
            pl.BlockSpec((1, local, rows), lambda b: (b, 0, 0)),
            pl.BlockSpec(heads.shape, lambda b: (0, 0)),
        ],
        out_specs=[
            slots_spec(features),
            slots_spec(features),
            slots_spec(1),
            pl.BlockSpec((1, local * slots, rows), lambda b: (b, 0, 0)),
            rows_spec(experts),
            rows_spec(1),
        ],
        out_shape=[
            slots_shape(features),
            slots_shape(features),
            slots_shape(1, F32),
            jax.ShapeDtypeStruct((blocks, local * slots, rows), BF16),
            jax.ShapeDtypeStruct((count, experts), F32),
            jax.ShapeDtypeStruct((count, 1), F32),
        ],
        compiler_params=pltpu.CompilerParams(vmem_limit_bytes=60 * MIB),
    )(x, g, slot, heads)


def outer_kernel(a_ref, b_ref, out_ref):
    out_ref[...] = rows_dot(a_ref[...].reshape(-1, a_ref.shape[-1]), b_ref[0]).astype(BF16)


def outer_call(rows, i, units):
    blocks, _, slots, features = rows.shape
    _, depth, n = units.shape
    tile = 512
    return pl.pallas_call(
        outer_kernel,
        grid=(features // tile,),
        in_specs=[
            pl.BlockSpec((blocks, 1, slots, tile), lambda j: (0, i, 0, j)),
            pl.BlockSpec((1, depth, n), lambda j: (i, 0, 0)),
        ],
        out_specs=pl.BlockSpec((tile, n), lambda j: (j, 0)),
        out_shape=jax.ShapeDtypeStruct((features, n), BF16),
        compiler_params=pltpu.CompilerParams(vmem_limit_bytes=62 * MIB),
    )(rows, units)


class Line:
    def __init__(self, parts, inner, sources, outs, sib, recv, bufs, sems):
        self.parts, self.inner, self.sources, self.outs = parts, inner, sources, outs
        self.sib, self.recv = sib, recv
        self.own_v, self.sib_v, self.send_v, self.out_v, self.turned_v = bufs
        self.own_sem, self.sib_sem, self.out_sem, self.sib_send, self.sib_recv, self.sent, self.got = sems
        self.chunks = len(sources) * parts
        self.slots = self.send_v.shape[0]
        self.rows = sources[0].shape[2] // parts
        g = lax.axis_index("grp")
        self.z, self.core = g // 2, lax.rem(g, 2)
        self.is_end = (self.z == 0) | (self.z == 3)
        self.is_mid = (self.z == 1) | (self.z == 2)

    def at(self, z, core):
        return {"grp": 2 * z + core}

    def span(self, q):
        return lax.div(q, self.parts), pl.ds(
            pl.multiple_of(lax.rem(q, self.parts) * self.rows, self.rows), self.rows
        )

    def swap(self, j, m, r, q):
        return pltpu.make_async_remote_copy(
            src_ref=self.sources[j].at[:, 1 - self.core, r],
            dst_ref=self.sib.at[m, :, r],
            send_sem=self.sib_send.at[q],
            recv_sem=self.sib_recv.at[q],
            device_id=self.at(self.z, 1 - self.core),
            device_id_type=MESH,
        )

    def swap_any(self, q):
        m, r = self.span(q)
        return self.swap(0, m, r, q)

    def when_summing(self, condition=None):
        if self.inner:
            condition = self.is_mid if condition is None else self.is_mid & condition
        return (lambda body: body()) if condition is None else pl.when(condition)

    def start_swaps(self):
        @self.when_summing()
        def _():
            for m in range(len(self.sources)):
                for h in range(self.parts):
                    self.swap(m, m, pl.ds(h * self.rows, self.rows), m * self.parts + h).start()

    def out_copy(self, j, r):
        ref, turned = self.outs[j]
        if turned:
            return pltpu.make_async_copy(self.turned_v, ref.at[:, r], self.out_sem)
        return pltpu.make_async_copy(self.out_v, ref.at[r], self.out_sem)

    def each_out(self, q, body):
        m, r = self.span(q)
        for j in range(len(self.sources)):

            @pl.when(m == j)
            def _():
                body(j, r)

    def hop(self, q, slot, target, place):
        m, r = self.span(q)
        return pltpu.make_async_remote_copy(
            src_ref=self.send_v.at[slot],
            dst_ref=self.recv.at[m, place, r],
            send_sem=self.sent.at[slot],
            recv_sem=self.got.at[q, place],
            device_id=self.at(target, self.core),
            device_id_type=MESH,
        )

    def arrived(self, q, place):
        self.hop(q, 0, self.z, place).wait_recv()

    def own_load(self, j, p, r, k):
        return pltpu.make_async_copy(self.sources[j].at[p, self.core, r], self.own_v.at[k], self.own_sem.at[k])

    def sib_load(self, m, p, r, k):
        return pltpu.make_async_copy(self.sib.at[m, p, r], self.sib_v.at[k], self.sib_sem.at[k])

    def start_base(self, q, p, k):
        m, r = self.span(q)
        for j in range(len(self.sources)):

            @pl.when(m == j)
            def _():
                self.own_load(j, p, r, k).start()

        self.sib_load(m, p, r, k).start()

    def base(self, k):
        r = pl.ds(0, self.rows)
        self.own_load(0, 0, r, k).wait()
        self.sib_load(0, 0, r, k).wait()
        return self.own_v[k].astype(F32) + self.sib_v[k].astype(F32)

    def fetch(self, q, place):
        self.arrived(q, place)
        m, r = self.span(q)
        return self.recv[m, place, r].astype(F32)

    def send(self, t, k, q, p, target, place, more, first):
        depth = self.slots // 3
        slot = lax.rem(t, depth) * 3 + k

        @pl.when(t >= depth + first)
        def _():
            self.hop(q, slot, target, place).wait_send()

        if more:
            extra = self.fetch(q, p)
            total = self.base(k) + extra
        else:
            total = self.base(k)
        self.send_v[slot] = total.astype(BF16)
        self.hop(q, slot, target, place).start()

    def turn(self, t):
        z, chunks = self.z, self.chunks
        to_end = self.is_end & (t >= 0) & (t < chunks)
        to_next = self.is_mid & (t >= 1) & (t < chunks + 1)
        to_last = self.is_mid & (t >= 2) & (t < chunks + 2)
        last = (t >= 3) & (t < chunks + 3)

        @self.when_summing((t >= 0) & (t < chunks))
        def _():
            self.swap_any(t).wait_recv()

        def end_piece(j):
            return jnp.where(z == 0, 3 - j, j)

        def next_piece(j):
            return jnp.where(z == 1, 3 - j, j)

        last_piece = jnp.where(z == 2, 3, 0)
        if not self.inner:

            @pl.when(to_end)
            def _():
                for j in range(3):
                    self.start_base(t, end_piece(j), j)

        @pl.when(to_next)
        def _():
            for j in range(2):
                self.start_base(t - 1, next_piece(j), j)

        @pl.when(to_last)
        def _():
            self.start_base(t - 2, last_piece, 2)

        @self.when_summing(last)
        def _():
            self.start_base(t - 3, z, 3)

        if not self.inner:

            @pl.when(to_end)
            def _():
                for j in range(3):
                    p = end_piece(j)
                    target = jnp.where(z == 0, 1, 2)
                    place = jnp.where((z == 3) & (p == 2), 4, p)
                    self.send(t, j, t, p, target, place, False, 0)

        @pl.when(to_next)
        def _():
            for j in range(2):
                p = next_piece(j)
                target = jnp.where(z == 1, 2, 1)
                place = jnp.where((z == 2) & (p == 1), 4, p)
                self.send(t, j, t - 1, p, target, place, not self.inner, 1)

        @pl.when(to_last)
        def _():
            place = jnp.where(z == 1, 4, last_piece)
            self.send(t, 2, t - 2, last_piece, last_piece, place, True, 2)

        @pl.when(last)
        def _():
            q = t - 3

            @pl.when(q >= 1)
            def _():
                self.each_out(q - 1, lambda j, r: self.out_copy(j, r).wait())

            if self.inner:

                @pl.when(z == 0)
                def _():
                    self.out_v[...] = self.fetch(q, 4)

                @pl.when(z == 3)
                def _():
                    self.out_v[...] = self.fetch(q, 3)

                @pl.when(z == 1)
                def _():
                    got = self.fetch(q, 4)
                    self.out_v[...] = self.base(3) + got

                @pl.when(z == 2)
                def _():
                    got = self.fetch(q, 2)
                    self.out_v[...] = self.base(3) + got

            else:
                self.out_v[...] = self.base(3)

                @pl.when(z > 0)
                def _():
                    self.out_v[...] = self.out_v[...] + self.fetch(q, z)

                @pl.when(z < 3)
                def _():
                    self.out_v[...] = self.out_v[...] + self.fetch(q, 4)

            def put(j, r):
                if self.outs[j][1]:
                    self.turned_v[...] = self.out_v[...].T
                self.out_copy(j, r).start()

            self.each_out(q, put)

    def finish(self):
        self.each_out(self.chunks - 1, lambda j, r: self.out_copy(j, r).wait())

        def body(q, carry):
            self.swap_any(q).wait_send()
            return carry

        @self.when_summing()
        def _():
            lax.fori_loop(0, self.chunks, body, 0)

        assert self.chunks >= self.slots // 3

        @self.when_summing()
        def _():
            for slot in range(self.slots):
                self.hop(0, slot, self.z, 0).wait_send()


def line_bufs(shape, slots, turned):
    return [pltpu.VMEM((4,) + shape, BF16)] * 2 + [
        pltpu.VMEM((slots,) + shape, BF16),
        pltpu.VMEM(shape, F32),
        pltpu.VMEM(shape[::-1] if turned else (8, 128), F32),
    ]


def line_sems(q, slots):
    return [
        pltpu.SemaphoreType.DMA((4,)),
        pltpu.SemaphoreType.DMA((4,)),
        pltpu.SemaphoreType.DMA,
        pltpu.SemaphoreType.DMA((q,)),
        pltpu.SemaphoreType.DMA((q,)),
        pltpu.SemaphoreType.DMA((slots,)),
        pltpu.SemaphoreType.DMA((q, 5)),
    ]


def line_kernel(n_down, n_shared, parts, shift, *refs):
    def take(n):
        nonlocal refs
        taken, refs = refs[:n], refs[n:]
        return taken

    downs, shared = take(n_down), take(n_shared)
    three, part_out, out_part, mixed, normed_part, tokens, base, vec, gain, bias_add = take(10)
    out_down, out_gate, out_up, out_sdown = take(4)
    out_four = take(4)
    output, grad_tokens, vec_out = take(3)
    sib_a, att, sib_b, sib_c, out_in = take(5)
    bufs_a, bufs_b, bufs_c = take(5), take(5), take(5)
    recv_a, recv_b, recv_c = take(3)
    vec_in, vec_own, vec_sib, vec_line, vec_send, parts_v, mixed_v, sum_v = take(8)
    relay_x, relay_y, got_x, got_y, sum_x, sum_y, gain_v, grad_v, vec_v = take(9)
    sems_a, sems_b, sems_c = take(7), take(7), take(7)
    plane_send, plane_recv, local_sems, vec_send_sems, vec_recv_sems, out_send, out_recv, norm_send, norm_recv = take(9)

    a = Line(parts, False, downs, [(out_down.at[j], True) for j in range(n_down)], sib_a, recv_a, bufs_a, sems_a)
    b = Line(1, False, [att.at[j] for j in range(4)], [(v, True) for v in out_four], sib_b, recv_b, bufs_b, sems_b)
    c = Line(parts, shift, shared, [(out_gate, False), (out_up, False), (out_sdown, True)], sib_c, recv_c, bufs_c, sems_c)
    z, core = a.z, a.core
    f = lax.axis_index("fsdp")
    fx = f + 1 - 2 * lax.rem(f, 2)
    fy = f + 2 - 4 * (f // 2)
    fd = fx + 2 - 4 * (fx // 2)
    peers = (fx, fy, fd)
    sibling = a.at(z, 1 - core)
    width = three.shape[3] // 4

    barrier = pltpu.get_barrier_semaphore()
    for other in (sibling,) + tuple({"fsdp": p} for p in peers):
        pl.semaphore_signal(barrier, inc=1, device_id=other, device_id_type=MESH)

    @pl.when(z > 0)
    def _():
        pl.semaphore_signal(barrier, inc=1, device_id=a.at(z - 1, core), device_id_type=MESH)

    @pl.when(z < 3)
    def _():
        pl.semaphore_signal(barrier, inc=1, device_id=a.at(z + 1, core), device_id_type=MESH)

    @pl.when(a.is_end)
    def _():
        pl.semaphore_wait(barrier, 5)

    @pl.when(a.is_mid)
    def _():
        pl.semaphore_wait(barrier, 6)

    a.start_swaps()
    c.start_swaps()

    def cols(p):
        return pl.ds(pl.multiple_of(p * width, width), width)

    def to_owner(k, p):
        return pltpu.make_async_remote_copy(
            src_ref=three.at[:, :, :, cols(p)], dst_ref=att.at[pl.ds(0, 3), f],
            send_sem=plane_send.at[k], recv_sem=plane_recv.at[k],
            device_id={"fsdp": p}, device_id_type=MESH,
        )

    def vec_owner(k, p):
        return pltpu.make_async_remote_copy(
            src_ref=vec_v.at[p], dst_ref=vec_in.at[k],
            send_sem=vec_send_sems.at[k], recv_sem=vec_recv_sems.at[k],
            device_id={"fsdp": p}, device_id_type=MESH,
        )

    def out_owner(k, p):
        return pltpu.make_async_remote_copy(
            src_ref=out_part.at[k + 1], dst_ref=out_in.at[k],
            send_sem=out_send.at[k], recv_sem=out_recv.at[k],
            device_id={"fsdp": p}, device_id_type=MESH,
        )

    for k, p in enumerate(peers):
        to_owner(k, p).start()

    rows_half = mixed.shape[0] // 2
    low, high = pl.ds(0, rows_half), pl.ds(rows_half, rows_half)

    def norm_copy(n, src, dst, target):
        return pltpu.make_async_remote_copy(
            src_ref=src, dst_ref=dst, send_sem=norm_send.at[n], recv_sem=norm_recv.at[n],
            device_id={"fsdp": target}, device_id_type=MESH,
        )

    norm_copies = [
        norm_copy(0, normed_part.at[3, low], relay_x, fx),
        norm_copy(1, normed_part.at[3, high], relay_y, fy),
        norm_copy(2, normed_part.at[1, low], got_x.at[low], fx),
        norm_copy(3, normed_part.at[2, high], got_y.at[high], fy),
        norm_copy(4, sum_y, got_y.at[low], fy),
        norm_copy(5, sum_x, got_x.at[high], fx),
    ]
    for copy in norm_copies[:4]:
        copy.start()

    def relay():
        loads = [
            pltpu.make_async_copy(normed_part.at[2, low], sum_y, local_sems.at[3]),
            pltpu.make_async_copy(normed_part.at[1, high], sum_x, local_sems.at[4]),
        ]
        for copy in loads:
            copy.start()
        for copy in loads:
            copy.wait()
        norm_copies[0].wait_recv()
        sum_y[...] = (sum_y[...].astype(F32) + relay_x[...].astype(F32)).astype(BF16)
        norm_copies[4].start()
        norm_copies[1].wait_recv()
        sum_x[...] = (sum_x[...].astype(F32) + relay_y[...].astype(F32)).astype(BF16)
        norm_copies[5].start()

    def finish_norm():
        for copy in norm_copies[2:]:
            copy.wait_recv()
        step = parts_v.shape[1]
        gain_v[...] = jnp.zeros_like(gain_v)

        def body(i, carry):
            r = pl.ds(pl.multiple_of(i * step, step), step)
            loads = [
                pltpu.make_async_copy(normed_part.at[0, r], parts_v.at[0], local_sems.at[3]),
                pltpu.make_async_copy(tokens.at[r], parts_v.at[1], local_sems.at[4]),
                pltpu.make_async_copy(base.at[r], mixed_v, local_sems.at[5]),
            ]
            for copy in loads:
                copy.start()
            for copy in loads:
                copy.wait()
            total = parts_v[0].astype(F32) + (got_x[r].astype(F32) + got_y[r].astype(F32))
            back, grad_gain = norm_back(parts_v[1].astype(F32), gain[...], total)
            gain_v[...] = gain_v[...] + grad_gain
            grad_v[...] = mixed_v[...] + back
            copy = pltpu.make_async_copy(grad_v, grad_tokens.at[r], local_sems.at[6])
            copy.start()
            copy.wait()
            return carry

        lax.fori_loop(0, mixed.shape[0] // step, body, 0)
        copy = pltpu.make_async_copy(vec, vec_v, local_sems.at[2])
        copy.start()
        copy.wait()
        for k in range(4):
            vec_v[k, 0:1, :] = gain_v[:, k * width : (k + 1) * width]
        for k, p in enumerate(peers):
            vec_owner(k, p).start()

    keep = (
        pltpu.make_async_copy(three.at[:, :, :, cols(f)], att.at[pl.ds(0, 3), f], local_sems.at[0]),
        pltpu.make_async_copy(part_out, att.at[3], local_sems.at[1]),
    )
    for copy in keep:
        copy.start()

    def vec_swap():
        return pltpu.make_async_remote_copy(
            src_ref=vec_own, dst_ref=vec_sib, send_sem=vec_send_sems.at[3], recv_sem=vec_recv_sems.at[3],
            device_id=sibling, device_id_type=MESH,
        )

    def vec_hop(k, target):
        return pltpu.make_async_remote_copy(
            src_ref=vec_send.at[k], dst_ref=vec_line.at[k], send_sem=vec_send_sems.at[4 + k],
            recv_sem=vec_recv_sems.at[4 + k], device_id=a.at(target, core), device_id_type=MESH,
        )

    def finish_output():
        for k, p in enumerate(peers):
            out_owner(k, p).wait_recv()
        step = parts_v.shape[1]

        def body(i, carry):
            r = pl.ds(pl.multiple_of(i * step, step), step)
            loads = [pltpu.make_async_copy(out_part.at[0, r], parts_v.at[0], local_sems.at[3])]
            loads += [
                pltpu.make_async_copy(out_in.at[k, r], parts_v.at[k + 1], local_sems.at[4 + k]) for k in range(3)
            ]
            loads.append(pltpu.make_async_copy(mixed.at[r], mixed_v, local_sems.at[7]))
            for copy in loads:
                copy.start()
            for copy in loads:
                copy.wait()
            total = (parts_v[0].astype(F32) + parts_v[1].astype(F32)) + (
                parts_v[2].astype(F32) + parts_v[3].astype(F32)
            )
            sum_v[...] = (mixed_v[...] + total).astype(BF16)
            copy = pltpu.make_async_copy(sum_v, output.at[r], local_sems.at[8])
            copy.start()
            copy.wait()
            return carry

        lax.fori_loop(0, mixed.shape[0] // step, body, 0)

    def side_work(t):
        @pl.when(t == 3)
        def _():
            for k, p in enumerate(peers):
                to_owner(k, p).wait_recv()
            for copy in keep:
                copy.wait()
            b.start_swaps()

        @pl.when(t == 4)
        def _():
            relay()
            for k, p in enumerate(peers):
                out_owner(k, p).start()

        @pl.when(t == 5)
        def _():
            finish_norm()

        @pl.when(t == 6)
        def _():
            for k, p in enumerate(peers):
                vec_owner(k, p).wait_recv()
            vec_own[...] = (vec_v[f] + vec_in[0]) + (vec_in[1] + vec_in[2]) + bias_add[...]
            vec_swap().start()

        @pl.when(t == 7)
        def _():
            vec_swap().wait_recv()
            vec_sib[...] = vec_sib[...] + vec_own[...]

            @pl.when(z == 0)
            def _():
                vec_send[0] = vec_sib[...]
                vec_hop(0, 1).start()

            @pl.when(z == 3)
            def _():
                vec_send[1] = vec_sib[...]
                vec_hop(1, 2).start()

        @pl.when((t == 8) & (z == 1))
        def _():
            vec_hop(0, 1).wait_recv()
            vec_send[0] = vec_sib[...] + vec_line[0]
            vec_hop(0, 2).start()

        @pl.when((t == 8) & (z == 2))
        def _():
            vec_hop(1, 2).wait_recv()
            vec_send[1] = vec_sib[...] + vec_line[1]
            vec_hop(1, 1).start()

        @pl.when(t == 8)
        def _():
            finish_output()

        @pl.when((t == 9) & (z == 2))
        def _():
            vec_hop(0, 2).wait_recv()
            vec_send[0] = vec_sib[...] + vec_line[0]
            vec_hop(0, 3).start()
            vec_out[...] = vec_send[0] + vec_line[1]

        @pl.when((t == 9) & (z == 1))
        def _():
            vec_hop(1, 1).wait_recv()
            vec_send[1] = vec_sib[...] + vec_line[1]
            vec_hop(1, 0).start()
            vec_out[...] = vec_send[1] + vec_line[0]

        @pl.when((t == 10) & (z == 3))
        def _():
            vec_hop(0, 3).wait_recv()
            vec_out[...] = vec_sib[...] + vec_line[0]

        @pl.when((t == 10) & (z == 0))
        def _():
            vec_hop(1, 0).wait_recv()
            vec_out[...] = vec_sib[...] + vec_line[1]

    def loop(t, carry):
        c.turn(t)
        a.turn(t)
        b.turn(t - a.chunks)
        side_work(t)
        return carry

    turns = max(a.chunks + b.chunks, c.chunks) + 3
    assert turns == 11
    lax.fori_loop(0, turns, loop, 0)
    for copy in norm_copies:
        copy.wait_send()
    a.finish()
    b.finish()
    c.finish()
    for k, p in enumerate(peers):
        vec_owner(k, p).wait_send()
        to_owner(k, p).wait_send()
        out_owner(k, p).wait_send()
    vec_swap().wait_send()

    @pl.when(z < 3)
    def _():
        vec_hop(0, 3).wait_send()

    @pl.when(z > 0)
    def _():
        vec_hop(1, 0).wait_send()


def line_call(
    downs, shared, three, part_out, out_part, mixed, normed_part, tokens, base, vec, gain, bias_add, parts, shift, collective_id
):
    _, _, rows, cols = shared[0].shape
    m, s = len(downs), len(shared)
    _, _, share, features = three.shape
    width = features // 4
    own_rows = mixed.shape[0]
    r = rows // parts
    slots = 9
    small = (16, width)
    step = own_rows // 4

    def shape(*dims, dtype=BF16):
        return jax.ShapeDtypeStruct(dims, dtype)

    outs = pl.pallas_call(
        functools.partial(line_kernel, m, s, parts, shift),
        out_shape=(
            shape(m, cols, rows, dtype=F32),
            shape(rows, cols, dtype=F32),
            shape(rows, cols, dtype=F32),
            shape(cols, rows, dtype=F32),
            shape(width, share, dtype=F32),
            shape(width, share, dtype=F32),
            shape(width, share, dtype=F32),
            shape(width, share, dtype=F32),
            shape(own_rows, features),
            shape(own_rows, features, dtype=F32),
            shape(*small, dtype=F32),
            shape(m, 4, rows, cols),
            shape(4, 4, 2, share, width),
            shape(4, 4, share, width),
            shape(s, 4, rows, cols),
            shape(3, own_rows, features),
        ),
        in_specs=[ANY] * (m + s + 8) + [VMEM] * 2,
        out_specs=(ANY,) * 10 + (VMEM,) + (ANY,) * 5,
        scratch_shapes=line_bufs((r, cols), slots, True)
        + line_bufs((share, width), slots, True)
        + line_bufs((r, cols), slots, True)
        + [
            pltpu.VMEM((m, 5, rows, cols), BF16),
            pltpu.VMEM((4, 5, share, width), BF16),
            pltpu.VMEM((s, 5, rows, cols), BF16),
            pltpu.VMEM((3,) + small, F32),
            pltpu.VMEM(small, F32),
            pltpu.VMEM(small, F32),
            pltpu.VMEM((2,) + small, F32),
            pltpu.VMEM((2,) + small, F32),
            pltpu.VMEM((4, step, features), BF16),
            pltpu.VMEM((step, features), F32),
            pltpu.VMEM((step, features), BF16),
            pltpu.VMEM((own_rows // 2, features), BF16),
            pltpu.VMEM((own_rows // 2, features), BF16),
            pltpu.VMEM((own_rows, features), BF16),
            pltpu.VMEM((own_rows, features), BF16),
            pltpu.VMEM((own_rows // 2, features), BF16),
            pltpu.VMEM((own_rows // 2, features), BF16),
            pltpu.VMEM((1, features), F32),
            pltpu.VMEM((step, features), F32),
            pltpu.VMEM((4,) + small, F32),
        ]
        + line_sems(m * parts, slots)
        + line_sems(4, slots)
        + line_sems(s * parts, slots)
        + [
            pltpu.SemaphoreType.DMA((3,)),
            pltpu.SemaphoreType.DMA((3,)),
            pltpu.SemaphoreType.DMA((9,)),
            pltpu.SemaphoreType.DMA((6,)),
            pltpu.SemaphoreType.DMA((6,)),
            pltpu.SemaphoreType.DMA((3,)),
            pltpu.SemaphoreType.DMA((3,)),
            pltpu.SemaphoreType.DMA((6,)),
            pltpu.SemaphoreType.DMA((6,)),
        ],
        compiler_params=pltpu.CompilerParams(
            collective_id=collective_id, has_side_effects=True, vmem_limit_bytes=60 * MIB
        ),
    )(*downs, *shared, three, part_out, out_part, mixed, normed_part, tokens, base, vec, gain, bias_add)
    return outs[0], outs[1:4], outs[4:8], outs[8], outs[9], outs[10]


def plane_neighbours():
    f = lax.axis_index("fsdp")
    by_x = f + 1 - 2 * lax.rem(f, 2)
    by_y = f + 2 - 4 * (f // 2)
    return {"fsdp": by_x}, {"fsdp": by_y}


def plane_barrier(by_x, by_y):
    barrier = pltpu.get_barrier_semaphore()
    for other in (by_x, by_y):
        pl.semaphore_signal(barrier, inc=1, device_id=other, device_id_type=MESH)
    pl.semaphore_wait(barrier, 2)


class Side:
    block = 512

    def __init__(self, arrays, jobs, later=()):
        self.arrays, self.jobs, self.later = list(arrays), list(jobs), dict(later)
        self.operands = sorted({o for job in self.jobs for pair in job for o in pair}, key=str)

    def shape(self, operand):
        number, axis, _ = operand
        full = self.arrays[number].shape
        return full if axis is None else full[:axis] + full[axis + 1 :]

    def out_shapes(self):
        return [
            jax.ShapeDtypeStruct((self.shape(job[0][0])[-1], self.shape(job[0][1])[-1]), BF16)
            for job in self.jobs
        ]

    def scratch(self):
        stages = sorted({self.shape(job[0][1])[-1] for job in self.jobs})
        self.stage_of = {n: k for k, n in enumerate(stages)}
        return (
            [pltpu.VMEM(self.shape(o), BF16) for o in self.operands if o not in self.later]
            + [pltpu.VMEM((2, self.block, n), BF16) for n in stages]
            + [
                pltpu.SemaphoreType.DMA((max(1, len(self.operands)),)),
                pltpu.SemaphoreType.DMA((max(1, 2 * len(stages)),)),
            ]
        )

    def bind(self, ins, outs, scratch):
        holders = [o for o in self.operands if o not in self.later]
        n = len(holders)
        self.ins, self.outs = ins, outs
        self.bufs = [scratch[holders.index(self.later.get(o, o))] for o in self.operands]
        self.stages = scratch[n:-2]
        self.load_sems, self.out_sems = scratch[-2:]
        self.loaded, self.pending, self.turn_of = set(), {}, {}
        self.units = [
            (j, k)
            for j, job in enumerate(self.jobs)
            for k in range(self.shape(job[0][0])[-1] // self.block)
        ]

    def load(self, k):
        number, axis, entry = self.operands[k]
        ref = self.ins[number]
        if axis is not None:
            ref = ref.at[(slice(None),) * axis + (entry,)]
        return pltpu.make_async_copy(ref, self.bufs[k], self.load_sems.at[k])

    def begin(self):
        for o in [o for job in self.jobs for pair in job for o in pair]:
            k = self.operands.index(o)
            if k not in self.loaded and o not in self.later:
                self.loaded.add(k)
                self.load(k).start()
        self.loaded = set()

    def step(self, number):
        for _ in range(number):
            if not self.units:
                return
            j, block = self.units.pop(0)
            pairs = [tuple(self.operands.index(o) for o in pair) for pair in self.jobs[j]]
            for k in [k for pair in pairs for k in pair]:
                if k not in self.loaded:
                    self.loaded.add(k)
                    self.load(k).wait()
            n = self.shape(self.jobs[j][0][1])[-1]
            stage = self.stage_of[n]
            slot = self.turn_of.get(stage, 0)
            self.turn_of[stage] = 1 - slot
            if (stage, slot) in self.pending:
                self.pending.pop((stage, slot)).wait()
            rows = pl.ds(block * self.block, self.block)
            total = None
            for ka, kb in pairs:
                left = self.bufs[ka][..., rows].reshape(-1, self.block)
                part = rows_dot(left, self.bufs[kb][...].reshape(-1, n))
                total = part if total is None else total + part
            self.stages[stage][slot] = total.astype(BF16)
            copy = pltpu.make_async_copy(
                self.stages[stage].at[slot], self.outs[j].at[rows], self.out_sems.at[2 * stage + slot]
            )
            copy.start()
            self.pending[(stage, slot)] = copy
            if not self.units or self.units[0][0] != j:
                for o in [o for pair in self.jobs[j] for o in pair]:
                    for k, heir in enumerate(self.operands):
                        if self.later.get(heir) == o:
                            self.load(k).start()

    def end(self):
        self.step(len(self.units))
        for copy in self.pending.values():
            copy.wait()


def mid_kernel(middle, chunks, gathers, n_in, n_out, side, *refs):
    n_side, n_jobs = len(side.arrays), len(side.jobs)
    partial, ins = refs[0], refs[1 : 1 + n_in]
    side_ins, refs = refs[1 + n_in : 1 + n_in + n_side], refs[1 + n_in + n_side :]
    outs, refs = refs[:n_out], refs[n_out:]
    gathered = None
    if gathers:
        gathered, refs = refs[0], refs[1:]
    side_outs, refs = refs[:n_jobs], refs[n_jobs:]
    relay_x, relay_y, got_x, got_y, sum_x, sum_y, own, send_sems, recv_sems, local_sems = refs[:10]
    if n_jobs:
        side.bind(side_ins, side_outs, refs[10:])
    rows = partial.shape[1]
    r = rows // chunks
    h = r // 2
    by_x, by_y = plane_neighbours()
    plane_barrier(by_x, by_y)

    def copy(i, kind, src, dst, target):
        return pltpu.make_async_remote_copy(
            src_ref=src, dst_ref=dst, send_sem=send_sems.at[i, kind], recv_sem=recv_sems.at[i, kind],
            device_id=target, device_id_type=MESH,
        )

    def sends(i):
        lo, hi = pl.ds(i * r, h), pl.ds(i * r + h, h)
        half = pl.ds(i * h, h)
        made = {
            0: lambda: copy(i, 0, partial.at[3, lo], relay_x.at[half], by_x),
            1: lambda: copy(i, 1, partial.at[3, hi], relay_y.at[half], by_y),
            2: lambda: copy(i, 2, partial.at[1, lo], got_x.at[lo], by_x),
            3: lambda: copy(i, 3, partial.at[2, hi], got_y.at[hi], by_y),
            4: lambda: copy(i, 4, sum_y.at[half], got_y.at[lo], by_y),
            5: lambda: copy(i, 5, sum_x.at[half], got_x.at[hi], by_x),
        }
        if gathers:
            made |= {
                6: lambda: copy(i, 6, own.at[lo], gathered.at[1, lo], by_x),
                7: lambda: copy(i, 7, own.at[hi], gathered.at[2, hi], by_y),
                8: lambda: copy(i, 8, own.at[hi], gathered.at[1, hi], by_x),
                9: lambda: copy(i, 9, own.at[lo], gathered.at[2, lo], by_y),
                10: lambda: copy(i, 10, gathered.at[1, lo], gathered.at[3, lo], by_y),
                11: lambda: copy(i, 11, gathered.at[2, hi], gathered.at[3, hi], by_x),
            }
        return made

    def keep(i):
        span = pl.ds(i * r, r)
        return pltpu.make_async_copy(own.at[span], gathered.at[0, span], local_sems.at[i])

    def stage(n, i):
        s = sends(i)
        lo, hi = pl.ds(i * r, h), pl.ds(i * r + h, h)
        half, span = pl.ds(i * h, h), pl.ds(i * r, r)
        if n == 0:
            for kind in (0, 1, 2, 3):
                s[kind]().start()
        elif n == 1:
            s[0]().wait_recv()
            sum_y[half] = (partial[2, lo].astype(F32) + relay_x[half].astype(F32)).astype(BF16)
            s[4]().start()
            s[1]().wait_recv()
            sum_x[half] = (partial[1, hi].astype(F32) + relay_y[half].astype(F32)).astype(BF16)
            s[5]().start()
        elif n == 2:
            for kind in (2, 3, 4, 5):
                s[kind]().wait_recv()
            total = partial[0, span].astype(F32) + (got_x[span].astype(F32) + got_y[span].astype(F32))
            given = middle(total, span, ins, outs)
            if gathers:
                own[span] = given
                for kind in (6, 7, 8, 9):
                    s[kind]().start()
                keep(i).start()
        elif n == 3 and gathers:
            s[6]().wait_recv()
            s[10]().start()
            s[7]().wait_recv()
            s[11]().start()
        elif n == 4:
            if gathers:
                for kind in (8, 9, 10, 11):
                    s[kind]().wait_recv()
                keep(i).wait()
            for kind in s:
                s[kind]().wait_send()

    turns = chunks + 4
    if n_jobs:
        side.begin()
        each = len(side.units) / (5 * chunks)
    steps = done = 0
    for t in range(turns):
        for n in range(5):
            if 0 <= t - n < chunks:
                stage(n, t - n)
                steps += 1
                if n_jobs and int(steps * each) > done:
                    side.step(int(steps * each) - done)
                    done = int(steps * each)
    if n_jobs:
        side.end()


def mid_call(middle, partial, ins, out_shapes, gathers, side, collective_id, chunks=4):
    _, rows, cols = partial.shape
    outs = tuple(out_shapes)
    specs = (VMEM,) * len(outs)
    if gathers:
        outs += (jax.ShapeDtypeStruct((4, rows, cols), BF16),)
        specs += (ANY,)
    outs += tuple(side.out_shapes())
    specs += (ANY,) * len(side.jobs)
    return pl.pallas_call(
        functools.partial(mid_kernel, middle, chunks, gathers, len(ins), len(out_shapes), side),
        out_shape=outs,
        in_specs=[VMEM] * (1 + len(ins)) + [ANY] * len(side.arrays),
        out_specs=specs,
        scratch_shapes=[
            pltpu.VMEM((rows // 2, cols), BF16),
            pltpu.VMEM((rows // 2, cols), BF16),
            pltpu.VMEM((rows, cols), BF16),
            pltpu.VMEM((rows, cols), BF16),
            pltpu.VMEM((rows // 2, cols), BF16),
            pltpu.VMEM((rows // 2, cols), BF16),
            pltpu.VMEM((rows, cols), BF16),
            pltpu.SemaphoreType.DMA((chunks, 12)),
            pltpu.SemaphoreType.DMA((chunks, 12)),
            pltpu.SemaphoreType.DMA((chunks,)),
        ]
        + (side.scratch() if side.jobs else []),
        compiler_params=pltpu.CompilerParams(
            collective_id=collective_id, has_side_effects=True, vmem_limit_bytes=60 * MIB
        ),
    )(partial, *ins, *side.arrays)


def start_kernel(
    tokens, small, marks, w_q, w_k, w_v,
    tokens_all, small_all, marks_all, w_cols, relay,
    send_sems, recv_sems, local_sems,
):
    f = lax.axis_index("fsdp")
    g = lax.axis_index("grp")
    core = lax.rem(g, 2)
    rows = tokens.shape[0]
    depth = w_q.shape[0]
    width = w_q.shape[1] // 4
    by_x, by_y = plane_neighbours()
    fx, fy = by_x["fsdp"], by_y["fsdp"]
    fd = fx + 2 - 4 * (fx // 2)
    z = g // 2
    odd = lax.rem(z, 2)
    by_d, sibling = {"fsdp": fd}, {"grp": g + 1 - 2 * core}
    by_z = {"grp": g + 2 - 4 * odd}
    barrier = pltpu.get_barrier_semaphore()
    for other in (by_x, by_y, by_d, sibling, by_z):
        pl.semaphore_signal(barrier, inc=1, device_id=other, device_id_type=MESH)
    pl.semaphore_wait(barrier, 5)

    def copy(n, src, dst, target):
        return pltpu.make_async_remote_copy(
            src_ref=src, dst_ref=dst, send_sem=send_sems.at[n], recv_sem=recv_sems.at[n],
            device_id=target, device_id_type=MESH,
        )

    def columns(j):
        return pl.ds(pl.multiple_of(j * width, width), width)

    quarter = depth // 4
    eighth = quarter // 2
    here, there = 2 * odd + core, 2 * (1 - odd) + core

    def block_rows(owner, q):
        return pl.ds(pl.multiple_of(owner * depth + q * quarter, quarter), quarter)

    mine = pl.ds(pl.multiple_of(here * quarter, quarter), quarter)
    all_sends = []

    def go(c):
        c.start()
        all_sends.append(c)
        return c

    waits = []
    n = 0
    for k, target in ((1, by_x), (2, by_y), (3, by_d)):
        waits.append(go(copy(n, small, small_all.at[k], target)))
        waits.append(go(copy(n + 1, marks, marks_all.at[k], target)))
        n += 2
    locals_ = [
        pltpu.make_async_copy(small, small_all.at[0], local_sems.at[0]),
        pltpu.make_async_copy(marks, marks_all.at[0], local_sems.at[1]),
        pltpu.make_async_copy(tokens, tokens_all.at[0], local_sems.at[2]),
    ]
    for j, w in enumerate((w_q, w_k, w_v)):
        locals_.append(
            pltpu.make_async_copy(
                w.at[:, columns(f)],
                w_cols.at[pl.ds(pl.multiple_of(f * depth, depth), depth), pl.ds(j * width, width)],
                local_sems.at[3 + j],
            )
        )
    for c in locals_:
        c.start()

    first = pl.ds(pl.multiple_of(here * quarter, eighth), eighth)
    second = pl.ds(pl.multiple_of(here * quarter + eighth, eighth), eighth)
    relays_x, relays_y, direct_x, direct_y = [], [], [], []
    for j, w in enumerate((w_q, w_k, w_v)):
        relays_x.append(go(copy(n, w.at[first, columns(fd)], relay.at[0, j], by_x)))
        relays_y.append(go(copy(n + 1, w.at[second, columns(fd)], relay.at[1, j], by_y)))
        n += 2
    for j, w in enumerate((w_q, w_k, w_v)):
        place = w_cols.at[block_rows(f, here), pl.ds(j * width, width)]
        direct_x.append(go(copy(n, w.at[mine, columns(fx)], place, by_x)))
        direct_y.append(go(copy(n + 1, w.at[mine, columns(fy)], place, by_y)))
        n += 2
    low, high = pl.ds(0, rows // 2), pl.ds(rows // 2, rows // 2)
    t_x0 = go(copy(n, tokens.at[low], tokens_all.at[1, low], by_x))
    t_y1 = go(copy(n + 1, tokens.at[high], tokens_all.at[2, high], by_y))
    t_x1 = go(copy(n + 2, tokens.at[high], tokens_all.at[1, high], by_x))
    t_y0 = go(copy(n + 3, tokens.at[low], tokens_all.at[2, low], by_y))
    n += 4
    forwarded = []
    for j in range(3):
        relays_x[j].wait_recv()
        forwarded.append(
            go(copy(
                n, relay.at[0, j],
                w_cols.at[pl.ds(pl.multiple_of(fx * depth + here * quarter, eighth), eighth), pl.ds(j * width, width)],
                by_y,
            ))
        )
        relays_y[j].wait_recv()
        forwarded.append(
            go(copy(
                n + 1, relay.at[1, j],
                w_cols.at[
                    pl.ds(pl.multiple_of(fy * depth + here * quarter + eighth, eighth), eighth), pl.ds(j * width, width)
                ],
                by_x,
            ))
        )
        n += 2
    shares, lent = [], []

    def share(owner, q, target):
        nonlocal n
        place = w_cols.at[block_rows(owner, q)]
        c = go(copy(n, place, place, target))
        n += 1
        return c

    def fetched(owner):
        lent.append(share(owner, here, by_z))
        shares.append(share(owner, here, sibling))

    for c in direct_x:
        c.wait_recv()
    fetched(fx)
    for c in direct_y:
        c.wait_recv()
    fetched(fy)
    t_x0.wait_recv()
    t_d0 = go(copy(n, tokens_all.at[1, low], tokens_all.at[3, low], by_y))
    t_y1.wait_recv()
    t_d1 = go(copy(n + 1, tokens_all.at[2, high], tokens_all.at[3, high], by_x))
    n += 2
    for c in forwarded:
        c.wait_recv()
    fetched(fd)
    for owner, c in zip((fx, fy, fd), lent):
        c.wait_recv()
        shares.append(share(owner, there, sibling))
    for c in waits + shares + [t_x1, t_y0, t_d0, t_d1]:
        c.wait_recv()
    for c in locals_:
        c.wait()
    for c in all_sends:
        c.wait_send()


def start_call(tokens, small, marks, w_q, w_k, w_v, collective_id):
    depth, features = w_q.shape
    width = features // 4
    n = 6 + 6 + 6 + 4 + 6 + 2 + 9
    return pl.pallas_call(
        start_kernel,
        out_shape=(
            jax.ShapeDtypeStruct((4,) + tokens.shape, tokens.dtype),
            jax.ShapeDtypeStruct((4,) + small.shape, small.dtype),
            jax.ShapeDtypeStruct((4,) + marks.shape, marks.dtype),
            jax.ShapeDtypeStruct((4 * depth, 3 * width), BF16),
            jax.ShapeDtypeStruct((2, 3, depth // 8, width), BF16),
        ),
        in_specs=[ANY] * 6,
        out_specs=(ANY,) * 5,
        scratch_shapes=[
            pltpu.SemaphoreType.DMA((n,)),
            pltpu.SemaphoreType.DMA((n,)),
            pltpu.SemaphoreType.DMA((6,)),
        ],
        compiler_params=pltpu.CompilerParams(
            collective_id=collective_id, has_side_effects=True, vmem_limit_bytes=16 * MIB
        ),
    )(tokens, small, marks, w_q, w_k, w_v)[:4]


def turn_half(x):
    return pltpu.roll(x, HEAD_DIM // 2, 1)


def hidden_bias(of_keys, of_queries):
    key_segment, key_position = of_keys[0], of_keys[4]
    seen = (
        (key_segment == of_queries[1]) | (key_segment == of_queries[2]) | (key_segment == of_queries[3])
    ) & (key_position <= of_queries[4])
    return jnp.where(seen, 0.0, MASK_FILL)


class Spread:
    def __init__(self, own, everyone, send_sems, recv_sems, local_sem):
        self.everyone, self.send_sems, self.recv_sems = everyone, send_sems, recv_sems
        self.by_x, self.by_y = plane_neighbours()
        rows = own.shape[0]
        low, high = pl.ds(0, rows // 2), pl.ds(rows // 2, rows // 2)
        self.kept = pltpu.make_async_copy(own, everyone.at[0], local_sem)
        self.first = [
            self.copy(0, own.at[low], (1, low), self.by_x),
            self.copy(1, own.at[high], (2, high), self.by_y),
            self.copy(2, own.at[high], (1, high), self.by_x),
            self.copy(3, own.at[low], (2, low), self.by_y),
        ]
        self.second = [
            self.copy(4, everyone.at[1, low], (3, low), self.by_y),
            self.copy(5, everyone.at[2, high], (3, high), self.by_x),
        ]

    def copy(self, n, src, place, target):
        return pltpu.make_async_remote_copy(
            src_ref=src, dst_ref=self.everyone.at[place], send_sem=self.send_sems.at[n],
            recv_sem=self.recv_sems.at[n], device_id=target, device_id_type=MESH,
        )

    def begin(self):
        plane_barrier(self.by_x, self.by_y)
        for c in self.first:
            c.start()
        self.kept.start()

    def middle(self):
        for got, onward in zip(self.first[:2], self.second):
            got.wait_recv()
            onward.start()

    def end(self):
        for c in self.first[2:] + self.second:
            c.wait_recv()
        for c in self.first + self.second:
            c.wait_send()
        self.kept.wait()


def attend_kernel(
    tokens, gain, w_cols, bias, w_out, cosine, sine, mark_cols, mark_rows, *refs
):
    spread = None
    if len(refs) > 5:
        own, refs = refs[0], refs[1:]
        normed, three, attended, branch, everyone, mask = refs[:6]
        spread = Spread(own, everyone, *refs[6:])
        spread.begin()
    else:
        normed, three, attended, branch, mask = refs
    count = tokens.shape[0]
    width = w_out.shape[0]
    scale = HEAD_DIM**-0.5
    step = 256
    rows_of = [mark_rows[j : j + 1, :] for j in range(5)]
    for a, n in pieces(count, step):
        s = pl.ds(a, n)
        x = tokens[s, :].astype(F32)
        factor = lax.rsqrt(jnp.mean(x * x, axis=-1, keepdims=True) + EPSILON)
        normed[s, :] = (x * factor * gain[...]).astype(BF16)
        cols_of = [mark_cols[s, j : j + 1] for j in range(5)]
        mask[s, :] = hidden_bias(rows_of, cols_of)
    for b, m in pieces(3 * width, 256):
        c = pl.ds(b, m)
        pre = plain_dot(normed[...], w_cols[:, c]) + bias[:, c]
        if b < 2 * width:
            for d in range(0, m, HEAD_DIM):
                x = pre[:, d : d + HEAD_DIM]
                three[:, b + d : b + d + HEAD_DIM] = (
                    x * cosine[...] + turn_half(x) * sine[...]
                ).astype(BF16)
        else:
            three[:, c] = pre.astype(BF16)
    if spread:
        spread.middle()
    for h in range(width // HEAD_DIM):
        q_cols = pl.ds(h * HEAD_DIM, HEAD_DIM)
        k_cols = pl.ds(width + h * HEAD_DIM, HEAD_DIM)
        v_cols = pl.ds(2 * width + h * HEAD_DIM, HEAD_DIM)
        for a, n in pieces(count, step):
            s = pl.ds(a, n)
            scores = trans_dot(three[s, q_cols], three[:, k_cols]) + mask[s, :]
            peak = jnp.max(scores, axis=-1, keepdims=True)
            expo = jnp.exp((scores - peak) * scale)
            total = jnp.sum(expo, axis=-1, keepdims=True)
            weights = (expo * (1.0 / total)).astype(BF16)
            attended[s, q_cols] = plain_dot(weights, three[:, v_cols]).astype(BF16)
    for b, m in pieces(w_out.shape[1], 512):
        c = pl.ds(b, m)
        branch[:, c] = plain_dot(attended[...], w_out[:, c]).astype(BF16)
    if spread:
        spread.end()


def attend_call(tokens, gain, w_cols, bias, w_out, cosine, sine, mark_cols, mark_rows, own=None, collective_id=None):
    count, features = tokens.shape
    width = w_out.shape[0]

    def shape(cols):
        return jax.ShapeDtypeStruct((count, cols), BF16)

    ins = [tokens, gain, w_cols, bias, w_out, cosine, sine, mark_cols, mark_rows]
    in_specs, out_specs = [VMEM] * 9, (VMEM,) * 4
    out_shape = (shape(features), shape(3 * width), shape(width), shape(features))
    scratch = [pltpu.VMEM((count, count), F32)]
    params = {}
    if own is not None:
        ins.append(own)
        in_specs.append(VMEM)
        out_specs += (VMEM,)
        out_shape += (jax.ShapeDtypeStruct((4,) + own.shape, own.dtype),)
        scratch += [pltpu.SemaphoreType.DMA((6,)), pltpu.SemaphoreType.DMA((6,)), pltpu.SemaphoreType.DMA]
        params = {"collective_id": collective_id, "has_side_effects": True}
    return pl.pallas_call(
        attend_kernel,
        in_specs=in_specs,
        out_specs=out_specs,
        out_shape=out_shape,
        scratch_shapes=scratch,
        compiler_params=pltpu.CompilerParams(vmem_limit_bytes=60 * MIB, **params),
    )(*ins)


def attend_back_kernel(
    grad, w_out, three, w_cols, cosine, sine, mark_cols, mark_rows,
    grad_three, partial, grad_bias, mask, grad_att,
):
    count = grad.shape[0]
    width = w_out.shape[0]
    scale = HEAD_DIM**-0.5
    step = 256
    for b, m in pieces(width, 256):
        c = pl.ds(b, m)
        grad_att[:, c] = trans_dot(grad[...], w_out[c, :]).astype(BF16)
    rows_of = [mark_rows[j : j + 1, :] for j in range(5)]
    for a, n in pieces(count, step):
        s = pl.ds(a, n)
        mask[s, :] = hidden_bias([mark_cols[s, j : j + 1] for j in range(5)], rows_of)
    for h in range(width // HEAD_DIM):
        q_cols = pl.ds(h * HEAD_DIM, HEAD_DIM)
        k_cols = pl.ds(width + h * HEAD_DIM, HEAD_DIM)
        v_cols = pl.ds(2 * width + h * HEAD_DIM, HEAD_DIM)
        grad_k = grad_v = None
        for a, n in pieces(count, step):
            s = pl.ds(a, n)
            query, g = three[s, q_cols], grad_att[s, q_cols]
            scores = trans_dot(three[:, k_cols], query) + mask[:, s]
            peak = jnp.max(scores, axis=0, keepdims=True)
            expo = jnp.exp((scores - peak) * scale)
            probs = expo * (1.0 / jnp.sum(expo, axis=0, keepdims=True))
            weight_grad = trans_dot(three[:, v_cols], g)
            diagonal = jnp.sum(probs * weight_grad, axis=0, keepdims=True)
            score_grad = (probs * (weight_grad - diagonal)).astype(BF16)
            part_v = plain_dot(probs.astype(BF16), g)
            part_k = plain_dot(score_grad, query)
            grad_v = part_v if grad_v is None else grad_v + part_v
            grad_k = part_k if grad_k is None else grad_k + part_k
            grad_q = rows_dot(score_grad, three[:, k_cols]) * scale
            grad_three[s, q_cols] = (
                grad_q * cosine[s, :] - turn_half(grad_q) * sine[s, :]
            ).astype(BF16)
        grad_k = grad_k * scale
        grad_three[:, k_cols] = (grad_k * cosine[...] - turn_half(grad_k) * sine[...]).astype(BF16)
        grad_three[:, v_cols] = grad_v.astype(BF16)
    for b, m in pieces(3 * width, 512):
        c = pl.ds(b, m)
        grad_bias[:, c] = jnp.sum(grad_three[:, c].astype(F32), axis=0, keepdims=True)
    for b, m in pieces(w_cols.shape[0], 512):
        c = pl.ds(b, m)
        partial[:, c] = trans_dot(grad_three[...], w_cols[c, :]).astype(BF16)


def attend_back_call(grad, w_out, three, w_cols, cosine, sine, mark_cols, mark_rows):
    count, features = grad.shape
    width = w_out.shape[0]

    def shape(rows, cols, dtype=BF16):
        return jax.ShapeDtypeStruct((rows, cols), dtype)

    return pl.pallas_call(
        attend_back_kernel,
        in_specs=[VMEM] * 8,
        out_specs=(VMEM,) * 3,
        out_shape=(shape(count, 3 * width), shape(count, features), shape(1, 3 * width, F32)),
        scratch_shapes=[pltpu.VMEM((count, count), F32), pltpu.VMEM((count, width), BF16)],
        compiler_params=pltpu.CompilerParams(vmem_limit_bytes=60 * MIB),
    )(grad, w_out, three, w_cols, cosine, sine, mark_cols, mark_rows)


class Load:
    def __init__(self, value):
        self.value = value

    def __getitem__(self, place):
        return self.value[place]


class Store:
    def __init__(self, shape):
        self.value = jnp.zeros(shape.shape, shape.dtype)

    def __getitem__(self, place):
        return self.value[place]

    def __setitem__(self, place, value):
        self.value = value.astype(self.value.dtype)


def first_middle(total, span, ins, outs):
    tokens, gain = ins
    mixed = tokens[span].astype(F32) + total
    factor = lax.rsqrt(jnp.mean(mixed * mixed, axis=-1, keepdims=True) + EPSILON)
    outs[0][span] = mixed
    return (mixed * factor * gain[...]).astype(BF16)


def norm_back(values, gain, grad):
    factor = lax.rsqrt(jnp.mean(values * values, axis=-1, keepdims=True) + EPSILON)
    weighted = gain * grad
    back = factor * weighted - values * (factor * factor * factor) * jnp.mean(
        weighted * values, axis=-1, keepdims=True
    )
    return back, jnp.sum(grad * values * factor, axis=0, keepdims=True)


def back_middle(total, span, ins, outs):
    values, gain, base = ins
    back, grad_gain = norm_back(values[span].astype(F32), gain[...], total)
    grad = base[span].astype(F32) + back
    outs[0][span] = grad
    outs[1][span if span == slice(None) else pl.ds(span.start // span.size, 1)] = grad_gain
    return grad.astype(BF16)


class Wires:
    def __init__(self, mesh):
        self.nf = mesh.shape["fsdp"]
        self.ng = mesh.shape["grp"]
        self.nz = self.ng // 2
        self.fast = self.nf == 4 and self.ng == 8
        self.chunks = 4 if self.fast else 1

    def xor(self, value, k):
        return lax.ppermute(value, "fsdp", [(i, i ^ k) for i in range(self.nf)])

    def inwards(self, value):
        if not self.fast:
            return None
        return lax.ppermute(value, "grp", [(0, 2), (1, 3), (6, 4), (7, 5)])

    def gather_list(self, value):
        return [value] + [self.xor(value, k) for k in range(1, self.nf)]

    def gather(self, value):
        return jnp.concatenate(self.gather_list(value), axis=0)

    def scatter_sum(self, value):
        rows = value.shape[0] // self.nf
        total = value[:rows].astype(F32)
        for k in range(1, self.nf):
            part = value[k * rows : (k + 1) * rows].astype(BF16)
            total = total + self.xor(part, k).astype(F32)
        return total

    def reduce_background(self, partial):
        return lax.psum_scatter(partial, "grp", scatter_dimension=0, tiled=True)

    def gather_start(self, tokens, small, marks, weights):
        if self.fast:
            return start_call(tokens, small, marks, *weights, 1)
        cols = jnp.concatenate(
            [lax.all_to_all(w, "fsdp", split_axis=1, concat_axis=0, tiled=True) for w in weights],
            axis=1,
        )
        return tuple(jnp.stack(self.gather_list(v)) for v in (tokens, small, marks)) + (cols,)

    def middle(self, body, partial, ins, out_shapes, gathers, number, arrays=(), jobs=(), later=()):
        nf = self.nf
        rows, cols = partial.shape[0] // nf, partial.shape[1]
        if self.fast:
            side = Side(arrays, jobs, later)
            return mid_call(body, partial.reshape(nf, rows, cols), ins, out_shapes, gathers, side, number)
        total = self.scatter_sum(partial)
        outs = [Store(s) for s in out_shapes]
        given = body(total, slice(None), [Load(v) for v in ins], outs)
        results = tuple(o.value for o in outs)
        if gathers:
            results += (jnp.stack(self.gather_list(given)),)

        def operand(o):
            number, axis, entry = o
            v = arrays[number] if axis is None else lax.index_in_dim(arrays[number], entry, axis, False)
            return v.reshape(-1, v.shape[-1])

        return results + tuple(
            sum(rows_dot(operand(a), operand(b)) for a, b in job).astype(BF16) for job in jobs
        )

    def last_sums(
        self, downs, shared, part_three, part_output, out_part, mixed, normed_part, tokens, base, vec, gain, bias_add, number
    ):
        nf, ng, nz = self.nf, self.ng, self.nz
        features, width = part_output.shape
        share = features // ng
        if self.fast:
            outs = line_call(
                [v.reshape(nz, 2, share, -1) for v in downs],
                [v.reshape(nz, 2, share, -1) for v in shared],
                part_three.reshape(3, 2, share, features),
                part_output.reshape(nz, 2, share, width),
                out_part.reshape(nf, -1, features),
                mixed,
                normed_part.reshape(nf, -1, features),
                tokens,
                base,
                vec.reshape(16, nf, width).transpose(1, 0, 2),
                gain,
                bias_add,
                2,
                True,
                number,
            )
            return outs
        down = jnp.stack([self.reduce_background(v).astype(F32).T for v in downs], axis=0)
        sums = [self.reduce_background(v).astype(F32) for v in shared]
        three = lax.all_to_all(
            part_three.reshape(3, width, features), "fsdp", split_axis=2, concat_axis=1, tiled=True
        )
        four = jnp.concatenate([three, part_output[None]], axis=0)
        four = lax.psum_scatter(four, "grp", scatter_dimension=1, tiled=True).astype(F32)
        back, grad_gain = norm_back(tokens.astype(F32), gain, self.scatter_sum(normed_part))
        vec = jnp.concatenate([grad_gain, vec[1:]], axis=0)
        vec = lax.psum_scatter(vec, "fsdp", scatter_dimension=1, tiled=True) + bias_add
        output = (mixed + self.scatter_sum(out_part)).astype(BF16)
        return down, (sums[0], sums[1], sums[2].T), four.transpose(0, 2, 1), output, base + back, lax.psum(vec, "grp")


def on_device(
    wires,
    tokens,
    cotangent,
    segment,
    ancestry,
    position,
    routes,
    attn_gain,
    w_query,
    w_key,
    w_value,
    b_query,
    b_key,
    b_value,
    w_output,
    moe_gain,
    w_router,
    shared_switch,
    shared_gate,
    shared_up,
    shared_down,
    expert_gate,
    routed_up_weight,
    expert_down,
):
    nf, ng = wires.nf, wires.ng
    me = lax.axis_index("fsdp")
    rows_dev, features = tokens.shape
    count = rows_dev * nf
    width = features // nf
    experts = w_router.shape[1]
    local_experts = experts // nf
    capacity = 5 * rows_dev // 8
    choose = routes.shape[1]

    small = jnp.concatenate([attn_gain[None], moe_gain[None], w_router.T, shared_switch[None]], axis=0)
    small = jnp.pad(small, ((0, -small.shape[0] % 16), (0, 0)))
    marks = jnp.concatenate([segment[None], ancestry.T, position[None], routes.T], axis=0)
    marks = jnp.pad(marks, ((0, -marks.shape[0] % 16), (0, 0)))
    tokens_all, small_blocks, marks_all, w_cols = wires.gather_start(
        tokens, small, marks, (w_query, w_key, w_value)
    )
    tokens_all = tokens_all.reshape(count, features)
    small_all = jnp.concatenate(
        [lax.dynamic_index_in_dim(small_blocks, me ^ i, 0, keepdims=False) for i in range(nf)], axis=1
    )
    gain_one = small_all[0:1].astype(F32)
    gain_two = small_all[1:2].astype(F32)
    heads_rows = small_all[2 : experts + 3]
    mark_rows = jnp.concatenate([marks_all[k] for k in range(nf)], axis=1)
    mark_cols = mark_rows.T
    routes_rows = mark_rows[5 : 5 + choose]


    halfway = HEAD_DIM // 2
    freqs = ROPE_BASE ** (-(jnp.arange(halfway, dtype=F32) * 2.0 / HEAD_DIM))
    turns = mark_cols[:, 4:5].astype(F32) * jnp.concatenate([freqs, freqs])[None, :]
    cosine = jnp.cos(turns)
    sine = jnp.sin(turns) * jnp.where(jnp.arange(HEAD_DIM) < halfway, -1.0, 1.0)[None, :]
    bias = jnp.concatenate([b_query, b_key, b_value]).astype(F32)[None]
    operands = (tokens_all, gain_one, w_cols, bias, w_output, cosine, sine, mark_cols, mark_rows)
    if wires.fast:
        normed, three, attended, branch, cot_all = attend_call(*operands, cotangent, 6)
        cot_all = cot_all.reshape(count, features)
    else:
        normed, three, attended, branch = attend_call(*operands)
        cot_all = wires.gather(cotangent)

    numbers = me * local_experts + jnp.arange(local_experts, dtype=jnp.int32)
    named = jnp.any(routes_rows[None] == numbers[:, None, None], axis=1)
    named = named.reshape(local_experts, nf, rows_dev)
    earlier = (jnp.arange(rows_dev)[None, :] < jnp.arange(rows_dev)[:, None]).astype(BF16)
    slot = jnp.einsum("ts,ebs->bet", earlier, named.astype(BF16), preferred_element_type=F32)
    slot = jnp.where(named.transpose(1, 0, 2), slot.astype(jnp.int32), -1)
    pick = jnp.arange(capacity, dtype=jnp.int32)[None, None, :, None] == slot[:, :, None, :]

    cot_other = wires.inwards(cot_all)
    mixed, moe_blocks = wires.middle(
        first_middle,
        branch,
        (tokens, gain_two),
        (jax.ShapeDtypeStruct((rows_dev, features), F32),),
        True,
        2,
    )
    moe_in = moe_blocks.reshape(count, features)
    moe_other = wires.inwards(moe_in)

    rows_in, rows_cot, gate, pick_b, router_probs, opener = dispatch_call(
        moe_in, cot_all, slot, heads_rows, capacity
    )
    if wires.fast:
        rows_cot, cot_other = lax.optimization_barrier((rows_cot, cot_other))
    hidden, d_gate, d_up, d_out, y_rows, dx_rows, sens_rows = expert_call(
        rows_in, rows_cot, gate, expert_gate, routed_up_weight, expert_down, nf // 2
    )

    gate_part = outer_call(rows_in, 0, d_gate)
    gate_sums = [wires.reduce_background(gate_part)]
    late_gates = [outer_call(rows_in, i, d_gate) for i in range(1, local_experts)]
    up_part = outer_call(rows_in, 0, d_up)
    gate_part, late_gates, up_part, hidden, sens_rows, y_rows, moe_other = lax.optimization_barrier(
        (gate_part, late_gates, up_part, hidden, sens_rows, y_rows, moe_other)
    )
    gate_sums += [wires.reduce_background(v) for v in late_gates]
    up_sums = [wires.reduce_background(up_part)]

    gate_grad = jnp.sum(jnp.where(pick, sens_rows, 0.0), axis=2)
    gate_grad = gate_grad.transpose(1, 0, 2).reshape(local_experts, count)
    prob_grad = sum(
        jnp.where(jnp.arange(experts)[None] == numbers[i], gate_grad[i][:, None], 0.0)
        for i in range(local_experts)
    )
    logit_grad = router_probs * (
        prob_grad - jnp.sum(prob_grad * router_probs, axis=-1, keepdims=True)
    )
    high = logit_grad.astype(BF16)
    lanes = jnp.concatenate([high, (logit_grad - high.astype(F32)).astype(BF16)], axis=1)
    router_rows = heads_rows[:experts]
    taken = (nf, local_experts * capacity, features)
    s_hidden, sd_gate, sd_up, sd_out, out_part, moe_part, gate_sens, *of_other = shared_call(
        moe_in,
        cot_all,
        opener,
        pick_b,
        y_rows.reshape(taken),
        dx_rows.reshape(taken),
        lanes,
        jnp.concatenate([router_rows, router_rows], axis=0),
        heads_rows[experts:].astype(F32),
        shared_gate,
        shared_up,
        shared_down,
        [moe_other, cot_other, heads_rows] if wires.fast else None,
    )
    sens_high = gate_sens.astype(BF16)
    sens_low = (gate_sens - sens_high.astype(F32)).astype(BF16)
    grad_heads = rows_dot(jnp.concatenate([lanes, sens_high, sens_low], axis=1), moe_in)
    grad_heads = jnp.concatenate(
        [
            grad_heads[:experts] + grad_heads[experts : 2 * experts],
            grad_heads[2 * experts : 2 * experts + 1] + grad_heads[2 * experts + 1 :],
        ],
        axis=0,
    )
    arrays = (rows_in, d_up, hidden, moe_in, sd_gate, sd_up, sd_out)
    if wires.fast:
        o_hidden, od_gate, od_up, od_out = of_other
        arrays += (moe_other, od_gate, od_up, s_hidden, od_out, o_hidden, d_out)
        later = {(13, 1, 1): (0, 1, 1), (2, 0, 1): (1, 0, 1)}
    else:
        arrays += (None, None, None, s_hidden, None, None, d_out)
        later = {}
    jobs = []
    for i in range(1, local_experts):
        jobs += [(((0, 1, i), (1, 0, i)),)]
    jobs += [(((13, 1, i), (2, 0, i)),) for i in range(local_experts)]

    def whole(*numbers):
        return tuple((n, None, 0) for n in numbers)

    if wires.fast:
        jobs += [(whole(3, 4), whole(7, 8)), (whole(3, 5), whole(7, 9)), (whole(6, 10), whole(11, 12))]
    else:
        jobs += [(whole(3, 4),), (whole(3, 5),), (whole(6, 10),)]
    grad_mixed, grad_gain_two, branch_grad, *parts = wires.middle(
        back_middle,
        moe_part,
        (mixed, gain_two, cotangent),
        (
            jax.ShapeDtypeStruct((rows_dev, features), F32),
            jax.ShapeDtypeStruct((wires.chunks, features), F32),
        ),
        True,
        3,
        arrays,
        jobs,
        later,
    )
    late = local_experts - 1
    parts, up_sums = lax.optimization_barrier((parts, up_sums))
    up_sums += [wires.reduce_background(v) for v in parts[:late]]
    down_parts, shared_parts = parts[late : late + local_experts], parts[late + local_experts :]
    branch_grad = branch_grad.reshape(count, features)
    grad_three, normed_part, grad_bias = attend_back_call(
        branch_grad, w_output, three, w_cols, cosine, sine, mark_cols, mark_rows
    )
    part_output = rows_dot(branch_grad, attended).astype(BF16)
    part_three = rows_dot(grad_three, normed).astype(BF16)

    vec = jnp.concatenate(
        [
            jnp.zeros_like(gain_one),
            jnp.sum(grad_gain_two, axis=0, keepdims=True),
            grad_heads,
        ],
        axis=0,
    )
    vec = jnp.pad(vec, ((0, 16 - vec.shape[0]), (0, 0)))
    bias_add = jnp.pad(grad_bias.reshape(3, width), ((experts + 3, 16 - experts - 6), (0, 0)))
    down_sums, shared_sums, four, output, grad_tokens, vec = wires.last_sums(
        down_parts,
        shared_parts,
        part_three,
        part_output,
        out_part,
        mixed,
        normed_part,
        tokens,
        grad_mixed,
        vec,
        gain_one,
        bias_add,
        5,
    )
    own = width // ng
    vec = lax.dynamic_slice_in_dim(vec, lax.axis_index("grp") * own, own, 1)
    return (
        output,
        grad_tokens,
        vec[0],
        four[0],
        four[1],
        four[2],
        vec[experts + 3],
        vec[experts + 4],
        vec[experts + 5],
        four[3],
        vec[1],
        vec[2 : experts + 2].T,
        vec[experts + 2],
        shared_sums[0],
        shared_sums[1],
        shared_sums[2],
        jnp.stack(gate_sums, axis=0).astype(F32),
        jnp.stack(up_sums, axis=0).astype(F32),
        down_sums,
    )


def solution(mesh):
    wires = Wires(mesh)

    def step(*args):
        return on_device(wires, *args)

    rows = P(("grp", "fsdp"))
    shard = P("fsdp")
    small = P(("fsdp", "grp"))
    return jax.shard_map(
        step,
        mesh=mesh,
        in_specs=(rows,) * 6
        + (shard,) * 11
        + (P(None, "fsdp"), P(None, "fsdp"), shard, shard, shard, shard),
        out_specs=(
            rows,
            rows,
            small,
            P("fsdp", "grp"),
            P("fsdp", "grp"),
            P("fsdp", "grp"),
            small,
            small,
            small,
            P("fsdp", "grp"),
            small,
            small,
            small,
            P("grp", "fsdp"),
            P("grp", "fsdp"),
            P("fsdp", "grp"),
            P("fsdp", "grp", None),
            P("fsdp", "grp", None),
            P("fsdp", None, "grp"),
        ),
        check_vma=False,
    )
```
